32 devices in a mesh: dom: 8 (over z, y), feat: 4 (over x, core).
Axes of the slice: x: 2, y: 2, z: 4, core: 2. Of those that a mesh axis runs over, the one named last changes fastest.
Arguments:
- features: bfloat16 [2048, 512], P('dom', 'feat'), may hold values from -6 to 6
- w_self: bfloat16 [512, 512], P('feat'), may hold values from -0.25 to 0.25
- w_neigh: bfloat16 [512, 512], P('feat'), may hold values from -0.25 to 0.25
- bias: bfloat16 [512], P('feat'), may hold values from -3 to 3
- cotangent: bfloat16 [2048, 512], P('dom', 'feat'), may hold values from -6 to 6
- tile_vals: bfloat16 [8, 4, 128, 128], P('dom'), may hold values from -0.375 to 0.375
- tile_pos: int32 [8, 4], P('dom'), may hold values from 0 to 3, as said below
- tile_count: int32 [8], P('dom'), may hold values from 1 to 4, as said below
- send_rows: int32 [8, 8, 48], P('dom'), may hold values from 0 to 255
- recv_dest: int32 [8, 8, 48], P('dom'), may hold values from 0 to 255
- ghost_weight: float32 [8, 8, 48], P('dom'), may hold values from 0.2 to 1.8
- recv_count: int32 [8, 8], P('dom'), may hold values from 0 to 48, as said below
- hub_rows: int32 [8, 2], P('dom'), may hold values from 0 to 255, as said below
- hub_weight: bfloat16 [2048, 16], P('dom'), may hold values from -1.5 to 1.5
Outputs:
- output: bfloat16 [2048, 512], P('dom', 'feat')
- grad_features: bfloat16 [2048, 512], P('dom', 'feat')
- grad_self: float32 [512, 512], P('feat')
- grad_neigh: float32 [512, 512], P('feat')
- grad_bias: float32 [512], P('feat')
The draws below stay inside these ranges and needn't reach their ends.
Inputs may be any that keep to these rules, and one draw needn't show every extreme that they name: `tile_pos`: within a partition the numbers are distinct. `tile_count`: some partition uses all 4 slots. `recv_count`: some partition receives 48 live slots from some peer. `hub_rows`: within a partition the rows are distinct.
All inputs are finite; a program needn't handle non-finite values.
Results may differ from the reference program's by a relative error of at most 0.017.
Values may be sent and summed in bfloat16 or wider, within the bound.
No kernel may reach another device: no remote copies, remote signals or barrier semaphores. Data moves between devices by JAX's collectives and lax.ppermute only.
A program may use at most 64 MiB of HBM per device.

```python
import math
import jax
import jax.numpy as jnp
from jax import lax

D = 512
TILE = 128
ROWS = 256
HUB_DEV = 2
DOMAINS = 8
NODES = 2048
BLOCKS = 2
TMAX = 4
SLOTS = 48
HUBS = 16


def draw_tile_pos(key, part):
    key = jax.random.fold_in(key, 11)
    keys = jax.random.split(key, DOMAINS)

    def one_domain(domain_key):
        return jax.random.permutation(domain_key, BLOCKS * BLOCKS)[:TMAX].astype(jnp.int32)
    return jax.vmap(one_domain)(keys)


def draw_tile_count(key, part):
    key = jax.random.fold_in(key, 12)
    key_counts, key_busy = jax.random.split(key)
    counts = jax.random.randint(key_counts, (DOMAINS,), TMAX // 4, TMAX // 2 + 1, dtype=jnp.int32)
    busiest = jax.random.randint(key_busy, (), 0, DOMAINS, dtype=jnp.int32)
    return counts.at[busiest].set(TMAX)


def draw_recv_count(key, part):
    key = jax.random.fold_in(key, 13)
    key_counts, key_busy = jax.random.split(key)
    counts = jax.random.randint(key_counts, (DOMAINS, DOMAINS), 0, SLOTS + 1, dtype=jnp.int32)
    busiest = jax.random.randint(key_busy, (2,), 0, DOMAINS, dtype=jnp.int32)
    return counts.at[busiest[0], busiest[1]].set(SLOTS)


def draw_hub_rows(key, part):
    key = jax.random.fold_in(key, 14)
    key_rows, key_pick = jax.random.split(key)
    keys = jax.random.split(key_rows, DOMAINS)
    top_domain = jax.random.randint(key_pick, (), 0, DOMAINS, dtype=jnp.int32)
    low_domain = (top_domain + 1) % DOMAINS

    def one_domain(domain_key, domain_index):
        drawn = jax.random.permutation(domain_key, ROWS)[:HUB_DEV].astype(jnp.int32)
        others = jax.random.permutation(domain_key, ROWS - 1)[:HUB_DEV - 1].astype(jnp.int32)
        with_top = jnp.concatenate([jnp.full((1,), ROWS - 1, jnp.int32), others])
        with_low = jnp.concatenate([jnp.zeros((1,), jnp.int32), others + 1])
        chosen = jnp.where(domain_index == top_domain, with_top, drawn)
        return jnp.where(domain_index == low_domain, with_low, chosen)
    return jax.vmap(one_domain)(keys, jnp.arange(DOMAINS, dtype=jnp.int32))


def with_ends(entries, key, low, high):
    extent = entries.shape
    spot = [jax.random.randint(jax.random.fold_in(key, axis), (), 0, extent[axis]) for axis in range(len(extent))]
    entries = entries.at[tuple(spot)].set(low)
    longest = extent.index(max(extent))
    spot[longest] = (spot[longest] + 1) % extent[longest]
    return entries.at[tuple(spot)].set(high)


def block_scale(key, dims, shards, smallest, largest):
    loudness = 1.0
    for axis_at, shards_of in shards:
        draws = jax.random.uniform(jax.random.fold_in(jax.random.fold_in(key, 6), axis_at), (shards_of,), jnp.float32, smallest / len(shards), largest / len(shards))
        loudness = loudness * jnp.repeat(jnp.exp(draws), dims[axis_at] // shards_of).reshape((-1,) + (1,) * (len(dims) - 1 - axis_at))
    return loudness


def normal_values(stream_key, shape, width, reach, cuts=(), kind=jnp.bfloat16):
    array = width * jax.random.normal(stream_key, shape, jnp.float32)
    if cuts:
        array = array * block_scale(stream_key, shape, cuts, -0.22, 0.18)
    return jnp.clip(array, -reach, reach).astype(kind)


def setup_inputs(seed: int = 0) -> dict:
    arg_keys = jax.random.split(jax.random.key(seed), 15)
    features = normal_values(arg_keys[0], (NODES, D), 1.0, 6.0, ((0, 8), (1, 4)))
    w_self = normal_values(arg_keys[1], (D, D), D ** -0.5, 0.25, ((0, 4),))
    w_neigh = normal_values(arg_keys[2], (D, D), D ** -0.5, 0.25, ((0, 4),))
    bias = normal_values(arg_keys[3], (D,), 0.5, 3.0, ((0, 4),))
    cotangent = normal_values(arg_keys[4], (NODES, D), 1.0, 6.0, ((0, 8), (1, 4)))
    tile_vals = normal_values(arg_keys[5], (DOMAINS, TMAX, TILE, TILE), (2 * TILE) ** -0.5, 0.375, ((0, 8),))
    tile_pos = draw_tile_pos(jax.random.fold_in(arg_keys[14], 71), 0)
    tile_count = draw_tile_count(jax.random.fold_in(arg_keys[14], 71), 0)
    send_rows = with_ends(jax.random.randint(arg_keys[8], (DOMAINS, DOMAINS, SLOTS), 0, ROWS), jax.random.fold_in(arg_keys[8], 1), 0, ROWS - 1).astype(jnp.int32)
    recv_dest = with_ends(jax.random.randint(arg_keys[9], (DOMAINS, DOMAINS, SLOTS), 0, ROWS), jax.random.fold_in(arg_keys[9], 1), 0, ROWS - 1).astype(jnp.int32)
    ghost_weight = jnp.clip(0.2 + 1.5999999 * jax.random.uniform(arg_keys[10], (DOMAINS, DOMAINS, SLOTS), jnp.float32) ** block_scale(arg_keys[10], (DOMAINS, DOMAINS, SLOTS), ((0, 8),), -0.2, 0.2), 0.2, 1.8)
    recv_count = draw_recv_count(jax.random.fold_in(arg_keys[14], 71), 0)
    hub_rows = draw_hub_rows(jax.random.fold_in(arg_keys[14], 71), 0)
    hub_weight = normal_values(arg_keys[13], (NODES, HUBS), HUBS ** -0.5, 1.5, ((0, 8),))
    return {"features": features, "w_self": w_self, "w_neigh": w_neigh, "bias": bias, "cotangent": cotangent, "tile_vals": tile_vals, "tile_pos": tile_pos, "tile_count": tile_count, "send_rows": send_rows, "recv_dest": recv_dest, "ghost_weight": ghost_weight, "recv_count": recv_count, "hub_rows": hub_rows, "hub_weight": hub_weight}


def ghost_coef(ghost_weight, recv_count):
    live = jnp.arange(SLOTS, dtype=jnp.int32)[None, None, :] < recv_count[:, :, None]
    return jnp.where(live, ghost_weight, jnp.zeros_like(ghost_weight))

def local_forward(tile_vals, tile_pos, tile_count, features):

    def per_domain(packed):
        tiles_here, places, count_here, rows_here = packed
        blocks = rows_here.reshape(BLOCKS, TILE, D).astype(jnp.float32)
        taken = blocks[places % BLOCKS]
        used = (jnp.arange(TMAX, dtype=jnp.int32) < count_here).astype(jnp.float32)
        product = jnp.einsum('tij,tjd->tid', tiles_here.astype(jnp.float32), taken) * used[:, None, None]
        summed = jax.ops.segment_sum(product, places // BLOCKS, num_segments=BLOCKS)
        return summed.reshape(ROWS, D)
    packed_all = (tile_vals, tile_pos, tile_count, features.reshape(DOMAINS, ROWS, D))
    return lax.map(per_domain, packed_all).reshape(NODES, D)

def local_backward(tile_vals, tile_pos, tile_count, neigh_grad):

    def per_domain(packed):
        tiles_here, places, count_here, rows_here = packed
        blocks = rows_here.reshape(BLOCKS, TILE, D).astype(jnp.float32)
        taken = blocks[places // BLOCKS]
        used = (jnp.arange(TMAX, dtype=jnp.int32) < count_here).astype(jnp.float32)
        product = jnp.einsum('tij,tid->tjd', tiles_here.astype(jnp.float32), taken) * used[:, None, None]
        summed = jax.ops.segment_sum(product, places % BLOCKS, num_segments=BLOCKS)
        return summed.reshape(ROWS, D)
    packed_all = (tile_vals, tile_pos, tile_count, neigh_grad.reshape(DOMAINS, ROWS, D))
    return lax.map(per_domain, packed_all).reshape(NODES, D)

def ghost_forward(features, send_rows, recv_dest, coef):
    senders = jnp.transpose(send_rows, (1, 0, 2))
    offsets = (jnp.arange(DOMAINS, dtype=jnp.int32) * ROWS)[:, None]

    def per_domain(packed):
        from_rows, dest_here, coef_here = packed
        pulled = features[(offsets + from_rows).astype(jnp.int32)].astype(jnp.float32)
        weighted = pulled * coef_here[:, :, None]
        return jax.ops.segment_sum(weighted.reshape(-1, D), dest_here.reshape(-1), num_segments=ROWS)
    return lax.map(per_domain, (senders, recv_dest, coef)).reshape(NODES, D)

def ghost_backward(neigh_grad, send_rows, recv_dest, coef):
    senders = jnp.transpose(send_rows, (1, 0, 2))
    offsets = (jnp.arange(DOMAINS, dtype=jnp.int32) * ROWS)[:, None]

    def step_domain(totals, packed):
        from_rows, dest_here, coef_here, grad_here = packed
        values = grad_here[dest_here].astype(jnp.float32) * coef_here[:, :, None]
        targets = (offsets + from_rows).astype(jnp.int32).reshape(-1)
        return (totals.at[targets].add(values.reshape(-1, D)), None)
    packed_all = (senders, recv_dest, coef, neigh_grad.reshape(DOMAINS, ROWS, D))
    totals, _ = lax.scan(step_domain, jnp.zeros((NODES, D), jnp.float32), packed_all)
    return totals

def reference(features, w_self, w_neigh, bias, cotangent, tile_vals, tile_pos, tile_count, send_rows, recv_dest, ghost_weight, recv_count, hub_rows, hub_weight):
    coef = ghost_coef(ghost_weight, recv_count)
    local_part = local_forward(tile_vals, tile_pos, tile_count, features)
    ghost_part = ghost_forward(features, send_rows, recv_dest, coef)
    hub_ids = (jnp.arange(DOMAINS, dtype=jnp.int32)[:, None] * ROWS + hub_rows).astype(jnp.int32).reshape(-1)
    hub_part = jnp.dot(hub_weight, features[hub_ids], preferred_element_type=jnp.float32)
    neigh = (local_part + ghost_part + hub_part).astype(jnp.bfloat16)
    preact = jnp.dot(features, w_self, preferred_element_type=jnp.float32) + jnp.dot(neigh, w_neigh, preferred_element_type=jnp.float32) + bias.astype(jnp.float32)
    output = jax.nn.silu(preact).astype(jnp.bfloat16)
    logistic = jax.nn.sigmoid(preact)
    grad_pre = (cotangent.astype(jnp.float32) * logistic * (1.0 + preact * (1.0 - logistic))).astype(jnp.bfloat16)
    neigh_grad = jnp.dot(grad_pre, w_neigh.T, preferred_element_type=jnp.float32).astype(jnp.bfloat16)
    hub_grad = jnp.dot(hub_weight.T, neigh_grad, preferred_element_type=jnp.float32)
    hub_back = jnp.zeros((NODES, D), jnp.float32).at[hub_ids].add(hub_grad)
    grad_total = jnp.dot(grad_pre, w_self.T, preferred_element_type=jnp.float32)
    grad_total = grad_total + local_backward(tile_vals, tile_pos, tile_count, neigh_grad)
    grad_total = grad_total + ghost_backward(neigh_grad, send_rows, recv_dest, coef) + hub_back
    grad_features = grad_total.astype(jnp.bfloat16)
    scale = 1.0 / math.sqrt(NODES)
    grad_self = jnp.dot(features.T, grad_pre, preferred_element_type=jnp.float32) * scale
    grad_neigh = jnp.dot(neigh.T, grad_pre, preferred_element_type=jnp.float32) * scale
    grad_bias = lax.optimization_barrier(jnp.sum(grad_pre.astype(jnp.float32), axis=0)) * scale
    return (output, grad_features, grad_self, grad_neigh, grad_bias)
```

```python
import functools
import math

import jax
import jax.numpy as jnp
from jax import lax
from jax.experimental import pallas as pl
from jax.experimental.pallas import tpu as pltpu
from jax.sharding import PartitionSpec as P

BF = jnp.bfloat16
F32 = jnp.float32


def spread_rows(table, width):
    peers, slots = table.shape
    lanes = peers * width
    lane = lax.broadcasted_iota(jnp.int32, (slots, lanes), 1)
    slot = lax.broadcasted_iota(jnp.int32, (slots, lanes), 0)
    place = jnp.where(lane % width == slot, 1.0, 0.0).astype(BF)
    wide = jnp.dot(table.astype(BF), place, preferred_element_type=F32)
    peer = lax.broadcasted_iota(jnp.int32, (peers, lanes), 0)
    at = lax.broadcasted_iota(jnp.int32, (peers, lanes), 1)
    return jnp.sum(jnp.where(at // width == peer, wide, 0.0), axis=0, keepdims=True)


def source_matrix(send, hubs, rows, width):
    peers, slots = send.shape
    hub_here = hubs.shape[1]
    lanes = peers * width
    lane = lax.broadcasted_iota(jnp.int32, (1, lanes), 1) % width
    index = spread_rows(send.astype(F32), width)
    for k in range(hub_here):
        index = jnp.where(lane == slots + k, hubs[0:1, k : k + 1].astype(F32), index)
    index = jnp.where(lane < slots + hub_here, index, -1.0)
    row = lax.broadcasted_iota(jnp.int32, (rows, lanes), 0).astype(F32)
    return jnp.where(row == index, 1.0, 0.0).astype(BF)


def send_kernel(width, x_ref, cot_ref, ws_ref, wn_ref, bias_ref, send_ref, hub_ref, out_ref, pack_ref):
    rows, cols = x_ref.shape
    depth, full = ws_ref.shape
    mark = source_matrix(send_ref[0], hub_ref[...], rows, width)
    taken = lax.dot_general(
        mark, x_ref[...], (((0,), (0,)), ((), ())), preferred_element_type=F32
    ).astype(BF)
    out_ref[...] = taken.reshape(out_ref.shape)
    blocks = full // cols
    for j in range(blocks):
        pack_ref[j * depth : (j + 1) * depth, :] = ws_ref[:, j * cols : (j + 1) * cols]
        pack_ref[(blocks + j) * depth : (blocks + j + 1) * depth, :] = wn_ref[:, j * cols : (j + 1) * cols]
    base = 2 * blocks * depth
    pack_ref[base : base + rows, :] = x_ref[...]
    pack_ref[base + rows : base + 2 * rows, :] = cot_ref[...]
    pack_ref[base + 2 * rows :, :] = jnp.broadcast_to(bias_ref[...], (16, cols))


def neigh_kernel(
    width, pos_ref, count_ref, live_ref, x_ref, got_ref, tile_ref, dest_ref, gw_ref, hw_ref, mix_ref, neigh_ref
):
    rows, cols = x_ref.shape
    tile = tile_ref.shape[-1]
    tiles = tile_ref.shape[1]
    peers, slots = dest_ref.shape[1:]
    side = rows // tile
    lanes = peers * width
    hubs = hw_ref.shape[1]
    hub_here = hubs // peers
    for r in range(side):
        for c in range(side):
            total = jnp.zeros((tile, tile), BF)
            for t in range(tiles):
                used = jnp.logical_and(pos_ref[0, t] == r * side + c, t < count_ref[0])
                total = jnp.where(used, tile_ref[0, t], total)
            mix_ref[r * tile : (r + 1) * tile, c * tile : (c + 1) * tile] = total
    dest = spread_rows(dest_ref[0].astype(F32), width)
    coef = spread_rows(gw_ref[0], width)
    lane = lax.broadcasted_iota(jnp.int32, (1, lanes), 1)
    limit = jnp.zeros((1, lanes), jnp.int32)
    for q in range(peers):
        limit = jnp.where(lane // width == q, live_ref[0, q], limit)
    coef = jnp.where(lane % width < jnp.minimum(limit, slots), coef, 0.0)
    row = lax.broadcasted_iota(jnp.int32, (rows, lanes), 0).astype(F32)
    ghost = jnp.where(row == dest, coef, 0.0)
    hub = lax.broadcasted_iota(jnp.int32, (hubs, lanes), 0)
    at = lax.broadcasted_iota(jnp.int32, (hubs, lanes), 1)
    place = jnp.where(
        jnp.logical_and(at // width == hub // hub_here, at % width == slots + hub % hub_here), 1.0, 0.0
    ).astype(BF)
    hub_mix = jnp.dot(hw_ref[...], place, preferred_element_type=F32)
    far = (ghost + hub_mix).astype(BF)
    mix_ref[:, rows:] = far
    total = jnp.dot(mix_ref[:, :rows], x_ref[...], preferred_element_type=F32)
    total = total + jnp.dot(far, got_ref[...].reshape(lanes, cols), preferred_element_type=F32)
    neigh_ref[...] = total.astype(BF)


def dense_kernel(
    slots, hub_here, me_ref, x_ref, ws_ref, wn_ref, p0_ref, p1_ref, p2_ref, p3_ref, n_ref, mix_ref,
    out_ref, back_ref, send_ref, pre_ref, cot_ref, bias_ref,
):
    rows, cols = x_ref.shape
    depth, full = ws_ref.shape
    blocks = full // cols
    peers, height = send_ref.shape[:2]
    lanes = mix_ref.shape[1] - rows
    width = lanes // peers
    me = me_ref[0]
    base = 2 * blocks * depth
    pre = jnp.zeros((rows, full), F32)
    for d, pack in enumerate((p0_ref, p1_ref, p2_ref, p3_ref)):
        owner = me ^ d
        cut = pl.ds(pl.multiple_of(owner * cols, cols), cols)
        cot_ref[:, cut] = pack[base + rows : base + 2 * rows, :]
        bias_ref[:, cut] = pack[base + 2 * rows : base + 2 * rows + 16, :]
        w_s = jnp.concatenate([pack[j * depth : (j + 1) * depth, :] for j in range(blocks)], axis=1)
        w_n = jnp.concatenate([pack[(blocks + j) * depth : (blocks + j + 1) * depth, :] for j in range(blocks)], axis=1)
        left = jnp.concatenate([pack[base : base + rows, :], n_ref[owner]], axis=1)
        right = jnp.concatenate([w_s, w_n], axis=0)
        pre = pre + jnp.dot(left, right, preferred_element_type=F32)
    pre = pre + bias_ref[0:1, :].astype(F32)
    pre_ref[...] = pre
    sig = jax.nn.sigmoid(pre)
    grad = (cot_ref[...].astype(F32) * sig * (1.0 + pre * (1.0 - sig))).astype(BF)
    cot_ref[...] = grad
    mine = pl.ds(pl.multiple_of(me * cols, cols), cols)
    own = pre_ref[:, mine]
    out_ref[...] = (own * jax.nn.sigmoid(own)).astype(BF)
    both = jnp.concatenate([ws_ref[...], wn_ref[...]], axis=0)
    into = lax.dot_general(grad, both, (((1,), (1,)), ((), ())), preferred_element_type=F32)
    neigh_grad = into[:, depth:].astype(BF)
    spread = lax.dot_general(
        mix_ref[...], neigh_grad, (((0,), (0,)), ((), ())), preferred_element_type=F32
    )
    back_ref[...] = into[:, :depth] + spread[:rows]
    sums = jnp.sum(cot_ref[:, mine].astype(F32), axis=0, keepdims=True)
    high = sums.astype(BF).astype(F32)
    line = lax.broadcasted_iota(jnp.int32, (lanes, cols), 0) % width
    away = jnp.where(line == slots + hub_here, high, spread[rows:])
    away = jnp.where(line == slots + hub_here + 1, sums - high, away)
    send_ref[:, :width, :] = away.astype(BF).reshape(peers, width, cols)
    pair = jnp.concatenate([x_ref[...], n_ref[me]], axis=1)
    weights = lax.dot_general(pair, grad, (((0,), (0,)), ((), ())), preferred_element_type=F32).astype(BF)
    share = height - width
    for j in range(blocks):
        for kind in range(2):
            block = weights[kind * depth : (kind + 1) * depth, j * cols : (j + 1) * cols]
            at = (j * 2 + kind) * depth
            for part in range(depth // share):
                send_ref[at // share + part, width:, :] = block[part * share : (part + 1) * share]


def gather_kernel(scale, slots, width, got_ref, back_ref, send_ref, hub_ref, grad_ref, bias_ref, part_ref):
    rows, cols = back_ref.shape
    peers = got_ref.shape[0]
    hub_here = hub_ref.shape[1]
    mark = source_matrix(send_ref[0], hub_ref[...], rows, width)
    near = got_ref[:, :width, :]
    total = back_ref[...] + jnp.dot(mark, near.reshape(peers * width, cols), preferred_element_type=F32)
    grad_ref[...] = total.astype(BF)
    first = slots + hub_here
    bias = jnp.zeros((2, cols), F32)
    share = jnp.zeros(part_ref.shape[1:], F32)
    for q in range(peers):
        bias = bias + got_ref[q, first : first + 2, :].astype(F32)
        share = share + got_ref[q, width:, :].astype(F32)
    bias_ref[...] = jnp.sum(bias, axis=0, keepdims=True) * scale
    part_ref[...] = jnp.broadcast_to(share.astype(BF), part_ref.shape)


def spread_kernel(scale, got_ref, self_ref, neigh_ref):
    depth, full = self_ref.shape
    peers, share, cols = got_ref.shape
    whole = got_ref[...].reshape(peers * share, cols).astype(F32) * scale
    for j in range(full // cols):
        at = 2 * j * depth
        self_ref[:, j * cols : (j + 1) * cols] = whole[at : at + depth]
        neigh_ref[:, j * cols : (j + 1) * cols] = whole[at + depth : at + 2 * depth]


VMEM = pl.BlockSpec(memory_space=pltpu.VMEM)
SMEM = pl.BlockSpec(memory_space=pltpu.SMEM)
PARAMS = pltpu.CompilerParams(vmem_limit_bytes=40 * 1024 * 1024)


def shape(dims, kind):
    return jax.ShapeDtypeStruct(dims, kind)


def on_device(
    features,
    w_self,
    w_neigh,
    bias,
    cotangent,
    tile_vals,
    tile_pos,
    tile_count,
    send_rows,
    recv_dest,
    ghost_weight,
    recv_count,
    hub_rows,
    hub_weight,
):
    rows, cols = features.shape
    depth, full = w_self.shape
    blocks = full // cols
    peers, slots = send_rows.shape[1:]
    hub_here = hub_rows.shape[-1]
    width = -(-(slots + hub_here + 2) // 16) * 16
    lanes = peers * width
    share = 2 * blocks * depth // peers
    scale = 1.0 / math.sqrt(peers * rows)
    feats = lax.axis_size("feat")
    me = lax.axis_index("feat").astype(jnp.int32).reshape(1)

    outgoing, pack = pl.pallas_call(
        functools.partial(send_kernel, width),
        out_shape=(
            shape((peers, width, cols), BF),
            shape((2 * blocks * depth + 2 * rows + 16, cols), BF),
        ),
        in_specs=[VMEM] * 7,
        out_specs=(VMEM, VMEM),
        compiler_params=PARAMS,
    )(features, cotangent, w_self, w_neigh, bias.reshape(1, cols), send_rows, hub_rows)

    far = lax.ppermute(pack, "feat", [(i, i ^ 2) for i in range(feats)])
    near = lax.ppermute(pack, "feat", [(i, i ^ 1) for i in range(feats)])
    last = lax.ppermute(far, "feat", [(i, i ^ 1) for i in range(feats)])

    incoming = lax.all_to_all(outgoing, "dom", split_axis=0, concat_axis=0, tiled=True)
    mix, neigh = pl.pallas_call(
        functools.partial(neigh_kernel, width),
        out_shape=(shape((rows, rows + lanes), BF), shape((rows, cols), BF)),
        in_specs=[SMEM] * 3 + [VMEM] * 6,
        out_specs=(VMEM, VMEM),
        compiler_params=PARAMS,
    )(tile_pos, tile_count, recv_count, features, incoming, tile_vals, recv_dest, ghost_weight, hub_weight)
    every = lax.all_gather(neigh, "feat", axis=0, tiled=False)

    output, back, returned = pl.pallas_call(
        functools.partial(dense_kernel, slots, hub_here),
        out_shape=(
            shape((rows, cols), BF),
            shape((rows, cols), F32),
            shape((peers, width + share, cols), BF),
        ),
        in_specs=[SMEM] + [VMEM] * 9,
        out_specs=(VMEM,) * 3,
        scratch_shapes=[
            pltpu.VMEM((rows, full), F32),
            pltpu.VMEM((rows, full), BF),
            pltpu.VMEM((16, full), BF),
        ],
        compiler_params=PARAMS,
    )(me, features, w_self, w_neigh, pack, near, far, last, every, mix)

    arrived = lax.all_to_all(returned, "dom", split_axis=0, concat_axis=0, tiled=True)
    grad_features, grad_bias, parts = pl.pallas_call(
        functools.partial(gather_kernel, scale, slots, width),
        out_shape=(
            shape((rows, cols), BF),
            shape((1, cols), F32),
            shape((peers, share, cols), BF),
        ),
        in_specs=[VMEM] * 4,
        out_specs=(VMEM,) * 3,
        compiler_params=PARAMS,
    )(arrived, back, send_rows, hub_rows)
    whole = lax.all_to_all(parts, "dom", split_axis=0, concat_axis=0, tiled=True)
    grad_self, grad_neigh = pl.pallas_call(
        functools.partial(spread_kernel, scale),
        out_shape=(shape((depth, full), F32), shape((depth, full), F32)),
        in_specs=[VMEM],
        out_specs=(VMEM, VMEM),
        compiler_params=PARAMS,
    )(whole)
    return output, grad_features, grad_self, grad_neigh, grad_bias.reshape(cols)


def solution(mesh):
    placed = (
        P("dom", "feat"),
        P("feat", None),
        P("feat", None),
        P("feat"),
        P("dom", "feat"),
        P("dom", None, None, None),
        P("dom", None),
        P("dom"),
        P("dom", None, None),
        P("dom", None, None),
        P("dom", None, None),
        P("dom", None),
        P("dom", None),
        P("dom", None),
    )
    return jax.shard_map(
        on_device,
        mesh=mesh,
        in_specs=placed,
        out_specs=(P("dom", "feat"), P("dom", "feat"), P("feat", None), P("feat", None), P("feat")),
        check_vma=False,
    )
```

```python
import functools
import math

import jax
import jax.numpy as jnp
from jax import lax
from jax.experimental import pallas as pl
from jax.experimental.pallas import tpu as pltpu
from jax.sharding import PartitionSpec as P

BF = jnp.bfloat16
F32 = jnp.float32


def spread_rows(table, width):
    peers, slots = table.shape
    lanes = peers * width
    lane = lax.broadcasted_iota(jnp.int32, (slots, lanes), 1)
    slot = lax.broadcasted_iota(jnp.int32, (slots, lanes), 0)
    place = jnp.where(lane % width == slot, 1.0, 0.0).astype(BF)
    wide = jnp.dot(table.astype(BF), place, preferred_element_type=F32)
    peer = lax.broadcasted_iota(jnp.int32, (peers, lanes), 0)
    at = lax.broadcasted_iota(jnp.int32, (peers, lanes), 1)
    return jnp.sum(jnp.where(at // width == peer, wide, 0.0), axis=0, keepdims=True)


def source_matrix(send, hubs, rows, width):
    peers, slots = send.shape
    hub_here = hubs.shape[1]
    lanes = peers * width
    lane = lax.broadcasted_iota(jnp.int32, (1, lanes), 1) % width
    index = spread_rows(send.astype(F32), width)
    for k in range(hub_here):
        index = jnp.where(lane == slots + k, hubs[0:1, k : k + 1].astype(F32), index)
    index = jnp.where(lane < slots + hub_here, index, -1.0)
    row = lax.broadcasted_iota(jnp.int32, (rows, lanes), 0).astype(F32)
    return jnp.where(row == index, 1.0, 0.0).astype(BF)


def ordered(refs, hold_ref, me):
    if len(refs) == 1:
        return refs[0]
    for k, ref in enumerate(refs):
        hold_ref[me ^ k] = ref[...]
    return hold_ref


def routed(refs, hold_ref, me):
    if len(refs) > 1:
        for k, ref in enumerate(refs):
            ref[...] = hold_ref[me ^ k]


def send_kernel(width, count, me_ref, *refs):
    x_ref, cot_ref, ws_ref, wn_ref, bias_ref, send_ref, hub_ref = refs[:7]
    out_refs, pack_ref = refs[7 : 7 + count], refs[7 + count]
    hold_ref, send_v, hub_v, bias_v, sems = refs[8 + count :]
    rows, cols = x_ref.shape
    depth, full = ws_ref.shape
    blocks = full // cols
    base = 2 * blocks * depth
    moves = [
        (send_ref, send_v),
        (hub_ref, hub_v),
        (x_ref, pack_ref.at[base : base + rows, :]),
        (bias_ref, bias_v),
        (cot_ref, pack_ref.at[base + rows : base + 2 * rows, :]),
    ]
    for kind, w_ref in enumerate((ws_ref, wn_ref)):
        for j in range(blocks):
            at = (kind * blocks + j) * depth
            moves.append((w_ref.at[:, j * cols : (j + 1) * cols], pack_ref.at[at : at + depth, :]))
    copies = [pltpu.make_async_copy(src, dst, sems.at[i]) for i, (src, dst) in enumerate(moves)]
    for copy in copies:
        copy.start()
    for copy in copies[:3]:
        copy.wait()
    mark = source_matrix(send_v[0], hub_v[...], rows, width)
    taken = lax.dot_general(
        mark, pack_ref[base : base + rows, :], (((0,), (0,)), ((), ())), preferred_element_type=F32
    ).astype(BF)
    target = out_refs[0] if count == 1 else hold_ref
    target[...] = taken.reshape(target.shape)
    routed(out_refs, hold_ref, me_ref[0])
    for copy in copies[3:]:
        copy.wait()
    pack_ref[base + 2 * rows :, :] = jnp.broadcast_to(bias_v[...], (16, cols))


def neigh_kernel(width, me_ref, pos_ref, count_ref, live_ref, x_ref, tile_ref, dest_ref, gw_ref, hw_ref, far_ref, *refs):
    got_refs, (mix_ref, neigh_ref, passed_ref, hold_ref) = refs[:-4], refs[-4:]
    rows, cols = x_ref.shape
    tile = tile_ref.shape[-1]
    tiles = tile_ref.shape[1]
    peers, slots = dest_ref.shape[1:]
    side = rows // tile
    lanes = peers * width
    hubs = hw_ref.shape[1]
    hub_here = hubs // peers
    for r in range(side):
        for c in range(side):
            total = jnp.zeros((tile, tile), BF)
            for t in range(tiles):
                used = jnp.logical_and(pos_ref[0, t] == r * side + c, t < count_ref[0])
                total = jnp.where(used, tile_ref[0, t], total)
            mix_ref[r * tile : (r + 1) * tile, c * tile : (c + 1) * tile] = total
    dest = spread_rows(dest_ref[0].astype(F32), width)
    coef = spread_rows(gw_ref[0], width)
    lane = lax.broadcasted_iota(jnp.int32, (1, lanes), 1)
    limit = jnp.zeros((1, lanes), jnp.int32)
    for q in range(peers):
        limit = jnp.where(lane // width == q, live_ref[0, q], limit)
    coef = jnp.where(lane % width < jnp.minimum(limit, slots), coef, 0.0)
    row = lax.broadcasted_iota(jnp.int32, (rows, lanes), 0).astype(F32)
    ghost = jnp.where(row == dest, coef, 0.0)
    hub = lax.broadcasted_iota(jnp.int32, (hubs, lanes), 0)
    at = lax.broadcasted_iota(jnp.int32, (hubs, lanes), 1)
    place = jnp.where(
        jnp.logical_and(at // width == hub // hub_here, at % width == slots + hub % hub_here), 1.0, 0.0
    ).astype(BF)
    hub_mix = jnp.dot(hw_ref[...], place, preferred_element_type=F32)
    far = (ghost + hub_mix).astype(BF)
    mix_ref[:, rows:] = far
    near = ordered(got_refs, hold_ref, me_ref[0])[...]
    total = jnp.dot(mix_ref[:, :rows], x_ref[...], preferred_element_type=F32)
    total = total + jnp.dot(far, near.reshape(lanes, cols), preferred_element_type=F32)
    neigh_ref[...] = total.astype(BF)


def dense_kernel(slots, hub_here, feats, count, dom_ref, me_ref, x_ref, ws_ref, wn_ref, mix_ref, *refs):
    pack_refs, n_refs = refs[:feats], refs[feats : 2 * feats]
    out_ref, back_ref = refs[2 * feats : 2 * feats + 2]
    send_refs = refs[2 * feats + 2 : 2 * feats + 2 + count]
    hold_ref, pre_ref, cot_ref, bias_ref = refs[2 * feats + 2 + count :]
    send_ref = send_refs[0] if count == 1 else hold_ref
    rows, cols = x_ref.shape
    depth, full = ws_ref.shape
    blocks = full // cols
    peers, height = send_ref.shape[:2]
    lanes = mix_ref.shape[1] - rows
    width = lanes // peers
    me = me_ref[0]
    base = 2 * blocks * depth
    pre = jnp.zeros((rows, full), F32)
    for d, pack in enumerate(pack_refs):
        owner = me ^ d
        cut = pl.ds(pl.multiple_of(owner * cols, cols), cols)
        cot_ref[:, cut] = pack[base + rows : base + 2 * rows, :]
        bias_ref[:, cut] = pack[base + 2 * rows : base + 2 * rows + 16, :]
        w_s = jnp.concatenate([pack[j * depth : (j + 1) * depth, :] for j in range(blocks)], axis=1)
        w_n = jnp.concatenate([pack[(blocks + j) * depth : (blocks + j + 1) * depth, :] for j in range(blocks)], axis=1)
        left = jnp.concatenate([pack[base : base + rows, :], n_refs[d][...]], axis=1)
        right = jnp.concatenate([w_s, w_n], axis=0)
        pre = pre + jnp.dot(left, right, preferred_element_type=F32)
    pre = pre + bias_ref[0:1, :].astype(F32)
    pre_ref[...] = pre
    sig = jax.nn.sigmoid(pre)
    grad = (cot_ref[...].astype(F32) * sig * (1.0 + pre * (1.0 - sig))).astype(BF)
    cot_ref[...] = grad
    mine = pl.ds(pl.multiple_of(me * cols, cols), cols)
    own = pre_ref[:, mine]
    out_ref[...] = (own * jax.nn.sigmoid(own)).astype(BF)
    both = jnp.concatenate([ws_ref[...], wn_ref[...]], axis=0)
    into = lax.dot_general(grad, both, (((1,), (1,)), ((), ())), preferred_element_type=F32)
    neigh_grad = into[:, depth:].astype(BF)
    spread = lax.dot_general(
        mix_ref[...], neigh_grad, (((0,), (0,)), ((), ())), preferred_element_type=F32
    )
    back_ref[...] = into[:, :depth] + spread[:rows]
    sums = jnp.sum(cot_ref[:, mine].astype(F32), axis=0, keepdims=True)
    high = sums.astype(BF).astype(F32)
    line = lax.broadcasted_iota(jnp.int32, (lanes, cols), 0) % width
    away = jnp.where(line == slots + hub_here, high, spread[rows:])
    away = jnp.where(line == slots + hub_here + 1, sums - high, away)
    send_ref[:, :width, :] = away.astype(BF).reshape(peers, width, cols)
    pair = jnp.concatenate([x_ref[...], n_refs[0][...]], axis=1)
    weights = lax.dot_general(pair, grad, (((0,), (0,)), ((), ())), preferred_element_type=F32).astype(BF)
    share = height - width
    for j in range(blocks):
        for kind in range(2):
            block = weights[kind * depth : (kind + 1) * depth, j * cols : (j + 1) * cols]
            at = (j * 2 + kind) * depth
            for part in range(depth // share):
                send_ref[at // share + part, width:, :] = block[part * share : (part + 1) * share]
    routed(send_refs, hold_ref, dom_ref[0])


def gather_kernel(scale, slots, width, me_ref, back_ref, send_ref, hub_ref, *refs):
    got_refs, (grad_ref, bias_ref, part_ref, hold_ref) = refs[:-4], refs[-4:]
    rows, cols = back_ref.shape
    peers = send_ref.shape[1]
    hub_here = hub_ref.shape[1]
    mark = source_matrix(send_ref[0], hub_ref[...], rows, width)
    got_ref = ordered(got_refs, hold_ref, me_ref[0])
    near = got_ref[:, :width, :]
    total = back_ref[...] + jnp.dot(mark, near.reshape(peers * width, cols), preferred_element_type=F32)
    grad_ref[...] = total.astype(BF)
    first = slots + hub_here
    bias = jnp.zeros((2, cols), F32)
    share = jnp.zeros(part_ref.shape[-2:], F32)
    for q in range(peers):
        bias = bias + got_ref[q, first : first + 2, :].astype(F32)
        share = share + got_ref[q, width:, :].astype(F32)
    bias_ref[...] = jnp.sum(bias, axis=0, keepdims=True) * scale
    part_ref[...] = jnp.broadcast_to(share.astype(BF), part_ref.shape)


def spread_kernel(scale, me_ref, *refs):
    got_refs, (self_ref, neigh_ref, hold_ref) = refs[:-3], refs[-3:]
    depth, full = self_ref.shape
    got_ref = ordered(got_refs, hold_ref, me_ref[0])
    peers, share, cols = got_ref.shape
    whole = got_ref[...].reshape(peers * share, cols).astype(F32) * scale
    for j in range(full // cols):
        at = 2 * j * depth
        self_ref[:, j * cols : (j + 1) * cols] = whole[at : at + depth]
        neigh_ref[:, j * cols : (j + 1) * cols] = whole[at + depth : at + 2 * depth]


VMEM = pl.BlockSpec(memory_space=pltpu.VMEM)
SMEM = pl.BlockSpec(memory_space=pltpu.SMEM)
ANY = pl.BlockSpec(memory_space=pl.ANY)
PARAMS = pltpu.CompilerParams(vmem_limit_bytes=40 * 1024 * 1024)
DIRECT = 8


def shape(dims, kind):
    return jax.ShapeDtypeStruct(dims, kind)


def partner(block, axis, k):
    return lax.ppermute(block, axis, [(i, i ^ k) for i in range(lax.axis_size(axis))])


def exchange(blocks, axis):
    if len(blocks) == 1:
        return [lax.all_to_all(blocks[0], axis, split_axis=0, concat_axis=0, tiled=True)]
    return [blocks[0]] + [partner(block, axis, k) for k, block in enumerate(blocks) if k]


def on_device(
    features,
    w_self,
    w_neigh,
    bias,
    cotangent,
    tile_vals,
    tile_pos,
    tile_count,
    send_rows,
    recv_dest,
    ghost_weight,
    recv_count,
    hub_rows,
    hub_weight,
):
    rows, cols = features.shape
    depth, full = w_self.shape
    blocks = full // cols
    peers, slots = send_rows.shape[1:]
    hub_here = hub_rows.shape[-1]
    width = -(-(slots + hub_here + 2) // 16) * 16
    lanes = peers * width
    share = 2 * blocks * depth // peers
    scale = 1.0 / math.sqrt(peers * rows)
    feats = lax.axis_size("feat")
    me = lax.axis_index("feat").astype(jnp.int32).reshape(1)
    dom = lax.axis_index("dom").astype(jnp.int32).reshape(1)
    direct = peers <= DIRECT
    count = peers if direct else 1

    def stacked(height):
        return [shape((height, cols), BF)] * peers if direct else [shape((peers, height, cols), BF)]

    def hold(height):
        return pltpu.VMEM((peers, height, cols) if direct else (1, 16, cols), BF)

    pack_rows = 2 * blocks * depth + 2 * rows + 16
    *outgoing, pack = pl.pallas_call(
        functools.partial(send_kernel, width, count),
        out_shape=(*stacked(width), shape((pack_rows, cols), BF)),
        in_specs=[SMEM] + [ANY] * 7,
        out_specs=(VMEM,) * (count + 1),
        scratch_shapes=[
            hold(width),
            pltpu.VMEM(send_rows.shape, jnp.int32),
            pltpu.VMEM(hub_rows.shape, jnp.int32),
            pltpu.VMEM((1, cols), BF),
            pltpu.SemaphoreType.DMA((5 + 2 * blocks,)),
        ],
        compiler_params=PARAMS,
    )(dom, features, cotangent, w_self, w_neigh, bias.reshape(1, cols), send_rows, hub_rows)

    incoming = exchange(outgoing, "dom")
    far = partner(pack, "feat", 2)
    near = partner(pack, "feat", 1)
    mix, neigh, far = pl.pallas_call(
        functools.partial(neigh_kernel, width),
        out_shape=(shape((rows, rows + lanes), BF), shape((rows, cols), BF), shape((pack_rows, cols), BF)),
        in_specs=[SMEM] * 4 + [VMEM] * 5 + [ANY] + [VMEM] * count,
        out_specs=(VMEM, VMEM, ANY),
        scratch_shapes=[hold(width)],
        input_output_aliases={9: 2},
        compiler_params=PARAMS,
    )(dom, tile_pos, tile_count, recv_count, features, tile_vals, recv_dest, ghost_weight, hub_weight, far, *incoming)
    last = partner(far, "feat", 1)
    every = [neigh] + [partner(neigh, "feat", k) for k in range(1, feats)]

    output, back, *returned = pl.pallas_call(
        functools.partial(dense_kernel, slots, hub_here, feats, count),
        out_shape=(
            shape((rows, cols), BF),
            shape((rows, cols), F32),
            *stacked(width + share),
        ),
        in_specs=[SMEM] * 2 + [VMEM] * (4 + 2 * feats),
        out_specs=(VMEM,) * (2 + count),
        scratch_shapes=[
            hold(width + share),
            pltpu.VMEM((rows, full), F32),
            pltpu.VMEM((rows, full), BF),
            pltpu.VMEM((16, full), BF),
        ],
        compiler_params=PARAMS,
    )(dom, me, features, w_self, w_neigh, mix, pack, near, far, last, *every)

    arrived = exchange(returned, "dom")
    grad_features, grad_bias, part = pl.pallas_call(
        functools.partial(gather_kernel, scale, slots, width),
        out_shape=(
            shape((rows, cols), BF),
            shape((1, cols), F32),
            shape((share, cols) if direct else (peers, share, cols), BF),
        ),
        in_specs=[SMEM] + [VMEM] * (3 + count),
        out_specs=(VMEM,) * 3,
        scratch_shapes=[hold(width + share)],
        compiler_params=PARAMS,
    )(dom, back, send_rows, hub_rows, *arrived)
    parts = exchange([part] * count, "dom")
    grad_self, grad_neigh = pl.pallas_call(
        functools.partial(spread_kernel, scale),
        out_shape=(shape((depth, full), F32), shape((depth, full), F32)),
        in_specs=[SMEM] + [VMEM] * count,
        out_specs=(VMEM, VMEM),
        scratch_shapes=[hold(share)],
        compiler_params=PARAMS,
    )(dom, *parts)
    return output, grad_features, grad_self, grad_neigh, grad_bias.reshape(cols)


def solution(mesh):
    placed = (
        P("dom", "feat"),
        P("feat", None),
        P("feat", None),
        P("feat"),
        P("dom", "feat"),
        P("dom", None, None, None),
        P("dom", None),
        P("dom"),
        P("dom", None, None),
        P("dom", None, None),
        P("dom", None, None),
        P("dom", None),
        P("dom", None),
        P("dom", None),
    )
    return jax.shard_map(
        on_device,
        mesh=mesh,
        in_specs=placed,
        out_specs=(P("dom", "feat"), P("dom", "feat"), P("feat", None), P("feat", None), P("feat")),
        check_vma=False,
    )
```

```python
import functools
import math

import jax
import jax.numpy as jnp
from jax import lax
from jax.experimental import pallas as pl
from jax.experimental.pallas import tpu as pltpu
from jax.sharding import PartitionSpec as P

BF = jnp.bfloat16
F32 = jnp.float32


def spread_rows(table, width):
    peers, slots = table.shape
    lanes = peers * width
    lane = lax.broadcasted_iota(jnp.int32, (slots, lanes), 1)
    slot = lax.broadcasted_iota(jnp.int32, (slots, lanes), 0)
    place = jnp.where(lane % width == slot, 1.0, 0.0).astype(BF)
    wide = jnp.dot(table.astype(BF), place, preferred_element_type=F32)
    peer = lax.broadcasted_iota(jnp.int32, (peers, lanes), 0)
    at = lax.broadcasted_iota(jnp.int32, (peers, lanes), 1)
    return jnp.sum(jnp.where(at // width == peer, wide, 0.0), axis=0, keepdims=True)


def source_matrix(send, hubs, rows, width):
    peers, slots = send.shape
    hub_here = hubs.shape[1]
    lanes = peers * width
    lane = lax.broadcasted_iota(jnp.int32, (1, lanes), 1) % width
    index = spread_rows(send.astype(F32), width)
    for k in range(hub_here):
        index = jnp.where(lane == slots + k, hubs[0:1, k : k + 1].astype(F32), index)
    index = jnp.where(lane < slots + hub_here, index, -1.0)
    row = lax.broadcasted_iota(jnp.int32, (rows, lanes), 0).astype(F32)
    return jnp.where(row == index, 1.0, 0.0).astype(BF)


def send_kernel(
    width, x_ref, cot_ref, ws_ref, wn_ref, bias_ref, send_ref, hub_ref, out_ref, pack_ref, send_v, hub_v, bias_v, sems
):
    rows, cols = x_ref.shape
    depth, full = ws_ref.shape
    blocks = full // cols
    base = 2 * blocks * depth
    moves = [
        (send_ref, send_v),
        (hub_ref, hub_v),
        (x_ref, pack_ref.at[base : base + rows, :]),
        (bias_ref, bias_v),
        (cot_ref, pack_ref.at[base + rows : base + 2 * rows, :]),
    ]
    for kind, w_ref in enumerate((ws_ref, wn_ref)):
        for j in range(blocks):
            at = (kind * blocks + j) * depth
            moves.append((w_ref.at[:, j * cols : (j + 1) * cols], pack_ref.at[at : at + depth, :]))
    copies = [pltpu.make_async_copy(src, dst, sems.at[i]) for i, (src, dst) in enumerate(moves)]
    for copy in copies:
        copy.start()
    for copy in copies[:3]:
        copy.wait()
    mark = source_matrix(send_v[0], hub_v[...], rows, width)
    taken = lax.dot_general(
        mark, pack_ref[base : base + rows, :], (((0,), (0,)), ((), ())), preferred_element_type=F32
    ).astype(BF)
    out_ref[...] = taken.reshape(out_ref.shape)
    for copy in copies[3:]:
        copy.wait()
    pack_ref[base + 2 * rows :, :] = jnp.broadcast_to(bias_v[...], (16, cols))


def neigh_kernel(
    width, pos_ref, count_ref, live_ref, x_ref, tile_ref, dest_ref, gw_ref, hw_ref, far_ref, got_ref,
    mix_ref, neigh_ref, passed_ref,
):
    rows, cols = x_ref.shape
    tile = tile_ref.shape[-1]
    tiles = tile_ref.shape[1]
    peers, slots = dest_ref.shape[1:]
    side = rows // tile
    lanes = peers * width
    hubs = hw_ref.shape[1]
    hub_here = hubs // peers
    for r in range(side):
        for c in range(side):
            total = jnp.zeros((tile, tile), BF)
            for t in range(tiles):
                used = jnp.logical_and(pos_ref[0, t] == r * side + c, t < count_ref[0])
                total = jnp.where(used, tile_ref[0, t], total)
            mix_ref[r * tile : (r + 1) * tile, c * tile : (c + 1) * tile] = total
    dest = spread_rows(dest_ref[0].astype(F32), width)
    coef = spread_rows(gw_ref[0], width)
    lane = lax.broadcasted_iota(jnp.int32, (1, lanes), 1)
    limit = jnp.zeros((1, lanes), jnp.int32)
    for q in range(peers):
        limit = jnp.where(lane // width == q, live_ref[0, q], limit)
    coef = jnp.where(lane % width < jnp.minimum(limit, slots), coef, 0.0)
    row = lax.broadcasted_iota(jnp.int32, (rows, lanes), 0).astype(F32)
    ghost = jnp.where(row == dest, coef, 0.0)
    hub = lax.broadcasted_iota(jnp.int32, (hubs, lanes), 0)
    at = lax.broadcasted_iota(jnp.int32, (hubs, lanes), 1)
    place = jnp.where(
        jnp.logical_and(at // width == hub // hub_here, at % width == slots + hub % hub_here), 1.0, 0.0
    ).astype(BF)
    hub_mix = jnp.dot(hw_ref[...], place, preferred_element_type=F32)
    far = (ghost + hub_mix).astype(BF)
    mix_ref[:, rows:] = far
    total = jnp.dot(mix_ref[:, :rows], x_ref[...], preferred_element_type=F32)
    total = total + jnp.dot(far, got_ref[...].reshape(lanes, cols), preferred_element_type=F32)
    neigh_ref[...] = total.astype(BF)


def dense_kernel(slots, hub_here, feats, me_ref, x_ref, ws_ref, wn_ref, mix_ref, *refs):
    pack_refs, n_refs = refs[:feats], refs[feats : 2 * feats]
    out_ref, back_ref, send_ref, pre_ref, cot_ref, bias_ref = refs[2 * feats :]
    rows, cols = x_ref.shape
    depth, full = ws_ref.shape
    blocks = full // cols
    peers, height = send_ref.shape[:2]
    lanes = mix_ref.shape[1] - rows
    width = lanes // peers
    me = me_ref[0]
    base = 2 * blocks * depth
    pre = jnp.zeros((rows, full), F32)
    for d, pack in enumerate(pack_refs):
        owner = me ^ d
        cut = pl.ds(pl.multiple_of(owner * cols, cols), cols)
        cot_ref[:, cut] = pack[base + rows : base + 2 * rows, :]
        bias_ref[:, cut] = pack[base + 2 * rows : base + 2 * rows + 16, :]
        w_s = jnp.concatenate([pack[j * depth : (j + 1) * depth, :] for j in range(blocks)], axis=1)
        w_n = jnp.concatenate([pack[(blocks + j) * depth : (blocks + j + 1) * depth, :] for j in range(blocks)], axis=1)
        left = jnp.concatenate([pack[base : base + rows, :], n_refs[d][...]], axis=1)
        right = jnp.concatenate([w_s, w_n], axis=0)
        pre = pre + jnp.dot(left, right, preferred_element_type=F32)
    pre = pre + bias_ref[0:1, :].astype(F32)
    pre_ref[...] = pre
    sig = jax.nn.sigmoid(pre)
    grad = (cot_ref[...].astype(F32) * sig * (1.0 + pre * (1.0 - sig))).astype(BF)
    cot_ref[...] = grad
    mine = pl.ds(pl.multiple_of(me * cols, cols), cols)
    own = pre_ref[:, mine]
    out_ref[...] = (own * jax.nn.sigmoid(own)).astype(BF)
    both = jnp.concatenate([ws_ref[...], wn_ref[...]], axis=0)
    into = lax.dot_general(grad, both, (((1,), (1,)), ((), ())), preferred_element_type=F32)
    neigh_grad = into[:, depth:].astype(BF)
    spread = lax.dot_general(
        mix_ref[...], neigh_grad, (((0,), (0,)), ((), ())), preferred_element_type=F32
    )
    back_ref[...] = into[:, :depth] + spread[:rows]
    sums = jnp.sum(cot_ref[:, mine].astype(F32), axis=0, keepdims=True)
    high = sums.astype(BF).astype(F32)
    line = lax.broadcasted_iota(jnp.int32, (lanes, cols), 0) % width
    away = jnp.where(line == slots + hub_here, high, spread[rows:])
    away = jnp.where(line == slots + hub_here + 1, sums - high, away)
    send_ref[:, :width, :] = away.astype(BF).reshape(peers, width, cols)
    pair = jnp.concatenate([x_ref[...], n_refs[0][...]], axis=1)
    weights = lax.dot_general(pair, grad, (((0,), (0,)), ((), ())), preferred_element_type=F32).astype(BF)
    share = height - width
    for j in range(blocks):
        for kind in range(2):
            block = weights[kind * depth : (kind + 1) * depth, j * cols : (j + 1) * cols]
            at = (j * 2 + kind) * depth
            for part in range(depth // share):
                send_ref[at // share + part, width:, :] = block[part * share : (part + 1) * share]


def gather_kernel(scale, slots, width, back_ref, send_ref, hub_ref, got_ref, grad_ref, bias_ref, part_ref):
    rows, cols = back_ref.shape
    peers = send_ref.shape[1]
    hub_here = hub_ref.shape[1]
    mark = source_matrix(send_ref[0], hub_ref[...], rows, width)
    near = got_ref[:, :width, :]
    total = back_ref[...] + jnp.dot(mark, near.reshape(peers * width, cols), preferred_element_type=F32)
    grad_ref[...] = total.astype(BF)
    first = slots + hub_here
    bias = jnp.zeros((2, cols), F32)
    share = jnp.zeros(part_ref.shape[-2:], F32)
    for q in range(peers):
        bias = bias + got_ref[q, first : first + 2, :].astype(F32)
        share = share + got_ref[q, width:, :].astype(F32)
    bias_ref[...] = jnp.sum(bias, axis=0, keepdims=True) * scale
    part_ref[...] = jnp.broadcast_to(share.astype(BF), part_ref.shape)


def spread_kernel(scale, got_ref, self_ref, neigh_ref):
    depth, full = self_ref.shape
    peers, share, cols = got_ref.shape
    whole = got_ref[...].reshape(peers * share, cols).astype(F32) * scale
    for j in range(full // cols):
        at = 2 * j * depth
        self_ref[:, j * cols : (j + 1) * cols] = whole[at : at + depth]
        neigh_ref[:, j * cols : (j + 1) * cols] = whole[at + depth : at + 2 * depth]


VMEM = pl.BlockSpec(memory_space=pltpu.VMEM)
SMEM = pl.BlockSpec(memory_space=pltpu.SMEM)
ANY = pl.BlockSpec(memory_space=pl.ANY)
HBM = pl.BlockSpec(memory_space=pltpu.HBM)
PARAMS = pltpu.CompilerParams(vmem_limit_bytes=40 * 1024 * 1024)


def shape(dims, kind):
    return jax.ShapeDtypeStruct(dims, kind)


def partner(block, axis, k):
    return lax.ppermute(block, axis, [(i, i ^ k) for i in range(lax.axis_size(axis))])


def exchange(blocks):
    return lax.all_to_all(blocks, "dom", split_axis=0, concat_axis=0, tiled=True)


def on_device(
    features,
    w_self,
    w_neigh,
    bias,
    cotangent,
    tile_vals,
    tile_pos,
    tile_count,
    send_rows,
    recv_dest,
    ghost_weight,
    recv_count,
    hub_rows,
    hub_weight,
):
    rows, cols = features.shape
    depth, full = w_self.shape
    blocks = full // cols
    peers, slots = send_rows.shape[1:]
    hub_here = hub_rows.shape[-1]
    width = -(-(slots + hub_here + 2) // 16) * 16
    lanes = peers * width
    share = 2 * blocks * depth // peers
    scale = 1.0 / math.sqrt(peers * rows)
    feats = lax.axis_size("feat")
    me = lax.axis_index("feat").astype(jnp.int32).reshape(1)
    pack_rows = 2 * blocks * depth + 2 * rows + 16

    raw = (features, cotangent, w_self, w_neigh, bias.reshape(1, cols), send_rows, hub_rows)
    outgoing, pack = pl.pallas_call(
        functools.partial(send_kernel, width),
        out_shape=(shape((peers, width, cols), BF), shape((pack_rows, cols), BF)),
        in_specs=[HBM] * 7,
        out_specs=(VMEM, VMEM),
        scratch_shapes=[
            pltpu.VMEM(send_rows.shape, jnp.int32),
            pltpu.VMEM(hub_rows.shape, jnp.int32),
            pltpu.VMEM((1, cols), BF),
            pltpu.SemaphoreType.DMA((5 + 2 * blocks,)),
        ],
        compiler_params=PARAMS,
    )(*(pltpu.with_memory_space_constraint(a, pltpu.HBM) for a in raw))

    far = partner(pack, "feat", 2)
    near = partner(pack, "feat", 1)
    incoming = exchange(outgoing)
    mix, neigh, far = pl.pallas_call(
        functools.partial(neigh_kernel, width),
        out_shape=(shape((rows, rows + lanes), BF), shape((rows, cols), BF), shape((pack_rows, cols), BF)),
        in_specs=[SMEM] * 3 + [VMEM] * 5 + [ANY, VMEM],
        out_specs=(VMEM, VMEM, ANY),
        input_output_aliases={8: 2},
        compiler_params=PARAMS,
    )(tile_pos, tile_count, recv_count, features, tile_vals, recv_dest, ghost_weight, hub_weight, far, incoming)
    last = partner(far, "feat", 1)
    far_neigh = partner(neigh, "feat", 2)
    every = [neigh, partner(neigh, "feat", 1), far_neigh, partner(far_neigh, "feat", 1)]

    output, back, returned = pl.pallas_call(
        functools.partial(dense_kernel, slots, hub_here, feats),
        out_shape=(
            shape((rows, cols), BF),
            shape((rows, cols), F32),
            shape((peers, width + share, cols), BF),
        ),
        in_specs=[SMEM] + [VMEM] * (4 + 2 * feats),
        out_specs=(VMEM,) * 3,
        scratch_shapes=[
            pltpu.VMEM((rows, full), F32),
            pltpu.VMEM((rows, full), BF),
            pltpu.VMEM((16, full), BF),
        ],
        compiler_params=PARAMS,
    )(me, features, w_self, w_neigh, mix, pack, near, far, last, *every)

    arrived = exchange(returned)
    grad_features, grad_bias, part = pl.pallas_call(
        functools.partial(gather_kernel, scale, slots, width),
        out_shape=(
            shape((rows, cols), BF),
            shape((1, cols), F32),
            shape((peers, share, cols), BF),
        ),
        in_specs=[VMEM] * 4,
        out_specs=(VMEM,) * 3,
        compiler_params=PARAMS,
    )(back, send_rows, hub_rows, arrived)
    parts = exchange(part)
    grad_self, grad_neigh = pl.pallas_call(
        functools.partial(spread_kernel, scale),
        out_shape=(shape((depth, full), F32), shape((depth, full), F32)),
        in_specs=[VMEM],
        out_specs=(VMEM, VMEM),
        compiler_params=PARAMS,
    )(parts)
    return output, grad_features, grad_self, grad_neigh, grad_bias.reshape(cols)


def solution(mesh):
    placed = (
        P("dom", "feat"),
        P("feat", None),
        P("feat", None),
        P("feat"),
        P("dom", "feat"),
        P("dom", None, None, None),
        P("dom", None),
        P("dom"),
        P("dom", None, None),
        P("dom", None, None),
        P("dom", None, None),
        P("dom", None),
        P("dom", None),
        P("dom", None),
    )
    return jax.shard_map(
        on_device,
        mesh=mesh,
        in_specs=placed,
        out_specs=(P("dom", "feat"), P("dom", "feat"), P("feat", None), P("feat", None), P("feat")),
        check_vma=False,
    )
```

```python
import functools
import math

import jax
import jax.numpy as jnp
from jax import lax
from jax.experimental import pallas as pl
from jax.experimental.pallas import tpu as pltpu
from jax.sharding import PartitionSpec as P

BF = jnp.bfloat16
F32 = jnp.float32


def spread_rows(table, width):
    peers, slots = table.shape
    lanes = peers * width
    lane = lax.broadcasted_iota(jnp.int32, (slots, lanes), 1)
    slot = lax.broadcasted_iota(jnp.int32, (slots, lanes), 0)
    place = jnp.where(lane % width == slot, 1.0, 0.0).astype(BF)
    wide = jnp.dot(table.astype(BF), place, preferred_element_type=F32)
    peer = lax.broadcasted_iota(jnp.int32, (peers, lanes), 0)
    at = lax.broadcasted_iota(jnp.int32, (peers, lanes), 1)
    return jnp.sum(jnp.where(at // width == peer, wide, 0.0), axis=0, keepdims=True)


def source_matrix(send, hubs, rows, width):
    peers, slots = send.shape
    hub_here = hubs.shape[1]
    lanes = peers * width
    lane = lax.broadcasted_iota(jnp.int32, (1, lanes), 1) % width
    index = spread_rows(send.astype(F32), width)
    for k in range(hub_here):
        index = jnp.where(lane == slots + k, hubs[0:1, k : k + 1].astype(F32), index)
    index = jnp.where(lane < slots + hub_here, index, -1.0)
    row = lax.broadcasted_iota(jnp.int32, (rows, lanes), 0).astype(F32)
    return jnp.where(row == index, 1.0, 0.0).astype(BF)


def send_kernel(
    width, x_ref, cot_ref, ws_ref, wn_ref, bias_ref, send_ref, hub_ref,
    out_ref, pack_ref, mark_ref, send_v, hub_v, bias_v, sems
):
    rows, cols = x_ref.shape
    depth, full = ws_ref.shape
    blocks = full // cols
    base = 2 * blocks * depth
    moves = [
        (send_ref, send_v),
        (hub_ref, hub_v),
        (x_ref, pack_ref.at[base : base + rows, :]),
        (bias_ref, bias_v),
        (cot_ref, pack_ref.at[base + rows : base + 2 * rows, :]),
    ]
    for kind, w_ref in enumerate((ws_ref, wn_ref)):
        for j in range(blocks):
            at = (kind * blocks + j) * depth
            moves.append((w_ref.at[:, j * cols : (j + 1) * cols], pack_ref.at[at : at + depth, :]))
    copies = [pltpu.make_async_copy(src, dst, sems.at[i]) for i, (src, dst) in enumerate(moves)]
    for copy in copies:
        copy.start()
    for copy in copies[:3]:
        copy.wait()
    mark = source_matrix(send_v[0], hub_v[...], rows, width)
    mark_ref[...] = mark
    taken = lax.dot_general(
        mark, pack_ref[base : base + rows, :], (((0,), (0,)), ((), ())), preferred_element_type=F32
    ).astype(BF)
    out_ref[...] = taken.reshape(out_ref.shape)
    for copy in copies[3:]:
        copy.wait()
    pack_ref[base + 2 * rows :, :] = jnp.broadcast_to(bias_v[...], (16, cols))


def neigh_kernel(
    width, pos_ref, live_ref, count_ref, x_ref, tile_ref, dest_ref, gw_ref, hw_ref, far_ref, near_ref, got_ref,
    mix_ref, neigh_ref, passed_far_ref, passed_near_ref,
):
    rows, cols = x_ref.shape
    tile = tile_ref.shape[-1]
    tiles = tile_ref.shape[1]
    peers, slots = dest_ref.shape[1:]
    side = rows // tile
    lanes = peers * width
    hubs = hw_ref.shape[0]
    hub_here = hubs // peers
    for r in range(side):
        for c in range(side):
            total = jnp.zeros((tile, tile), BF)
            for t in range(tiles):
                used = jnp.logical_and(pos_ref[0, t] == r * side + c, t < count_ref[...])
                total = jnp.where(used, tile_ref[0, t], total)
            mix_ref[r * tile : (r + 1) * tile, c * tile : (c + 1) * tile] = total
    dest = spread_rows(dest_ref[0].astype(F32), width)
    coef = spread_rows(gw_ref[0], width)
    lane = lax.broadcasted_iota(jnp.int32, (1, lanes), 1)
    limit = jnp.zeros((1, lanes), jnp.int32)
    for q in range(peers):
        limit = jnp.where(lane // width == q, live_ref[0, q], limit)
    coef = jnp.where(lane % width < jnp.minimum(limit, slots), coef, 0.0)
    row = lax.broadcasted_iota(jnp.int32, (rows, lanes), 0).astype(F32)
    ghost = jnp.where(row == dest, coef, 0.0)
    hub = lax.broadcasted_iota(jnp.int32, (hubs, lanes), 0)
    at = lax.broadcasted_iota(jnp.int32, (hubs, lanes), 1)
    place = jnp.where(
        jnp.logical_and(at // width == hub // hub_here, at % width == slots + hub % hub_here), 1.0, 0.0
    ).astype(BF)
    hub_mix = lax.dot_general(hw_ref[...], place, (((0,), (0,)), ((), ())), preferred_element_type=F32)
    far = (ghost + hub_mix).astype(BF)
    mix_ref[:, rows:] = far
    total = jnp.dot(mix_ref[:, :rows], x_ref[...], preferred_element_type=F32)
    total = total + jnp.dot(far, got_ref[...].reshape(lanes, cols), preferred_element_type=F32)
    neigh_ref[...] = total.astype(BF)


def dense_kernel(slots, hub_here, feats, me_ref, x_ref, ws_ref, wn_ref, mix_ref, *refs):
    pack_refs, n_refs = refs[:feats], refs[feats : 2 * feats]
    out_ref, back_ref, send_ref, pre_ref, cot_ref, bias_ref = refs[2 * feats :]
    rows, cols = x_ref.shape
    depth, full = ws_ref.shape
    blocks = full // cols
    peers, height = send_ref.shape[:2]
    lanes = mix_ref.shape[1] - rows
    width = lanes // peers
    me = me_ref[0]
    base = 2 * blocks * depth
    pre = jnp.zeros((rows, full), F32)
    for d, pack in enumerate(pack_refs):
        owner = me ^ d
        cut = pl.ds(pl.multiple_of(owner * cols, cols), cols)
        cot_ref[:, cut] = pack[base + rows : base + 2 * rows, :]
        bias_ref[:, cut] = pack[base + 2 * rows : base + 2 * rows + 16, :]
        w_s = jnp.concatenate([pack[j * depth : (j + 1) * depth, :] for j in range(blocks)], axis=1)
        w_n = jnp.concatenate([pack[(blocks + j) * depth : (blocks + j + 1) * depth, :] for j in range(blocks)], axis=1)
        left = jnp.concatenate([pack[base : base + rows, :], n_refs[d][...]], axis=1)
        right = jnp.concatenate([w_s, w_n], axis=0)
        pre = pre + jnp.dot(left, right, preferred_element_type=F32)
    pre = pre + bias_ref[0:1, :].astype(F32)
    pre_ref[...] = pre
    sig = jax.nn.sigmoid(pre)
    grad = (cot_ref[...].astype(F32) * sig * (1.0 + pre * (1.0 - sig))).astype(BF)
    cot_ref[...] = grad
    mine = pl.ds(pl.multiple_of(me * cols, cols), cols)
    own = pre_ref[:, mine]
    out_ref[...] = (own * jax.nn.sigmoid(own)).astype(BF)
    both = jnp.concatenate([ws_ref[...], wn_ref[...]], axis=0)
    into = lax.dot_general(grad, both, (((1,), (1,)), ((), ())), preferred_element_type=F32)
    neigh_grad = into[:, depth:].astype(BF)
    spread = lax.dot_general(
        mix_ref[...], neigh_grad, (((0,), (0,)), ((), ())), preferred_element_type=F32
    )
    back_ref[...] = into[:, :depth] + spread[:rows]
    sums = jnp.sum(cot_ref[:, mine].astype(F32), axis=0, keepdims=True)
    high = sums.astype(BF).astype(F32)
    line = lax.broadcasted_iota(jnp.int32, (lanes, cols), 0) % width
    away = jnp.where(line == slots + hub_here, high, spread[rows:])
    away = jnp.where(line == slots + hub_here + 1, sums - high, away)
    send_ref[:, :width, :] = away.astype(BF).reshape(peers, width, cols)
    pair = jnp.concatenate([x_ref[...], n_refs[0][...]], axis=1)
    weights = lax.dot_general(pair, grad, (((0,), (0,)), ((), ())), preferred_element_type=F32).astype(BF)
    share = height - width
    for j in range(blocks):
        for kind in range(2):
            block = weights[kind * depth : (kind + 1) * depth, j * cols : (j + 1) * cols]
            at = (j * 2 + kind) * depth
            for part in range(depth // share):
                send_ref[at // share + part, width:, :] = block[part * share : (part + 1) * share]


def gather_kernel(scale, slots, hub_here, width, back_ref, mark_ref, got_ref, grad_ref, bias_ref, part_ref):
    rows, cols = back_ref.shape
    peers = got_ref.shape[0]
    near = got_ref[:, :width, :]
    total = back_ref[...] + jnp.dot(mark_ref[...], near.reshape(peers * width, cols), preferred_element_type=F32)
    grad_ref[...] = total.astype(BF)
    first = slots + hub_here
    bias = jnp.zeros((2, cols), F32)
    share = jnp.zeros(part_ref.shape[-2:], F32)
    for q in range(peers):
        bias = bias + got_ref[q, first : first + 2, :].astype(F32)
        share = share + got_ref[q, width:, :].astype(F32)
    bias_ref[...] = jnp.sum(bias, axis=0, keepdims=True) * scale
    part_ref[...] = jnp.broadcast_to(share.astype(BF), part_ref.shape)


def spread_kernel(scale, got_ref, self_ref, neigh_ref):
    depth, full = self_ref.shape
    peers, share, cols = got_ref.shape
    whole = got_ref[...].reshape(peers * share, cols).astype(F32) * scale
    for j in range(full // cols):
        at = 2 * j * depth
        self_ref[:, j * cols : (j + 1) * cols] = whole[at : at + depth]
        neigh_ref[:, j * cols : (j + 1) * cols] = whole[at + depth : at + 2 * depth]


VMEM = pl.BlockSpec(memory_space=pltpu.VMEM)
SMEM = pl.BlockSpec(memory_space=pltpu.SMEM)
ANY = pl.BlockSpec(memory_space=pl.ANY)
HBM = pl.BlockSpec(memory_space=pltpu.HBM)
PARAMS = pltpu.CompilerParams(vmem_limit_bytes=40 * 1024 * 1024)


def shape(dims, kind):
    return jax.ShapeDtypeStruct(dims, kind)


def partner(block, axis, k):
    return lax.ppermute(block, axis, [(i, i ^ k) for i in range(lax.axis_size(axis))])


def exchange(blocks):
    return lax.all_to_all(blocks, "dom", split_axis=0, concat_axis=0, tiled=True)


def on_device(
    features,
    w_self,
    w_neigh,
    bias,
    cotangent,
    tile_vals,
    tile_pos,
    tile_count,
    send_rows,
    recv_dest,
    ghost_weight,
    recv_count,
    hub_rows,
    hub_weight,
):
    rows, cols = features.shape
    depth, full = w_self.shape
    blocks = full // cols
    peers, slots = send_rows.shape[1:]
    hub_here = hub_rows.shape[-1]
    width = -(-(slots + hub_here + 2) // 16) * 16
    lanes = peers * width
    share = 2 * blocks * depth // peers
    scale = 1.0 / math.sqrt(peers * rows)
    feats = lax.axis_size("feat")
    me = lax.axis_index("feat").astype(jnp.int32).reshape(1)
    pack_rows = 2 * blocks * depth + 2 * rows + 16

    raw = (features, cotangent, w_self, w_neigh, bias.reshape(1, cols), send_rows, hub_rows)
    outgoing, pack, mark = pl.pallas_call(
        functools.partial(send_kernel, width),
        out_shape=(shape((peers, width, cols), BF), shape((pack_rows, cols), BF), shape((rows, lanes), BF)),
        in_specs=[HBM] * 7,
        out_specs=(VMEM,) * 3,
        scratch_shapes=[
            pltpu.VMEM(send_rows.shape, jnp.int32),
            pltpu.VMEM(hub_rows.shape, jnp.int32),
            pltpu.VMEM((1, cols), BF),
            pltpu.SemaphoreType.DMA((5 + 2 * blocks,)),
        ],
        compiler_params=PARAMS,
    )(*(pltpu.with_memory_space_constraint(a, pltpu.HBM) for a in raw))

    far = partner(pack, "feat", 2)
    incoming = exchange(outgoing)
    mix, neigh, far, pack = pl.pallas_call(
        functools.partial(neigh_kernel, width),
        out_shape=(
            shape((rows, rows + lanes), BF),
            shape((rows, cols), BF),
            shape((pack_rows, cols), BF),
            shape((pack_rows, cols), BF),
        ),
        in_specs=[SMEM] * 2 + [VMEM] * 6 + [ANY, ANY, VMEM],
        out_specs=(VMEM, VMEM, ANY, ANY),
        input_output_aliases={8: 2, 9: 3},
        compiler_params=PARAMS,
    )(
        tile_pos, recv_count, tile_count.reshape(1, 1), features, tile_vals, recv_dest, ghost_weight, hub_weight.T,
        far, pack, incoming,
    )
    near = partner(pack, "feat", 1)
    last = partner(far, "feat", 1)
    far_neigh = partner(neigh, "feat", 2)
    every = [neigh, partner(neigh, "feat", 1), far_neigh, partner(far_neigh, "feat", 1)]

    output, back, returned = pl.pallas_call(
        functools.partial(dense_kernel, slots, hub_here, feats),
        out_shape=(
            shape((rows, cols), BF),
            shape((rows, cols), F32),
            shape((peers, width + share, cols), BF),
        ),
        in_specs=[SMEM] + [VMEM] * (4 + 2 * feats),
        out_specs=(VMEM,) * 3,
        scratch_shapes=[
            pltpu.VMEM((rows, full), F32),
            pltpu.VMEM((rows, full), BF),
            pltpu.VMEM((16, full), BF),
        ],
        compiler_params=PARAMS,
    )(me, features, w_self, w_neigh, mix, pack, near, far, last, *every)

    arrived = exchange(returned)
    grad_features, grad_bias, part = pl.pallas_call(
        functools.partial(gather_kernel, scale, slots, hub_here, width),
        out_shape=(
            shape((rows, cols), BF),
            shape((1, cols), F32),
            shape((peers, share, cols), BF),
        ),
        in_specs=[VMEM] * 3,
        out_specs=(VMEM,) * 3,
        compiler_params=PARAMS,
    )(back, mark, arrived)
    parts = exchange(part)
    grad_self, grad_neigh = pl.pallas_call(
        functools.partial(spread_kernel, scale),
        out_shape=(shape((depth, full), F32), shape((depth, full), F32)),
        in_specs=[VMEM],
        out_specs=(VMEM, VMEM),
        compiler_params=PARAMS,
    )(parts)
    return output, grad_features, grad_self, grad_neigh, grad_bias.reshape(cols)


def solution(mesh):
    placed = (
        P("dom", "feat"),
        P("feat", None),
        P("feat", None),
        P("feat"),
        P("dom", "feat"),
        P("dom", None, None, None),
        P("dom", None),
        P("dom"),
        P("dom", None, None),
        P("dom", None, None),
        P("dom", None, None),
        P("dom", None),
        P("dom", None),
        P("dom", None),
    )
    return jax.shard_map(
        on_device,
        mesh=mesh,
        in_specs=placed,
        out_specs=(P("dom", "feat"), P("dom", "feat"), P("feat", None), P("feat", None), P("feat")),
        check_vma=False,
    )
```

```python
import functools
import math

import jax
import jax.numpy as jnp
from jax import lax
from jax.experimental import pallas as pl
from jax.experimental.pallas import tpu as pltpu
from jax.sharding import PartitionSpec as P

BF = jnp.bfloat16
F32 = jnp.float32


def spread_rows(table, width):
    peers, slots = table.shape
    lanes = peers * width
    lane = lax.broadcasted_iota(jnp.int32, (slots, lanes), 1)
    slot = lax.broadcasted_iota(jnp.int32, (slots, lanes), 0)
    place = jnp.where(lane % width == slot, 1.0, 0.0).astype(BF)
    wide = jnp.dot(table.astype(BF), place, preferred_element_type=F32)
    peer = lax.broadcasted_iota(jnp.int32, (peers, lanes), 0)
    at = lax.broadcasted_iota(jnp.int32, (peers, lanes), 1)
    return jnp.sum(jnp.where(at // width == peer, wide, 0.0), axis=0, keepdims=True)


def source_matrix(send, hubs, rows, width):
    peers, slots = send.shape
    hub_here = hubs.shape[1]
    lanes = peers * width
    lane = lax.broadcasted_iota(jnp.int32, (1, lanes), 1) % width
    index = spread_rows(send.astype(F32), width)
    for k in range(hub_here):
        index = jnp.where(lane == slots + k, hubs[0:1, k : k + 1].astype(F32), index)
    index = jnp.where(lane < slots + hub_here, index, -1.0)
    row = lax.broadcasted_iota(jnp.int32, (rows, lanes), 0).astype(F32)
    return jnp.where(row == index, 1.0, 0.0).astype(BF)


def source_rows(send, hubs, rows, width):
    peers, slots = send.shape
    hub_here = hubs.shape[1]
    lanes = peers * width
    slot = lax.broadcasted_iota(jnp.int32, (lanes, slots), 0) % width
    place = jnp.where(slot == lax.broadcasted_iota(jnp.int32, (lanes, slots), 1), 1.0, 0.0).astype(BF)
    wide = lax.dot_general(
        place, send.astype(F32).astype(BF), (((1,), (1,)), ((), ())), preferred_element_type=F32
    )
    line = lax.broadcasted_iota(jnp.int32, (lanes, peers), 0)
    for k in range(hub_here):
        wide = jnp.where(line % width == slots + k, hubs[0:1, k : k + 1].astype(F32), wide)
    wide = jnp.where(line % width < slots + hub_here, wide, -1.0)
    wide = jnp.where(line // width == lax.broadcasted_iota(jnp.int32, (lanes, peers), 1), wide, 0.0)
    index = jnp.dot(wide.astype(BF), jnp.ones((peers, rows), BF), preferred_element_type=F32)
    row = lax.broadcasted_iota(jnp.int32, (lanes, rows), 1).astype(F32)
    return jnp.where(row == index, 1.0, 0.0).astype(BF)


def send_kernel(
    width, x_ref, cot_ref, ws_ref, wn_ref, bias_ref, send_ref, hub_ref, out_ref, pack_ref, send_v, hub_v, bias_v, sems
):
    rows, cols = x_ref.shape
    depth, full = ws_ref.shape
    blocks = full // cols
    base = 2 * blocks * depth
    moves = [
        (send_ref, send_v),
        (hub_ref, hub_v),
        (x_ref, pack_ref.at[base : base + rows, :]),
        (bias_ref, bias_v),
        (cot_ref, pack_ref.at[base + rows : base + 2 * rows, :]),
    ]
    for kind, w_ref in enumerate((ws_ref, wn_ref)):
        for j in range(blocks):
            at = (kind * blocks + j) * depth
            moves.append((w_ref.at[:, j * cols : (j + 1) * cols], pack_ref.at[at : at + depth, :]))
    copies = [pltpu.make_async_copy(src, dst, sems.at[i]) for i, (src, dst) in enumerate(moves)]
    for copy in copies:
        copy.start()
    for copy in copies[:2]:
        copy.wait()
    mark = source_rows(send_v[0], hub_v[...], rows, width)
    copies[2].wait()
    taken = jnp.dot(mark, pack_ref[base : base + rows, :], preferred_element_type=F32).astype(BF)
    out_ref[...] = taken.reshape(out_ref.shape)
    for copy in copies[3:]:
        copy.wait()
    pack_ref[base + 2 * rows :, :] = jnp.broadcast_to(bias_v[...], (16, cols))


def mix_kernel(
    width, count_ref, pos_ref, live_ref, tile_ref, dest_ref, gw_ref, hw_ref, send_ref, hub_ref,
    mix_ref, turned_ref, mark_ref, pos_v, live_v, tile_v, dest_v, gw_v, hw_v, send_v, hub_v, sems,
):
    pairs = (
        (pos_ref, pos_v), (live_ref, live_v), (tile_ref, tile_v), (dest_ref, dest_v),
        (gw_ref, gw_v), (hw_ref, hw_v), (send_ref, send_v), (hub_ref, hub_v),
    )
    copies = [pltpu.make_async_copy(src, dst, sems.at[i]) for i, (src, dst) in enumerate(pairs)]
    for copy in copies:
        copy.start()
    for copy in copies:
        copy.wait()
    rows = mix_ref.shape[0]
    tiles, tile = tile_v.shape[1:3]
    peers, slots = dest_v.shape[1:]
    side = rows // tile
    lanes = peers * width
    hubs = hw_v.shape[0]
    hub_here = hubs // peers
    for r in range(side):
        for c in range(side):
            total = jnp.zeros((tile, tile), BF)
            for t in range(tiles):
                used = jnp.logical_and(pos_v[0:1, t : t + 1] == r * side + c, t < count_ref[...])
                total = jnp.where(used, tile_v[0, t], total)
            mix_ref[r * tile : (r + 1) * tile, c * tile : (c + 1) * tile] = total
    dest = spread_rows(dest_v[0].astype(F32), width)
    coef = spread_rows(gw_v[0], width)
    peer = lax.broadcasted_iota(jnp.int32, (peers, lanes), 0)
    at = lax.broadcasted_iota(jnp.int32, (peers, lanes), 1)
    owner = jnp.where(at // width == peer, 1.0, 0.0).astype(BF)
    limit = jnp.dot(live_v[...].astype(F32).astype(BF), owner, preferred_element_type=F32)
    lane = lax.broadcasted_iota(jnp.int32, (1, lanes), 1) % width
    coef = jnp.where(jnp.logical_and(lane.astype(F32) < limit, lane < slots), coef, 0.0)
    row = lax.broadcasted_iota(jnp.int32, (rows, lanes), 0).astype(F32)
    ghost = jnp.where(row == dest, coef, 0.0)
    hub = lax.broadcasted_iota(jnp.int32, (hubs, lanes), 0)
    at = lax.broadcasted_iota(jnp.int32, (hubs, lanes), 1)
    place = jnp.where(
        jnp.logical_and(at // width == hub // hub_here, at % width == slots + hub % hub_here), 1.0, 0.0
    ).astype(BF)
    hub_mix = lax.dot_general(hw_v[...], place, (((0,), (0,)), ((), ())), preferred_element_type=F32)
    mix_ref[:, rows:] = (ghost + hub_mix).astype(BF)
    turned_ref[...] = mix_ref[...].T
    mark_ref[...] = source_matrix(send_v[0], hub_v[...], rows, width)


def neigh_kernel(x_ref, mix_ref, far_ref, got_ref, neigh_ref, passed_ref):
    rows, cols = x_ref.shape
    lanes = mix_ref.shape[1] - rows
    total = jnp.dot(mix_ref[:, :rows], x_ref[...], preferred_element_type=F32)
    total = total + jnp.dot(mix_ref[:, rows:], got_ref[...].reshape(lanes, cols), preferred_element_type=F32)
    neigh_ref[...] = total.astype(BF)


def dense_kernel(slots, hub_here, feats, me_ref, x_ref, ws_ref, wn_ref, turned_ref, *refs):
    pack_refs, n_refs = refs[:feats], refs[feats : 2 * feats]
    out_ref, back_ref, send_ref, pre_ref, cot_ref, bias_ref = refs[2 * feats :]
    rows, cols = x_ref.shape
    depth, full = ws_ref.shape
    blocks = full // cols
    peers, height = send_ref.shape[:2]
    lanes = turned_ref.shape[0] - rows
    width = lanes // peers
    me = me_ref[0]
    base = 2 * blocks * depth
    pre = jnp.zeros((rows, full), F32)
    for d, pack in enumerate(pack_refs):
        owner = me ^ d
        cut = pl.ds(pl.multiple_of(owner * cols, cols), cols)
        cot_ref[:, cut] = pack[base + rows : base + 2 * rows, :]
        bias_ref[:, cut] = pack[base + 2 * rows : base + 2 * rows + 16, :]
        w_s = jnp.concatenate([pack[j * depth : (j + 1) * depth, :] for j in range(blocks)], axis=1)
        w_n = jnp.concatenate([pack[(blocks + j) * depth : (blocks + j + 1) * depth, :] for j in range(blocks)], axis=1)
        left = jnp.concatenate([pack[base : base + rows, :], n_refs[d][...]], axis=1)
        right = jnp.concatenate([w_s, w_n], axis=0)
        pre = pre + jnp.dot(left, right, preferred_element_type=F32)
    pre = pre + bias_ref[0:1, :].astype(F32)
    pre_ref[...] = pre
    sig = jax.nn.sigmoid(pre)
    grad = (cot_ref[...].astype(F32) * sig * (1.0 + pre * (1.0 - sig))).astype(BF)
    cot_ref[...] = grad
    mine = pl.ds(pl.multiple_of(me * cols, cols), cols)
    own = pre_ref[:, mine]
    out_ref[...] = (own * jax.nn.sigmoid(own)).astype(BF)
    both = jnp.concatenate([ws_ref[...], wn_ref[...]], axis=0)
    into = lax.dot_general(grad, both, (((1,), (1,)), ((), ())), preferred_element_type=F32)
    neigh_grad = into[:, depth:].astype(BF)
    spread = jnp.dot(turned_ref[...], neigh_grad, preferred_element_type=F32)
    back_ref[...] = into[:, :depth] + spread[:rows]
    sums = jnp.sum(cot_ref[:, mine].astype(F32), axis=0, keepdims=True)
    high = sums.astype(BF).astype(F32)
    line = lax.broadcasted_iota(jnp.int32, (lanes, cols), 0) % width
    away = jnp.where(line == slots + hub_here, high, spread[rows:])
    away = jnp.where(line == slots + hub_here + 1, sums - high, away)
    send_ref[:, :width, :] = away.astype(BF).reshape(peers, width, cols)
    pair = jnp.concatenate([x_ref[...], n_refs[0][...]], axis=1)
    weights = lax.dot_general(pair, grad, (((0,), (0,)), ((), ())), preferred_element_type=F32).astype(BF)
    share = height - width
    for j in range(blocks):
        for kind in range(2):
            block = weights[kind * depth : (kind + 1) * depth, j * cols : (j + 1) * cols]
            at = (j * 2 + kind) * depth
            for part in range(depth // share):
                send_ref[at // share + part, width:, :] = block[part * share : (part + 1) * share]


def gather_kernel(scale, slots, hub_here, width, back_ref, mark_ref, got_ref, grad_ref, bias_ref, part_ref):
    rows, cols = back_ref.shape
    peers = got_ref.shape[0]
    near = got_ref[:, :width, :]
    total = back_ref[...] + jnp.dot(mark_ref[...], near.reshape(peers * width, cols), preferred_element_type=F32)
    grad_ref[...] = total.astype(BF)
    first = slots + hub_here
    bias = jnp.zeros((2, cols), F32)
    share = jnp.zeros(part_ref.shape[-2:], F32)
    for q in range(peers):
        bias = bias + got_ref[q, first : first + 2, :].astype(F32)
        share = share + got_ref[q, width:, :].astype(F32)
    bias_ref[...] = jnp.sum(bias, axis=0, keepdims=True) * scale
    part_ref[...] = jnp.broadcast_to(share.astype(BF), part_ref.shape)


def spread_kernel(scale, got_ref, self_ref, neigh_ref):
    depth, full = self_ref.shape
    peers, share, cols = got_ref.shape
    whole = got_ref[...].reshape(peers * share, cols).astype(F32) * scale
    for j in range(full // cols):
        at = 2 * j * depth
        self_ref[:, j * cols : (j + 1) * cols] = whole[at : at + depth]
        neigh_ref[:, j * cols : (j + 1) * cols] = whole[at + depth : at + 2 * depth]


VMEM = pl.BlockSpec(memory_space=pltpu.VMEM)
SMEM = pl.BlockSpec(memory_space=pltpu.SMEM)
ANY = pl.BlockSpec(memory_space=pl.ANY)
HBM = pl.BlockSpec(memory_space=pltpu.HBM)
PARAMS = pltpu.CompilerParams(vmem_limit_bytes=40 * 1024 * 1024)


def shape(dims, kind):
    return jax.ShapeDtypeStruct(dims, kind)


def partner(block, axis, k):
    return lax.ppermute(block, axis, [(i, i ^ k) for i in range(lax.axis_size(axis))])


def exchange(blocks):
    return lax.all_to_all(blocks, "dom", split_axis=0, concat_axis=0, tiled=True)


def on_device(
    features,
    w_self,
    w_neigh,
    bias,
    cotangent,
    tile_vals,
    tile_pos,
    tile_count,
    send_rows,
    recv_dest,
    ghost_weight,
    recv_count,
    hub_rows,
    hub_weight,
):
    rows, cols = features.shape
    depth, full = w_self.shape
    blocks = full // cols
    peers, slots = send_rows.shape[1:]
    hub_here = hub_rows.shape[-1]
    width = -(-(slots + hub_here + 2) // 16) * 16
    lanes = peers * width
    share = 2 * blocks * depth // peers
    scale = 1.0 / math.sqrt(peers * rows)
    feats = lax.axis_size("feat")
    me = lax.axis_index("feat").astype(jnp.int32).reshape(1)
    pack_rows = 2 * blocks * depth + 2 * rows + 16

    def pinned(*arrays):
        return [pltpu.with_memory_space_constraint(a, pltpu.HBM) for a in arrays]

    first = pinned(features, cotangent, w_self, w_neigh, bias.reshape(1, cols), send_rows, hub_rows)
    outgoing, pack = pl.pallas_call(
        functools.partial(send_kernel, width),
        out_shape=(shape((peers, width, cols), BF), shape((pack_rows, cols), BF)),
        in_specs=[HBM] * len(first),
        out_specs=(VMEM,) * 2,
        scratch_shapes=[
            pltpu.VMEM(send_rows.shape, jnp.int32),
            pltpu.VMEM(hub_rows.shape, jnp.int32),
            pltpu.VMEM((1, cols), BF),
            pltpu.SemaphoreType.DMA((5 + 2 * blocks,)),
        ],
        compiler_params=PARAMS,
    )(*first)

    far = partner(pack, "feat", 2)
    near = partner(pack, "feat", 1)
    incoming = exchange(outgoing)
    edges = pinned(
        tile_pos, recv_count, tile_vals, recv_dest, ghost_weight, hub_weight.T, send_rows, hub_rows
    )
    mix, turned, mark = pl.pallas_call(
        functools.partial(mix_kernel, width),
        out_shape=(
            shape((rows, rows + lanes), BF),
            shape((rows + lanes, rows), BF),
            shape((rows, lanes), BF),
        ),
        in_specs=[VMEM] + [HBM] * len(edges),
        out_specs=(VMEM,) * 3,
        scratch_shapes=[pltpu.VMEM(a.shape, a.dtype) for a in edges] + [pltpu.SemaphoreType.DMA((len(edges),))],
        compiler_params=PARAMS,
        cost_estimate=pl.CostEstimate(flops=10**8, bytes_accessed=3 * 10**6, transcendentals=0),
    )(tile_count.reshape(1, 1), *edges)
    neigh, far = pl.pallas_call(
        neigh_kernel,
        out_shape=(shape((rows, cols), BF), shape((pack_rows, cols), BF)),
        in_specs=[VMEM, VMEM, ANY, VMEM],
        out_specs=(VMEM, ANY),
        input_output_aliases={2: 1},
        compiler_params=PARAMS,
    )(features, mix, far, incoming)
    last = partner(far, "feat", 1)
    far_neigh = partner(neigh, "feat", 2)
    every = [neigh, partner(neigh, "feat", 1), far_neigh, partner(far_neigh, "feat", 1)]

    output, back, returned = pl.pallas_call(
        functools.partial(dense_kernel, slots, hub_here, feats),
        out_shape=(
            shape((rows, cols), BF),
            shape((rows, cols), F32),
            shape((peers, width + share, cols), BF),
        ),
        in_specs=[SMEM] + [VMEM] * (4 + 2 * feats),
        out_specs=(VMEM,) * 3,
        scratch_shapes=[
            pltpu.VMEM((rows, full), F32),
            pltpu.VMEM((rows, full), BF),
            pltpu.VMEM((16, full), BF),
        ],
        compiler_params=PARAMS,
    )(me, features, w_self, w_neigh, turned, pack, near, far, last, *every)

    arrived = exchange(returned)
    grad_features, grad_bias, part = pl.pallas_call(
        functools.partial(gather_kernel, scale, slots, hub_here, width),
        out_shape=(
            shape((rows, cols), BF),
            shape((1, cols), F32),
            shape((peers, share, cols), BF),
        ),
        in_specs=[VMEM] * 3,
        out_specs=(VMEM,) * 3,
        compiler_params=PARAMS,
    )(back, mark, arrived)
    parts = exchange(part)
    grad_self, grad_neigh = pl.pallas_call(
        functools.partial(spread_kernel, scale),
        out_shape=(shape((depth, full), F32), shape((depth, full), F32)),
        in_specs=[VMEM],
        out_specs=(VMEM, VMEM),
        compiler_params=PARAMS,
    )(parts)
    return output, grad_features, grad_self, grad_neigh, grad_bias.reshape(cols)


def solution(mesh):
    placed = (
        P("dom", "feat"),
        P("feat", None),
        P("feat", None),
        P("feat"),
        P("dom", "feat"),
        P("dom", None, None, None),
        P("dom", None),
        P("dom"),
        P("dom", None, None),
        P("dom", None, None),
        P("dom", None, None),
        P("dom", None),
        P("dom", None),
        P("dom", None),
    )
    return jax.shard_map(
        on_device,
        mesh=mesh,
        in_specs=placed,
        out_specs=(P("dom", "feat"), P("dom", "feat"), P("feat", None), P("feat", None), P("feat")),
        check_vma=False,
    )
```

```python
import functools
import math

import jax
import jax.numpy as jnp
from jax import lax
from jax.experimental import pallas as pl
from jax.experimental.pallas import tpu as pltpu
from jax.sharding import PartitionSpec as P

BF = jnp.bfloat16
F32 = jnp.float32


def spread_rows(table, width):
    peers, slots = table.shape
    lanes = peers * width
    lane = lax.broadcasted_iota(jnp.int32, (slots, lanes), 1)
    slot = lax.broadcasted_iota(jnp.int32, (slots, lanes), 0)
    place = jnp.where(lane % width == slot, 1.0, 0.0).astype(BF)
    wide = jnp.dot(table.astype(BF), place, preferred_element_type=F32)
    peer = lax.broadcasted_iota(jnp.int32, (peers, lanes), 0)
    at = lax.broadcasted_iota(jnp.int32, (peers, lanes), 1)
    return jnp.sum(jnp.where(at // width == peer, wide, 0.0), axis=0, keepdims=True)


def source_matrix(send, hubs, rows, width):
    peers, slots = send.shape
    hub_here = hubs.shape[1]
    lanes = peers * width
    lane = lax.broadcasted_iota(jnp.int32, (1, lanes), 1) % width
    index = spread_rows(send.astype(F32), width)
    for k in range(hub_here):
        index = jnp.where(lane == slots + k, hubs[0:1, k : k + 1].astype(F32), index)
    index = jnp.where(lane < slots + hub_here, index, -1.0)
    row = lax.broadcasted_iota(jnp.int32, (rows, lanes), 0).astype(F32)
    return jnp.where(row == index, 1.0, 0.0).astype(BF)


def source_rows(send, hubs, rows, width):
    peers, slots = send.shape
    hub_here = hubs.shape[1]
    lanes = peers * width
    slot = lax.broadcasted_iota(jnp.int32, (lanes, slots), 0) % width
    place = jnp.where(slot == lax.broadcasted_iota(jnp.int32, (lanes, slots), 1), 1.0, 0.0).astype(BF)
    wide = lax.dot_general(
        place, send.astype(F32).astype(BF), (((1,), (1,)), ((), ())), preferred_element_type=F32
    )
    line = lax.broadcasted_iota(jnp.int32, (lanes, peers), 0)
    for k in range(hub_here):
        wide = jnp.where(line % width == slots + k, hubs[0:1, k : k + 1].astype(F32), wide)
    wide = jnp.where(line % width < slots + hub_here, wide, -1.0)
    wide = jnp.where(line // width == lax.broadcasted_iota(jnp.int32, (lanes, peers), 1), wide, 0.0)
    index = jnp.dot(wide.astype(BF), jnp.ones((peers, rows), BF), preferred_element_type=F32)
    row = lax.broadcasted_iota(jnp.int32, (lanes, rows), 1).astype(F32)
    return jnp.where(row == index, 1.0, 0.0).astype(BF)


def send_kernel(
    width, x_ref, cot_ref, ws_ref, wn_ref, bias_ref, send_ref, hub_ref, out_ref, pack_ref, send_v, hub_v, bias_v, sems
):
    rows, cols = x_ref.shape
    depth, full = ws_ref.shape
    blocks = full // cols
    base = 2 * blocks * depth
    moves = [
        (send_ref, send_v),
        (hub_ref, hub_v),
        (x_ref, pack_ref.at[base : base + rows, :]),
        (bias_ref, bias_v),
        (cot_ref, pack_ref.at[base + rows : base + 2 * rows, :]),
    ]
    for kind, w_ref in enumerate((ws_ref, wn_ref)):
        for j in range(blocks):
            at = (kind * blocks + j) * depth
            moves.append((w_ref.at[:, j * cols : (j + 1) * cols], pack_ref.at[at : at + depth, :]))
    copies = [pltpu.make_async_copy(src, dst, sems.at[i]) for i, (src, dst) in enumerate(moves)]
    for copy in copies:
        copy.start()
    for copy in copies[:2]:
        copy.wait()
    mark = source_rows(send_v[0], hub_v[...], rows, width)
    copies[2].wait()
    taken = jnp.dot(mark, pack_ref[base : base + rows, :], preferred_element_type=F32).astype(BF)
    out_ref[...] = taken.reshape(out_ref.shape)
    for copy in copies[3:]:
        copy.wait()
    pack_ref[base + 2 * rows :, :] = jnp.broadcast_to(bias_v[...], (16, cols))


def mix_kernel(
    width, count_ref, pos_ref, live_ref, tile_ref, dest_ref, gw_ref, hw_ref, send_ref, hub_ref,
    mix_ref, turned_ref, mark_ref, pos_v, live_v, tile_v, dest_v, gw_v, hw_v, send_v, hub_v, sems,
):
    pairs = (
        (pos_ref, pos_v), (live_ref, live_v), (tile_ref, tile_v), (dest_ref, dest_v),
        (gw_ref, gw_v), (hw_ref, hw_v), (send_ref, send_v), (hub_ref, hub_v),
    )
    copies = [pltpu.make_async_copy(src, dst, sems.at[i]) for i, (src, dst) in enumerate(pairs)]
    for copy in copies:
        copy.start()
    for copy in copies:
        copy.wait()
    rows = mix_ref.shape[0]
    tiles, tile = tile_v.shape[1:3]
    peers, slots = dest_v.shape[1:]
    side = rows // tile
    lanes = peers * width
    hubs = hw_v.shape[0]
    hub_here = hubs // peers
    for r in range(side):
        for c in range(side):
            total = jnp.zeros((tile, tile), BF)
            for t in range(tiles):
                used = jnp.logical_and(pos_v[0:1, t : t + 1] == r * side + c, t < count_ref[...])
                total = jnp.where(used, tile_v[0, t], total)
            mix_ref[r * tile : (r + 1) * tile, c * tile : (c + 1) * tile] = total
    dest = spread_rows(dest_v[0].astype(F32), width)
    coef = spread_rows(gw_v[0], width)
    peer = lax.broadcasted_iota(jnp.int32, (peers, lanes), 0)
    at = lax.broadcasted_iota(jnp.int32, (peers, lanes), 1)
    owner = jnp.where(at // width == peer, 1.0, 0.0).astype(BF)
    limit = jnp.dot(live_v[...].astype(F32).astype(BF), owner, preferred_element_type=F32)
    lane = lax.broadcasted_iota(jnp.int32, (1, lanes), 1) % width
    coef = jnp.where(jnp.logical_and(lane.astype(F32) < limit, lane < slots), coef, 0.0)
    row = lax.broadcasted_iota(jnp.int32, (rows, lanes), 0).astype(F32)
    ghost = jnp.where(row == dest, coef, 0.0)
    hub = lax.broadcasted_iota(jnp.int32, (hubs, lanes), 0)
    at = lax.broadcasted_iota(jnp.int32, (hubs, lanes), 1)
    place = jnp.where(
        jnp.logical_and(at // width == hub // hub_here, at % width == slots + hub % hub_here), 1.0, 0.0
    ).astype(BF)
    hub_mix = lax.dot_general(hw_v[...], place, (((0,), (0,)), ((), ())), preferred_element_type=F32)
    mix_ref[:, rows:] = (ghost + hub_mix).astype(BF)
    turned_ref[...] = mix_ref[...].T
    mark_ref[...] = source_matrix(send_v[0], hub_v[...], rows, width)


def neigh_kernel(x_ref, mix_ref, far_ref, got_ref, neigh_ref, passed_ref):
    rows, cols = x_ref.shape
    lanes = mix_ref.shape[1] - rows
    total = jnp.dot(mix_ref[:, :rows], x_ref[...], preferred_element_type=F32)
    total = total + jnp.dot(mix_ref[:, rows:], got_ref[...].reshape(lanes, cols), preferred_element_type=F32)
    neigh_ref[...] = total.astype(BF)


def dense_kernel(slots, hub_here, feats, width, me_ref, side_ref, x_ref, ws_ref, wn_ref, turned_ref, *refs):
    pack_refs, n_refs = refs[:feats], refs[feats : 2 * feats]
    out_ref, back_ref, send_ref, pre_ref, cot_ref, bias_ref, hold_ref = refs[2 * feats :]
    rows, cols = x_ref.shape
    depth, full = ws_ref.shape
    blocks = full // cols
    half, height = send_ref.shape[:2]
    lanes = turned_ref.shape[0] - rows
    me = me_ref[0]
    base = 2 * blocks * depth
    pre = jnp.zeros((rows, full), F32)
    for d, pack in enumerate(pack_refs):
        owner = me ^ d
        cut = pl.ds(pl.multiple_of(owner * cols, cols), cols)
        cot_ref[:, cut] = pack[base + rows : base + 2 * rows, :]
        bias_ref[:, cut] = pack[base + 2 * rows : base + 2 * rows + 16, :]
        w_s = jnp.concatenate([pack[j * depth : (j + 1) * depth, :] for j in range(blocks)], axis=1)
        w_n = jnp.concatenate([pack[(blocks + j) * depth : (blocks + j + 1) * depth, :] for j in range(blocks)], axis=1)
        left = jnp.concatenate([pack[base : base + rows, :], n_refs[d][...]], axis=1)
        right = jnp.concatenate([w_s, w_n], axis=0)
        pre = pre + jnp.dot(left, right, preferred_element_type=F32)
    pre = pre + bias_ref[0:1, :].astype(F32)
    pre_ref[...] = pre
    sig = jax.nn.sigmoid(pre)
    grad = (cot_ref[...].astype(F32) * sig * (1.0 + pre * (1.0 - sig))).astype(BF)
    cot_ref[...] = grad
    mine = pl.ds(pl.multiple_of(me * cols, cols), cols)
    own = pre_ref[:, mine]
    out_ref[...] = (own * jax.nn.sigmoid(own)).astype(BF)
    both = jnp.concatenate([ws_ref[...], wn_ref[...]], axis=0)
    into = lax.dot_general(grad, both, (((1,), (1,)), ((), ())), preferred_element_type=F32)
    neigh_grad = into[:, depth:].astype(BF)
    spread = jnp.dot(turned_ref[...], neigh_grad, preferred_element_type=F32)
    back_ref[...] = into[:, :depth] + spread[:rows]
    sums = jnp.sum(cot_ref[:, mine].astype(F32), axis=0, keepdims=True)
    high = sums.astype(BF).astype(F32)
    line = lax.broadcasted_iota(jnp.int32, (lanes, cols), 0) % width
    away = jnp.where(line == slots + hub_here, high, spread[rows:])
    away = jnp.where(line == slots + hub_here + 1, sums - high, away)
    hold_ref[...] = away.astype(BF).reshape(hold_ref.shape)
    here = side_ref[0] * half
    send_ref[:, :width, :] = hold_ref[pl.ds(here, half)]
    send_ref[:, width : 2 * width, :] = hold_ref[pl.ds(half - here, half)]
    pair = jnp.concatenate([x_ref[...], n_refs[0][...]], axis=1)
    weights = lax.dot_general(pair, grad, (((0,), (0,)), ((), ())), preferred_element_type=F32).astype(BF)
    share = height - 2 * width
    step = min(share, depth)
    for j in range(blocks):
        for kind in range(2):
            block = weights[kind * depth : (kind + 1) * depth, j * cols : (j + 1) * cols]
            for part in range(depth // step):
                at = (j * 2 + kind) * depth + part * step
                low = 2 * width + at % share
                send_ref[at // share, low : low + step, :] = block[part * step : (part + 1) * step]


def sum_kernel(width, got_ref, sum_ref, relay_ref):
    half = got_ref.shape[0]
    total = jnp.zeros(sum_ref.shape, F32)
    for j in range(half):
        total = total + got_ref[j, 2 * width :, :].astype(F32)
    sum_ref[...] = total.astype(BF)
    relay_ref[...] = got_ref[:, width : 2 * width, :]


def total_kernel(own_ref, other_ref, relay_ref, part_ref, passed_ref):
    total = (own_ref[...].astype(F32) + other_ref[...].astype(F32)).astype(BF)
    part_ref[...] = jnp.broadcast_to(total, part_ref.shape)


def near_rows(slots, hub_here, width, start, mark_ref, got_ref):
    half = got_ref.shape[0]
    cols = got_ref.shape[-1]
    cut = pl.ds(pl.multiple_of(start * width, 128), half * width)
    rows = got_ref[:, :width, :]
    added = jnp.dot(mark_ref[:, cut], rows.reshape(half * width, cols), preferred_element_type=F32)
    first = slots + hub_here
    bias = jnp.zeros((2, cols), F32)
    for j in range(half):
        bias = bias + got_ref[j, first : first + 2, :].astype(F32)
    return added, jnp.sum(bias, axis=0, keepdims=True)


def near_kernel(slots, hub_here, width, side_ref, back_ref, mark_ref, got_ref, sum_ref, bias_ref):
    half = got_ref.shape[0]
    added, bias = near_rows(slots, hub_here, width, side_ref[0] * half, mark_ref, got_ref)
    sum_ref[...] = back_ref[...] + added
    bias_ref[...] = bias


def last_kernel(
    scale, slots, hub_here, width, side_ref, back_ref, near_ref, mark_ref, got_ref, part_ref,
    grad_ref, bias_ref, self_ref, neigh_ref,
):
    depth, full = self_ref.shape
    half, share, cols = part_ref.shape
    whole = part_ref[...].reshape(half * share, cols).astype(F32) * scale
    for j in range(full // cols):
        at = 2 * j * depth
        self_ref[:, j * cols : (j + 1) * cols] = whole[at : at + depth]
        neigh_ref[:, j * cols : (j + 1) * cols] = whole[at + depth : at + 2 * depth]
    added, bias = near_rows(slots, hub_here, width, half - side_ref[0] * half, mark_ref, got_ref)
    grad_ref[...] = (back_ref[...] + added).astype(BF)
    bias_ref[...] = (near_ref[...] + bias) * scale


VMEM = pl.BlockSpec(memory_space=pltpu.VMEM)
SMEM = pl.BlockSpec(memory_space=pltpu.SMEM)
ANY = pl.BlockSpec(memory_space=pl.ANY)
HBM = pl.BlockSpec(memory_space=pltpu.HBM)
PARAMS = pltpu.CompilerParams(vmem_limit_bytes=40 * 1024 * 1024)


def shape(dims, kind):
    return jax.ShapeDtypeStruct(dims, kind)


def partner(block, axis, k):
    return lax.ppermute(block, axis, [(i, i ^ k) for i in range(lax.axis_size(axis))])


def exchange(blocks, groups=None):
    return lax.all_to_all(blocks, "dom", split_axis=0, concat_axis=0, axis_index_groups=groups, tiled=True)


def on_device(
    features,
    w_self,
    w_neigh,
    bias,
    cotangent,
    tile_vals,
    tile_pos,
    tile_count,
    send_rows,
    recv_dest,
    ghost_weight,
    recv_count,
    hub_rows,
    hub_weight,
):
    rows, cols = features.shape
    depth, full = w_self.shape
    blocks = full // cols
    peers, slots = send_rows.shape[1:]
    hub_here = hub_rows.shape[-1]
    width = -(-(slots + hub_here + 2) // 16) * 16
    lanes = peers * width
    half = peers // 2
    share = 2 * blocks * depth // half
    halves = [list(range(half)), list(range(half, peers))]
    scale = 1.0 / math.sqrt(peers * rows)
    feats = lax.axis_size("feat")
    me = lax.axis_index("feat").astype(jnp.int32).reshape(1)
    side = (lax.axis_index("dom") >= half).astype(jnp.int32).reshape(1)
    pack_rows = 2 * blocks * depth + 2 * rows + 16

    def pinned(*arrays):
        return [pltpu.with_memory_space_constraint(a, pltpu.HBM) for a in arrays]

    first = pinned(features, cotangent, w_self, w_neigh, bias.reshape(1, cols), send_rows, hub_rows)
    outgoing, pack = pl.pallas_call(
        functools.partial(send_kernel, width),
        out_shape=(shape((peers, width, cols), BF), shape((pack_rows, cols), BF)),
        in_specs=[HBM] * len(first),
        out_specs=(VMEM,) * 2,
        scratch_shapes=[
            pltpu.VMEM(send_rows.shape, jnp.int32),
            pltpu.VMEM(hub_rows.shape, jnp.int32),
            pltpu.VMEM((1, cols), BF),
            pltpu.SemaphoreType.DMA((5 + 2 * blocks,)),
        ],
        compiler_params=PARAMS,
    )(*first)

    far = partner(pack, "feat", 2)
    near = partner(pack, "feat", 1)
    incoming = exchange(outgoing)
    edges = pinned(
        tile_pos, recv_count, tile_vals, recv_dest, ghost_weight, hub_weight.T, send_rows, hub_rows
    )
    mix, turned, mark = pl.pallas_call(
        functools.partial(mix_kernel, width),
        out_shape=(
            shape((rows, rows + lanes), BF),
            shape((rows + lanes, rows), BF),
            shape((rows, lanes), BF),
        ),
        in_specs=[VMEM] + [HBM] * len(edges),
        out_specs=(VMEM,) * 3,
        scratch_shapes=[pltpu.VMEM(a.shape, a.dtype) for a in edges] + [pltpu.SemaphoreType.DMA((len(edges),))],
        compiler_params=PARAMS,
        cost_estimate=pl.CostEstimate(flops=10**8, bytes_accessed=3 * 10**6, transcendentals=0),
    )(tile_count.reshape(1, 1), *edges)
    neigh, far = pl.pallas_call(
        neigh_kernel,
        out_shape=(shape((rows, cols), BF), shape((pack_rows, cols), BF)),
        in_specs=[VMEM, VMEM, ANY, VMEM],
        out_specs=(VMEM, ANY),
        input_output_aliases={2: 1},
        compiler_params=PARAMS,
    )(features, mix, far, incoming)
    last = partner(far, "feat", 1)
    far_neigh = partner(neigh, "feat", 2)
    every = [neigh, partner(neigh, "feat", 1), far_neigh, partner(far_neigh, "feat", 1)]

    output, back, returned = pl.pallas_call(
        functools.partial(dense_kernel, slots, hub_here, feats, width),
        out_shape=(
            shape((rows, cols), BF),
            shape((rows, cols), F32),
            shape((half, 2 * width + share, cols), BF),
        ),
        in_specs=[SMEM] * 2 + [VMEM] * (4 + 2 * feats),
        out_specs=(VMEM,) * 3,
        scratch_shapes=[
            pltpu.VMEM((rows, full), F32),
            pltpu.VMEM((rows, full), BF),
            pltpu.VMEM((16, full), BF),
            pltpu.VMEM((peers, width, cols), BF),
        ],
        compiler_params=PARAMS,
    )(me, side, features, w_self, w_neigh, turned, pack, near, far, last, *every)

    arrived = exchange(returned, halves)
    half_sum, relay = pl.pallas_call(
        functools.partial(sum_kernel, width),
        out_shape=(shape((share, cols), BF), shape((half, width, cols), BF)),
        in_specs=[VMEM],
        out_specs=(VMEM,) * 2,
        compiler_params=PARAMS,
    )(arrived)
    other_sum = partner(half_sum, "dom", half)
    back, near_bias = pl.pallas_call(
        functools.partial(near_kernel, slots, hub_here, width),
        out_shape=(shape((rows, cols), F32), shape((1, cols), F32)),
        in_specs=[SMEM] + [VMEM] * 3,
        out_specs=(VMEM,) * 2,
        compiler_params=PARAMS,
        cost_estimate=pl.CostEstimate(flops=10**8, bytes_accessed=10**6, transcendentals=0),
    )(side, back, mark, arrived)
    part, relay = pl.pallas_call(
        total_kernel,
        out_shape=(shape((half, share, cols), BF), shape((half, width, cols), BF)),
        in_specs=[VMEM, VMEM, ANY],
        out_specs=(VMEM, ANY),
        input_output_aliases={2: 1},
        compiler_params=PARAMS,
    )(half_sum, other_sum, relay)
    crossed = partner(relay, "dom", half)
    parts = exchange(part, halves)
    grad_features, grad_bias, grad_self, grad_neigh = pl.pallas_call(
        functools.partial(last_kernel, scale, slots, hub_here, width),
        out_shape=(
            shape((rows, cols), BF),
            shape((1, cols), F32),
            shape((depth, full), F32),
            shape((depth, full), F32),
        ),
        in_specs=[SMEM] + [VMEM] * 5,
        out_specs=(VMEM,) * 4,
        compiler_params=PARAMS,
    )(side, back, near_bias, mark, crossed, parts)
    return output, grad_features, grad_self, grad_neigh, grad_bias.reshape(cols)


def solution(mesh):
    placed = (
        P("dom", "feat"),
        P("feat", None),
        P("feat", None),
        P("feat"),
        P("dom", "feat"),
        P("dom", None, None, None),
        P("dom", None),
        P("dom"),
        P("dom", None, None),
        P("dom", None, None),
        P("dom", None, None),
        P("dom", None),
        P("dom", None),
        P("dom", None),
    )
    return jax.shard_map(
        on_device,
        mesh=mesh,
        in_specs=placed,
        out_specs=(P("dom", "feat"), P("dom", "feat"), P("feat", None), P("feat", None), P("feat")),
        check_vma=False,
    )
```

```python
import functools
import math

import jax
import jax.numpy as jnp
from jax import lax
from jax.experimental import pallas as pl
from jax.experimental.pallas import tpu as pltpu
from jax.sharding import PartitionSpec as P

BF = jnp.bfloat16
F32 = jnp.float32


def spread_rows(table, width):
    peers, slots = table.shape
    lanes = peers * width
    lane = lax.broadcasted_iota(jnp.int32, (slots, lanes), 1)
    slot = lax.broadcasted_iota(jnp.int32, (slots, lanes), 0)
    place = jnp.where(lane % width == slot, 1.0, 0.0).astype(BF)
    wide = jnp.dot(table.astype(BF), place, preferred_element_type=F32)
    peer = lax.broadcasted_iota(jnp.int32, (peers, lanes), 0)
    at = lax.broadcasted_iota(jnp.int32, (peers, lanes), 1)
    return jnp.sum(jnp.where(at // width == peer, wide, 0.0), axis=0, keepdims=True)


def source_matrix(send, hubs, rows, width):
    peers, slots = send.shape
    hub_here = hubs.shape[1]
    lanes = peers * width
    lane = lax.broadcasted_iota(jnp.int32, (1, lanes), 1) % width
    index = spread_rows(send.astype(F32), width)
    for k in range(hub_here):
        index = jnp.where(lane == slots + k, hubs[0:1, k : k + 1].astype(F32), index)
    index = jnp.where(lane < slots + hub_here, index, -1.0)
    row = lax.broadcasted_iota(jnp.int32, (rows, lanes), 0).astype(F32)
    return jnp.where(row == index, 1.0, 0.0).astype(BF)


def source_rows(send, hubs, rows, width):
    peers, slots = send.shape
    hub_here = hubs.shape[1]
    lanes = peers * width
    slot = lax.broadcasted_iota(jnp.int32, (lanes, slots), 0) % width
    place = jnp.where(slot == lax.broadcasted_iota(jnp.int32, (lanes, slots), 1), 1.0, 0.0).astype(BF)
    wide = lax.dot_general(
        place, send.astype(F32).astype(BF), (((1,), (1,)), ((), ())), preferred_element_type=F32
    )
    line = lax.broadcasted_iota(jnp.int32, (lanes, peers), 0)
    for k in range(hub_here):
        wide = jnp.where(line % width == slots + k, hubs[0:1, k : k + 1].astype(F32), wide)
    wide = jnp.where(line % width < slots + hub_here, wide, -1.0)
    wide = jnp.where(line // width == lax.broadcasted_iota(jnp.int32, (lanes, peers), 1), wide, 0.0)
    index = jnp.dot(wide.astype(BF), jnp.ones((peers, rows), BF), preferred_element_type=F32)
    row = lax.broadcasted_iota(jnp.int32, (lanes, rows), 1).astype(F32)
    return jnp.where(row == index, 1.0, 0.0).astype(BF)


def send_kernel(
    width, x_ref, cot_ref, ws_ref, wn_ref, bias_ref, send_ref, hub_ref, pos_ref, live_ref, tile_ref, dest_ref, gw_ref, hw_ref,
    out_ref, pack_ref, send_v, hub_v, pos_v, live_v, tile_v, dest_v, gw_v, hw_v, bias_v, sems,
):
    rows, cols = x_ref.shape
    depth, full = ws_ref.shape
    blocks = full // cols
    base = 2 * blocks * depth
    moves = [
        (send_ref, send_v),
        (hub_ref, hub_v),
        (x_ref, pack_ref.at[base : base + rows, :]),
        (bias_ref, bias_v),
        (cot_ref, pack_ref.at[base + rows : base + 2 * rows, :]),
    ]
    for kind, w_ref in enumerate((ws_ref, wn_ref)):
        for j in range(blocks):
            at = (kind * blocks + j) * depth
            moves.append((w_ref.at[:, j * cols : (j + 1) * cols], pack_ref.at[at : at + depth, :]))
    moves += [
        (pos_ref, pos_v), (live_ref, live_v), (tile_ref, tile_v), (dest_ref, dest_v),
        (gw_ref, gw_v), (hw_ref, hw_v),
    ]
    copies = [pltpu.make_async_copy(src, dst, sems.at[i]) for i, (src, dst) in enumerate(moves)]
    for copy in copies:
        copy.start()
    for copy in copies[:2]:
        copy.wait()
    mark = source_rows(send_v[0], hub_v[...], rows, width)
    copies[2].wait()
    taken = jnp.dot(mark, pack_ref[base : base + rows, :], preferred_element_type=F32).astype(BF)
    out_ref[...] = taken.reshape(out_ref.shape)
    for copy in copies[3:]:
        copy.wait()
    pack_ref[base + 2 * rows :, :] = jnp.broadcast_to(bias_v[...], (16, cols))


def mix_kernel(width, count_ref, send_v, hub_v, pos_v, live_v, tile_v, dest_v, gw_v, hw_v, mix_ref, turned_ref, mark_ref):
    rows = mix_ref.shape[0]
    tiles, tile = tile_v.shape[1:3]
    peers, slots = dest_v.shape[1:]
    side = rows // tile
    lanes = peers * width
    hubs = hw_v.shape[0]
    hub_here = hubs // peers
    for r in range(side):
        for c in range(side):
            total = jnp.zeros((tile, tile), BF)
            for t in range(tiles):
                used = jnp.logical_and(pos_v[0:1, t : t + 1] == r * side + c, t < count_ref[...])
                total = jnp.where(used, tile_v[0, t], total)
            mix_ref[r * tile : (r + 1) * tile, c * tile : (c + 1) * tile] = total
    dest = spread_rows(dest_v[0].astype(F32), width)
    coef = spread_rows(gw_v[0], width)
    peer = lax.broadcasted_iota(jnp.int32, (peers, lanes), 0)
    at = lax.broadcasted_iota(jnp.int32, (peers, lanes), 1)
    owner = jnp.where(at // width == peer, 1.0, 0.0).astype(BF)
    limit = jnp.dot(live_v[...].astype(F32).astype(BF), owner, preferred_element_type=F32)
    lane = lax.broadcasted_iota(jnp.int32, (1, lanes), 1) % width
    coef = jnp.where(jnp.logical_and(lane.astype(F32) < limit, lane < slots), coef, 0.0)
    row = lax.broadcasted_iota(jnp.int32, (rows, lanes), 0).astype(F32)
    ghost = jnp.where(row == dest, coef, 0.0)
    hub = lax.broadcasted_iota(jnp.int32, (hubs, lanes), 0)
    at = lax.broadcasted_iota(jnp.int32, (hubs, lanes), 1)
    place = jnp.where(
        jnp.logical_and(at // width == hub // hub_here, at % width == slots + hub % hub_here), 1.0, 0.0
    ).astype(BF)
    hub_mix = lax.dot_general(hw_v[...], place, (((0,), (0,)), ((), ())), preferred_element_type=F32)
    mix_ref[:, rows:] = (ghost + hub_mix).astype(BF)
    turned_ref[...] = mix_ref[...].T
    mark_ref[...] = source_matrix(send_v[0], hub_v[...], rows, width)


def pass_kernel(after_ref, far_ref, passed_ref):
    pass


def neigh_kernel(x_ref, mix_ref, got_ref, neigh_ref):
    rows, cols = x_ref.shape
    lanes = mix_ref.shape[1] - rows
    total = jnp.dot(mix_ref[:, :rows], x_ref[...], preferred_element_type=F32)
    total = total + jnp.dot(mix_ref[:, rows:], got_ref[...].reshape(lanes, cols), preferred_element_type=F32)
    neigh_ref[...] = total.astype(BF)


def dense_kernel(slots, hub_here, feats, width, me_ref, side_ref, x_ref, ws_ref, wn_ref, turned_ref, *refs):
    pack_refs, n_refs = refs[:feats], refs[feats : 2 * feats]
    out_ref, back_ref, send_ref, pre_ref, cot_ref, bias_ref = refs[2 * feats :]
    rows, cols = x_ref.shape
    depth, full = ws_ref.shape
    blocks = full // cols
    half, height = send_ref.shape[:2]
    me = me_ref[0]
    base = 2 * blocks * depth
    pre = jnp.zeros((rows, full), F32)
    for d, pack in enumerate(pack_refs):
        owner = me ^ d
        cut = pl.ds(pl.multiple_of(owner * cols, cols), cols)
        cot_ref[:, cut] = pack[base + rows : base + 2 * rows, :]
        bias_ref[:, cut] = pack[base + 2 * rows : base + 2 * rows + 16, :]
        w_s = jnp.concatenate([pack[j * depth : (j + 1) * depth, :] for j in range(blocks)], axis=1)
        w_n = jnp.concatenate([pack[(blocks + j) * depth : (blocks + j + 1) * depth, :] for j in range(blocks)], axis=1)
        left = jnp.concatenate([pack[base : base + rows, :], n_refs[d][...]], axis=1)
        right = jnp.concatenate([w_s, w_n], axis=0)
        pre = pre + jnp.dot(left, right, preferred_element_type=F32)
    pre = pre + bias_ref[0:1, :].astype(F32)
    pre_ref[...] = pre
    sig = jax.nn.sigmoid(pre)
    grad = (cot_ref[...].astype(F32) * sig * (1.0 + pre * (1.0 - sig))).astype(BF)
    cot_ref[...] = grad
    mine = pl.ds(pl.multiple_of(me * cols, cols), cols)
    own = pre_ref[:, mine]
    out_ref[...] = (own * jax.nn.sigmoid(own)).astype(BF)
    both = jnp.concatenate([ws_ref[...], wn_ref[...]], axis=0)
    into = lax.dot_general(grad, both, (((1,), (1,)), ((), ())), preferred_element_type=F32)
    neigh_grad = into[:, depth:].astype(BF)
    back_ref[...] = into[:, :depth] + jnp.dot(turned_ref[:rows, :], neigh_grad, preferred_element_type=F32)
    sums = jnp.sum(cot_ref[:, mine].astype(F32), axis=0, keepdims=True)
    high = sums.astype(BF).astype(F32)
    line = lax.broadcasted_iota(jnp.int32, (half * width, cols), 0) % width
    here = side_ref[0] * half
    for at, start in ((0, here), (width, half - here)):
        cut = pl.ds(pl.multiple_of(rows + start * width, 128), half * width)
        away = jnp.dot(turned_ref[cut, :], neigh_grad, preferred_element_type=F32)
        away = jnp.where(line == slots + hub_here, high, away)
        away = jnp.where(line == slots + hub_here + 1, sums - high, away)
        send_ref[:, at : at + width, :] = away.astype(BF).reshape(half, width, cols)
    pair = jnp.concatenate([x_ref[...], n_refs[0][...]], axis=1)
    weights = lax.dot_general(pair, grad, (((0,), (0,)), ((), ())), preferred_element_type=F32).astype(BF)
    share = height - 2 * width
    step = min(share, depth)
    for j in range(blocks):
        for kind in range(2):
            block = weights[kind * depth : (kind + 1) * depth, j * cols : (j + 1) * cols]
            for part in range(depth // step):
                at = (j * 2 + kind) * depth + part * step
                low = 2 * width + at % share
                send_ref[at // share, low : low + step, :] = block[part * step : (part + 1) * step]


def sum_kernel(width, got_ref, sum_ref, relay_ref):
    half = got_ref.shape[0]
    total = jnp.zeros(sum_ref.shape, F32)
    for j in range(half):
        total = total + got_ref[j, 2 * width :, :].astype(F32)
    sum_ref[...] = total.astype(BF)
    relay_ref[...] = got_ref[:, width : 2 * width, :]


def total_kernel(own_ref, other_ref, part_ref):
    total = (own_ref[...].astype(F32) + other_ref[...].astype(F32)).astype(BF)
    part_ref[...] = jnp.broadcast_to(total, part_ref.shape)


def near_rows(slots, hub_here, width, start, mark_ref, got_ref):
    half = got_ref.shape[0]
    cols = got_ref.shape[-1]
    cut = pl.ds(pl.multiple_of(start * width, 128), half * width)
    rows = got_ref[:, :width, :]
    added = jnp.dot(mark_ref[:, cut], rows.reshape(half * width, cols), preferred_element_type=F32)
    first = slots + hub_here
    bias = jnp.zeros((2, cols), F32)
    for j in range(half):
        bias = bias + got_ref[j, first : first + 2, :].astype(F32)
    return added, jnp.sum(bias, axis=0, keepdims=True)


def near_kernel(slots, hub_here, width, side_ref, back_ref, mark_ref, got_ref, sum_ref, bias_ref):
    half = got_ref.shape[0]
    added, bias = near_rows(slots, hub_here, width, side_ref[0] * half, mark_ref, got_ref)
    sum_ref[...] = back_ref[...] + added
    bias_ref[...] = bias


def last_kernel(
    scale, slots, hub_here, width, side_ref, back_ref, near_ref, mark_ref, got_ref, part_ref,
    grad_ref, bias_ref, self_ref, neigh_ref,
):
    depth, full = self_ref.shape
    half, share, cols = part_ref.shape
    whole = part_ref[...].reshape(half * share, cols).astype(F32) * scale
    for j in range(full // cols):
        at = 2 * j * depth
        self_ref[:, j * cols : (j + 1) * cols] = whole[at : at + depth]
        neigh_ref[:, j * cols : (j + 1) * cols] = whole[at + depth : at + 2 * depth]
    added, bias = near_rows(slots, hub_here, width, half - side_ref[0] * half, mark_ref, got_ref)
    grad_ref[...] = (back_ref[...] + added).astype(BF)
    bias_ref[...] = (near_ref[...] + bias) * scale


VMEM = pl.BlockSpec(memory_space=pltpu.VMEM)
SMEM = pl.BlockSpec(memory_space=pltpu.SMEM)
ANY = pl.BlockSpec(memory_space=pl.ANY)
HBM = pl.BlockSpec(memory_space=pltpu.HBM)
PARAMS = pltpu.CompilerParams(vmem_limit_bytes=40 * 1024 * 1024)


def shape(dims, kind):
    return jax.ShapeDtypeStruct(dims, kind)


def partner(block, axis, k):
    return lax.ppermute(block, axis, [(i, i ^ k) for i in range(lax.axis_size(axis))])


def exchange(blocks, groups=None):
    return lax.all_to_all(blocks, "dom", split_axis=0, concat_axis=0, axis_index_groups=groups, tiled=True)


def on_device(
    features,
    w_self,
    w_neigh,
    bias,
    cotangent,
    tile_vals,
    tile_pos,
    tile_count,
    send_rows,
    recv_dest,
    ghost_weight,
    recv_count,
    hub_rows,
    hub_weight,
):
    rows, cols = features.shape
    depth, full = w_self.shape
    blocks = full // cols
    peers, slots = send_rows.shape[1:]
    hub_here = hub_rows.shape[-1]
    width = -(-(slots + hub_here + 2) // 16) * 16
    lanes = peers * width
    half = peers // 2
    share = 2 * blocks * depth // half
    halves = [list(range(half)), list(range(half, peers))]
    scale = 1.0 / math.sqrt(peers * rows)
    feats = lax.axis_size("feat")
    me = lax.axis_index("feat").astype(jnp.int32).reshape(1)
    side = (lax.axis_index("dom") >= half).astype(jnp.int32).reshape(1)
    pack_rows = 2 * blocks * depth + 2 * rows + 16

    def pinned(*arrays):
        return [pltpu.with_memory_space_constraint(a, pltpu.HBM) for a in arrays]

    first = pinned(features, cotangent, w_self, w_neigh, bias.reshape(1, cols), send_rows, hub_rows)
    edges = pinned(tile_pos, recv_count, tile_vals, recv_dest, ghost_weight, hub_weight.T)
    moved = (send_rows, hub_rows, *edges)
    outgoing, pack, *moved = pl.pallas_call(
        functools.partial(send_kernel, width),
        out_shape=(
            shape((peers, width, cols), BF),
            shape((pack_rows, cols), BF),
            *(shape(a.shape, a.dtype) for a in moved),
        ),
        in_specs=[HBM] * (len(first) + len(edges)),
        out_specs=(VMEM,) * (2 + len(moved)),
        scratch_shapes=[
            pltpu.VMEM((1, cols), BF),
            pltpu.SemaphoreType.DMA((11 + 2 * blocks,)),
        ],
        compiler_params=PARAMS,
    )(*first, *edges)

    far = partner(pack, "feat", 2)
    near = partner(pack, "feat", 1)
    incoming = exchange(outgoing)
    mix, turned, mark = pl.pallas_call(
        functools.partial(mix_kernel, width),
        out_shape=(
            shape((rows, rows + lanes), BF),
            shape((rows + lanes, rows), BF),
            shape((rows, lanes), BF),
        ),
        in_specs=[VMEM] * (1 + len(moved)),
        out_specs=(VMEM,) * 3,
        compiler_params=PARAMS,
        cost_estimate=pl.CostEstimate(flops=10**8, bytes_accessed=3 * 10**6, transcendentals=0),
    )(tile_count.reshape(1, 1), *moved)
    neigh = pl.pallas_call(
        neigh_kernel,
        out_shape=shape((rows, cols), BF),
        in_specs=[VMEM] * 3,
        out_specs=VMEM,
        compiler_params=PARAMS,
    )(features, mix, incoming)
    far_neigh = partner(neigh, "feat", 2)
    near_neigh = partner(neigh, "feat", 1)
    far = pl.pallas_call(
        pass_kernel,
        out_shape=shape((pack_rows, cols), BF),
        in_specs=[ANY, ANY],
        out_specs=ANY,
        input_output_aliases={1: 0},
        compiler_params=PARAMS,
    )(near_neigh, far)
    last = partner(far, "feat", 1)
    every = [neigh, near_neigh, far_neigh, partner(far_neigh, "feat", 1)]

    output, back, returned = pl.pallas_call(
        functools.partial(dense_kernel, slots, hub_here, feats, width),
        out_shape=(
            shape((rows, cols), BF),
            shape((rows, cols), F32),
            shape((half, 2 * width + share, cols), BF),
        ),
        in_specs=[SMEM] * 2 + [VMEM] * (4 + 2 * feats),
        out_specs=(VMEM,) * 3,
        scratch_shapes=[
            pltpu.VMEM((rows, full), F32),
            pltpu.VMEM((rows, full), BF),
            pltpu.VMEM((16, full), BF),
        ],
        compiler_params=PARAMS,
    )(me, side, features, w_self, w_neigh, turned, pack, near, far, last, *every)

    arrived = exchange(returned, halves)
    half_sum, relay = pl.pallas_call(
        functools.partial(sum_kernel, width),
        out_shape=(shape((share, cols), BF), shape((half, width, cols), BF)),
        in_specs=[VMEM],
        out_specs=(VMEM,) * 2,
        compiler_params=PARAMS,
    )(arrived)
    other_sum = partner(half_sum, "dom", half)
    back, near_bias = pl.pallas_call(
        functools.partial(near_kernel, slots, hub_here, width),
        out_shape=(shape((rows, cols), F32), shape((1, cols), F32)),
        in_specs=[SMEM] + [VMEM] * 3,
        out_specs=(VMEM,) * 2,
        compiler_params=PARAMS,
        cost_estimate=pl.CostEstimate(flops=10**8, bytes_accessed=10**6, transcendentals=0),
    )(side, back, mark, arrived)
    crossed = partner(relay, "dom", half)
    part = pl.pallas_call(
        total_kernel,
        out_shape=shape((half, share, cols), BF),
        in_specs=[VMEM, VMEM],
        out_specs=VMEM,
        compiler_params=PARAMS,
    )(half_sum, other_sum)
    parts = exchange(part, halves)
    grad_features, grad_bias, grad_self, grad_neigh = pl.pallas_call(
        functools.partial(last_kernel, scale, slots, hub_here, width),
        out_shape=(
            shape((rows, cols), BF),
            shape((1, cols), F32),
            shape((depth, full), F32),
            shape((depth, full), F32),
        ),
        in_specs=[SMEM] + [VMEM] * 5,
        out_specs=(VMEM,) * 4,
        compiler_params=PARAMS,
    )(side, back, near_bias, mark, crossed, parts)
    return output, grad_features, grad_self, grad_neigh, grad_bias.reshape(cols)


def solution(mesh):
    placed = (
        P("dom", "feat"),
        P("feat", None),
        P("feat", None),
        P("feat"),
        P("dom", "feat"),
        P("dom", None, None, None),
        P("dom", None),
        P("dom"),
        P("dom", None, None),
        P("dom", None, None),
        P("dom", None, None),
        P("dom", None),
        P("dom", None),
        P("dom", None),
    )
    return jax.shard_map(
        on_device,
        mesh=mesh,
        in_specs=placed,
        out_specs=(P("dom", "feat"), P("dom", "feat"), P("feat", None), P("feat", None), P("feat")),
        check_vma=False,
    )
```

```python
import functools
import math

import jax
import jax.numpy as jnp
from jax import lax
from jax.experimental import pallas as pl
from jax.experimental.pallas import tpu as pltpu
from jax.sharding import PartitionSpec as P

BF = jnp.bfloat16
F32 = jnp.float32


def spread_rows(table, width):
    peers, slots = table.shape
    lanes = peers * width
    lane = lax.broadcasted_iota(jnp.int32, (slots, lanes), 1)
    slot = lax.broadcasted_iota(jnp.int32, (slots, lanes), 0)
    place = jnp.where(lane % width == slot, 1.0, 0.0).astype(BF)
    wide = jnp.dot(table.astype(BF), place, preferred_element_type=F32)
    peer = lax.broadcasted_iota(jnp.int32, (peers, lanes), 0)
    at = lax.broadcasted_iota(jnp.int32, (peers, lanes), 1)
    return jnp.sum(jnp.where(at // width == peer, wide, 0.0), axis=0, keepdims=True)


def source_matrix(send, hubs, rows, width):
    peers, slots = send.shape
    hub_here = hubs.shape[1]
    lanes = peers * width
    lane = lax.broadcasted_iota(jnp.int32, (1, lanes), 1) % width
    index = spread_rows(send.astype(F32), width)
    for k in range(hub_here):
        index = jnp.where(lane == slots + k, hubs[0:1, k : k + 1].astype(F32), index)
    index = jnp.where(lane < slots + hub_here, index, -1.0)
    row = lax.broadcasted_iota(jnp.int32, (rows, lanes), 0).astype(F32)
    return jnp.where(row == index, 1.0, 0.0).astype(BF)


def source_rows(send, hubs, rows, width):
    peers, slots = send.shape
    hub_here = hubs.shape[1]
    lanes = peers * width
    slot = lax.broadcasted_iota(jnp.int32, (lanes, slots), 0) % width
    place = jnp.where(slot == lax.broadcasted_iota(jnp.int32, (lanes, slots), 1), 1.0, 0.0).astype(BF)
    wide = lax.dot_general(
        place, send.astype(F32).astype(BF), (((1,), (1,)), ((), ())), preferred_element_type=F32
    )
    line = lax.broadcasted_iota(jnp.int32, (lanes, peers), 0)
    for k in range(hub_here):
        wide = jnp.where(line % width == slots + k, hubs[0:1, k : k + 1].astype(F32), wide)
    wide = jnp.where(line % width < slots + hub_here, wide, -1.0)
    wide = jnp.where(line // width == lax.broadcasted_iota(jnp.int32, (lanes, peers), 1), wide, 0.0)
    index = jnp.dot(wide.astype(BF), jnp.ones((peers, rows), BF), preferred_element_type=F32)
    row = lax.broadcasted_iota(jnp.int32, (lanes, rows), 1).astype(F32)
    return jnp.where(row == index, 1.0, 0.0).astype(BF)


def send_kernel(
    width, x_ref, cot_ref, ws_ref, wn_ref, bias_ref, send_ref, hub_ref, pos_ref, live_ref, tile_ref, dest_ref, gw_ref, hw_ref,
    out_ref, pack_ref, send_v, hub_v, pos_v, live_v, tile_v, dest_v, gw_v, hw_v, bias_v, sems,
):
    rows, cols = x_ref.shape
    depth, full = ws_ref.shape
    blocks = full // cols
    base = 2 * blocks * depth
    moves = [
        (send_ref, send_v),
        (hub_ref, hub_v),
        (x_ref, pack_ref.at[base : base + rows, :]),
        (bias_ref, bias_v),
        (cot_ref, pack_ref.at[base + rows : base + 2 * rows, :]),
    ]
    for kind, w_ref in enumerate((ws_ref, wn_ref)):
        for j in range(blocks):
            at = (kind * blocks + j) * depth
            moves.append((w_ref.at[:, j * cols : (j + 1) * cols], pack_ref.at[at : at + depth, :]))
    moves += [
        (pos_ref, pos_v), (live_ref, live_v), (tile_ref, tile_v), (dest_ref, dest_v),
        (gw_ref, gw_v), (hw_ref, hw_v),
    ]
    copies = [pltpu.make_async_copy(src, dst, sems.at[i]) for i, (src, dst) in enumerate(moves)]
    for copy in copies:
        copy.start()
    for copy in copies[:2]:
        copy.wait()
    mark = source_rows(send_v[0], hub_v[...], rows, width)
    copies[2].wait()
    taken = jnp.dot(mark, pack_ref[base : base + rows, :], preferred_element_type=F32).astype(BF)
    out_ref[...] = taken.reshape(out_ref.shape)
    for copy in copies[3:]:
        copy.wait()
    pack_ref[base + 2 * rows :, :] = jnp.broadcast_to(bias_v[...], (16, cols))


def mix_kernel(width, count_ref, send_v, hub_v, pos_v, live_v, tile_v, dest_v, gw_v, hw_v, mix_ref, turned_ref, mark_ref):
    rows = mix_ref.shape[0]
    tiles, tile = tile_v.shape[1:3]
    peers, slots = dest_v.shape[1:]
    side = rows // tile
    lanes = peers * width
    hubs = hw_v.shape[0]
    hub_here = hubs // peers
    for r in range(side):
        for c in range(side):
            total = jnp.zeros((tile, tile), BF)
            for t in range(tiles):
                used = jnp.logical_and(pos_v[0:1, t : t + 1] == r * side + c, t < count_ref[...])
                total = jnp.where(used, tile_v[0, t], total)
            mix_ref[r * tile : (r + 1) * tile, c * tile : (c + 1) * tile] = total
    dest = spread_rows(dest_v[0].astype(F32), width)
    coef = spread_rows(gw_v[0], width)
    peer = lax.broadcasted_iota(jnp.int32, (peers, lanes), 0)
    at = lax.broadcasted_iota(jnp.int32, (peers, lanes), 1)
    owner = jnp.where(at // width == peer, 1.0, 0.0).astype(BF)
    limit = jnp.dot(live_v[...].astype(F32).astype(BF), owner, preferred_element_type=F32)
    lane = lax.broadcasted_iota(jnp.int32, (1, lanes), 1) % width
    coef = jnp.where(jnp.logical_and(lane.astype(F32) < limit, lane < slots), coef, 0.0)
    row = lax.broadcasted_iota(jnp.int32, (rows, lanes), 0).astype(F32)
    ghost = jnp.where(row == dest, coef, 0.0)
    hub = lax.broadcasted_iota(jnp.int32, (hubs, lanes), 0)
    at = lax.broadcasted_iota(jnp.int32, (hubs, lanes), 1)
    place = jnp.where(
        jnp.logical_and(at // width == hub // hub_here, at % width == slots + hub % hub_here), 1.0, 0.0
    ).astype(BF)
    hub_mix = lax.dot_general(hw_v[...], place, (((0,), (0,)), ((), ())), preferred_element_type=F32)
    mix_ref[:, rows:] = (ghost + hub_mix).astype(BF)
    turned_ref[...] = mix_ref[...].T
    mark_ref[...] = source_matrix(send_v[0], hub_v[...], rows, width)


def neigh_kernel(x_ref, mix_ref, far_ref, got_ref, neigh_ref, passed_ref):
    rows, cols = x_ref.shape
    lanes = mix_ref.shape[1] - rows
    total = jnp.dot(mix_ref[:, :rows], x_ref[...], preferred_element_type=F32)
    total = total + jnp.dot(mix_ref[:, rows:], got_ref[...].reshape(lanes, cols), preferred_element_type=F32)
    neigh_ref[...] = total.astype(BF)


def dense_kernel(slots, hub_here, feats, width, count, me_ref, side_ref, seat_ref, x_ref, ws_ref, wn_ref, turned_ref, *refs):
    pack_refs, n_refs = refs[:feats], refs[feats : 2 * feats]
    out_ref, back_ref = refs[2 * feats : 2 * feats + 2]
    send_refs = refs[2 * feats + 2 : 2 * feats + 2 + count]
    pre_ref, cot_ref, bias_ref, hold_ref = refs[2 * feats + 2 + count :]
    send_ref = send_refs[0] if count == 1 else hold_ref
    rows, cols = x_ref.shape
    depth, full = ws_ref.shape
    blocks = full // cols
    half, height = send_ref.shape[:2]
    me = me_ref[0]
    base = 2 * blocks * depth
    pre = jnp.zeros((rows, full), F32)
    for d, pack in enumerate(pack_refs):
        owner = me ^ d
        cut = pl.ds(pl.multiple_of(owner * cols, cols), cols)
        cot_ref[:, cut] = pack[base + rows : base + 2 * rows, :]
        bias_ref[:, cut] = pack[base + 2 * rows : base + 2 * rows + 16, :]
        w_s = jnp.concatenate([pack[j * depth : (j + 1) * depth, :] for j in range(blocks)], axis=1)
        w_n = jnp.concatenate([pack[(blocks + j) * depth : (blocks + j + 1) * depth, :] for j in range(blocks)], axis=1)
        left = jnp.concatenate([pack[base : base + rows, :], n_refs[d][...]], axis=1)
        right = jnp.concatenate([w_s, w_n], axis=0)
        pre = pre + jnp.dot(left, right, preferred_element_type=F32)
    pre = pre + bias_ref[0:1, :].astype(F32)
    pre_ref[...] = pre
    sig = jax.nn.sigmoid(pre)
    grad = (cot_ref[...].astype(F32) * sig * (1.0 + pre * (1.0 - sig))).astype(BF)
    cot_ref[...] = grad
    mine = pl.ds(pl.multiple_of(me * cols, cols), cols)
    own = pre_ref[:, mine]
    out_ref[...] = (own * jax.nn.sigmoid(own)).astype(BF)
    both = jnp.concatenate([ws_ref[...], wn_ref[...]], axis=0)
    into = lax.dot_general(grad, both, (((1,), (1,)), ((), ())), preferred_element_type=F32)
    neigh_grad = into[:, depth:].astype(BF)
    back_ref[...] = into[:, :depth] + jnp.dot(turned_ref[:rows, :], neigh_grad, preferred_element_type=F32)
    sums = jnp.sum(cot_ref[:, mine].astype(F32), axis=0, keepdims=True)
    high = sums.astype(BF).astype(F32)
    line = lax.broadcasted_iota(jnp.int32, (half * width, cols), 0) % width
    here = side_ref[0] * half
    for at, start in ((0, here), (width, half - here)):
        cut = pl.ds(pl.multiple_of(rows + start * width, 128), half * width)
        away = jnp.dot(turned_ref[cut, :], neigh_grad, preferred_element_type=F32)
        away = jnp.where(line == slots + hub_here, high, away)
        away = jnp.where(line == slots + hub_here + 1, sums - high, away)
        send_ref[:, at : at + width, :] = away.astype(BF).reshape(half, width, cols)
    pair = jnp.concatenate([x_ref[...], n_refs[0][...]], axis=1)
    weights = lax.dot_general(pair, grad, (((0,), (0,)), ((), ())), preferred_element_type=F32).astype(BF)
    share = height - 2 * width
    step = min(share, depth)
    for j in range(blocks):
        for kind in range(2):
            block = weights[kind * depth : (kind + 1) * depth, j * cols : (j + 1) * cols]
            for part in range(depth // step):
                at = (j * 2 + kind) * depth + part * step
                low = 2 * width + at % share
                send_ref[at // share, low : low + step, :] = block[part * step : (part + 1) * step]
    if count > 1:
        for k, ref in enumerate(send_refs):
            ref[...] = hold_ref[seat_ref[0] ^ k]


def seated(refs, seat):
    if len(refs) == 1:
        return [(j, refs[0].at[j]) for j in range(refs[0].shape[0])]
    return [(seat ^ k, ref) for k, ref in enumerate(refs)]


def sum_kernel(width, seat_ref, *refs):
    got_refs, (sum_ref, near_ref, relay_ref) = refs[:-3], refs[-3:]
    total = jnp.zeros(sum_ref.shape, F32)
    for j, got_ref in seated(got_refs, seat_ref[0]):
        total = total + got_ref[2 * width :, :].astype(F32)
        near_ref[j] = got_ref[:width, :]
        relay_ref[j] = got_ref[width : 2 * width, :]
    sum_ref[...] = total.astype(BF)


def total_kernel(own_ref, other_ref, part_ref):
    total = (own_ref[...].astype(F32) + other_ref[...].astype(F32)).astype(BF)
    part_ref[...] = jnp.broadcast_to(total, part_ref.shape)


def near_rows(slots, hub_here, start, mark_ref, got_ref):
    half, width, cols = got_ref.shape
    cut = pl.ds(pl.multiple_of(start * width, 128), half * width)
    added = jnp.dot(mark_ref[:, cut], got_ref[...].reshape(half * width, cols), preferred_element_type=F32)
    first = slots + hub_here
    bias = jnp.zeros((2, cols), F32)
    for j in range(half):
        bias = bias + got_ref[j, first : first + 2, :].astype(F32)
    return added, jnp.sum(bias, axis=0, keepdims=True)


def near_kernel(slots, hub_here, side_ref, back_ref, mark_ref, got_ref, sum_ref, bias_ref):
    half = got_ref.shape[0]
    added, bias = near_rows(slots, hub_here, side_ref[0] * half, mark_ref, got_ref)
    sum_ref[...] = back_ref[...] + added
    bias_ref[...] = bias


def grad_kernel(scale, slots, hub_here, side_ref, back_ref, near_ref, mark_ref, got_ref, grad_ref, bias_ref):
    half = got_ref.shape[0]
    added, bias = near_rows(slots, hub_here, half - side_ref[0] * half, mark_ref, got_ref)
    grad_ref[...] = (back_ref[...] + added).astype(BF)
    bias_ref[...] = (near_ref[...] + bias) * scale


def spread_kernel(scale, seat_ref, *refs):
    got_refs, (self_ref, neigh_ref) = refs[:-2], refs[-2:]
    depth, full = self_ref.shape
    cols = got_refs[0].shape[-1]
    if len(got_refs) > 1:
        for j, ref in seated(got_refs, seat_ref[0]):
            cut = pl.ds(pl.multiple_of(j * cols, cols), cols)
            self_ref[:, cut] = ref[:depth, :].astype(F32) * scale
            neigh_ref[:, cut] = ref[depth:, :].astype(F32) * scale
        return
    whole = got_refs[0][...].reshape(2 * (full // cols) * depth, cols).astype(F32) * scale
    for j in range(full // cols):
        at = 2 * j * depth
        self_ref[:, j * cols : (j + 1) * cols] = whole[at : at + depth]
        neigh_ref[:, j * cols : (j + 1) * cols] = whole[at + depth : at + 2 * depth]


VMEM = pl.BlockSpec(memory_space=pltpu.VMEM)
SMEM = pl.BlockSpec(memory_space=pltpu.SMEM)
ANY = pl.BlockSpec(memory_space=pl.ANY)
HBM = pl.BlockSpec(memory_space=pltpu.HBM)
PARAMS = pltpu.CompilerParams(vmem_limit_bytes=40 * 1024 * 1024)


def shape(dims, kind):
    return jax.ShapeDtypeStruct(dims, kind)


def partner(block, axis, k):
    return lax.ppermute(block, axis, [(i, i ^ k) for i in range(lax.axis_size(axis))])


def exchange(blocks, groups=None):
    return lax.all_to_all(blocks, "dom", split_axis=0, concat_axis=0, axis_index_groups=groups, tiled=True)


def swap(blocks):
    return [blocks[0]] + [partner(block, "dom", k) for k, block in enumerate(blocks) if k]


def on_device(
    features,
    w_self,
    w_neigh,
    bias,
    cotangent,
    tile_vals,
    tile_pos,
    tile_count,
    send_rows,
    recv_dest,
    ghost_weight,
    recv_count,
    hub_rows,
    hub_weight,
):
    rows, cols = features.shape
    depth, full = w_self.shape
    blocks = full // cols
    peers, slots = send_rows.shape[1:]
    hub_here = hub_rows.shape[-1]
    width = -(-(slots + hub_here + 2) // 16) * 16
    lanes = peers * width
    half = peers // 2
    share = 2 * blocks * depth // half
    direct = half == blocks
    count = half if direct else 1
    halves = [list(range(half)), list(range(half, peers))]
    scale = 1.0 / math.sqrt(peers * rows)
    feats = lax.axis_size("feat")
    me = lax.axis_index("feat").astype(jnp.int32).reshape(1)
    side = (lax.axis_index("dom") >= half).astype(jnp.int32).reshape(1)
    seat = lax.rem(lax.axis_index("dom"), half).astype(jnp.int32).reshape(1)
    pack_rows = 2 * blocks * depth + 2 * rows + 16

    def pinned(*arrays):
        return [pltpu.with_memory_space_constraint(a, pltpu.HBM) for a in arrays]

    first = pinned(features, cotangent, w_self, w_neigh, bias.reshape(1, cols), send_rows, hub_rows)
    edges = pinned(tile_pos, recv_count, tile_vals, recv_dest, ghost_weight, hub_weight.T)
    moved = (send_rows, hub_rows, *edges)
    outgoing, pack, *moved = pl.pallas_call(
        functools.partial(send_kernel, width),
        out_shape=(
            shape((peers, width, cols), BF),
            shape((pack_rows, cols), BF),
            *(shape(a.shape, a.dtype) for a in moved),
        ),
        in_specs=[HBM] * (len(first) + len(edges)),
        out_specs=(VMEM,) * (2 + len(moved)),
        scratch_shapes=[
            pltpu.VMEM((1, cols), BF),
            pltpu.SemaphoreType.DMA((11 + 2 * blocks,)),
        ],
        compiler_params=PARAMS,
    )(*first, *edges)

    far = partner(pack, "feat", 2)
    near = partner(pack, "feat", 1)
    incoming = exchange(outgoing)
    mix, turned, mark = pl.pallas_call(
        functools.partial(mix_kernel, width),
        out_shape=(
            shape((rows, rows + lanes), BF),
            shape((rows + lanes, rows), BF),
            shape((rows, lanes), BF),
        ),
        in_specs=[VMEM] * (1 + len(moved)),
        out_specs=(VMEM,) * 3,
        compiler_params=PARAMS,
        cost_estimate=pl.CostEstimate(flops=10**8, bytes_accessed=3 * 10**6, transcendentals=0),
    )(tile_count.reshape(1, 1), *moved)
    neigh, far = pl.pallas_call(
        neigh_kernel,
        out_shape=(shape((rows, cols), BF), shape((pack_rows, cols), BF)),
        in_specs=[VMEM, VMEM, ANY, VMEM],
        out_specs=(VMEM, ANY),
        input_output_aliases={2: 1},
        compiler_params=PARAMS,
    )(features, mix, far, incoming)
    last = partner(far, "feat", 1)
    far_neigh = partner(neigh, "feat", 2)
    every = [neigh, partner(neigh, "feat", 1), far_neigh, partner(far_neigh, "feat", 1)]

    height = 2 * width + share
    output, back, *returned = pl.pallas_call(
        functools.partial(dense_kernel, slots, hub_here, feats, width, count),
        out_shape=(
            shape((rows, cols), BF),
            shape((rows, cols), F32),
            *([shape((height, cols), BF)] * half if direct else [shape((half, height, cols), BF)]),
        ),
        in_specs=[SMEM] * 3 + [VMEM] * (4 + 2 * feats),
        out_specs=(VMEM,) * (2 + count),
        scratch_shapes=[
            pltpu.VMEM((rows, full), F32),
            pltpu.VMEM((rows, full), BF),
            pltpu.VMEM((16, full), BF),
            pltpu.VMEM((half, height, cols) if direct else (1, 16, cols), BF),
        ],
        compiler_params=PARAMS,
    )(me, side, seat, features, w_self, w_neigh, turned, pack, near, far, last, *every)

    arrived = swap(returned) if direct else [exchange(returned[0], halves)]
    half_sum, near_ghosts, relay = pl.pallas_call(
        functools.partial(sum_kernel, width),
        out_shape=(shape((share, cols), BF), shape((half, width, cols), BF), shape((half, width, cols), BF)),
        in_specs=[SMEM] + [VMEM] * count,
        out_specs=(VMEM,) * 3,
        compiler_params=PARAMS,
    )(seat, *arrived)
    other_sum = partner(half_sum, "dom", half)
    crossed = partner(relay, "dom", half)
    back, near_bias = pl.pallas_call(
        functools.partial(near_kernel, slots, hub_here),
        out_shape=(shape((rows, cols), F32), shape((1, cols), F32)),
        in_specs=[SMEM] + [VMEM] * 3,
        out_specs=(VMEM,) * 2,
        compiler_params=PARAMS,
        cost_estimate=pl.CostEstimate(flops=10**8, bytes_accessed=10**6, transcendentals=0),
    )(side, back, mark, near_ghosts)
    part = pl.pallas_call(
        total_kernel,
        out_shape=shape((share, cols) if direct else (half, share, cols), BF),
        in_specs=[VMEM, VMEM],
        out_specs=VMEM,
        compiler_params=PARAMS,
    )(half_sum, other_sum)
    parts = swap([part] * half) if direct else [exchange(part, halves)]
    grad_features, grad_bias = pl.pallas_call(
        functools.partial(grad_kernel, scale, slots, hub_here),
        out_shape=(shape((rows, cols), BF), shape((1, cols), F32)),
        in_specs=[SMEM] + [VMEM] * 4,
        out_specs=(VMEM,) * 2,
        compiler_params=PARAMS,
        cost_estimate=pl.CostEstimate(flops=2 * 10**9, bytes_accessed=10**6, transcendentals=0),
    )(side, back, near_bias, mark, crossed)
    grad_self, grad_neigh = pl.pallas_call(
        functools.partial(spread_kernel, scale),
        out_shape=(shape((depth, full), F32), shape((depth, full), F32)),
        in_specs=[SMEM] + [VMEM] * count,
        out_specs=(VMEM,) * 2,
        compiler_params=PARAMS,
    )(seat, *parts)
    return output, grad_features, grad_self, grad_neigh, grad_bias.reshape(cols)


def solution(mesh):
    placed = (
        P("dom", "feat"),
        P("feat", None),
        P("feat", None),
        P("feat"),
        P("dom", "feat"),
        P("dom", None, None, None),
        P("dom", None),
        P("dom"),
        P("dom", None, None),
        P("dom", None, None),
        P("dom", None, None),
        P("dom", None),
        P("dom", None),
        P("dom", None),
    )
    return jax.shard_map(
        on_device,
        mesh=mesh,
        in_specs=placed,
        out_specs=(P("dom", "feat"), P("dom", "feat"), P("feat", None), P("feat", None), P("feat")),
        check_vma=False,
    )
```

```python
import functools
import math

import jax
import jax.numpy as jnp
from jax import lax
from jax.experimental import pallas as pl
from jax.experimental.pallas import tpu as pltpu
from jax.sharding import PartitionSpec as P

BF = jnp.bfloat16
F32 = jnp.float32


def spread_rows(table, width):
    peers, slots = table.shape
    lanes = peers * width
    lane = lax.broadcasted_iota(jnp.int32, (slots, lanes), 1)
    slot = lax.broadcasted_iota(jnp.int32, (slots, lanes), 0)
    place = jnp.where(lane % width == slot, 1.0, 0.0).astype(BF)
    wide = jnp.dot(table.astype(BF), place, preferred_element_type=F32)
    peer = lax.broadcasted_iota(jnp.int32, (peers, lanes), 0)
    at = lax.broadcasted_iota(jnp.int32, (peers, lanes), 1)
    return jnp.sum(jnp.where(at // width == peer, wide, 0.0), axis=0, keepdims=True)


def source_matrix(send, hubs, rows, width):
    peers, slots = send.shape
    hub_here = hubs.shape[1]
    lanes = peers * width
    lane = lax.broadcasted_iota(jnp.int32, (1, lanes), 1) % width
    index = spread_rows(send.astype(F32), width)
    for k in range(hub_here):
        index = jnp.where(lane == slots + k, hubs[0:1, k : k + 1].astype(F32), index)
    index = jnp.where(lane < slots + hub_here, index, -1.0)
    row = lax.broadcasted_iota(jnp.int32, (rows, lanes), 0).astype(F32)
    return jnp.where(row == index, 1.0, 0.0).astype(BF)


def source_rows(send, hubs, rows, width):
    peers, slots = send.shape
    hub_here = hubs.shape[1]
    lanes = peers * width
    slot = lax.broadcasted_iota(jnp.int32, (lanes, slots), 0) % width
    place = jnp.where(slot == lax.broadcasted_iota(jnp.int32, (lanes, slots), 1), 1.0, 0.0).astype(BF)
    wide = lax.dot_general(
        place, send.astype(F32).astype(BF), (((1,), (1,)), ((), ())), preferred_element_type=F32
    )
    line = lax.broadcasted_iota(jnp.int32, (lanes, peers), 0)
    for k in range(hub_here):
        wide = jnp.where(line % width == slots + k, hubs[0:1, k : k + 1].astype(F32), wide)
    wide = jnp.where(line % width < slots + hub_here, wide, -1.0)
    wide = jnp.where(line // width == lax.broadcasted_iota(jnp.int32, (lanes, peers), 1), wide, 0.0)
    index = jnp.dot(wide.astype(BF), jnp.ones((peers, rows), BF), preferred_element_type=F32)
    row = lax.broadcasted_iota(jnp.int32, (lanes, rows), 1).astype(F32)
    return jnp.where(row == index, 1.0, 0.0).astype(BF)


def send_kernel(
    width, x_ref, cot_ref, ws_ref, wn_ref, bias_ref, send_ref, hub_ref, pos_ref, live_ref, tile_ref, dest_ref, gw_ref, hw_ref,
    out_ref, pack_ref, send_v, hub_v, pos_v, live_v, tile_v, dest_v, gw_v, hw_v, bias_v, sems,
):
    rows, cols = x_ref.shape
    depth, full = ws_ref.shape
    blocks = full // cols
    base = 2 * blocks * depth
    moves = [
        (send_ref, send_v),
        (hub_ref, hub_v),
        (x_ref, pack_ref.at[base : base + rows, :]),
        (bias_ref, bias_v),
        (cot_ref, pack_ref.at[base + rows : base + 2 * rows, :]),
    ]
    for kind, w_ref in enumerate((ws_ref, wn_ref)):
        for j in range(blocks):
            at = (kind * blocks + j) * depth
            moves.append((w_ref.at[:, j * cols : (j + 1) * cols], pack_ref.at[at : at + depth, :]))
    moves += [
        (pos_ref, pos_v), (live_ref, live_v), (tile_ref, tile_v), (dest_ref, dest_v),
        (gw_ref, gw_v), (hw_ref, hw_v),
    ]
    copies = [pltpu.make_async_copy(src, dst, sems.at[i]) for i, (src, dst) in enumerate(moves)]
    for copy in copies:
        copy.start()
    for copy in copies[:2]:
        copy.wait()
    mark = source_rows(send_v[0], hub_v[...], rows, width)
    copies[2].wait()
    taken = jnp.dot(mark, pack_ref[base : base + rows, :], preferred_element_type=F32).astype(BF)
    out_ref[...] = taken.reshape(out_ref.shape)
    for copy in copies[3:]:
        copy.wait()
    pack_ref[base + 2 * rows :, :] = jnp.broadcast_to(bias_v[...], (16, cols))


def mix_kernel(width, count_ref, send_v, hub_v, pos_v, live_v, tile_v, dest_v, gw_v, hw_v, mix_ref, turned_ref, mark_ref):
    rows = mix_ref.shape[0]
    tiles, tile = tile_v.shape[1:3]
    peers, slots = dest_v.shape[1:]
    side = rows // tile
    lanes = peers * width
    hubs = hw_v.shape[0]
    hub_here = hubs // peers
    for r in range(side):
        for c in range(side):
            total = jnp.zeros((tile, tile), BF)
            for t in range(tiles):
                used = jnp.logical_and(pos_v[0:1, t : t + 1] == r * side + c, t < count_ref[...])
                total = jnp.where(used, tile_v[0, t], total)
            mix_ref[r * tile : (r + 1) * tile, c * tile : (c + 1) * tile] = total
    dest = spread_rows(dest_v[0].astype(F32), width)
    coef = spread_rows(gw_v[0], width)
    peer = lax.broadcasted_iota(jnp.int32, (peers, lanes), 0)
    at = lax.broadcasted_iota(jnp.int32, (peers, lanes), 1)
    owner = jnp.where(at // width == peer, 1.0, 0.0).astype(BF)
    limit = jnp.dot(live_v[...].astype(F32).astype(BF), owner, preferred_element_type=F32)
    lane = lax.broadcasted_iota(jnp.int32, (1, lanes), 1) % width
    coef = jnp.where(jnp.logical_and(lane.astype(F32) < limit, lane < slots), coef, 0.0)
    row = lax.broadcasted_iota(jnp.int32, (rows, lanes), 0).astype(F32)
    ghost = jnp.where(row == dest, coef, 0.0)
    hub = lax.broadcasted_iota(jnp.int32, (hubs, lanes), 0)
    at = lax.broadcasted_iota(jnp.int32, (hubs, lanes), 1)
    place = jnp.where(
        jnp.logical_and(at // width == hub // hub_here, at % width == slots + hub % hub_here), 1.0, 0.0
    ).astype(BF)
    hub_mix = lax.dot_general(hw_v[...], place, (((0,), (0,)), ((), ())), preferred_element_type=F32)
    mix_ref[:, rows:] = (ghost + hub_mix).astype(BF)
    turned_ref[...] = mix_ref[...].T
    mark_ref[...] = source_matrix(send_v[0], hub_v[...], rows, width)


def neigh_kernel(x_ref, mix_ref, far_ref, got_ref, neigh_ref, passed_ref):
    rows, cols = x_ref.shape
    lanes = mix_ref.shape[1] - rows
    total = jnp.dot(mix_ref[:, :rows], x_ref[...], preferred_element_type=F32)
    total = total + jnp.dot(mix_ref[:, rows:], got_ref[...].reshape(lanes, cols), preferred_element_type=F32)
    neigh_ref[...] = total.astype(BF)


def dense_kernel(slots, hub_here, feats, width, count, me_ref, side_ref, seat_ref, x_ref, ws_ref, wn_ref, turned_ref, *refs):
    pack_refs, n_refs = refs[:feats], refs[feats : 2 * feats]
    out_ref, back_ref, mirror_ref = refs[2 * feats : 2 * feats + 3]
    send_refs = refs[2 * feats + 3 : 2 * feats + 3 + count]
    pre_ref, cot_ref, bias_ref, hold_ref, turn_ref = refs[2 * feats + 3 + count :]
    send_ref = send_refs[0] if count == 1 else hold_ref
    rows, cols = x_ref.shape
    depth, full = ws_ref.shape
    blocks = full // cols
    half, height = send_ref.shape[:2]
    me = me_ref[0]
    base = 2 * blocks * depth
    left, right = [], []
    for d, pack in enumerate(pack_refs):
        owner = me ^ d
        cut = pl.ds(pl.multiple_of(owner * cols, cols), cols)
        cot_ref[:, cut] = pack[base + rows : base + 2 * rows, :]
        bias_ref[:, cut] = pack[base + 2 * rows : base + 2 * rows + 16, :]
        w_s = jnp.concatenate([pack[j * depth : (j + 1) * depth, :] for j in range(blocks)], axis=1)
        w_n = jnp.concatenate([pack[(blocks + j) * depth : (blocks + j + 1) * depth, :] for j in range(blocks)], axis=1)
        left += [pack[base : base + rows, :], n_refs[d][...]]
        right += [w_s, w_n]
    pre = jnp.dot(jnp.concatenate(left, axis=1), jnp.concatenate(right, axis=0), preferred_element_type=F32)
    pre = pre + bias_ref[0:1, :].astype(F32)
    pre_ref[...] = pre
    sig = jax.nn.sigmoid(pre)
    grad = (cot_ref[...].astype(F32) * sig * (1.0 + pre * (1.0 - sig))).astype(BF)
    cot_ref[...] = grad
    mine = pl.ds(pl.multiple_of(me * cols, cols), cols)
    own = pre_ref[:, mine]
    out_ref[...] = (own * jax.nn.sigmoid(own)).astype(BF)
    both = jnp.concatenate([ws_ref[...], wn_ref[...]], axis=0)
    into = lax.dot_general(grad, both, (((1,), (1,)), ((), ())), preferred_element_type=F32)
    neigh_grad = into[:, depth:].astype(BF)
    back_ref[...] = into[:, :depth] + jnp.dot(turned_ref[:rows, :], neigh_grad, preferred_element_type=F32)
    sums = jnp.sum(cot_ref[:, mine].astype(F32), axis=0, keepdims=True)
    high = sums.astype(BF).astype(F32)
    line = lax.broadcasted_iota(jnp.int32, (half * width, cols), 0) % width
    here = side_ref[0] * half
    for target, start in ((send_ref, here), (turn_ref, half - here)):
        cut = pl.ds(pl.multiple_of(rows + start * width, 128), half * width)
        away = jnp.dot(turned_ref[cut, :], neigh_grad, preferred_element_type=F32)
        away = jnp.where(line == slots + hub_here, high, away)
        away = jnp.where(line == slots + hub_here + 1, sums - high, away)
        target[:, :width, :] = away.astype(BF).reshape(half, width, cols)
    for k in range(half):
        mirror_ref[k] = turn_ref[seat_ref[0] ^ k if count > 1 else k]
    pair = jnp.concatenate([x_ref[...], n_refs[0][...]], axis=1)
    weights = lax.dot_general(pair, grad, (((0,), (0,)), ((), ())), preferred_element_type=F32).astype(BF)
    share = height - width
    step = min(share, depth)
    for j in range(blocks):
        for kind in range(2):
            block = weights[kind * depth : (kind + 1) * depth, j * cols : (j + 1) * cols]
            for part in range(depth // step):
                at = (j * 2 + kind) * depth + part * step
                low = width + at % share
                send_ref[at // share, low : low + step, :] = block[part * step : (part + 1) * step]
    if count > 1:
        for k, ref in enumerate(send_refs):
            ref[...] = hold_ref[seat_ref[0] ^ k]


def seated(refs, seat):
    if len(refs) == 1:
        return [(j, refs[0].at[j]) for j in range(refs[0].shape[0])]
    return [(seat ^ k, ref) for k, ref in enumerate(refs)]


def sum_kernel(width, seat_ref, *refs):
    got_refs, (sum_ref, near_ref) = refs[:-2], refs[-2:]
    total = jnp.zeros(sum_ref.shape, F32)
    for j, got_ref in seated(got_refs, seat_ref[0]):
        total = total + got_ref[width:, :].astype(F32)
        near_ref[j] = got_ref[:width, :]
    sum_ref[...] = total.astype(BF)


def deal_kernel(got_ref, *out_refs):
    for k, ref in enumerate(out_refs):
        ref[...] = got_ref[k]


def total_kernel(own_ref, other_ref, part_ref):
    total = (own_ref[...].astype(F32) + other_ref[...].astype(F32)).astype(BF)
    part_ref[...] = jnp.broadcast_to(total, part_ref.shape)


def near_rows(slots, hub_here, start, mark_ref, got_ref):
    half, width, cols = got_ref.shape
    cut = pl.ds(pl.multiple_of(start * width, 128), half * width)
    added = jnp.dot(mark_ref[:, cut], got_ref[...].reshape(half * width, cols), preferred_element_type=F32)
    first = slots + hub_here
    bias = jnp.zeros((2, cols), F32)
    for j in range(half):
        bias = bias + got_ref[j, first : first + 2, :].astype(F32)
    return added, jnp.sum(bias, axis=0, keepdims=True)


def near_kernel(slots, hub_here, side_ref, back_ref, mark_ref, got_ref, sum_ref, bias_ref):
    half = got_ref.shape[0]
    added, bias = near_rows(slots, hub_here, side_ref[0] * half, mark_ref, got_ref)
    sum_ref[...] = back_ref[...] + added
    bias_ref[...] = bias


def grad_kernel(scale, slots, hub_here, side_ref, seat_ref, back_ref, near_ref, mark_ref, *refs):
    got_refs, (grad_ref, bias_ref, hold_ref) = refs[:-3], refs[-3:]
    half = hold_ref.shape[0]
    for j, got_ref in seated(got_refs, seat_ref[0]):
        hold_ref[j] = got_ref[...]
    added, bias = near_rows(slots, hub_here, half - side_ref[0] * half, mark_ref, hold_ref)
    grad_ref[...] = (back_ref[...] + added).astype(BF)
    bias_ref[...] = (near_ref[...] + bias) * scale


def spread_kernel(scale, seat_ref, *refs):
    got_refs, (self_ref, neigh_ref) = refs[:-2], refs[-2:]
    depth, full = self_ref.shape
    cols = got_refs[0].shape[-1]
    if len(got_refs) > 1:
        for j, ref in seated(got_refs, seat_ref[0]):
            cut = pl.ds(pl.multiple_of(j * cols, cols), cols)
            self_ref[:, cut] = ref[:depth, :].astype(F32) * scale
            neigh_ref[:, cut] = ref[depth:, :].astype(F32) * scale
        return
    whole = got_refs[0][...].reshape(2 * (full // cols) * depth, cols).astype(F32) * scale
    for j in range(full // cols):
        at = 2 * j * depth
        self_ref[:, j * cols : (j + 1) * cols] = whole[at : at + depth]
        neigh_ref[:, j * cols : (j + 1) * cols] = whole[at + depth : at + 2 * depth]


VMEM = pl.BlockSpec(memory_space=pltpu.VMEM)
SMEM = pl.BlockSpec(memory_space=pltpu.SMEM)
ANY = pl.BlockSpec(memory_space=pl.ANY)
HBM = pl.BlockSpec(memory_space=pltpu.HBM)
PARAMS = pltpu.CompilerParams(vmem_limit_bytes=40 * 1024 * 1024)


def shape(dims, kind):
    return jax.ShapeDtypeStruct(dims, kind)


def partner(block, axis, k):
    return lax.ppermute(block, axis, [(i, i ^ k) for i in range(lax.axis_size(axis))])


def exchange(blocks, groups=None):
    return lax.all_to_all(blocks, "dom", split_axis=0, concat_axis=0, axis_index_groups=groups, tiled=True)


def swap(blocks):
    return [blocks[0]] + [partner(block, "dom", k) for k, block in enumerate(blocks) if k]


def on_device(
    features,
    w_self,
    w_neigh,
    bias,
    cotangent,
    tile_vals,
    tile_pos,
    tile_count,
    send_rows,
    recv_dest,
    ghost_weight,
    recv_count,
    hub_rows,
    hub_weight,
):
    rows, cols = features.shape
    depth, full = w_self.shape
    blocks = full // cols
    peers, slots = send_rows.shape[1:]
    hub_here = hub_rows.shape[-1]
    width = -(-(slots + hub_here + 2) // 16) * 16
    lanes = peers * width
    half = peers // 2
    share = 2 * blocks * depth // half
    direct = half == blocks
    count = half if direct else 1
    halves = [list(range(half)), list(range(half, peers))]
    scale = 1.0 / math.sqrt(peers * rows)
    feats = lax.axis_size("feat")
    me = lax.axis_index("feat").astype(jnp.int32).reshape(1)
    side = (lax.axis_index("dom") >= half).astype(jnp.int32).reshape(1)
    seat = lax.rem(lax.axis_index("dom"), half).astype(jnp.int32).reshape(1)
    pack_rows = 2 * blocks * depth + 2 * rows + 16

    def pinned(*arrays):
        return [pltpu.with_memory_space_constraint(a, pltpu.HBM) for a in arrays]

    first = pinned(features, cotangent, w_self, w_neigh, bias.reshape(1, cols), send_rows, hub_rows)
    edges = pinned(tile_pos, recv_count, tile_vals, recv_dest, ghost_weight, hub_weight.T)
    moved = (send_rows, hub_rows, *edges)
    outgoing, pack, *moved = pl.pallas_call(
        functools.partial(send_kernel, width),
        out_shape=(
            shape((peers, width, cols), BF),
            shape((pack_rows, cols), BF),
            *(shape(a.shape, a.dtype) for a in moved),
        ),
        in_specs=[HBM] * (len(first) + len(edges)),
        out_specs=(VMEM,) * (2 + len(moved)),
        scratch_shapes=[
            pltpu.VMEM((1, cols), BF),
            pltpu.SemaphoreType.DMA((11 + 2 * blocks,)),
        ],
        compiler_params=PARAMS,
    )(*first, *edges)

    far = partner(pack, "feat", 2)
    near = partner(pack, "feat", 1)
    incoming = exchange(outgoing)
    mix, turned, mark = pl.pallas_call(
        functools.partial(mix_kernel, width),
        out_shape=(
            shape((rows, rows + lanes), BF),
            shape((rows + lanes, rows), BF),
            shape((rows, lanes), BF),
        ),
        in_specs=[VMEM] * (1 + len(moved)),
        out_specs=(VMEM,) * 3,
        compiler_params=PARAMS,
        cost_estimate=pl.CostEstimate(flops=10**8, bytes_accessed=3 * 10**6, transcendentals=0),
    )(tile_count.reshape(1, 1), *moved)
    neigh, far = pl.pallas_call(
        neigh_kernel,
        out_shape=(shape((rows, cols), BF), shape((pack_rows, cols), BF)),
        in_specs=[VMEM, VMEM, ANY, VMEM],
        out_specs=(VMEM, ANY),
        input_output_aliases={2: 1},
        compiler_params=PARAMS,
    )(features, mix, far, incoming)
    last = partner(far, "feat", 1)
    far_neigh = partner(neigh, "feat", 2)
    every = [neigh, partner(neigh, "feat", 1), far_neigh, partner(far_neigh, "feat", 1)]

    height = width + share
    output, back, mirror, *returned = pl.pallas_call(
        functools.partial(dense_kernel, slots, hub_here, feats, width, count),
        out_shape=(
            shape((rows, cols), BF),
            shape((rows, cols), F32),
            shape((half, width, cols), BF),
            *([shape((height, cols), BF)] * half if direct else [shape((half, height, cols), BF)]),
        ),
        in_specs=[SMEM] * 3 + [VMEM] * (4 + 2 * feats),
        out_specs=(VMEM,) * (3 + count),
        scratch_shapes=[
            pltpu.VMEM((rows, full), F32),
            pltpu.VMEM((rows, full), BF),
            pltpu.VMEM((16, full), BF),
            pltpu.VMEM((half, height, cols) if direct else (1, 16, cols), BF),
            pltpu.VMEM((half, width, cols), BF),
        ],
        compiler_params=PARAMS,
    )(me, side, seat, features, w_self, w_neigh, turned, pack, near, far, last, *every)

    arrived = swap(returned) if direct else [exchange(returned[0], halves)]
    mirror = partner(mirror, "dom", half)
    half_sum, near_ghosts = pl.pallas_call(
        functools.partial(sum_kernel, width),
        out_shape=(shape((share, cols), BF), shape((half, width, cols), BF)),
        in_specs=[SMEM] + [VMEM] * count,
        out_specs=(VMEM,) * 2,
        compiler_params=PARAMS,
    )(seat, *arrived)
    other_sum = partner(half_sum, "dom", half)
    if direct:
        crossed = swap(
            pl.pallas_call(
                deal_kernel,
                out_shape=(shape((width, cols), BF),) * half,
                in_specs=[VMEM],
                out_specs=(VMEM,) * half,
                compiler_params=PARAMS,
            )(mirror)
        )
    else:
        crossed = [exchange(mirror, halves)]
    back, near_bias = pl.pallas_call(
        functools.partial(near_kernel, slots, hub_here),
        out_shape=(shape((rows, cols), F32), shape((1, cols), F32)),
        in_specs=[SMEM] + [VMEM] * 3,
        out_specs=(VMEM,) * 2,
        compiler_params=PARAMS,
        cost_estimate=pl.CostEstimate(flops=10**8, bytes_accessed=10**6, transcendentals=0),
    )(side, back, mark, near_ghosts)
    part = pl.pallas_call(
        total_kernel,
        out_shape=shape((share, cols) if direct else (half, share, cols), BF),
        in_specs=[VMEM, VMEM],
        out_specs=VMEM,
        compiler_params=PARAMS,
    )(half_sum, other_sum)
    parts = swap([part] * half) if direct else [exchange(part, halves)]
    grad_features, grad_bias = pl.pallas_call(
        functools.partial(grad_kernel, scale, slots, hub_here),
        out_shape=(shape((rows, cols), BF), shape((1, cols), F32)),
        in_specs=[SMEM] * 2 + [VMEM] * (3 + count),
        out_specs=(VMEM,) * 2,
        scratch_shapes=[pltpu.VMEM((half, width, cols), BF)],
        compiler_params=PARAMS,
        cost_estimate=pl.CostEstimate(flops=2 * 10**9, bytes_accessed=10**6, transcendentals=0),
    )(side, seat, back, near_bias, mark, *crossed)
    grad_self, grad_neigh = pl.pallas_call(
        functools.partial(spread_kernel, scale),
        out_shape=(shape((depth, full), F32), shape((depth, full), F32)),
        in_specs=[SMEM] + [VMEM] * count,
        out_specs=(VMEM,) * 2,
        compiler_params=PARAMS,
    )(seat, *parts)
    return output, grad_features, grad_self, grad_neigh, grad_bias.reshape(cols)


def solution(mesh):
    placed = (
        P("dom", "feat"),
        P("feat", None),
        P("feat", None),
        P("feat"),
        P("dom", "feat"),
        P("dom", None, None, None),
        P("dom", None),
        P("dom"),
        P("dom", None, None),
        P("dom", None, None),
        P("dom", None, None),
        P("dom", None),
        P("dom", None),
        P("dom", None),
    )
    return jax.shard_map(
        on_device,
        mesh=mesh,
        in_specs=placed,
        out_specs=(P("dom", "feat"), P("dom", "feat"), P("feat", None), P("feat", None), P("feat")),
        check_vma=False,
    )
```

```python
import functools
import math

import jax
import jax.numpy as jnp
from jax import lax
from jax.experimental import pallas as pl
from jax.experimental.pallas import tpu as pltpu
from jax.sharding import PartitionSpec as P

BF = jnp.bfloat16
F32 = jnp.float32


def spread_rows(table, width):
    peers, slots = table.shape
    lanes = peers * width
    lane = lax.broadcasted_iota(jnp.int32, (slots, lanes), 1)
    slot = lax.broadcasted_iota(jnp.int32, (slots, lanes), 0)
    place = jnp.where(lane % width == slot, 1.0, 0.0).astype(BF)
    wide = jnp.dot(table.astype(BF), place, preferred_element_type=F32)
    peer = lax.broadcasted_iota(jnp.int32, (peers, lanes), 0)
    at = lax.broadcasted_iota(jnp.int32, (peers, lanes), 1)
    return jnp.sum(jnp.where(at // width == peer, wide, 0.0), axis=0, keepdims=True)


def source_matrix(send, hubs, rows, width):
    peers, slots = send.shape
    hub_here = hubs.shape[1]
    lanes = peers * width
    lane = lax.broadcasted_iota(jnp.int32, (1, lanes), 1) % width
    index = spread_rows(send.astype(F32), width)
    for k in range(hub_here):
        index = jnp.where(lane == slots + k, hubs[0:1, k : k + 1].astype(F32), index)
    index = jnp.where(lane < slots + hub_here, index, -1.0)
    row = lax.broadcasted_iota(jnp.int32, (rows, lanes), 0).astype(F32)
    return jnp.where(row == index, 1.0, 0.0).astype(BF)


def source_rows(send, hubs, rows, width):
    peers, slots = send.shape
    hub_here = hubs.shape[1]
    lanes = peers * width
    slot = lax.broadcasted_iota(jnp.int32, (lanes, slots), 0) % width
    place = jnp.where(slot == lax.broadcasted_iota(jnp.int32, (lanes, slots), 1), 1.0, 0.0).astype(BF)
    wide = lax.dot_general(
        place, send.astype(F32).astype(BF), (((1,), (1,)), ((), ())), preferred_element_type=F32
    )
    line = lax.broadcasted_iota(jnp.int32, (lanes, peers), 0)
    for k in range(hub_here):
        wide = jnp.where(line % width == slots + k, hubs[0:1, k : k + 1].astype(F32), wide)
    wide = jnp.where(line % width < slots + hub_here, wide, -1.0)
    wide = jnp.where(line // width == lax.broadcasted_iota(jnp.int32, (lanes, peers), 1), wide, 0.0)
    index = jnp.dot(wide.astype(BF), jnp.ones((peers, rows), BF), preferred_element_type=F32)
    row = lax.broadcasted_iota(jnp.int32, (lanes, rows), 1).astype(F32)
    return jnp.where(row == index, 1.0, 0.0).astype(BF)


def send_kernel(
    width, x_ref, cot_ref, ws_ref, wn_ref, bias_ref, send_ref, hub_ref, pos_ref, live_ref, tile_ref, dest_ref, gw_ref, hw_ref,
    out_ref, pack_ref, send_v, hub_v, pos_v, live_v, tile_v, dest_v, gw_v, hw_v, bias_v, sems,
):
    rows, cols = x_ref.shape
    depth, full = ws_ref.shape
    blocks = full // cols
    base = 2 * blocks * depth
    moves = [
        (send_ref, send_v),
        (hub_ref, hub_v),
        (x_ref, pack_ref.at[base : base + rows, :]),
        (bias_ref, bias_v),
        (cot_ref, pack_ref.at[base + rows : base + 2 * rows, :]),
    ]
    for kind, w_ref in enumerate((ws_ref, wn_ref)):
        for j in range(blocks):
            at = (kind * blocks + j) * depth
            moves.append((w_ref.at[:, j * cols : (j + 1) * cols], pack_ref.at[at : at + depth, :]))
    moves += [
        (pos_ref, pos_v), (live_ref, live_v), (tile_ref, tile_v), (dest_ref, dest_v),
        (gw_ref, gw_v), (hw_ref, hw_v),
    ]
    copies = [pltpu.make_async_copy(src, dst, sems.at[i]) for i, (src, dst) in enumerate(moves)]
    for copy in copies:
        copy.start()
    for copy in copies[:2]:
        copy.wait()
    mark = source_rows(send_v[0], hub_v[...], rows, width)
    copies[2].wait()
    taken = jnp.dot(mark, pack_ref[base : base + rows, :], preferred_element_type=F32).astype(BF)
    out_ref[...] = taken.reshape(out_ref.shape)
    for copy in copies[3:]:
        copy.wait()
    pack_ref[base + 2 * rows :, :] = jnp.broadcast_to(bias_v[...], (16, cols))


def mix_kernel(width, count_ref, send_v, hub_v, pos_v, live_v, tile_v, dest_v, gw_v, hw_v, mix_ref, turned_ref, mark_ref):
    rows = mix_ref.shape[0]
    tiles, tile = tile_v.shape[1:3]
    peers, slots = dest_v.shape[1:]
    side = rows // tile
    lanes = peers * width
    hubs = hw_v.shape[0]
    hub_here = hubs // peers
    for r in range(side):
        for c in range(side):
            total = jnp.zeros((tile, tile), BF)
            for t in range(tiles):
                used = jnp.logical_and(pos_v[0:1, t : t + 1] == r * side + c, t < count_ref[...])
                total = jnp.where(used, tile_v[0, t], total)
            mix_ref[r * tile : (r + 1) * tile, c * tile : (c + 1) * tile] = total
    dest = spread_rows(dest_v[0].astype(F32), width)
    coef = spread_rows(gw_v[0], width)
    peer = lax.broadcasted_iota(jnp.int32, (peers, lanes), 0)
    at = lax.broadcasted_iota(jnp.int32, (peers, lanes), 1)
    owner = jnp.where(at // width == peer, 1.0, 0.0).astype(BF)
    limit = jnp.dot(live_v[...].astype(F32).astype(BF), owner, preferred_element_type=F32)
    lane = lax.broadcasted_iota(jnp.int32, (1, lanes), 1) % width
    coef = jnp.where(jnp.logical_and(lane.astype(F32) < limit, lane < slots), coef, 0.0)
    row = lax.broadcasted_iota(jnp.int32, (rows, lanes), 0).astype(F32)
    ghost = jnp.where(row == dest, coef, 0.0)
    hub = lax.broadcasted_iota(jnp.int32, (hubs, lanes), 0)
    at = lax.broadcasted_iota(jnp.int32, (hubs, lanes), 1)
    place = jnp.where(
        jnp.logical_and(at // width == hub // hub_here, at % width == slots + hub % hub_here), 1.0, 0.0
    ).astype(BF)
    hub_mix = lax.dot_general(hw_v[...], place, (((0,), (0,)), ((), ())), preferred_element_type=F32)
    mix_ref[:, rows:] = (ghost + hub_mix).astype(BF)
    turned_ref[...] = mix_ref[...].T
    mark_ref[...] = source_matrix(send_v[0], hub_v[...], rows, width)


def neigh_kernel(x_ref, mix_ref, far_ref, got_ref, neigh_ref, passed_ref):
    rows, cols = x_ref.shape
    lanes = mix_ref.shape[1] - rows
    total = jnp.dot(mix_ref[:, :rows], x_ref[...], preferred_element_type=F32)
    total = total + jnp.dot(mix_ref[:, rows:], got_ref[...].reshape(lanes, cols), preferred_element_type=F32)
    neigh_ref[...] = total.astype(BF)


def dense_kernel(slots, hub_here, feats, width, count, me_ref, side_ref, seat_ref, x_ref, ws_ref, wn_ref, turned_ref, *refs):
    pack_refs, n_refs = refs[:feats], refs[feats : 2 * feats]
    out_ref, back_ref, mirror_ref = refs[2 * feats : 2 * feats + 3]
    send_refs = refs[2 * feats + 3 : 2 * feats + 3 + count]
    pre_ref, cot_ref, bias_ref = refs[2 * feats + 3 + count :]
    rows, cols = x_ref.shape
    depth, full = ws_ref.shape
    blocks = full // cols
    half = mirror_ref.shape[0]
    height = send_refs[0].shape[-2]
    me = me_ref[0]
    base = 2 * blocks * depth
    left, right = [], []
    for d, pack in enumerate(pack_refs):
        owner = me ^ d
        cut = pl.ds(pl.multiple_of(owner * cols, cols), cols)
        cot_ref[:, cut] = pack[base + rows : base + 2 * rows, :]
        bias_ref[:, cut] = pack[base + 2 * rows : base + 2 * rows + 16, :]
        w_s = jnp.concatenate([pack[j * depth : (j + 1) * depth, :] for j in range(blocks)], axis=1)
        w_n = jnp.concatenate([pack[(blocks + j) * depth : (blocks + j + 1) * depth, :] for j in range(blocks)], axis=1)
        left += [pack[base : base + rows, :], n_refs[d][...]]
        right += [w_s, w_n]
    pre = jnp.dot(jnp.concatenate(left, axis=1), jnp.concatenate(right, axis=0), preferred_element_type=F32)
    pre = pre + bias_ref[0:1, :].astype(F32)
    pre_ref[...] = pre
    sig = jax.nn.sigmoid(pre)
    grad = (cot_ref[...].astype(F32) * sig * (1.0 + pre * (1.0 - sig))).astype(BF)
    cot_ref[...] = grad
    mine = pl.ds(pl.multiple_of(me * cols, cols), cols)
    own = pre_ref[:, mine]
    out_ref[...] = (own * jax.nn.sigmoid(own)).astype(BF)
    both = jnp.concatenate([ws_ref[...], wn_ref[...]], axis=0)
    into = lax.dot_general(grad, both, (((1,), (1,)), ((), ())), preferred_element_type=F32)
    neigh_grad = into[:, depth:].astype(BF)
    back_ref[...] = into[:, :depth] + jnp.dot(turned_ref[:rows, :], neigh_grad, preferred_element_type=F32)
    sums = jnp.sum(cot_ref[:, mine].astype(F32), axis=0, keepdims=True)
    high = sums.astype(BF).astype(F32)
    here = side_ref[0] * half
    share = height - width

    def ghosts(start, peers):
        line = lax.broadcasted_iota(jnp.int32, (peers * width, cols), 0) % width
        cut = pl.ds(pl.multiple_of(rows + start * width, 16), peers * width)
        away = jnp.dot(turned_ref[cut, :], neigh_grad, preferred_element_type=F32)
        away = jnp.where(line == slots + hub_here, high, away)
        away = jnp.where(line == slots + hub_here + 1, sums - high, away)
        return away.astype(BF)

    pair = jnp.concatenate([x_ref[...], n_refs[0][...]], axis=1).T
    if count > 1:
        for k, ref in enumerate(send_refs):
            peer = seat_ref[0] ^ k
            ref[:width, :] = ghosts(here + peer, 1)
            mirror_ref[k] = ghosts(half - here + peer, 1)
            block = cot_ref[:, pl.ds(pl.multiple_of(peer * cols, cols), cols)]
            ref[width:, :] = jnp.dot(pair, block, preferred_element_type=F32).astype(BF)
        return
    send_ref = send_refs[0]
    send_ref[:, :width, :] = ghosts(here, half).reshape(half, width, cols)
    mirror_ref[...] = ghosts(half - here, half).reshape(half, width, cols)
    weights = jnp.dot(pair, grad, preferred_element_type=F32).astype(BF)
    step = min(share, depth)
    for j in range(blocks):
        for kind in range(2):
            block = weights[kind * depth : (kind + 1) * depth, j * cols : (j + 1) * cols]
            for part in range(depth // step):
                at = (j * 2 + kind) * depth + part * step
                low = width + at % share
                send_ref[at // share, low : low + step, :] = block[part * step : (part + 1) * step]


def seated(refs, seat):
    if len(refs) == 1:
        return [(j, refs[0].at[j]) for j in range(refs[0].shape[0])]
    return [(seat ^ k, ref) for k, ref in enumerate(refs)]


def sum_kernel(width, seat_ref, *refs):
    got_refs, (sum_ref, near_ref) = refs[:-2], refs[-2:]
    total = jnp.zeros(sum_ref.shape, F32)
    for j, got_ref in seated(got_refs[::-1], seat_ref[0]):
        total = total + got_ref[width:, :].astype(F32)
        near_ref[j] = got_ref[:width, :]
    sum_ref[...] = total.astype(BF)


def deal_kernel(got_ref, *out_refs):
    for k, ref in enumerate(out_refs):
        ref[...] = got_ref[k]


def total_kernel(own_ref, other_ref, part_ref):
    total = (own_ref[...].astype(F32) + other_ref[...].astype(F32)).astype(BF)
    part_ref[...] = jnp.broadcast_to(total, part_ref.shape)


def near_rows(slots, hub_here, start, mark_ref, got_ref):
    half, width, cols = got_ref.shape
    cut = pl.ds(pl.multiple_of(start * width, 128), half * width)
    added = jnp.dot(mark_ref[:, cut], got_ref[...].reshape(half * width, cols), preferred_element_type=F32)
    first = slots + hub_here
    bias = jnp.zeros((2, cols), F32)
    for j in range(half):
        bias = bias + got_ref[j, first : first + 2, :].astype(F32)
    return added, jnp.sum(bias, axis=0, keepdims=True)


def near_kernel(slots, hub_here, side_ref, back_ref, mark_ref, got_ref, sum_ref, bias_ref):
    half = got_ref.shape[0]
    added, bias = near_rows(slots, hub_here, side_ref[0] * half, mark_ref, got_ref)
    sum_ref[...] = back_ref[...] + added
    bias_ref[...] = bias


def grad_kernel(scale, slots, hub_here, side_ref, seat_ref, back_ref, near_ref, mark_ref, *refs):
    got_refs, (grad_ref, bias_ref, hold_ref) = refs[:-3], refs[-3:]
    half = hold_ref.shape[0]
    for j, got_ref in seated(got_refs, seat_ref[0]):
        hold_ref[j] = got_ref[...]
    added, bias = near_rows(slots, hub_here, half - side_ref[0] * half, mark_ref, hold_ref)
    grad_ref[...] = (back_ref[...] + added).astype(BF)
    bias_ref[...] = (near_ref[...] + bias) * scale


def spread_kernel(scale, seat_ref, *refs):
    got_refs, (self_ref, neigh_ref) = refs[:-2], refs[-2:]
    depth, full = self_ref.shape
    cols = got_refs[0].shape[-1]
    if len(got_refs) > 1:
        for j, ref in seated(got_refs, seat_ref[0]):
            cut = pl.ds(pl.multiple_of(j * cols, cols), cols)
            self_ref[:, cut] = ref[:depth, :].astype(F32) * scale
            neigh_ref[:, cut] = ref[depth:, :].astype(F32) * scale
        return
    whole = got_refs[0][...].reshape(2 * (full // cols) * depth, cols).astype(F32) * scale
    for j in range(full // cols):
        at = 2 * j * depth
        self_ref[:, j * cols : (j + 1) * cols] = whole[at : at + depth]
        neigh_ref[:, j * cols : (j + 1) * cols] = whole[at + depth : at + 2 * depth]


VMEM = pl.BlockSpec(memory_space=pltpu.VMEM)
SMEM = pl.BlockSpec(memory_space=pltpu.SMEM)
ANY = pl.BlockSpec(memory_space=pl.ANY)
HBM = pl.BlockSpec(memory_space=pltpu.HBM)
PARAMS = pltpu.CompilerParams(vmem_limit_bytes=40 * 1024 * 1024)


def shape(dims, kind):
    return jax.ShapeDtypeStruct(dims, kind)


def partner(block, axis, k):
    return lax.ppermute(block, axis, [(i, i ^ k) for i in range(lax.axis_size(axis))])


def exchange(blocks, groups=None):
    return lax.all_to_all(blocks, "dom", split_axis=0, concat_axis=0, axis_index_groups=groups, tiled=True)


def swap(blocks):
    return [blocks[0]] + [partner(block, "dom", k) for k, block in enumerate(blocks) if k]


def on_device(
    features,
    w_self,
    w_neigh,
    bias,
    cotangent,
    tile_vals,
    tile_pos,
    tile_count,
    send_rows,
    recv_dest,
    ghost_weight,
    recv_count,
    hub_rows,
    hub_weight,
):
    rows, cols = features.shape
    depth, full = w_self.shape
    blocks = full // cols
    peers, slots = send_rows.shape[1:]
    hub_here = hub_rows.shape[-1]
    width = -(-(slots + hub_here + 2) // 16) * 16
    lanes = peers * width
    half = peers // 2
    share = 2 * blocks * depth // half
    direct = half == blocks
    count = half if direct else 1
    halves = [list(range(half)), list(range(half, peers))]
    scale = 1.0 / math.sqrt(peers * rows)
    feats = lax.axis_size("feat")
    me = lax.axis_index("feat").astype(jnp.int32).reshape(1)
    side = (lax.axis_index("dom") >= half).astype(jnp.int32).reshape(1)
    seat = lax.rem(lax.axis_index("dom"), half).astype(jnp.int32).reshape(1)
    pack_rows = 2 * blocks * depth + 2 * rows + 16

    def pinned(*arrays):
        return [pltpu.with_memory_space_constraint(a, pltpu.HBM) for a in arrays]

    first = pinned(features, cotangent, w_self, w_neigh, bias.reshape(1, cols), send_rows, hub_rows)
    edges = pinned(tile_pos, recv_count, tile_vals, recv_dest, ghost_weight, hub_weight.T)
    moved = (send_rows, hub_rows, *edges)
    outgoing, pack, *moved = pl.pallas_call(
        functools.partial(send_kernel, width),
        out_shape=(
            shape((peers, width, cols), BF),
            shape((pack_rows, cols), BF),
            *(shape(a.shape, a.dtype) for a in moved),
        ),
        in_specs=[HBM] * (len(first) + len(edges)),
        out_specs=(VMEM,) * (2 + len(moved)),
        scratch_shapes=[
            pltpu.VMEM((1, cols), BF),
            pltpu.SemaphoreType.DMA((11 + 2 * blocks,)),
        ],
        compiler_params=PARAMS,
    )(*first, *edges)

    far = partner(pack, "feat", 2)
    near = partner(pack, "feat", 1)
    incoming = exchange(outgoing)
    mix, turned, mark = pl.pallas_call(
        functools.partial(mix_kernel, width),
        out_shape=(
            shape((rows, rows + lanes), BF),
            shape((rows + lanes, rows), BF),
            shape((rows, lanes), BF),
        ),
        in_specs=[VMEM] * (1 + len(moved)),
        out_specs=(VMEM,) * 3,
        compiler_params=PARAMS,
        cost_estimate=pl.CostEstimate(flops=10**8, bytes_accessed=3 * 10**6, transcendentals=0),
    )(tile_count.reshape(1, 1), *moved)
    neigh, far = pl.pallas_call(
        neigh_kernel,
        out_shape=(shape((rows, cols), BF), shape((pack_rows, cols), BF)),
        in_specs=[VMEM, VMEM, ANY, VMEM],
        out_specs=(VMEM, ANY),
        input_output_aliases={2: 1},
        compiler_params=PARAMS,
    )(features, mix, far, incoming)
    last = partner(far, "feat", 1)
    far_neigh = partner(neigh, "feat", 2)
    every = [neigh, partner(neigh, "feat", 1), far_neigh, partner(far_neigh, "feat", 1)]

    height = width + share
    output, back, mirror, *returned = pl.pallas_call(
        functools.partial(dense_kernel, slots, hub_here, feats, width, count),
        out_shape=(
            shape((rows, cols), BF),
            shape((rows, cols), F32),
            shape((half, width, cols), BF),
            *([shape((height, cols), BF)] * half if direct else [shape((half, height, cols), BF)]),
        ),
        in_specs=[SMEM] * 3 + [VMEM] * (4 + 2 * feats),
        out_specs=(VMEM,) * (3 + count),
        scratch_shapes=[
            pltpu.VMEM((rows, full), F32),
            pltpu.VMEM((rows, full), BF),
            pltpu.VMEM((16, full), BF),
        ],
        compiler_params=PARAMS,
    )(me, side, seat, features, w_self, w_neigh, turned, pack, near, far, last, *every)

    arrived = swap(returned)[::-1] if direct else [exchange(returned[0], halves)]
    mirror = partner(mirror, "dom", half)
    half_sum, near_ghosts = pl.pallas_call(
        functools.partial(sum_kernel, width),
        out_shape=(shape((share, cols), BF), shape((half, width, cols), BF)),
        in_specs=[SMEM] + [VMEM] * count,
        out_specs=(VMEM,) * 2,
        compiler_params=PARAMS,
    )(seat, *arrived)
    other_sum = partner(half_sum, "dom", half)
    if direct:
        crossed = swap(
            pl.pallas_call(
                deal_kernel,
                out_shape=(shape((width, cols), BF),) * half,
                in_specs=[VMEM],
                out_specs=(VMEM,) * half,
                compiler_params=PARAMS,
            )(mirror)
        )
    else:
        crossed = [exchange(mirror, halves)]
    back, near_bias = pl.pallas_call(
        functools.partial(near_kernel, slots, hub_here),
        out_shape=(shape((rows, cols), F32), shape((1, cols), F32)),
        in_specs=[SMEM] + [VMEM] * 3,
        out_specs=(VMEM,) * 2,
        compiler_params=PARAMS,
        cost_estimate=pl.CostEstimate(flops=10**8, bytes_accessed=10**6, transcendentals=0),
    )(side, back, mark, near_ghosts)
    part = pl.pallas_call(
        total_kernel,
        out_shape=shape((share, cols) if direct else (half, share, cols), BF),
        in_specs=[VMEM, VMEM],
        out_specs=VMEM,
        compiler_params=PARAMS,
    )(half_sum, other_sum)
    parts = swap([part] * half) if direct else [exchange(part, halves)]
    grad_features, grad_bias = pl.pallas_call(
        functools.partial(grad_kernel, scale, slots, hub_here),
        out_shape=(shape((rows, cols), BF), shape((1, cols), F32)),
        in_specs=[SMEM] * 2 + [VMEM] * (3 + count),
        out_specs=(VMEM,) * 2,
        scratch_shapes=[pltpu.VMEM((half, width, cols), BF)],
        compiler_params=PARAMS,
        cost_estimate=pl.CostEstimate(flops=2 * 10**9, bytes_accessed=10**6, transcendentals=0),
    )(side, seat, back, near_bias, mark, *crossed)
    grad_self, grad_neigh = pl.pallas_call(
        functools.partial(spread_kernel, scale),
        out_shape=(shape((depth, full), F32), shape((depth, full), F32)),
        in_specs=[SMEM] + [VMEM] * count,
        out_specs=(VMEM,) * 2,
        compiler_params=PARAMS,
    )(seat, *parts)
    return output, grad_features, grad_self, grad_neigh, grad_bias.reshape(cols)


def solution(mesh):
    placed = (
        P("dom", "feat"),
        P("feat", None),
        P("feat", None),
        P("feat"),
        P("dom", "feat"),
        P("dom", None, None, None),
        P("dom", None),
        P("dom"),
        P("dom", None, None),
        P("dom", None, None),
        P("dom", None, None),
        P("dom", None),
        P("dom", None),
        P("dom", None),
    )
    return jax.shard_map(
        on_device,
        mesh=mesh,
        in_specs=placed,
        out_specs=(P("dom", "feat"), P("dom", "feat"), P("feat", None), P("feat", None), P("feat")),
        check_vma=False,
    )
```

```python
import functools
import math

import jax
import jax.numpy as jnp
from jax import lax
from jax.experimental import pallas as pl
from jax.experimental.pallas import tpu as pltpu
from jax.sharding import PartitionSpec as P

BF = jnp.bfloat16
F32 = jnp.float32


def spread_rows(table, width):
    peers, slots = table.shape
    lanes = peers * width
    lane = lax.broadcasted_iota(jnp.int32, (slots, lanes), 1)
    slot = lax.broadcasted_iota(jnp.int32, (slots, lanes), 0)
    place = jnp.where(lane % width == slot, 1.0, 0.0).astype(BF)
    wide = jnp.dot(table.astype(BF), place, preferred_element_type=F32)
    peer = lax.broadcasted_iota(jnp.int32, (peers, lanes), 0)
    at = lax.broadcasted_iota(jnp.int32, (peers, lanes), 1)
    return jnp.sum(jnp.where(at // width == peer, wide, 0.0), axis=0, keepdims=True)


def source_matrix(send, hubs, rows, width):
    peers, slots = send.shape
    hub_here = hubs.shape[1]
    lanes = peers * width
    lane = lax.broadcasted_iota(jnp.int32, (1, lanes), 1) % width
    index = spread_rows(send.astype(F32), width)
    for k in range(hub_here):
        index = jnp.where(lane == slots + k, hubs[0:1, k : k + 1].astype(F32), index)
    index = jnp.where(lane < slots + hub_here, index, -1.0)
    row = lax.broadcasted_iota(jnp.int32, (rows, lanes), 0).astype(F32)
    return jnp.where(row == index, 1.0, 0.0).astype(BF)


def source_places(peers, slots, width):
    lanes = peers * width
    slot = lax.broadcasted_iota(jnp.int32, (lanes, slots), 0) % width
    return jnp.where(slot == lax.broadcasted_iota(jnp.int32, (lanes, slots), 1), 1.0, 0.0).astype(BF)


def source_rows(place, send, hubs, rows, width):
    peers, slots = send.shape
    hub_here = hubs.shape[1]
    lanes = peers * width
    wide = lax.dot_general(
        place, send.astype(F32).astype(BF), (((1,), (1,)), ((), ())), preferred_element_type=F32
    )
    line = lax.broadcasted_iota(jnp.int32, (lanes, peers), 0)
    for k in range(hub_here):
        wide = jnp.where(line % width == slots + k, hubs[0:1, k : k + 1].astype(F32), wide)
    wide = jnp.where(line % width < slots + hub_here, wide, -1.0)
    wide = jnp.where(line // width == lax.broadcasted_iota(jnp.int32, (lanes, peers), 1), wide, 0.0)
    index = jnp.dot(wide.astype(BF), jnp.ones((peers, rows), BF), preferred_element_type=F32)
    row = lax.broadcasted_iota(jnp.int32, (lanes, rows), 1).astype(F32)
    return jnp.where(row == index, 1.0, 0.0).astype(BF)


def send_kernel(
    width, x_ref, cot_ref, ws_ref, wn_ref, bias_ref, send_ref, hub_ref, pos_ref, live_ref, tile_ref, dest_ref, gw_ref, hw_ref,
    out_ref, pack_ref, send_v, hub_v, pos_v, live_v, tile_v, dest_v, gw_v, hw_v, bias_v, place_ref, sems,
):
    rows, cols = x_ref.shape
    depth, full = ws_ref.shape
    blocks = full // cols
    base = 2 * blocks * depth
    moves = [
        (send_ref, send_v),
        (hub_ref, hub_v),
        (x_ref, pack_ref.at[base : base + rows, :]),
        (bias_ref, bias_v),
        (cot_ref, pack_ref.at[base + rows : base + 2 * rows, :]),
    ]
    for kind, w_ref in enumerate((ws_ref, wn_ref)):
        for j in range(blocks):
            at = (kind * blocks + j) * depth
            moves.append((w_ref.at[:, j * cols : (j + 1) * cols], pack_ref.at[at : at + depth, :]))
    moves += [
        (pos_ref, pos_v), (live_ref, live_v), (tile_ref, tile_v), (dest_ref, dest_v),
        (gw_ref, gw_v), (hw_ref, hw_v),
    ]
    copies = [pltpu.make_async_copy(src, dst, sems.at[i]) for i, (src, dst) in enumerate(moves)]
    for copy in copies:
        copy.start()
    peers, slots = send_v.shape[1:]
    place_ref[...] = source_places(peers, slots, width)
    for copy in copies[:2]:
        copy.wait()
    mark = source_rows(place_ref[...], send_v[0], hub_v[...], rows, width)
    copies[2].wait()
    taken = jnp.dot(mark, pack_ref[base : base + rows, :], preferred_element_type=F32).astype(BF)
    out_ref[...] = taken.reshape(out_ref.shape)
    for copy in copies[3:]:
        copy.wait()
    pack_ref[base + 2 * rows :, :] = jnp.broadcast_to(bias_v[...], (16, cols))


def mix_kernel(width, count_ref, send_v, hub_v, pos_v, live_v, tile_v, dest_v, gw_v, hw_v, mix_ref, turned_ref, mark_ref):
    rows = mix_ref.shape[0]
    tiles, tile = tile_v.shape[1:3]
    peers, slots = dest_v.shape[1:]
    side = rows // tile
    lanes = peers * width
    hubs = hw_v.shape[0]
    hub_here = hubs // peers
    for r in range(side):
        for c in range(side):
            total = jnp.zeros((tile, tile), BF)
            for t in range(tiles):
                used = jnp.logical_and(pos_v[0:1, t : t + 1] == r * side + c, t < count_ref[...])
                total = jnp.where(used, tile_v[0, t], total)
            mix_ref[r * tile : (r + 1) * tile, c * tile : (c + 1) * tile] = total
    dest = spread_rows(dest_v[0].astype(F32), width)
    coef = spread_rows(gw_v[0], width)
    peer = lax.broadcasted_iota(jnp.int32, (peers, lanes), 0)
    at = lax.broadcasted_iota(jnp.int32, (peers, lanes), 1)
    owner = jnp.where(at // width == peer, 1.0, 0.0).astype(BF)
    limit = jnp.dot(live_v[...].astype(F32).astype(BF), owner, preferred_element_type=F32)
    lane = lax.broadcasted_iota(jnp.int32, (1, lanes), 1) % width
    coef = jnp.where(jnp.logical_and(lane.astype(F32) < limit, lane < slots), coef, 0.0)
    row = lax.broadcasted_iota(jnp.int32, (rows, lanes), 0).astype(F32)
    ghost = jnp.where(row == dest, coef, 0.0)
    hub = lax.broadcasted_iota(jnp.int32, (hubs, lanes), 0)
    at = lax.broadcasted_iota(jnp.int32, (hubs, lanes), 1)
    place = jnp.where(
        jnp.logical_and(at // width == hub // hub_here, at % width == slots + hub % hub_here), 1.0, 0.0
    ).astype(BF)
    hub_mix = lax.dot_general(hw_v[...], place, (((0,), (0,)), ((), ())), preferred_element_type=F32)
    mix_ref[:, rows:] = (ghost + hub_mix).astype(BF)
    turned_ref[...] = mix_ref[...].T
    mark_ref[...] = source_matrix(send_v[0], hub_v[...], rows, width)


def neigh_kernel(x_ref, mix_ref, far_ref, got_ref, neigh_ref, passed_ref):
    rows, cols = x_ref.shape
    lanes = mix_ref.shape[1] - rows
    total = jnp.dot(mix_ref[:, :rows], x_ref[...], preferred_element_type=F32)
    total = total + jnp.dot(mix_ref[:, rows:], got_ref[...].reshape(lanes, cols), preferred_element_type=F32)
    neigh_ref[...] = total.astype(BF)


def dense_kernel(slots, hub_here, feats, width, count, me_ref, side_ref, seat_ref, x_ref, ws_ref, wn_ref, turned_ref, *refs):
    pack_refs, n_refs = refs[:feats], refs[feats : 2 * feats]
    out_ref, back_ref, mirror_ref = refs[2 * feats : 2 * feats + 3]
    send_refs = refs[2 * feats + 3 : 2 * feats + 3 + count]
    pre_ref, cot_ref, bias_ref = refs[2 * feats + 3 + count :]
    rows, cols = x_ref.shape
    depth, full = ws_ref.shape
    blocks = full // cols
    half = mirror_ref.shape[0]
    height = send_refs[0].shape[-2]
    me = me_ref[0]
    base = 2 * blocks * depth
    left = []
    for d, pack in enumerate(pack_refs):
        owner = me ^ d
        cut = pl.ds(pl.multiple_of(owner * cols, cols), cols)
        cot_ref[:, cut] = pack[base + rows : base + 2 * rows, :]
        bias_ref[:, cut] = pack[base + 2 * rows : base + 2 * rows + 16, :]
        left += [pack[base : base + rows, :], n_refs[d][...]]
    left = jnp.concatenate(left, axis=1)
    both = jnp.concatenate([ws_ref[...], wn_ref[...]], axis=0)
    into = jnp.zeros((rows, 2 * depth), F32)
    span = 2
    for j in range(0, blocks, span):
        right = [
            jnp.concatenate([pack[(kind * blocks + i) * depth : (kind * blocks + i + 1) * depth, :] for i in range(j, j + span)], axis=1)
            for pack in pack_refs
            for kind in range(2)
        ]
        cut = slice(j * cols, (j + span) * cols)
        pre = jnp.dot(left, jnp.concatenate(right, axis=0), preferred_element_type=F32)
        pre = pre + bias_ref[0:1, cut].astype(F32)
        pre_ref[:, cut] = pre
        sig = jax.nn.sigmoid(pre)
        grad = (cot_ref[:, cut].astype(F32) * sig * (1.0 + pre * (1.0 - sig))).astype(BF)
        cot_ref[:, cut] = grad
        into = into + lax.dot_general(
            grad, both[:, cut], (((1,), (1,)), ((), ())), preferred_element_type=F32
        )
    mine = pl.ds(pl.multiple_of(me * cols, cols), cols)
    own = pre_ref[:, mine]
    out_ref[...] = (own * jax.nn.sigmoid(own)).astype(BF)
    neigh_grad = into[:, depth:].astype(BF)
    back_ref[...] = into[:, :depth] + jnp.dot(turned_ref[:rows, :], neigh_grad, preferred_element_type=F32)
    sums = jnp.sum(cot_ref[:, mine].astype(F32), axis=0, keepdims=True)
    high = sums.astype(BF).astype(F32)
    here = side_ref[0] * half
    share = height - width

    def ghosts(start, peers):
        line = lax.broadcasted_iota(jnp.int32, (peers * width, cols), 0) % width
        cut = pl.ds(pl.multiple_of(rows + start * width, 16), peers * width)
        away = jnp.dot(turned_ref[cut, :], neigh_grad, preferred_element_type=F32)
        away = jnp.where(line == slots + hub_here, high, away)
        away = jnp.where(line == slots + hub_here + 1, sums - high, away)
        return away.astype(BF)

    pair = jnp.concatenate([x_ref[...], n_refs[0][...]], axis=1).T
    if count > 1:
        for k, ref in enumerate(send_refs):
            peer = seat_ref[0] ^ k
            ref[:width, :] = ghosts(here + peer, 1)
            mirror_ref[k] = ghosts(half - here + peer, 1)
            block = cot_ref[:, pl.ds(pl.multiple_of(peer * cols, cols), cols)]
            ref[width:, :] = jnp.dot(pair, block, preferred_element_type=F32).astype(BF)
        return
    send_ref = send_refs[0]
    send_ref[:, :width, :] = ghosts(here, half).reshape(half, width, cols)
    mirror_ref[...] = ghosts(half - here, half).reshape(half, width, cols)
    weights = jnp.dot(pair, cot_ref[...], preferred_element_type=F32).astype(BF)
    step = min(share, depth)
    for j in range(blocks):
        for kind in range(2):
            block = weights[kind * depth : (kind + 1) * depth, j * cols : (j + 1) * cols]
            for part in range(depth // step):
                at = (j * 2 + kind) * depth + part * step
                low = width + at % share
                send_ref[at // share, low : low + step, :] = block[part * step : (part + 1) * step]


def seated(refs, seat):
    if len(refs) == 1:
        return [(j, refs[0].at[j]) for j in range(refs[0].shape[0])]
    return [(seat ^ k, ref) for k, ref in enumerate(refs)]


def sum_kernel(width, seat_ref, *refs):
    got_refs, (sum_ref, near_ref) = refs[:-2], refs[-2:]
    total = jnp.zeros(sum_ref.shape, F32)
    for j, got_ref in seated(got_refs[::-1], seat_ref[0]):
        total = total + got_ref[width:, :].astype(F32)
        near_ref[j] = got_ref[:width, :]
    sum_ref[...] = total.astype(BF)


def deal_kernel(got_ref, *out_refs):
    for k, ref in enumerate(out_refs):
        ref[...] = got_ref[k]


def total_kernel(own_ref, other_ref, part_ref):
    total = (own_ref[...].astype(F32) + other_ref[...].astype(F32)).astype(BF)
    part_ref[...] = jnp.broadcast_to(total, part_ref.shape)


def near_rows(slots, hub_here, start, mark_ref, got_ref):
    half, width, cols = got_ref.shape
    cut = pl.ds(pl.multiple_of(start * width, 128), half * width)
    added = jnp.dot(mark_ref[:, cut], got_ref[...].reshape(half * width, cols), preferred_element_type=F32)
    first = slots + hub_here
    bias = jnp.zeros((2, cols), F32)
    for j in range(half):
        bias = bias + got_ref[j, first : first + 2, :].astype(F32)
    return added, jnp.sum(bias, axis=0, keepdims=True)


def near_kernel(slots, hub_here, side_ref, back_ref, mark_ref, got_ref, sum_ref, bias_ref):
    half = got_ref.shape[0]
    added, bias = near_rows(slots, hub_here, side_ref[0] * half, mark_ref, got_ref)
    sum_ref[...] = back_ref[...] + added
    bias_ref[...] = bias


def grad_kernel(scale, slots, hub_here, side_ref, seat_ref, back_ref, near_ref, mark_ref, *refs):
    got_refs, (grad_ref, bias_ref, hold_ref) = refs[:-3], refs[-3:]
    half = hold_ref.shape[0]
    for j, got_ref in seated(got_refs, seat_ref[0]):
        hold_ref[j] = got_ref[...]
    added, bias = near_rows(slots, hub_here, half - side_ref[0] * half, mark_ref, hold_ref)
    grad_ref[...] = (back_ref[...] + added).astype(BF)
    bias_ref[...] = (near_ref[...] + bias) * scale


def spread_kernel(scale, seat_ref, *refs):
    got_refs, (self_ref, neigh_ref, wide_ref, sems) = refs[:-4], refs[-4:]
    depth, full = self_ref.shape
    cols = got_refs[0].shape[-1]
    blocks = full // cols
    if len(got_refs) > 1:
        parts = [(j, ref[...]) for j, ref in seated(got_refs, seat_ref[0])]
    else:
        whole = got_refs[0][...].reshape(2 * blocks * depth, cols)
        parts = [(j, whole[2 * j * depth : 2 * (j + 1) * depth]) for j in range(blocks)]
    copies = []
    for at, (j, part) in enumerate(parts):
        wide_ref[at] = part.astype(F32) * scale
        cut = pl.ds(pl.multiple_of(j * cols, cols), cols)
        for kind, out_ref in enumerate((self_ref, neigh_ref)):
            copy = pltpu.make_async_copy(
                wide_ref.at[at, kind * depth : (kind + 1) * depth, :], out_ref.at[:, cut], sems.at[2 * at + kind]
            )
            copy.start()
            copies.append(copy)
    for copy in copies:
        copy.wait()


VMEM = pl.BlockSpec(memory_space=pltpu.VMEM)
SMEM = pl.BlockSpec(memory_space=pltpu.SMEM)
ANY = pl.BlockSpec(memory_space=pl.ANY)
HBM = pl.BlockSpec(memory_space=pltpu.HBM)
PARAMS = pltpu.CompilerParams(vmem_limit_bytes=40 * 1024 * 1024)


def shape(dims, kind):
    return jax.ShapeDtypeStruct(dims, kind)


def partner(block, axis, k):
    return lax.ppermute(block, axis, [(i, i ^ k) for i in range(lax.axis_size(axis))])


def exchange(blocks, groups=None):
    return lax.all_to_all(blocks, "dom", split_axis=0, concat_axis=0, axis_index_groups=groups, tiled=True)


def swap(blocks):
    return [blocks[0]] + [partner(block, "dom", k) for k, block in enumerate(blocks) if k]


def on_device(
    features,
    w_self,
    w_neigh,
    bias,
    cotangent,
    tile_vals,
    tile_pos,
    tile_count,
    send_rows,
    recv_dest,
    ghost_weight,
    recv_count,
    hub_rows,
    hub_weight,
):
    rows, cols = features.shape
    depth, full = w_self.shape
    blocks = full // cols
    peers, slots = send_rows.shape[1:]
    hub_here = hub_rows.shape[-1]
    width = -(-(slots + hub_here + 2) // 16) * 16
    lanes = peers * width
    half = peers // 2
    share = 2 * blocks * depth // half
    direct = half == blocks
    count = half if direct else 1
    halves = [list(range(half)), list(range(half, peers))]
    scale = 1.0 / math.sqrt(peers * rows)
    feats = lax.axis_size("feat")
    me = lax.axis_index("feat").astype(jnp.int32).reshape(1)
    side = (lax.axis_index("dom") >= half).astype(jnp.int32).reshape(1)
    seat = lax.rem(lax.axis_index("dom"), half).astype(jnp.int32).reshape(1)
    pack_rows = 2 * blocks * depth + 2 * rows + 16

    def pinned(*arrays):
        return [pltpu.with_memory_space_constraint(a, pltpu.HBM) for a in arrays]

    first = pinned(features, cotangent, w_self, w_neigh, bias.reshape(1, cols), send_rows, hub_rows)
    edges = pinned(tile_pos, recv_count, tile_vals, recv_dest, ghost_weight, hub_weight.T)
    moved = (send_rows, hub_rows, *edges)
    outgoing, pack, *moved = pl.pallas_call(
        functools.partial(send_kernel, width),
        out_shape=(
            shape((peers, width, cols), BF),
            shape((pack_rows, cols), BF),
            *(shape(a.shape, a.dtype) for a in moved),
        ),
        in_specs=[HBM] * (len(first) + len(edges)),
        out_specs=(VMEM,) * (2 + len(moved)),
        scratch_shapes=[
            pltpu.VMEM((1, cols), BF),
            pltpu.VMEM((lanes, slots), BF),
            pltpu.SemaphoreType.DMA((11 + 2 * blocks,)),
        ],
        compiler_params=PARAMS,
    )(*first, *edges)

    far = partner(pack, "feat", 2)
    near = partner(pack, "feat", 1)
    incoming = exchange(outgoing)
    mix, turned, mark = pl.pallas_call(
        functools.partial(mix_kernel, width),
        out_shape=(
            shape((rows, rows + lanes), BF),
            shape((rows + lanes, rows), BF),
            shape((rows, lanes), BF),
        ),
        in_specs=[VMEM] * (1 + len(moved)),
        out_specs=(VMEM,) * 3,
        compiler_params=PARAMS,
        cost_estimate=pl.CostEstimate(flops=10**8, bytes_accessed=3 * 10**6, transcendentals=0),
    )(tile_count.reshape(1, 1), *moved)
    neigh, far = pl.pallas_call(
        neigh_kernel,
        out_shape=(shape((rows, cols), BF), shape((pack_rows, cols), BF)),
        in_specs=[VMEM, VMEM, ANY, VMEM],
        out_specs=(VMEM, ANY),
        input_output_aliases={2: 1},
        compiler_params=PARAMS,
    )(features, mix, far, incoming)
    last = partner(far, "feat", 1)
    far_neigh = partner(neigh, "feat", 2)
    every = [neigh, partner(neigh, "feat", 1), far_neigh, partner(far_neigh, "feat", 1)]

    height = width + share
    output, back, mirror, *returned = pl.pallas_call(
        functools.partial(dense_kernel, slots, hub_here, feats, width, count),
        out_shape=(
            shape((rows, cols), BF),
            shape((rows, cols), F32),
            shape((half, width, cols), BF),
            *([shape((height, cols), BF)] * half if direct else [shape((half, height, cols), BF)]),
        ),
        in_specs=[SMEM] * 3 + [VMEM] * (4 + 2 * feats),
        out_specs=(VMEM,) * (3 + count),
        scratch_shapes=[
            pltpu.VMEM((rows, full), F32),
            pltpu.VMEM((rows, full), BF),
            pltpu.VMEM((16, full), BF),
        ],
        compiler_params=PARAMS,
    )(me, side, seat, features, w_self, w_neigh, turned, pack, near, far, last, *every)

    arrived = swap(returned)[::-1] if direct else [exchange(returned[0], halves)]
    mirror = partner(mirror, "dom", half)
    half_sum, near_ghosts = pl.pallas_call(
        functools.partial(sum_kernel, width),
        out_shape=(shape((share, cols), BF), shape((half, width, cols), BF)),
        in_specs=[SMEM] + [VMEM] * count,
        out_specs=(VMEM,) * 2,
        compiler_params=PARAMS,
    )(seat, *arrived)
    other_sum = partner(half_sum, "dom", half)
    if direct:
        crossed = swap(
            pl.pallas_call(
                deal_kernel,
                out_shape=(shape((width, cols), BF),) * half,
                in_specs=[VMEM],
                out_specs=(VMEM,) * half,
                compiler_params=PARAMS,
            )(mirror)
        )
    else:
        crossed = [exchange(mirror, halves)]
    back, near_bias = pl.pallas_call(
        functools.partial(near_kernel, slots, hub_here),
        out_shape=(shape((rows, cols), F32), shape((1, cols), F32)),
        in_specs=[SMEM] + [VMEM] * 3,
        out_specs=(VMEM,) * 2,
        compiler_params=PARAMS,
        cost_estimate=pl.CostEstimate(flops=10**8, bytes_accessed=10**6, transcendentals=0),
    )(side, back, mark, near_ghosts)
    part = pl.pallas_call(
        total_kernel,
        out_shape=shape((share, cols) if direct else (half, share, cols), BF),
        in_specs=[VMEM, VMEM],
        out_specs=VMEM,
        compiler_params=PARAMS,
    )(half_sum, other_sum)
    parts = swap([part] * half) if direct else [exchange(part, halves)]
    grad_features, grad_bias = pl.pallas_call(
        functools.partial(grad_kernel, scale, slots, hub_here),
        out_shape=(shape((rows, cols), BF), shape((1, cols), F32)),
        in_specs=[SMEM] * 2 + [VMEM] * (3 + count),
        out_specs=(VMEM,) * 2,
        scratch_shapes=[pltpu.VMEM((half, width, cols), BF)],
        compiler_params=PARAMS,
        cost_estimate=pl.CostEstimate(flops=2 * 10**9, bytes_accessed=10**6, transcendentals=0),
    )(side, seat, back, near_bias, mark, *crossed)
    grad_self, grad_neigh = pl.pallas_call(
        functools.partial(spread_kernel, scale),
        out_shape=(shape((depth, full), F32), shape((depth, full), F32)),
        in_specs=[SMEM] + [VMEM] * count,
        out_specs=(HBM,) * 2,
        scratch_shapes=[pltpu.VMEM((blocks, 2 * depth, cols), F32), pltpu.SemaphoreType.DMA((2 * blocks,))],
        compiler_params=PARAMS,
    )(seat, *parts)
    return output, grad_features, grad_self, grad_neigh, grad_bias.reshape(cols)


def solution(mesh):
    placed = (
        P("dom", "feat"),
        P("feat", None),
        P("feat", None),
        P("feat"),
        P("dom", "feat"),
        P("dom", None, None, None),
        P("dom", None),
        P("dom"),
        P("dom", None, None),
        P("dom", None, None),
        P("dom", None, None),
        P("dom", None),
        P("dom", None),
        P("dom", None),
    )
    return jax.shard_map(
        on_device,
        mesh=mesh,
        in_specs=placed,
        out_specs=(P("dom", "feat"), P("dom", "feat"), P("feat", None), P("feat", None), P("feat")),
        check_vma=False,
    )
```

```python
import functools
import math

import jax
import jax.numpy as jnp
from jax import lax
from jax.experimental import pallas as pl
from jax.experimental.pallas import tpu as pltpu
from jax.sharding import PartitionSpec as P

BF = jnp.bfloat16
F32 = jnp.float32


def spread_rows(table, width):
    peers, slots = table.shape
    lanes = peers * width
    lane = lax.broadcasted_iota(jnp.int32, (slots, lanes), 1)
    slot = lax.broadcasted_iota(jnp.int32, (slots, lanes), 0)
    place = jnp.where(lane % width == slot, 1.0, 0.0).astype(BF)
    wide = jnp.dot(table.astype(BF), place, preferred_element_type=F32)
    peer = lax.broadcasted_iota(jnp.int32, (peers, lanes), 0)
    at = lax.broadcasted_iota(jnp.int32, (peers, lanes), 1)
    return jnp.sum(jnp.where(at // width == peer, wide, 0.0), axis=0, keepdims=True)


def source_matrix(send, hubs, rows, width):
    peers, slots = send.shape
    hub_here = hubs.shape[1]
    lanes = peers * width
    lane = lax.broadcasted_iota(jnp.int32, (1, lanes), 1) % width
    index = spread_rows(send.astype(F32), width)
    for k in range(hub_here):
        index = jnp.where(lane == slots + k, hubs[0:1, k : k + 1].astype(F32), index)
    index = jnp.where(lane < slots + hub_here, index, -1.0)
    row = lax.broadcasted_iota(jnp.int32, (rows, lanes), 0).astype(F32)
    return jnp.where(row == index, 1.0, 0.0).astype(BF)


def source_places(peers, slots, width):
    lanes = peers * width
    slot = lax.broadcasted_iota(jnp.int32, (lanes, slots), 0) % width
    return jnp.where(slot == lax.broadcasted_iota(jnp.int32, (lanes, slots), 1), 1.0, 0.0).astype(BF)


def source_rows(place, send, hubs, rows, width):
    peers, slots = send.shape
    hub_here = hubs.shape[1]
    lanes = peers * width
    wide = lax.dot_general(
        place, send.astype(F32).astype(BF), (((1,), (1,)), ((), ())), preferred_element_type=F32
    )
    line = lax.broadcasted_iota(jnp.int32, (lanes, peers), 0)
    for k in range(hub_here):
        wide = jnp.where(line % width == slots + k, hubs[0:1, k : k + 1].astype(F32), wide)
    wide = jnp.where(line % width < slots + hub_here, wide, -1.0)
    wide = jnp.where(line // width == lax.broadcasted_iota(jnp.int32, (lanes, peers), 1), wide, 0.0)
    index = jnp.dot(wide.astype(BF), jnp.ones((peers, rows), BF), preferred_element_type=F32)
    row = lax.broadcasted_iota(jnp.int32, (lanes, rows), 1).astype(F32)
    return jnp.where(row == index, 1.0, 0.0).astype(BF)


def send_kernel(
    width, x_ref, cot_ref, ws_ref, wn_ref, bias_ref, send_ref, hub_ref, pos_ref, live_ref, tile_ref, dest_ref, gw_ref, hw_ref,
    out_ref, pack_ref, send_v, hub_v, pos_v, live_v, tile_v, dest_v, gw_v, hw_v, bias_v, place_ref, sems,
):
    rows, cols = x_ref.shape
    depth, full = ws_ref.shape
    blocks = full // cols
    base = 2 * blocks * depth
    moves = [
        (send_ref, send_v),
        (hub_ref, hub_v),
        (x_ref, pack_ref.at[base : base + rows, :]),
        (bias_ref, bias_v),
        (cot_ref, pack_ref.at[base + rows : base + 2 * rows, :]),
    ]
    for kind, w_ref in enumerate((ws_ref, wn_ref)):
        for j in range(blocks):
            at = (kind * blocks + j) * depth
            moves.append((w_ref.at[:, j * cols : (j + 1) * cols], pack_ref.at[at : at + depth, :]))
    moves += [
        (pos_ref, pos_v), (live_ref, live_v), (tile_ref, tile_v), (dest_ref, dest_v),
        (gw_ref, gw_v), (hw_ref, hw_v),
    ]
    copies = [pltpu.make_async_copy(src, dst, sems.at[i]) for i, (src, dst) in enumerate(moves)]
    for copy in copies:
        copy.start()
    peers, slots = send_v.shape[1:]
    place_ref[...] = source_places(peers, slots, width)
    for copy in copies[:2]:
        copy.wait()
    mark = source_rows(place_ref[...], send_v[0], hub_v[...], rows, width)
    copies[2].wait()
    taken = jnp.dot(mark, pack_ref[base : base + rows, :], preferred_element_type=F32).astype(BF)
    out_ref[...] = taken.reshape(out_ref.shape)
    for copy in copies[3:]:
        copy.wait()
    pack_ref[base + 2 * rows :, :] = jnp.broadcast_to(bias_v[...], (16, cols))


def mix_kernel(width, count_ref, send_v, hub_v, pos_v, live_v, tile_v, dest_v, gw_v, hw_v, mix_ref, turned_ref, mark_ref):
    rows = mix_ref.shape[0]
    tiles, tile = tile_v.shape[1:3]
    peers, slots = dest_v.shape[1:]
    side = rows // tile
    lanes = peers * width
    hubs = hw_v.shape[0]
    hub_here = hubs // peers
    for r in range(side):
        for c in range(side):
            total = jnp.zeros((tile, tile), BF)
            for t in range(tiles):
                used = jnp.logical_and(pos_v[0:1, t : t + 1] == r * side + c, t < count_ref[...])
                total = jnp.where(used, tile_v[0, t], total)
            mix_ref[r * tile : (r + 1) * tile, c * tile : (c + 1) * tile] = total
    dest = spread_rows(dest_v[0].astype(F32), width)
    coef = spread_rows(gw_v[0], width)
    peer = lax.broadcasted_iota(jnp.int32, (peers, lanes), 0)
    at = lax.broadcasted_iota(jnp.int32, (peers, lanes), 1)
    owner = jnp.where(at // width == peer, 1.0, 0.0).astype(BF)
    limit = jnp.dot(live_v[...].astype(F32).astype(BF), owner, preferred_element_type=F32)
    lane = lax.broadcasted_iota(jnp.int32, (1, lanes), 1) % width
    coef = jnp.where(jnp.logical_and(lane.astype(F32) < limit, lane < slots), coef, 0.0)
    row = lax.broadcasted_iota(jnp.int32, (rows, lanes), 0).astype(F32)
    ghost = jnp.where(row == dest, coef, 0.0)
    hub = lax.broadcasted_iota(jnp.int32, (hubs, lanes), 0)
    at = lax.broadcasted_iota(jnp.int32, (hubs, lanes), 1)
    place = jnp.where(
        jnp.logical_and(at // width == hub // hub_here, at % width == slots + hub % hub_here), 1.0, 0.0
    ).astype(BF)
    hub_mix = lax.dot_general(hw_v[...], place, (((0,), (0,)), ((), ())), preferred_element_type=F32)
    mix_ref[:, rows:] = (ghost + hub_mix).astype(BF)
    turned_ref[...] = mix_ref[...].T
    mark_ref[...] = source_matrix(send_v[0], hub_v[...], rows, width)


def neigh_kernel(x_ref, mix_ref, far_ref, got_ref, neigh_ref, passed_ref):
    rows, cols = x_ref.shape
    lanes = mix_ref.shape[1] - rows
    total = jnp.dot(mix_ref[:, :rows], x_ref[...], preferred_element_type=F32)
    total = total + jnp.dot(mix_ref[:, rows:], got_ref[...].reshape(lanes, cols), preferred_element_type=F32)
    neigh_ref[...] = total.astype(BF)


def dense_kernel(slots, hub_here, feats, width, count, me_ref, side_ref, seat_ref, x_ref, ws_ref, wn_ref, turned_ref, *refs):
    pack_refs, n_refs = refs[:feats], refs[feats : 2 * feats]
    out_ref, back_ref, mirror_ref = refs[2 * feats : 2 * feats + 3]
    send_refs = refs[2 * feats + 3 : 2 * feats + 3 + count]
    pre_ref, cot_ref, bias_ref = refs[2 * feats + 3 + count :]
    rows, cols = x_ref.shape
    depth, full = ws_ref.shape
    blocks = full // cols
    half = mirror_ref.shape[0]
    height = send_refs[0].shape[-2]
    me = me_ref[0]
    base = 2 * blocks * depth
    left = []
    for d, pack in enumerate(pack_refs):
        owner = me ^ d
        cut = pl.ds(pl.multiple_of(owner * cols, cols), cols)
        cot_ref[:, cut] = pack[base + rows : base + 2 * rows, :]
        bias_ref[:, cut] = pack[base + 2 * rows : base + 2 * rows + 16, :]
        left += [pack[base : base + rows, :], n_refs[d][...]]
    left = jnp.concatenate(left, axis=1)
    both = jnp.concatenate([ws_ref[...], wn_ref[...]], axis=0)
    into = jnp.zeros((rows, 2 * depth), F32)
    span = 2
    for j in range(0, blocks, span):
        right = [
            jnp.concatenate([pack[(kind * blocks + i) * depth : (kind * blocks + i + 1) * depth, :] for i in range(j, j + span)], axis=1)
            for pack in pack_refs
            for kind in range(2)
        ]
        cut = slice(j * cols, (j + span) * cols)
        pre = jnp.dot(left, jnp.concatenate(right, axis=0), preferred_element_type=F32)
        pre = pre + bias_ref[0:1, cut].astype(F32)
        pre_ref[:, cut] = pre
        sig = jax.nn.sigmoid(pre)
        grad = (cot_ref[:, cut].astype(F32) * sig * (1.0 + pre * (1.0 - sig))).astype(BF)
        cot_ref[:, cut] = grad
        into = into + lax.dot_general(
            grad, both[:, cut], (((1,), (1,)), ((), ())), preferred_element_type=F32
        )
    mine = pl.ds(pl.multiple_of(me * cols, cols), cols)
    own = pre_ref[:, mine]
    out_ref[...] = (own * jax.nn.sigmoid(own)).astype(BF)
    neigh_grad = into[:, depth:].astype(BF)
    back_ref[...] = into[:, :depth] + jnp.dot(turned_ref[:rows, :], neigh_grad, preferred_element_type=F32)
    sums = jnp.sum(cot_ref[:, mine].astype(F32), axis=0, keepdims=True)
    high = sums.astype(BF).astype(F32)
    here = side_ref[0] * half
    share = height - width

    def ghosts(start, peers):
        line = lax.broadcasted_iota(jnp.int32, (peers * width, cols), 0) % width
        cut = pl.ds(pl.multiple_of(rows + start * width, 16), peers * width)
        away = jnp.dot(turned_ref[cut, :], neigh_grad, preferred_element_type=F32)
        away = jnp.where(line == slots + hub_here, high, away)
        away = jnp.where(line == slots + hub_here + 1, sums - high, away)
        return away.astype(BF)

    pair = jnp.concatenate([x_ref[...], n_refs[0][...]], axis=1).T
    if count > 1:
        for k, ref in enumerate(send_refs):
            peer = seat_ref[0] ^ k
            ref[:width, :] = ghosts(here + peer, 1)
            mirror_ref[k] = ghosts(half - here + peer, 1)
            block = cot_ref[:, pl.ds(pl.multiple_of(peer * cols, cols), cols)]
            ref[width:, :] = jnp.dot(pair, block, preferred_element_type=F32).astype(BF)
        return
    send_ref = send_refs[0]
    send_ref[:, :width, :] = ghosts(here, half).reshape(half, width, cols)
    mirror_ref[...] = ghosts(half - here, half).reshape(half, width, cols)
    weights = jnp.dot(pair, cot_ref[...], preferred_element_type=F32).astype(BF)
    step = min(share, depth)
    for j in range(blocks):
        for kind in range(2):
            block = weights[kind * depth : (kind + 1) * depth, j * cols : (j + 1) * cols]
            for part in range(depth // step):
                at = (j * 2 + kind) * depth + part * step
                low = width + at % share
                send_ref[at // share, low : low + step, :] = block[part * step : (part + 1) * step]


def seated(refs, seat):
    if len(refs) == 1:
        return [(j, refs[0].at[j]) for j in range(refs[0].shape[0])]
    return [(seat ^ k, ref) for k, ref in enumerate(refs)]


def store_kernel(held_ref, out_ref):
    out_ref[...] = held_ref[...]


def sum_kernel(width, seat_ref, stored_ref, *refs):
    got_refs, (sum_ref, near_ref) = refs[:-2], refs[-2:]
    total = jnp.zeros(sum_ref.shape, F32)
    for j, got_ref in seated(got_refs[::-1], seat_ref[0]):
        total = total + got_ref[width:, :].astype(F32)
        near_ref[j] = got_ref[:width, :]
    sum_ref[...] = total.astype(BF)


def deal_kernel(got_ref, *out_refs):
    for k, ref in enumerate(out_refs):
        ref[...] = got_ref[k]


def total_kernel(own_ref, other_ref, part_ref):
    total = (own_ref[...].astype(F32) + other_ref[...].astype(F32)).astype(BF)
    part_ref[...] = jnp.broadcast_to(total, part_ref.shape)


def near_rows(slots, hub_here, start, mark_ref, got_ref):
    half, width, cols = got_ref.shape
    cut = pl.ds(pl.multiple_of(start * width, 128), half * width)
    added = jnp.dot(mark_ref[:, cut], got_ref[...].reshape(half * width, cols), preferred_element_type=F32)
    first = slots + hub_here
    bias = jnp.zeros((2, cols), F32)
    for j in range(half):
        bias = bias + got_ref[j, first : first + 2, :].astype(F32)
    return added, jnp.sum(bias, axis=0, keepdims=True)


def near_kernel(slots, hub_here, side_ref, back_ref, mark_ref, got_ref, sum_ref, bias_ref):
    half = got_ref.shape[0]
    added, bias = near_rows(slots, hub_here, side_ref[0] * half, mark_ref, got_ref)
    sum_ref[...] = back_ref[...] + added
    bias_ref[...] = bias


def grad_kernel(scale, slots, hub_here, side_ref, seat_ref, back_ref, near_ref, mark_ref, *refs):
    got_refs, (grad_ref, bias_ref, hold_ref) = refs[:-3], refs[-3:]
    half = hold_ref.shape[0]
    for j, got_ref in seated(got_refs, seat_ref[0]):
        hold_ref[j] = got_ref[...]
    added, bias = near_rows(slots, hub_here, half - side_ref[0] * half, mark_ref, hold_ref)
    grad_ref[...] = (back_ref[...] + added).astype(BF)
    bias_ref[...] = (near_ref[...] + bias) * scale


def spread_kernel(scale, seat_ref, *refs):
    got_refs, (self_ref, neigh_ref, wide_ref, sems) = refs[:-4], refs[-4:]
    depth, full = self_ref.shape
    cols = got_refs[0].shape[-1]
    blocks = full // cols
    if len(got_refs) > 1:
        parts = [(j, ref[...]) for j, ref in seated(got_refs, seat_ref[0])]
    else:
        whole = got_refs[0][...].reshape(2 * blocks * depth, cols)
        parts = [(j, whole[2 * j * depth : 2 * (j + 1) * depth]) for j in range(blocks)]
    copies = []
    for at, (j, part) in enumerate(parts):
        wide_ref[at] = part.astype(F32) * scale
        cut = pl.ds(pl.multiple_of(j * cols, cols), cols)
        for kind, out_ref in enumerate((self_ref, neigh_ref)):
            copy = pltpu.make_async_copy(
                wide_ref.at[at, kind * depth : (kind + 1) * depth, :], out_ref.at[:, cut], sems.at[2 * at + kind]
            )
            copy.start()
            copies.append(copy)
    for copy in copies:
        copy.wait()


VMEM = pl.BlockSpec(memory_space=pltpu.VMEM)
SMEM = pl.BlockSpec(memory_space=pltpu.SMEM)
ANY = pl.BlockSpec(memory_space=pl.ANY)
HBM = pl.BlockSpec(memory_space=pltpu.HBM)
PARAMS = pltpu.CompilerParams(vmem_limit_bytes=40 * 1024 * 1024)


def shape(dims, kind):
    return jax.ShapeDtypeStruct(dims, kind)


def kept(dims, kind):
    return pltpu.VMEM(dims, kind)


def partner(block, axis, k):
    return lax.ppermute(block, axis, [(i, i ^ k) for i in range(lax.axis_size(axis))])


def exchange(blocks, groups=None):
    return lax.all_to_all(blocks, "dom", split_axis=0, concat_axis=0, axis_index_groups=groups, tiled=True)


def swap(blocks):
    return [blocks[0]] + [partner(block, "dom", k) for k, block in enumerate(blocks) if k]


def on_device(
    features,
    w_self,
    w_neigh,
    bias,
    cotangent,
    tile_vals,
    tile_pos,
    tile_count,
    send_rows,
    recv_dest,
    ghost_weight,
    recv_count,
    hub_rows,
    hub_weight,
):
    rows, cols = features.shape
    depth, full = w_self.shape
    blocks = full // cols
    peers, slots = send_rows.shape[1:]
    hub_here = hub_rows.shape[-1]
    width = -(-(slots + hub_here + 2) // 16) * 16
    lanes = peers * width
    half = peers // 2
    share = 2 * blocks * depth // half
    direct = half == blocks
    count = half if direct else 1
    halves = [list(range(half)), list(range(half, peers))]
    scale = 1.0 / math.sqrt(peers * rows)
    feats = lax.axis_size("feat")
    me = lax.axis_index("feat").astype(jnp.int32).reshape(1)
    side = (lax.axis_index("dom") >= half).astype(jnp.int32).reshape(1)
    seat = lax.rem(lax.axis_index("dom"), half).astype(jnp.int32).reshape(1)
    pack_rows = 2 * blocks * depth + 2 * rows + 16

    def pinned(*arrays):
        return [pltpu.with_memory_space_constraint(a, pltpu.HBM) for a in arrays]

    first = pinned(features, cotangent, w_self, w_neigh, bias.reshape(1, cols), send_rows, hub_rows)
    edges = pinned(tile_pos, recv_count, tile_vals, recv_dest, ghost_weight, hub_weight.T)
    moved = (send_rows, hub_rows, *edges)
    outgoing, pack, *moved = pl.pallas_call(
        functools.partial(send_kernel, width),
        out_shape=(
            kept((peers, width, cols), BF),
            shape((pack_rows, cols), BF),
            *(shape(a.shape, a.dtype) for a in moved),
        ),
        in_specs=[HBM] * (len(first) + len(edges)),
        out_specs=(VMEM,) * (2 + len(moved)),
        scratch_shapes=[
            pltpu.VMEM((1, cols), BF),
            pltpu.VMEM((lanes, slots), BF),
            pltpu.SemaphoreType.DMA((11 + 2 * blocks,)),
        ],
        compiler_params=PARAMS,
    )(*first, *edges)

    far = partner(pack, "feat", 2)
    near = partner(pack, "feat", 1)
    incoming = exchange(outgoing)
    mix, turned, mark = pl.pallas_call(
        functools.partial(mix_kernel, width),
        out_shape=(
            shape((rows, rows + lanes), BF),
            shape((rows + lanes, rows), BF),
            shape((rows, lanes), BF),
        ),
        in_specs=[VMEM] * (1 + len(moved)),
        out_specs=(VMEM,) * 3,
        compiler_params=PARAMS,
        cost_estimate=pl.CostEstimate(flops=10**8, bytes_accessed=3 * 10**6, transcendentals=0),
    )(tile_count.reshape(1, 1), *moved)
    neigh, far = pl.pallas_call(
        neigh_kernel,
        out_shape=(shape((rows, cols), BF), shape((pack_rows, cols), BF)),
        in_specs=[VMEM, VMEM, ANY, VMEM],
        out_specs=(VMEM, ANY),
        input_output_aliases={2: 1},
        compiler_params=PARAMS,
    )(features, mix, far, incoming)
    last = partner(far, "feat", 1)
    far_neigh = partner(neigh, "feat", 2)
    every = [neigh, partner(neigh, "feat", 1), far_neigh, partner(far_neigh, "feat", 1)]

    height = width + share
    output, back, mirror, *returned = pl.pallas_call(
        functools.partial(dense_kernel, slots, hub_here, feats, width, count),
        out_shape=(
            kept((rows, cols), BF),
            shape((rows, cols), F32),
            shape((half, width, cols), BF),
            *([shape((height, cols), BF)] * half if direct else [shape((half, height, cols), BF)]),
        ),
        in_specs=[SMEM] * 3 + [VMEM] * (4 + 2 * feats),
        out_specs=(VMEM,) * (3 + count),
        scratch_shapes=[
            pltpu.VMEM((rows, full), F32),
            pltpu.VMEM((rows, full), BF),
            pltpu.VMEM((16, full), BF),
        ],
        compiler_params=PARAMS,
    )(me, side, seat, features, w_self, w_neigh, turned, pack, near, far, last, *every)

    arrived = swap(returned)[::-1] if direct else [exchange(returned[0], halves)]
    mirror = partner(mirror, "dom", half)
    output = pl.pallas_call(
        store_kernel,
        out_shape=shape((rows, cols), BF),
        in_specs=[VMEM],
        out_specs=VMEM,
        compiler_params=PARAMS,
        cost_estimate=pl.CostEstimate(flops=10**8, bytes_accessed=10**6, transcendentals=0),
    )(output)
    half_sum, near_ghosts = pl.pallas_call(
        functools.partial(sum_kernel, width),
        out_shape=(shape((share, cols), BF), shape((half, width, cols), BF)),
        in_specs=[SMEM, HBM] + [VMEM] * count,
        out_specs=(VMEM,) * 2,
        compiler_params=PARAMS,
    )(seat, *pinned(output), *arrived)
    other_sum = partner(half_sum, "dom", half)
    if direct:
        crossed = swap(
            pl.pallas_call(
                deal_kernel,
                out_shape=(shape((width, cols), BF),) * half,
                in_specs=[VMEM],
                out_specs=(VMEM,) * half,
                compiler_params=PARAMS,
            )(mirror)
        )
    else:
        crossed = [exchange(mirror, halves)]
    back, near_bias = pl.pallas_call(
        functools.partial(near_kernel, slots, hub_here),
        out_shape=(shape((rows, cols), F32), shape((1, cols), F32)),
        in_specs=[SMEM] + [VMEM] * 3,
        out_specs=(VMEM,) * 2,
        compiler_params=PARAMS,
        cost_estimate=pl.CostEstimate(flops=10**8, bytes_accessed=10**6, transcendentals=0),
    )(side, back, mark, near_ghosts)
    part = pl.pallas_call(
        total_kernel,
        out_shape=shape((share, cols) if direct else (half, share, cols), BF),
        in_specs=[VMEM, VMEM],
        out_specs=VMEM,
        compiler_params=PARAMS,
    )(half_sum, other_sum)
    parts = swap([part] * half) if direct else [exchange(part, halves)]
    grad_features, grad_bias = pl.pallas_call(
        functools.partial(grad_kernel, scale, slots, hub_here),
        out_shape=(shape((rows, cols), BF), shape((1, cols), F32)),
        in_specs=[SMEM] * 2 + [VMEM] * (3 + count),
        out_specs=(VMEM,) * 2,
        scratch_shapes=[pltpu.VMEM((half, width, cols), BF)],
        compiler_params=PARAMS,
        cost_estimate=pl.CostEstimate(flops=2 * 10**9, bytes_accessed=10**6, transcendentals=0),
    )(side, seat, back, near_bias, mark, *crossed)
    grad_self, grad_neigh = pl.pallas_call(
        functools.partial(spread_kernel, scale),
        out_shape=(shape((depth, full), F32), shape((depth, full), F32)),
        in_specs=[SMEM] + [VMEM] * count,
        out_specs=(HBM,) * 2,
        scratch_shapes=[pltpu.VMEM((blocks, 2 * depth, cols), F32), pltpu.SemaphoreType.DMA((2 * blocks,))],
        compiler_params=PARAMS,
    )(seat, *parts)
    return output, grad_features, grad_self, grad_neigh, grad_bias.reshape(cols)


def solution(mesh):
    placed = (
        P("dom", "feat"),
        P("feat", None),
        P("feat", None),
        P("feat"),
        P("dom", "feat"),
        P("dom", None, None, None),
        P("dom", None),
        P("dom"),
        P("dom", None, None),
        P("dom", None, None),
        P("dom", None, None),
        P("dom", None),
        P("dom", None),
        P("dom", None),
    )
    return jax.shard_map(
        on_device,
        mesh=mesh,
        in_specs=placed,
        out_specs=(P("dom", "feat"), P("dom", "feat"), P("feat", None), P("feat", None), P("feat")),
        check_vma=False,
    )
```

```python
import functools
import math

import jax
import jax.numpy as jnp
from jax import lax
from jax.experimental import pallas as pl
from jax.experimental.pallas import tpu as pltpu
from jax.sharding import PartitionSpec as P

BF = jnp.bfloat16
F32 = jnp.float32


def spread_rows(table, width):
    peers, slots = table.shape
    lanes = peers * width
    lane = lax.broadcasted_iota(jnp.int32, (slots, lanes), 1)
    slot = lax.broadcasted_iota(jnp.int32, (slots, lanes), 0)
    place = jnp.where(lane % width == slot, 1.0, 0.0).astype(BF)
    wide = jnp.dot(table.astype(BF), place, preferred_element_type=F32)
    peer = lax.broadcasted_iota(jnp.int32, (peers, lanes), 0)
    at = lax.broadcasted_iota(jnp.int32, (peers, lanes), 1)
    return jnp.sum(jnp.where(at // width == peer, wide, 0.0), axis=0, keepdims=True)


def source_matrix(send, hubs, rows, width):
    peers, slots = send.shape
    hub_here = hubs.shape[1]
    lanes = peers * width
    lane = lax.broadcasted_iota(jnp.int32, (1, lanes), 1) % width
    index = spread_rows(send.astype(F32), width)
    for k in range(hub_here):
        index = jnp.where(lane == slots + k, hubs[0:1, k : k + 1].astype(F32), index)
    index = jnp.where(lane < slots + hub_here, index, -1.0)
    row = lax.broadcasted_iota(jnp.int32, (rows, lanes), 0).astype(F32)
    return jnp.where(row == index, 1.0, 0.0).astype(BF)


def source_places(peers, slots, width):
    lanes = peers * width
    slot = lax.broadcasted_iota(jnp.int32, (lanes, slots), 0) % width
    return jnp.where(slot == lax.broadcasted_iota(jnp.int32, (lanes, slots), 1), 1.0, 0.0).astype(BF)


def source_rows(place, send, hubs, rows, width):
    peers, slots = send.shape
    hub_here = hubs.shape[1]
    lanes = peers * width
    wide = lax.dot_general(
        place, send.astype(F32).astype(BF), (((1,), (1,)), ((), ())), preferred_element_type=F32
    )
    line = lax.broadcasted_iota(jnp.int32, (lanes, peers), 0)
    for k in range(hub_here):
        wide = jnp.where(line % width == slots + k, hubs[0:1, k : k + 1].astype(F32), wide)
    wide = jnp.where(line % width < slots + hub_here, wide, -1.0)
    wide = jnp.where(line // width == lax.broadcasted_iota(jnp.int32, (lanes, peers), 1), wide, 0.0)
    index = jnp.dot(wide.astype(BF), jnp.ones((peers, rows), BF), preferred_element_type=F32)
    row = lax.broadcasted_iota(jnp.int32, (lanes, rows), 1).astype(F32)
    return jnp.where(row == index, 1.0, 0.0).astype(BF)


def send_kernel(
    width, x_ref, cot_ref, ws_ref, wn_ref, bias_ref, send_ref, hub_ref, pos_ref, live_ref, tile_ref, dest_ref, gw_ref, hw_ref,
    out_ref, pack_ref, send_v, hub_v, pos_v, live_v, tile_v, dest_v, gw_v, hw_v, bias_v, place_ref, sems,
):
    rows, cols = x_ref.shape
    depth, full = ws_ref.shape
    blocks = full // cols
    base = 2 * blocks * depth
    moves = [
        (send_ref, send_v),
        (hub_ref, hub_v),
        (x_ref, pack_ref.at[base : base + rows, :]),
        (bias_ref, bias_v),
        (cot_ref, pack_ref.at[base + rows : base + 2 * rows, :]),
    ]
    for kind, w_ref in enumerate((ws_ref, wn_ref)):
        for j in range(blocks):
            at = (kind * blocks + j) * depth
            moves.append((w_ref.at[:, j * cols : (j + 1) * cols], pack_ref.at[at : at + depth, :]))
    moves += [
        (pos_ref, pos_v), (live_ref, live_v), (tile_ref, tile_v), (dest_ref, dest_v),
        (gw_ref, gw_v), (hw_ref, hw_v),
    ]
    copies = [pltpu.make_async_copy(src, dst, sems.at[i]) for i, (src, dst) in enumerate(moves)]
    for copy in copies:
        copy.start()
    peers, slots = send_v.shape[1:]
    place_ref[...] = source_places(peers, slots, width)
    for copy in copies[:2]:
        copy.wait()
    mark = source_rows(place_ref[...], send_v[0], hub_v[...], rows, width)
    copies[2].wait()
    taken = jnp.dot(mark, pack_ref[base : base + rows, :], preferred_element_type=F32).astype(BF)
    out_ref[...] = taken.reshape(out_ref.shape)
    for copy in copies[3:]:
        copy.wait()
    pack_ref[base + 2 * rows :, :] = jnp.broadcast_to(bias_v[...], (16, cols))


def mix_kernel(width, count_ref, send_v, hub_v, pos_v, live_v, tile_v, dest_v, gw_v, hw_v, mix_ref, turned_ref, mark_ref):
    rows = mix_ref.shape[0]
    tiles, tile = tile_v.shape[1:3]
    peers, slots = dest_v.shape[1:]
    side = rows // tile
    lanes = peers * width
    hubs = hw_v.shape[0]
    hub_here = hubs // peers
    for r in range(side):
        for c in range(side):
            total = jnp.zeros((tile, tile), BF)
            for t in range(tiles):
                used = jnp.logical_and(pos_v[0:1, t : t + 1] == r * side + c, t < count_ref[...])
                total = jnp.where(used, tile_v[0, t], total)
            mix_ref[r * tile : (r + 1) * tile, c * tile : (c + 1) * tile] = total
    dest = spread_rows(dest_v[0].astype(F32), width)
    coef = spread_rows(gw_v[0], width)
    peer = lax.broadcasted_iota(jnp.int32, (peers, lanes), 0)
    at = lax.broadcasted_iota(jnp.int32, (peers, lanes), 1)
    owner = jnp.where(at // width == peer, 1.0, 0.0).astype(BF)
    limit = jnp.dot(live_v[...].astype(F32).astype(BF), owner, preferred_element_type=F32)
    lane = lax.broadcasted_iota(jnp.int32, (1, lanes), 1) % width
    coef = jnp.where(jnp.logical_and(lane.astype(F32) < limit, lane < slots), coef, 0.0)
    row = lax.broadcasted_iota(jnp.int32, (rows, lanes), 0).astype(F32)
    ghost = jnp.where(row == dest, coef, 0.0)
    hub = lax.broadcasted_iota(jnp.int32, (hubs, lanes), 0)
    at = lax.broadcasted_iota(jnp.int32, (hubs, lanes), 1)
    place = jnp.where(
        jnp.logical_and(at // width == hub // hub_here, at % width == slots + hub % hub_here), 1.0, 0.0
    ).astype(BF)
    hub_mix = lax.dot_general(hw_v[...], place, (((0,), (0,)), ((), ())), preferred_element_type=F32)
    mix_ref[:, rows:] = (ghost + hub_mix).astype(BF)
    turned_ref[...] = mix_ref[...].T
    mark_ref[...] = source_matrix(send_v[0], hub_v[...], rows, width)


def neigh_kernel(x_ref, mix_ref, far_ref, got_ref, neigh_ref, passed_ref):
    rows, cols = x_ref.shape
    lanes = mix_ref.shape[1] - rows
    total = jnp.dot(mix_ref[:, :rows], x_ref[...], preferred_element_type=F32)
    total = total + jnp.dot(mix_ref[:, rows:], got_ref[...].reshape(lanes, cols), preferred_element_type=F32)
    neigh_ref[...] = total.astype(BF)


def dense_kernel(slots, hub_here, feats, width, count, me_ref, side_ref, seat_ref, x_ref, ws_ref, wn_ref, turned_ref, *refs):
    pack_refs, n_refs = refs[:feats], refs[feats : 2 * feats]
    out_ref, back_ref, mirror_ref = refs[2 * feats : 2 * feats + 3]
    send_refs = refs[2 * feats + 3 : 2 * feats + 3 + count]
    pre_ref, cot_ref, bias_ref = refs[2 * feats + 3 + count :]
    rows, cols = x_ref.shape
    depth, full = ws_ref.shape
    blocks = full // cols
    half = mirror_ref.shape[0]
    height = send_refs[0].shape[-2]
    me = me_ref[0]
    base = 2 * blocks * depth
    left = []
    for d, pack in enumerate(pack_refs):
        owner = me ^ d
        cut = pl.ds(pl.multiple_of(owner * cols, cols), cols)
        cot_ref[:, cut] = pack[base + rows : base + 2 * rows, :]
        bias_ref[:, cut] = pack[base + 2 * rows : base + 2 * rows + 16, :]
        left += [pack[base : base + rows, :], n_refs[d][...]]
    left = jnp.concatenate(left, axis=1)
    both = jnp.concatenate([ws_ref[...], wn_ref[...]], axis=0)
    into = jnp.zeros((rows, 2 * depth), F32)
    span = 2
    for j in range(0, blocks, span):
        right = [
            jnp.concatenate([pack[(kind * blocks + i) * depth : (kind * blocks + i + 1) * depth, :] for i in range(j, j + span)], axis=1)
            for pack in pack_refs
            for kind in range(2)
        ]
        cut = slice(j * cols, (j + span) * cols)
        pre = jnp.dot(left, jnp.concatenate(right, axis=0), preferred_element_type=F32)
        pre = pre + bias_ref[0:1, cut].astype(F32)
        pre_ref[:, cut] = pre
        sig = jax.nn.sigmoid(pre)
        grad = (cot_ref[:, cut].astype(F32) * sig * (1.0 + pre * (1.0 - sig))).astype(BF)
        cot_ref[:, cut] = grad
        into = into + lax.dot_general(
            grad, both[:, cut], (((1,), (1,)), ((), ())), preferred_element_type=F32
        )
    mine = pl.ds(pl.multiple_of(me * cols, cols), cols)
    own = pre_ref[:, mine]
    out_ref[...] = (own * jax.nn.sigmoid(own)).astype(BF)
    neigh_grad = into[:, depth:].astype(BF)
    back_ref[...] = into[:, :depth] + jnp.dot(turned_ref[:rows, :], neigh_grad, preferred_element_type=F32)
    sums = jnp.sum(cot_ref[:, mine].astype(F32), axis=0, keepdims=True)
    high = sums.astype(BF).astype(F32)
    here = side_ref[0] * half
    share = height - width

    def ghosts(start, peers):
        line = lax.broadcasted_iota(jnp.int32, (peers * width, cols), 0) % width
        cut = pl.ds(pl.multiple_of(rows + start * width, 16), peers * width)
        away = jnp.dot(turned_ref[cut, :], neigh_grad, preferred_element_type=F32)
        away = jnp.where(line == slots + hub_here, high, away)
        away = jnp.where(line == slots + hub_here + 1, sums - high, away)
        return away.astype(BF)

    pair = jnp.concatenate([x_ref[...], n_refs[0][...]], axis=1).T
    if count > 1:
        for k, ref in enumerate(send_refs):
            peer = seat_ref[0] ^ k
            ref[:width, :] = ghosts(here + peer, 1)
            mirror_ref[k] = ghosts(half - here + peer, 1)
            block = cot_ref[:, pl.ds(pl.multiple_of(peer * cols, cols), cols)]
            ref[width:, :] = jnp.dot(pair, block, preferred_element_type=F32).astype(BF)
        return
    send_ref = send_refs[0]
    send_ref[:, :width, :] = ghosts(here, half).reshape(half, width, cols)
    mirror_ref[...] = ghosts(half - here, half).reshape(half, width, cols)
    weights = jnp.dot(pair, cot_ref[...], preferred_element_type=F32).astype(BF)
    step = min(share, depth)
    for j in range(blocks):
        for kind in range(2):
            block = weights[kind * depth : (kind + 1) * depth, j * cols : (j + 1) * cols]
            for part in range(depth // step):
                at = (j * 2 + kind) * depth + part * step
                low = width + at % share
                send_ref[at // share, low : low + step, :] = block[part * step : (part + 1) * step]


def seated(refs, seat):
    if len(refs) == 1:
        return [(j, refs[0].at[j]) for j in range(refs[0].shape[0])]
    return [(seat ^ k, ref) for k, ref in enumerate(refs)]


def store_kernel(held_ref, out_ref):
    out_ref[...] = held_ref[...]


def sum_kernel(width, seat_ref, stored_ref, *refs):
    got_refs, (sum_ref, near_ref) = refs[:-2], refs[-2:]
    total = jnp.zeros(sum_ref.shape, F32)
    for j, got_ref in seated(got_refs[::-1], seat_ref[0]):
        total = total + got_ref[width:, :].astype(F32)
        near_ref[j] = got_ref[:width, :]
    sum_ref[...] = total.astype(BF)


def total_kernel(own_ref, other_ref, mirror_ref, *out_refs):
    share = own_ref.shape[0]
    total = (own_ref[...].astype(F32) + other_ref[...].astype(F32)).astype(BF)
    for k in range(mirror_ref.shape[0]):
        out_ref = out_refs[k] if len(out_refs) > 1 else out_refs[0].at[k]
        out_ref[:share, :] = total
        out_ref[share:, :] = mirror_ref[k]


def near_rows(slots, hub_here, start, mark_ref, got_ref):
    half, width, cols = got_ref.shape
    cut = pl.ds(pl.multiple_of(start * width, 128), half * width)
    added = jnp.dot(mark_ref[:, cut], got_ref[...].reshape(half * width, cols), preferred_element_type=F32)
    first = slots + hub_here
    bias = jnp.zeros((2, cols), F32)
    for j in range(half):
        bias = bias + got_ref[j, first : first + 2, :].astype(F32)
    return added, jnp.sum(bias, axis=0, keepdims=True)


def near_kernel(slots, hub_here, side_ref, back_ref, mark_ref, got_ref, sum_ref, bias_ref):
    half = got_ref.shape[0]
    added, bias = near_rows(slots, hub_here, side_ref[0] * half, mark_ref, got_ref)
    sum_ref[...] = back_ref[...] + added
    bias_ref[...] = bias


def last_kernel(scale, slots, hub_here, side_ref, seat_ref, back_ref, near_ref, mark_ref, *refs):
    got_refs, (grad_ref, bias_ref, self_ref, neigh_ref, hold_ref, wide_ref, sems) = refs[:-7], refs[-7:]
    depth, full = self_ref.shape
    half, width, cols = hold_ref.shape
    blocks = full // cols
    share = got_refs[0].shape[-2] - width
    parts = seated(got_refs, seat_ref[0])
    for j, ref in parts:
        hold_ref[j] = ref[share:, :]
    if len(got_refs) > 1:
        parts = [(j, ref[:share, :]) for j, ref in parts]
    else:
        whole = got_refs[0][:, :share, :].reshape(half * share, cols)
        parts = [(j, whole[2 * j * depth : 2 * (j + 1) * depth]) for j in range(blocks)]
    copies = []
    for at, (j, part) in enumerate(parts):
        wide_ref[at] = part.astype(F32) * scale
        cut = pl.ds(pl.multiple_of(j * cols, cols), cols)
        for kind, out_ref in enumerate((self_ref, neigh_ref)):
            copy = pltpu.make_async_copy(
                wide_ref.at[at, kind * depth : (kind + 1) * depth, :], out_ref.at[:, cut], sems.at[2 * at + kind]
            )
            copy.start()
            copies.append(copy)
    added, bias = near_rows(slots, hub_here, half - side_ref[0] * half, mark_ref, hold_ref)
    grad_ref[...] = (back_ref[...] + added).astype(BF)
    bias_ref[...] = (near_ref[...] + bias) * scale
    for copy in copies:
        copy.wait()


VMEM = pl.BlockSpec(memory_space=pltpu.VMEM)
SMEM = pl.BlockSpec(memory_space=pltpu.SMEM)
ANY = pl.BlockSpec(memory_space=pl.ANY)
HBM = pl.BlockSpec(memory_space=pltpu.HBM)
PARAMS = pltpu.CompilerParams(vmem_limit_bytes=40 * 1024 * 1024)


def shape(dims, kind):
    return jax.ShapeDtypeStruct(dims, kind)


def kept(dims, kind):
    return pltpu.VMEM(dims, kind)


def partner(block, axis, k):
    return lax.ppermute(block, axis, [(i, i ^ k) for i in range(lax.axis_size(axis))])


def exchange(blocks, groups=None):
    return lax.all_to_all(blocks, "dom", split_axis=0, concat_axis=0, axis_index_groups=groups, tiled=True)


def swap(blocks):
    return [blocks[0]] + [partner(block, "dom", k) for k, block in enumerate(blocks) if k]


def on_device(
    features,
    w_self,
    w_neigh,
    bias,
    cotangent,
    tile_vals,
    tile_pos,
    tile_count,
    send_rows,
    recv_dest,
    ghost_weight,
    recv_count,
    hub_rows,
    hub_weight,
):
    rows, cols = features.shape
    depth, full = w_self.shape
    blocks = full // cols
    peers, slots = send_rows.shape[1:]
    hub_here = hub_rows.shape[-1]
    width = -(-(slots + hub_here + 2) // 16) * 16
    lanes = peers * width
    half = peers // 2
    share = 2 * blocks * depth // half
    direct = half == blocks
    count = half if direct else 1
    halves = [list(range(half)), list(range(half, peers))]
    scale = 1.0 / math.sqrt(peers * rows)
    feats = lax.axis_size("feat")
    me = lax.axis_index("feat").astype(jnp.int32).reshape(1)
    side = (lax.axis_index("dom") >= half).astype(jnp.int32).reshape(1)
    seat = lax.rem(lax.axis_index("dom"), half).astype(jnp.int32).reshape(1)
    pack_rows = 2 * blocks * depth + 2 * rows + 16

    def pinned(*arrays):
        return [pltpu.with_memory_space_constraint(a, pltpu.HBM) for a in arrays]

    first = pinned(features, cotangent, w_self, w_neigh, bias.reshape(1, cols), send_rows, hub_rows)
    edges = pinned(tile_pos, recv_count, tile_vals, recv_dest, ghost_weight, hub_weight.T)
    moved = (send_rows, hub_rows, *edges)
    outgoing, pack, *moved = pl.pallas_call(
        functools.partial(send_kernel, width),
        out_shape=(
            kept((peers, width, cols), BF),
            shape((pack_rows, cols), BF),
            *(shape(a.shape, a.dtype) for a in moved),
        ),
        in_specs=[HBM] * (len(first) + len(edges)),
        out_specs=(VMEM,) * (2 + len(moved)),
        scratch_shapes=[
            pltpu.VMEM((1, cols), BF),
            pltpu.VMEM((lanes, slots), BF),
            pltpu.SemaphoreType.DMA((11 + 2 * blocks,)),
        ],
        compiler_params=PARAMS,
    )(*first, *edges)

    far = partner(pack, "feat", 2)
    near = partner(pack, "feat", 1)
    incoming = exchange(outgoing)
    mix, turned, mark = pl.pallas_call(
        functools.partial(mix_kernel, width),
        out_shape=(
            shape((rows, rows + lanes), BF),
            shape((rows + lanes, rows), BF),
            shape((rows, lanes), BF),
        ),
        in_specs=[VMEM] * (1 + len(moved)),
        out_specs=(VMEM,) * 3,
        compiler_params=PARAMS,
        cost_estimate=pl.CostEstimate(flops=10**8, bytes_accessed=3 * 10**6, transcendentals=0),
    )(tile_count.reshape(1, 1), *moved)
    neigh, far = pl.pallas_call(
        neigh_kernel,
        out_shape=(shape((rows, cols), BF), shape((pack_rows, cols), BF)),
        in_specs=[VMEM, VMEM, ANY, VMEM],
        out_specs=(VMEM, ANY),
        input_output_aliases={2: 1},
        compiler_params=PARAMS,
    )(features, mix, far, incoming)
    last = partner(far, "feat", 1)
    far_neigh = partner(neigh, "feat", 2)
    every = [neigh, partner(neigh, "feat", 1), far_neigh, partner(far_neigh, "feat", 1)]

    height = width + share
    output, back, mirror, *returned = pl.pallas_call(
        functools.partial(dense_kernel, slots, hub_here, feats, width, count),
        out_shape=(
            kept((rows, cols), BF),
            shape((rows, cols), F32),
            shape((half, width, cols), BF),
            *([shape((height, cols), BF)] * half if direct else [shape((half, height, cols), BF)]),
        ),
        in_specs=[SMEM] * 3 + [VMEM] * (4 + 2 * feats),
        out_specs=(VMEM,) * (3 + count),
        scratch_shapes=[
            pltpu.VMEM((rows, full), F32),
            pltpu.VMEM((rows, full), BF),
            pltpu.VMEM((16, full), BF),
        ],
        compiler_params=PARAMS,
    )(me, side, seat, features, w_self, w_neigh, turned, pack, near, far, last, *every)

    arrived = swap(returned)[::-1] if direct else [exchange(returned[0], halves)]
    mirror = partner(mirror, "dom", half)
    output = pl.pallas_call(
        store_kernel,
        out_shape=shape((rows, cols), BF),
        in_specs=[VMEM],
        out_specs=VMEM,
        compiler_params=PARAMS,
        cost_estimate=pl.CostEstimate(flops=10**8, bytes_accessed=10**6, transcendentals=0),
    )(output)
    half_sum, near_ghosts = pl.pallas_call(
        functools.partial(sum_kernel, width),
        out_shape=(shape((share, cols), BF), shape((half, width, cols), BF)),
        in_specs=[SMEM, HBM] + [VMEM] * count,
        out_specs=(VMEM,) * 2,
        compiler_params=PARAMS,
    )(seat, *pinned(output), *arrived)
    other_sum = partner(half_sum, "dom", half)
    back, near_bias = pl.pallas_call(
        functools.partial(near_kernel, slots, hub_here),
        out_shape=(shape((rows, cols), F32), shape((1, cols), F32)),
        in_specs=[SMEM] + [VMEM] * 3,
        out_specs=(VMEM,) * 2,
        compiler_params=PARAMS,
        cost_estimate=pl.CostEstimate(flops=10**8, bytes_accessed=10**6, transcendentals=0),
    )(side, back, mark, near_ghosts)
    parts = pl.pallas_call(
        total_kernel,
        out_shape=[shape((height, cols), BF)] * half if direct else [shape((half, height, cols), BF)],
        in_specs=[VMEM] * 3,
        out_specs=[VMEM] * count,
        compiler_params=PARAMS,
    )(half_sum, other_sum, mirror)
    parts = swap(parts) if direct else [exchange(parts[0], halves)]
    grad_features, grad_bias, grad_self, grad_neigh = pl.pallas_call(
        functools.partial(last_kernel, scale, slots, hub_here),
        out_shape=(
            shape((rows, cols), BF),
            shape((1, cols), F32),
            shape((depth, full), F32),
            shape((depth, full), F32),
        ),
        in_specs=[SMEM] * 2 + [VMEM] * (3 + count),
        out_specs=(VMEM,) * 2 + (HBM,) * 2,
        scratch_shapes=[
            pltpu.VMEM((half, width, cols), BF),
            pltpu.VMEM((blocks, 2 * depth, cols), F32),
            pltpu.SemaphoreType.DMA((2 * blocks,)),
        ],
        compiler_params=PARAMS,
    )(side, seat, back, near_bias, mark, *parts)
    return output, grad_features, grad_self, grad_neigh, grad_bias.reshape(cols)


def solution(mesh):
    placed = (
        P("dom", "feat"),
        P("feat", None),
        P("feat", None),
        P("feat"),
        P("dom", "feat"),
        P("dom", None, None, None),
        P("dom", None),
        P("dom"),
        P("dom", None, None),
        P("dom", None, None),
        P("dom", None, None),
        P("dom", None),
        P("dom", None),
        P("dom", None),
    )
    return jax.shard_map(
        on_device,
        mesh=mesh,
        in_specs=placed,
        out_specs=(P("dom", "feat"), P("dom", "feat"), P("feat", None), P("feat", None), P("feat")),
        check_vma=False,
    )
```

```python
import functools
import math

import jax
import jax.numpy as jnp
from jax import lax
from jax.experimental import pallas as pl
from jax.experimental.pallas import tpu as pltpu
from jax.sharding import PartitionSpec as P

BF = jnp.bfloat16
F32 = jnp.float32


def spread_rows(table, width):
    peers, slots = table.shape
    lanes = peers * width
    lane = lax.broadcasted_iota(jnp.int32, (slots, lanes), 1)
    slot = lax.broadcasted_iota(jnp.int32, (slots, lanes), 0)
    place = jnp.where(lane % width == slot, 1.0, 0.0).astype(BF)
    wide = jnp.dot(table.astype(BF), place, preferred_element_type=F32)
    peer = lax.broadcasted_iota(jnp.int32, (peers, lanes), 0)
    at = lax.broadcasted_iota(jnp.int32, (peers, lanes), 1)
    return jnp.sum(jnp.where(at // width == peer, wide, 0.0), axis=0, keepdims=True)


def source_matrix(send, hubs, rows, width):
    peers, slots = send.shape
    hub_here = hubs.shape[1]
    lanes = peers * width
    lane = lax.broadcasted_iota(jnp.int32, (1, lanes), 1) % width
    index = spread_rows(send.astype(F32), width)
    for k in range(hub_here):
        index = jnp.where(lane == slots + k, hubs[0:1, k : k + 1].astype(F32), index)
    index = jnp.where(lane < slots + hub_here, index, -1.0)
    row = lax.broadcasted_iota(jnp.int32, (rows, lanes), 0).astype(F32)
    return jnp.where(row == index, 1.0, 0.0).astype(BF)


def source_places(peers, slots, width):
    lanes = peers * width
    slot = lax.broadcasted_iota(jnp.int32, (lanes, slots), 0) % width
    return jnp.where(slot == lax.broadcasted_iota(jnp.int32, (lanes, slots), 1), 1.0, 0.0).astype(BF)


def source_rows(place, send, hubs, rows, width):
    peers, slots = send.shape
    hub_here = hubs.shape[1]
    lanes = peers * width
    wide = lax.dot_general(
        place, send.astype(F32).astype(BF), (((1,), (1,)), ((), ())), preferred_element_type=F32
    )
    line = lax.broadcasted_iota(jnp.int32, (lanes, peers), 0)
    for k in range(hub_here):
        wide = jnp.where(line % width == slots + k, hubs[0:1, k : k + 1].astype(F32), wide)
    wide = jnp.where(line % width < slots + hub_here, wide, -1.0)
    wide = jnp.where(line // width == lax.broadcasted_iota(jnp.int32, (lanes, peers), 1), wide, 0.0)
    index = jnp.dot(wide.astype(BF), jnp.ones((peers, rows), BF), preferred_element_type=F32)
    row = lax.broadcasted_iota(jnp.int32, (lanes, rows), 1).astype(F32)
    return jnp.where(row == index, 1.0, 0.0).astype(BF)


def send_kernel(
    width, x_ref, cot_ref, ws_ref, wn_ref, bias_ref, send_ref, hub_ref, pos_ref, live_ref, tile_ref, dest_ref, gw_ref, hw_ref,
    out_ref, pack_ref, send_v, hub_v, pos_v, live_v, tile_v, dest_v, gw_v, hw_v, bias_v, place_ref, sems,
):
    rows, cols = x_ref.shape
    depth, full = ws_ref.shape
    blocks = full // cols
    base = 2 * blocks * depth
    moves = [
        (send_ref, send_v),
        (hub_ref, hub_v),
        (x_ref, pack_ref.at[base : base + rows, :]),
        (bias_ref, bias_v),
        (cot_ref, pack_ref.at[base + rows : base + 2 * rows, :]),
    ]
    for kind, w_ref in enumerate((ws_ref, wn_ref)):
        for j in range(blocks):
            at = (kind * blocks + j) * depth
            moves.append((w_ref.at[:, j * cols : (j + 1) * cols], pack_ref.at[at : at + depth, :]))
    moves += [
        (pos_ref, pos_v), (live_ref, live_v), (tile_ref, tile_v), (dest_ref, dest_v),
        (gw_ref, gw_v), (hw_ref, hw_v),
    ]
    copies = [pltpu.make_async_copy(src, dst, sems.at[i]) for i, (src, dst) in enumerate(moves)]
    for copy in copies:
        copy.start()
    peers, slots = send_v.shape[1:]
    place_ref[...] = source_places(peers, slots, width)
    for copy in copies[:2]:
        copy.wait()
    mark = source_rows(place_ref[...], send_v[0], hub_v[...], rows, width)
    copies[2].wait()
    taken = jnp.dot(mark, pack_ref[base : base + rows, :], preferred_element_type=F32).astype(BF)
    out_ref[...] = taken.reshape(out_ref.shape)
    for copy in copies[3:]:
        copy.wait()
    pack_ref[base + 2 * rows :, :] = jnp.broadcast_to(bias_v[...], (16, cols))


def mix_kernel(width, count_ref, send_v, hub_v, pos_v, live_v, tile_v, dest_v, gw_v, hw_v, mix_ref, turned_ref, mark_ref):
    rows = mix_ref.shape[0]
    tiles, tile = tile_v.shape[1:3]
    peers, slots = dest_v.shape[1:]
    side = rows // tile
    lanes = peers * width
    hubs = hw_v.shape[0]
    hub_here = hubs // peers
    for r in range(side):
        for c in range(side):
            total = jnp.zeros((tile, tile), BF)
            for t in range(tiles):
                used = jnp.logical_and(pos_v[0:1, t : t + 1] == r * side + c, t < count_ref[...])
                total = jnp.where(used, tile_v[0, t], total)
            mix_ref[r * tile : (r + 1) * tile, c * tile : (c + 1) * tile] = total
    dest = spread_rows(dest_v[0].astype(F32), width)
    coef = spread_rows(gw_v[0], width)
    peer = lax.broadcasted_iota(jnp.int32, (peers, lanes), 0)
    at = lax.broadcasted_iota(jnp.int32, (peers, lanes), 1)
    owner = jnp.where(at // width == peer, 1.0, 0.0).astype(BF)
    limit = jnp.dot(live_v[...].astype(F32).astype(BF), owner, preferred_element_type=F32)
    lane = lax.broadcasted_iota(jnp.int32, (1, lanes), 1) % width
    coef = jnp.where(jnp.logical_and(lane.astype(F32) < limit, lane < slots), coef, 0.0)
    row = lax.broadcasted_iota(jnp.int32, (rows, lanes), 0).astype(F32)
    ghost = jnp.where(row == dest, coef, 0.0)
    hub = lax.broadcasted_iota(jnp.int32, (hubs, lanes), 0)
    at = lax.broadcasted_iota(jnp.int32, (hubs, lanes), 1)
    place = jnp.where(
        jnp.logical_and(at // width == hub // hub_here, at % width == slots + hub % hub_here), 1.0, 0.0
    ).astype(BF)
    hub_mix = lax.dot_general(hw_v[...], place, (((0,), (0,)), ((), ())), preferred_element_type=F32)
    mix_ref[:, rows:] = (ghost + hub_mix).astype(BF)
    turned_ref[...] = mix_ref[...].T
    mark_ref[...] = source_matrix(send_v[0], hub_v[...], rows, width)


def neigh_kernel(x_ref, mix_ref, far_ref, got_ref, neigh_ref, passed_ref):
    rows, cols = x_ref.shape
    lanes = mix_ref.shape[1] - rows
    total = jnp.dot(mix_ref[:, :rows], x_ref[...], preferred_element_type=F32)
    total = total + jnp.dot(mix_ref[:, rows:], got_ref[...].reshape(lanes, cols), preferred_element_type=F32)
    neigh_ref[...] = total.astype(BF)


def dense_kernel(slots, hub_here, feats, width, count, me_ref, side_ref, seat_ref, x_ref, ws_ref, wn_ref, turned_ref, *refs):
    pack_refs, n_refs = refs[:feats], refs[feats : 2 * feats]
    out_ref, back_ref, ghost_ref, mirror_ref = refs[2 * feats : 2 * feats + 4]
    send_refs = refs[2 * feats + 4 : 2 * feats + 4 + count]
    pre_ref, cot_ref, bias_ref = refs[2 * feats + 4 + count :]
    rows, cols = x_ref.shape
    depth, full = ws_ref.shape
    blocks = full // cols
    half = mirror_ref.shape[0]
    share = send_refs[0].shape[-2]
    me = me_ref[0]
    base = 2 * blocks * depth
    left = []
    for d, pack in enumerate(pack_refs):
        owner = me ^ d
        cut = pl.ds(pl.multiple_of(owner * cols, cols), cols)
        cot_ref[:, cut] = pack[base + rows : base + 2 * rows, :]
        bias_ref[:, cut] = pack[base + 2 * rows : base + 2 * rows + 16, :]
        left += [pack[base : base + rows, :], n_refs[d][...]]
    left = jnp.concatenate(left, axis=1)
    both = jnp.concatenate([ws_ref[...], wn_ref[...]], axis=0)
    into = jnp.zeros((rows, 2 * depth), F32)
    span = 2
    for j in range(0, blocks, span):
        right = [
            jnp.concatenate([pack[(kind * blocks + i) * depth : (kind * blocks + i + 1) * depth, :] for i in range(j, j + span)], axis=1)
            for pack in pack_refs
            for kind in range(2)
        ]
        cut = slice(j * cols, (j + span) * cols)
        pre = jnp.dot(left, jnp.concatenate(right, axis=0), preferred_element_type=F32)
        pre = pre + bias_ref[0:1, cut].astype(F32)
        pre_ref[:, cut] = pre
        sig = jax.nn.sigmoid(pre)
        grad = (cot_ref[:, cut].astype(F32) * sig * (1.0 + pre * (1.0 - sig))).astype(BF)
        cot_ref[:, cut] = grad
        into = into + lax.dot_general(
            grad, both[:, cut], (((1,), (1,)), ((), ())), preferred_element_type=F32
        )
    mine = pl.ds(pl.multiple_of(me * cols, cols), cols)
    own = pre_ref[:, mine]
    out_ref[...] = (own * jax.nn.sigmoid(own)).astype(BF)
    neigh_grad = into[:, depth:].astype(BF)
    back_ref[...] = into[:, :depth] + jnp.dot(turned_ref[:rows, :], neigh_grad, preferred_element_type=F32)
    sums = jnp.sum(cot_ref[:, mine].astype(F32), axis=0, keepdims=True)
    high = sums.astype(BF).astype(F32)
    here = side_ref[0] * half

    def ghosts(start, peers):
        line = lax.broadcasted_iota(jnp.int32, (peers * width, cols), 0) % width
        cut = pl.ds(pl.multiple_of(rows + start * width, 16), peers * width)
        away = jnp.dot(turned_ref[cut, :], neigh_grad, preferred_element_type=F32)
        away = jnp.where(line == slots + hub_here, high, away)
        away = jnp.where(line == slots + hub_here + 1, sums - high, away)
        return away.astype(BF)

    pair = jnp.concatenate([x_ref[...], n_refs[0][...]], axis=1).T
    if count > 1:
        for k, ref in enumerate(send_refs):
            peer = seat_ref[0] ^ k
            ghost_ref[k] = ghosts(here + peer, 1)
            mirror_ref[k] = ghosts(half - here + peer, 1)
            block = cot_ref[:, pl.ds(pl.multiple_of(peer * cols, cols), cols)]
            ref[...] = jnp.dot(pair, block, preferred_element_type=F32).astype(BF)
        return
    send_ref = send_refs[0]
    ghost_ref[...] = ghosts(here, half).reshape(half, width, cols)
    mirror_ref[...] = ghosts(half - here, half).reshape(half, width, cols)
    weights = jnp.dot(pair, cot_ref[...], preferred_element_type=F32).astype(BF)
    step = min(share, depth)
    for j in range(blocks):
        for kind in range(2):
            block = weights[kind * depth : (kind + 1) * depth, j * cols : (j + 1) * cols]
            for part in range(depth // step):
                at = (j * 2 + kind) * depth + part * step
                low = at % share
                send_ref[at // share, low : low + step, :] = block[part * step : (part + 1) * step]


def seated(refs, seat):
    if len(refs) == 1:
        return [(j, refs[0].at[j]) for j in range(refs[0].shape[0])]
    return [(seat ^ k, ref) for k, ref in enumerate(refs)]


def store_kernel(held_ref, out_ref):
    out_ref[...] = held_ref[...]


def sum_kernel(stored_ref, *refs):
    got_refs, sum_ref = refs[:-1], refs[-1]
    total = jnp.zeros(sum_ref.shape, F32)
    for got_ref in got_refs if len(got_refs) > 1 else [got_refs[0].at[j] for j in range(got_refs[0].shape[0])]:
        total = total + got_ref[...].astype(F32)
    sum_ref[...] = total.astype(BF)


def deal_kernel(ghost_ref, mirror_ref, *out_refs):
    width = ghost_ref.shape[1]
    for k in range(ghost_ref.shape[0]):
        out_ref = out_refs[k] if len(out_refs) > 1 else out_refs[0].at[k]
        out_ref[:width, :] = ghost_ref[k]
        out_ref[width:, :] = mirror_ref[k]


def total_kernel(own_ref, other_ref, part_ref):
    total = (own_ref[...].astype(F32) + other_ref[...].astype(F32)).astype(BF)
    part_ref[...] = jnp.broadcast_to(total, part_ref.shape)


def near_rows(slots, hub_here, start, mark_ref, got_ref):
    half, width, cols = got_ref.shape
    cut = pl.ds(pl.multiple_of(start * width, 128), half * width)
    added = jnp.dot(mark_ref[:, cut], got_ref[...].reshape(half * width, cols), preferred_element_type=F32)
    first = slots + hub_here
    bias = jnp.zeros((2, cols), F32)
    for j in range(half):
        bias = bias + got_ref[j, first : first + 2, :].astype(F32)
    return added, jnp.sum(bias, axis=0, keepdims=True)


def grad_kernel(scale, slots, hub_here, side_ref, seat_ref, back_ref, mark_ref, *refs):
    got_refs, (grad_ref, bias_ref, near_ref, far_ref) = refs[:-4], refs[-4:]
    half, width = near_ref.shape[:2]
    for j, got_ref in seated(got_refs, seat_ref[0]):
        near_ref[j] = got_ref[:width, :]
        far_ref[j] = got_ref[width:, :]
    here = side_ref[0] * half
    near, near_bias = near_rows(slots, hub_here, here, mark_ref, near_ref)
    far, far_bias = near_rows(slots, hub_here, half - here, mark_ref, far_ref)
    grad_ref[...] = (back_ref[...] + near + far).astype(BF)
    bias_ref[...] = (near_bias + far_bias) * scale


def spread_kernel(scale, seat_ref, *refs):
    got_refs, (self_ref, neigh_ref, wide_ref, sems) = refs[:-4], refs[-4:]
    depth, full = self_ref.shape
    cols = got_refs[0].shape[-1]
    blocks = full // cols
    if len(got_refs) > 1:
        parts = [(j, ref[...]) for j, ref in seated(got_refs, seat_ref[0])]
    else:
        whole = got_refs[0][...].reshape(2 * blocks * depth, cols)
        parts = [(j, whole[2 * j * depth : 2 * (j + 1) * depth]) for j in range(blocks)]
    copies = []
    for at, (j, part) in enumerate(parts):
        wide_ref[at] = part.astype(F32) * scale
        cut = pl.ds(pl.multiple_of(j * cols, cols), cols)
        for kind, out_ref in enumerate((self_ref, neigh_ref)):
            copy = pltpu.make_async_copy(
                wide_ref.at[at, kind * depth : (kind + 1) * depth, :], out_ref.at[:, cut], sems.at[2 * at + kind]
            )
            copy.start()
            copies.append(copy)
    for copy in copies:
        copy.wait()


VMEM = pl.BlockSpec(memory_space=pltpu.VMEM)
SMEM = pl.BlockSpec(memory_space=pltpu.SMEM)
ANY = pl.BlockSpec(memory_space=pl.ANY)
HBM = pl.BlockSpec(memory_space=pltpu.HBM)
PARAMS = pltpu.CompilerParams(vmem_limit_bytes=40 * 1024 * 1024)


def shape(dims, kind):
    return jax.ShapeDtypeStruct(dims, kind)


def kept(dims, kind):
    return pltpu.VMEM(dims, kind)


def partner(block, axis, k):
    return lax.ppermute(block, axis, [(i, i ^ k) for i in range(lax.axis_size(axis))])


def exchange(blocks, groups=None):
    return lax.all_to_all(blocks, "dom", split_axis=0, concat_axis=0, axis_index_groups=groups, tiled=True)


def swap(blocks):
    return [blocks[0]] + [partner(block, "dom", k) for k, block in enumerate(blocks) if k]


def on_device(
    features,
    w_self,
    w_neigh,
    bias,
    cotangent,
    tile_vals,
    tile_pos,
    tile_count,
    send_rows,
    recv_dest,
    ghost_weight,
    recv_count,
    hub_rows,
    hub_weight,
):
    rows, cols = features.shape
    depth, full = w_self.shape
    blocks = full // cols
    peers, slots = send_rows.shape[1:]
    hub_here = hub_rows.shape[-1]
    width = -(-(slots + hub_here + 2) // 16) * 16
    lanes = peers * width
    half = peers // 2
    share = 2 * blocks * depth // half
    direct = half == blocks
    count = half if direct else 1
    halves = [list(range(half)), list(range(half, peers))]
    scale = 1.0 / math.sqrt(peers * rows)
    feats = lax.axis_size("feat")
    me = lax.axis_index("feat").astype(jnp.int32).reshape(1)
    side = (lax.axis_index("dom") >= half).astype(jnp.int32).reshape(1)
    seat = lax.rem(lax.axis_index("dom"), half).astype(jnp.int32).reshape(1)
    pack_rows = 2 * blocks * depth + 2 * rows + 16

    def pinned(*arrays):
        return [pltpu.with_memory_space_constraint(a, pltpu.HBM) for a in arrays]

    first = pinned(features, cotangent, w_self, w_neigh, bias.reshape(1, cols), send_rows, hub_rows)
    edges = pinned(tile_pos, recv_count, tile_vals, recv_dest, ghost_weight, hub_weight.T)
    moved = (send_rows, hub_rows, *edges)
    outgoing, pack, *moved = pl.pallas_call(
        functools.partial(send_kernel, width),
        out_shape=(
            kept((peers, width, cols), BF),
            shape((pack_rows, cols), BF),
            *(shape(a.shape, a.dtype) for a in moved),
        ),
        in_specs=[HBM] * (len(first) + len(edges)),
        out_specs=(VMEM,) * (2 + len(moved)),
        scratch_shapes=[
            pltpu.VMEM((1, cols), BF),
            pltpu.VMEM((lanes, slots), BF),
            pltpu.SemaphoreType.DMA((11 + 2 * blocks,)),
        ],
        compiler_params=PARAMS,
    )(*first, *edges)

    far = partner(pack, "feat", 2)
    near = partner(pack, "feat", 1)
    incoming = exchange(outgoing)
    mix, turned, mark = pl.pallas_call(
        functools.partial(mix_kernel, width),
        out_shape=(
            shape((rows, rows + lanes), BF),
            shape((rows + lanes, rows), BF),
            shape((rows, lanes), BF),
        ),
        in_specs=[VMEM] * (1 + len(moved)),
        out_specs=(VMEM,) * 3,
        compiler_params=PARAMS,
        cost_estimate=pl.CostEstimate(flops=10**8, bytes_accessed=3 * 10**6, transcendentals=0),
    )(tile_count.reshape(1, 1), *moved)
    neigh, far = pl.pallas_call(
        neigh_kernel,
        out_shape=(shape((rows, cols), BF), shape((pack_rows, cols), BF)),
        in_specs=[VMEM, VMEM, ANY, VMEM],
        out_specs=(VMEM, ANY),
        input_output_aliases={2: 1},
        compiler_params=PARAMS,
    )(features, mix, far, incoming)
    last = partner(far, "feat", 1)
    far_neigh = partner(neigh, "feat", 2)
    every = [neigh, partner(neigh, "feat", 1), far_neigh, partner(far_neigh, "feat", 1)]

    output, back, ghosts, mirror, *returned = pl.pallas_call(
        functools.partial(dense_kernel, slots, hub_here, feats, width, count),
        out_shape=(
            kept((rows, cols), BF),
            shape((rows, cols), F32),
            shape((half, width, cols), BF),
            shape((half, width, cols), BF),
            *([shape((share, cols), BF)] * half if direct else [shape((half, share, cols), BF)]),
        ),
        in_specs=[SMEM] * 3 + [VMEM] * (4 + 2 * feats),
        out_specs=(VMEM,) * (4 + count),
        scratch_shapes=[
            pltpu.VMEM((rows, full), F32),
            pltpu.VMEM((rows, full), BF),
            pltpu.VMEM((16, full), BF),
        ],
        compiler_params=PARAMS,
    )(me, side, seat, features, w_self, w_neigh, turned, pack, near, far, last, *every)

    arrived = swap(returned)[::-1] if direct else [exchange(returned[0], halves)]
    mirror = partner(mirror, "dom", half)
    output = pl.pallas_call(
        store_kernel,
        out_shape=shape((rows, cols), BF),
        in_specs=[VMEM],
        out_specs=VMEM,
        compiler_params=PARAMS,
        cost_estimate=pl.CostEstimate(flops=10**8, bytes_accessed=10**6, transcendentals=0),
    )(output)
    half_sum = pl.pallas_call(
        sum_kernel,
        out_shape=shape((share, cols), BF),
        in_specs=[HBM] + [VMEM] * count,
        out_specs=VMEM,
        compiler_params=PARAMS,
    )(*pinned(output), *arrived)
    other_sum = partner(half_sum, "dom", half)
    dealt = pl.pallas_call(
        deal_kernel,
        out_shape=[shape((2 * width, cols), BF)] * half if direct else [shape((half, 2 * width, cols), BF)],
        in_specs=[VMEM] * 2,
        out_specs=[VMEM] * count,
        compiler_params=PARAMS,
    )(ghosts, mirror)
    dealt = swap(dealt) if direct else [exchange(dealt[0], halves)]
    part = pl.pallas_call(
        total_kernel,
        out_shape=shape((share, cols) if direct else (half, share, cols), BF),
        in_specs=[VMEM, VMEM],
        out_specs=VMEM,
        compiler_params=PARAMS,
    )(half_sum, other_sum)
    parts = swap([part] * half) if direct else [exchange(part, halves)]
    grad_features, grad_bias = pl.pallas_call(
        functools.partial(grad_kernel, scale, slots, hub_here),
        out_shape=(shape((rows, cols), BF), shape((1, cols), F32)),
        in_specs=[SMEM] * 2 + [VMEM] * (2 + count),
        out_specs=(VMEM,) * 2,
        scratch_shapes=[pltpu.VMEM((half, width, cols), BF)] * 2,
        compiler_params=PARAMS,
        cost_estimate=pl.CostEstimate(flops=2 * 10**9, bytes_accessed=10**6, transcendentals=0),
    )(side, seat, back, mark, *dealt)
    grad_self, grad_neigh = pl.pallas_call(
        functools.partial(spread_kernel, scale),
        out_shape=(shape((depth, full), F32), shape((depth, full), F32)),
        in_specs=[SMEM] + [VMEM] * count,
        out_specs=(HBM,) * 2,
        scratch_shapes=[pltpu.VMEM((blocks, 2 * depth, cols), F32), pltpu.SemaphoreType.DMA((2 * blocks,))],
        compiler_params=PARAMS,
    )(seat, *parts)
    return output, grad_features, grad_self, grad_neigh, grad_bias.reshape(cols)


def solution(mesh):
    placed = (
        P("dom", "feat"),
        P("feat", None),
        P("feat", None),
        P("feat"),
        P("dom", "feat"),
        P("dom", None, None, None),
        P("dom", None),
        P("dom"),
        P("dom", None, None),
        P("dom", None, None),
        P("dom", None, None),
        P("dom", None),
        P("dom", None),
        P("dom", None),
    )
    return jax.shard_map(
        on_device,
        mesh=mesh,
        in_specs=placed,
        out_specs=(P("dom", "feat"), P("dom", "feat"), P("feat", None), P("feat", None), P("feat")),
        check_vma=False,
    )
```

```python
import functools
import math

import jax
import jax.numpy as jnp
from jax import lax
from jax.experimental import pallas as pl
from jax.experimental.pallas import tpu as pltpu
from jax.sharding import PartitionSpec as P

BF = jnp.bfloat16
F32 = jnp.float32


def spread_rows(table, width):
    peers, slots = table.shape
    lanes = peers * width
    lane = lax.broadcasted_iota(jnp.int32, (slots, lanes), 1)
    slot = lax.broadcasted_iota(jnp.int32, (slots, lanes), 0)
    place = jnp.where(lane % width == slot, 1.0, 0.0).astype(BF)
    wide = jnp.dot(table.astype(BF), place, preferred_element_type=F32)
    peer = lax.broadcasted_iota(jnp.int32, (peers, lanes), 0)
    at = lax.broadcasted_iota(jnp.int32, (peers, lanes), 1)
    return jnp.sum(jnp.where(at // width == peer, wide, 0.0), axis=0, keepdims=True)


def source_matrix(send, hubs, rows, width):
    peers, slots = send.shape
    hub_here = hubs.shape[1]
    lanes = peers * width
    lane = lax.broadcasted_iota(jnp.int32, (1, lanes), 1) % width
    index = spread_rows(send.astype(F32), width)
    for k in range(hub_here):
        index = jnp.where(lane == slots + k, hubs[0:1, k : k + 1].astype(F32), index)
    index = jnp.where(lane < slots + hub_here, index, -1.0)
    row = lax.broadcasted_iota(jnp.int32, (rows, lanes), 0).astype(F32)
    return jnp.where(row == index, 1.0, 0.0).astype(BF)


def source_places(peers, slots, width):
    lanes = peers * width
    slot = lax.broadcasted_iota(jnp.int32, (lanes, slots), 0) % width
    return jnp.where(slot == lax.broadcasted_iota(jnp.int32, (lanes, slots), 1), 1.0, 0.0).astype(BF)


def source_rows(place, send, hubs, rows, width):
    peers, slots = send.shape
    hub_here = hubs.shape[1]
    lanes = peers * width
    wide = lax.dot_general(
        place, send.astype(F32).astype(BF), (((1,), (1,)), ((), ())), preferred_element_type=F32
    )
    line = lax.broadcasted_iota(jnp.int32, (lanes, peers), 0)
    for k in range(hub_here):
        wide = jnp.where(line % width == slots + k, hubs[0:1, k : k + 1].astype(F32), wide)
    wide = jnp.where(line % width < slots + hub_here, wide, -1.0)
    wide = jnp.where(line // width == lax.broadcasted_iota(jnp.int32, (lanes, peers), 1), wide, 0.0)
    index = jnp.dot(wide.astype(BF), jnp.ones((peers, rows), BF), preferred_element_type=F32)
    row = lax.broadcasted_iota(jnp.int32, (lanes, rows), 1).astype(F32)
    return jnp.where(row == index, 1.0, 0.0).astype(BF)


def send_kernel(
    width, x_ref, cot_ref, ws_ref, wn_ref, bias_ref, send_ref, hub_ref, pos_ref, live_ref, tile_ref, dest_ref, gw_ref, hw_ref,
    out_ref, pack_ref, send_v, hub_v, pos_v, live_v, tile_v, dest_v, gw_v, hw_v, bias_v, place_ref, sems,
):
    rows, cols = x_ref.shape
    depth, full = ws_ref.shape
    blocks = full // cols
    base = 2 * blocks * depth
    moves = [
        (send_ref, send_v),
        (hub_ref, hub_v),
        (x_ref, pack_ref.at[base : base + rows, :]),
        (bias_ref, bias_v),
        (cot_ref, pack_ref.at[base + rows : base + 2 * rows, :]),
    ]
    for kind, w_ref in enumerate((ws_ref, wn_ref)):
        for j in range(blocks):
            at = (kind * blocks + j) * depth
            moves.append((w_ref.at[:, j * cols : (j + 1) * cols], pack_ref.at[at : at + depth, :]))
    moves += [
        (pos_ref, pos_v), (live_ref, live_v), (tile_ref, tile_v), (dest_ref, dest_v),
        (gw_ref, gw_v), (hw_ref, hw_v),
    ]
    copies = [pltpu.make_async_copy(src, dst, sems.at[i]) for i, (src, dst) in enumerate(moves)]
    for copy in copies:
        copy.start()
    peers, slots = send_v.shape[1:]
    place_ref[...] = source_places(peers, slots, width)
    for copy in copies[:2]:
        copy.wait()
    mark = source_rows(place_ref[...], send_v[0], hub_v[...], rows, width)
    copies[2].wait()
    taken = jnp.dot(mark, pack_ref[base : base + rows, :], preferred_element_type=F32).astype(BF)
    out_ref[...] = taken.reshape(out_ref.shape)
    for copy in copies[3:]:
        copy.wait()
    pack_ref[base + 2 * rows :, :] = jnp.broadcast_to(bias_v[...], (16, cols))


def mix_kernel(width, count_ref, send_v, hub_v, pos_v, live_v, tile_v, dest_v, gw_v, hw_v, mix_ref, turned_ref, mark_ref):
    rows = mix_ref.shape[0]
    tiles, tile = tile_v.shape[1:3]
    peers, slots = dest_v.shape[1:]
    side = rows // tile
    lanes = peers * width
    hubs = hw_v.shape[0]
    hub_here = hubs // peers
    for r in range(side):
        for c in range(side):
            total = jnp.zeros((tile, tile), BF)
            for t in range(tiles):
                used = jnp.logical_and(pos_v[0:1, t : t + 1] == r * side + c, t < count_ref[...])
                total = jnp.where(used, tile_v[0, t], total)
            mix_ref[r * tile : (r + 1) * tile, c * tile : (c + 1) * tile] = total
    dest = spread_rows(dest_v[0].astype(F32), width)
    coef = spread_rows(gw_v[0], width)
    peer = lax.broadcasted_iota(jnp.int32, (peers, lanes), 0)
    at = lax.broadcasted_iota(jnp.int32, (peers, lanes), 1)
    owner = jnp.where(at // width == peer, 1.0, 0.0).astype(BF)
    limit = jnp.dot(live_v[...].astype(F32).astype(BF), owner, preferred_element_type=F32)
    lane = lax.broadcasted_iota(jnp.int32, (1, lanes), 1) % width
    coef = jnp.where(jnp.logical_and(lane.astype(F32) < limit, lane < slots), coef, 0.0)
    row = lax.broadcasted_iota(jnp.int32, (rows, lanes), 0).astype(F32)
    ghost = jnp.where(row == dest, coef, 0.0)
    hub = lax.broadcasted_iota(jnp.int32, (hubs, lanes), 0)
    at = lax.broadcasted_iota(jnp.int32, (hubs, lanes), 1)
    place = jnp.where(
        jnp.logical_and(at // width == hub // hub_here, at % width == slots + hub % hub_here), 1.0, 0.0
    ).astype(BF)
    hub_mix = lax.dot_general(hw_v[...], place, (((0,), (0,)), ((), ())), preferred_element_type=F32)
    mix_ref[:, rows:] = (ghost + hub_mix).astype(BF)
    turned_ref[...] = mix_ref[...].T
    mark_ref[...] = source_matrix(send_v[0], hub_v[...], rows, width)


def neigh_kernel(x_ref, mix_ref, far_ref, got_ref, neigh_ref, passed_ref):
    rows, cols = x_ref.shape
    lanes = mix_ref.shape[1] - rows
    total = jnp.dot(mix_ref[:, :rows], x_ref[...], preferred_element_type=F32)
    total = total + jnp.dot(mix_ref[:, rows:], got_ref[...].reshape(lanes, cols), preferred_element_type=F32)
    neigh_ref[...] = total.astype(BF)


def dense_kernel(slots, hub_here, feats, width, count, me_ref, side_ref, seat_ref, x_ref, ws_ref, wn_ref, turned_ref, *refs):
    pack_refs, n_refs = refs[:feats], refs[feats : 2 * feats]
    out_ref, back_ref, ghost_ref, mirror_ref = refs[2 * feats : 2 * feats + 4]
    send_refs = refs[2 * feats + 4 : 2 * feats + 4 + count]
    pre_ref, cot_ref, bias_ref = refs[2 * feats + 4 + count :]
    rows, cols = x_ref.shape
    depth, full = ws_ref.shape
    blocks = full // cols
    half = mirror_ref.shape[0]
    share = send_refs[0].shape[-2]
    me = me_ref[0]
    base = 2 * blocks * depth
    left = []
    for d, pack in enumerate(pack_refs):
        owner = me ^ d
        cut = pl.ds(pl.multiple_of(owner * cols, cols), cols)
        cot_ref[:, cut] = pack[base + rows : base + 2 * rows, :]
        bias_ref[:, cut] = pack[base + 2 * rows : base + 2 * rows + 16, :]
        left += [pack[base : base + rows, :], n_refs[d][...]]
    left = jnp.concatenate(left, axis=1)
    both = jnp.concatenate([ws_ref[...], wn_ref[...]], axis=0)
    into = jnp.zeros((rows, 2 * depth), F32)
    span = 2
    for j in range(0, blocks, span):
        right = [
            jnp.concatenate([pack[(kind * blocks + i) * depth : (kind * blocks + i + 1) * depth, :] for i in range(j, j + span)], axis=1)
            for pack in pack_refs
            for kind in range(2)
        ]
        cut = slice(j * cols, (j + span) * cols)
        pre = jnp.dot(left, jnp.concatenate(right, axis=0), preferred_element_type=F32)
        pre = pre + bias_ref[0:1, cut].astype(F32)
        pre_ref[:, cut] = pre
        sig = jax.nn.sigmoid(pre)
        grad = (cot_ref[:, cut].astype(F32) * sig * (1.0 + pre * (1.0 - sig))).astype(BF)
        cot_ref[:, cut] = grad
        into = into + lax.dot_general(
            grad, both[:, cut], (((1,), (1,)), ((), ())), preferred_element_type=F32
        )
    mine = pl.ds(pl.multiple_of(me * cols, cols), cols)
    own = pre_ref[:, mine]
    out_ref[...] = (own * jax.nn.sigmoid(own)).astype(BF)
    neigh_grad = into[:, depth:].astype(BF)
    back_ref[...] = into[:, :depth] + jnp.dot(turned_ref[:rows, :], neigh_grad, preferred_element_type=F32)
    sums = jnp.sum(cot_ref[:, mine].astype(F32), axis=0, keepdims=True)
    high = sums.astype(BF).astype(F32)
    here = side_ref[0] * half

    def ghosts(start, peers):
        line = lax.broadcasted_iota(jnp.int32, (peers * width, cols), 0) % width
        cut = pl.ds(pl.multiple_of(rows + start * width, 16), peers * width)
        away = jnp.dot(turned_ref[cut, :], neigh_grad, preferred_element_type=F32)
        away = jnp.where(line == slots + hub_here, high, away)
        away = jnp.where(line == slots + hub_here + 1, sums - high, away)
        return away.astype(BF)

    pair = jnp.concatenate([x_ref[...], n_refs[0][...]], axis=1).T
    if count > 1:
        for k, ref in enumerate(send_refs):
            peer = seat_ref[0] ^ k
            ghost_ref[k] = ghosts(here + peer, 1)
            mirror_ref[k] = ghosts(half - here + peer, 1)
            block = cot_ref[:, pl.ds(pl.multiple_of(peer * cols, cols), cols)]
            ref[...] = jnp.dot(pair, block, preferred_element_type=F32).astype(BF)
        return
    send_ref = send_refs[0]
    ghost_ref[...] = ghosts(here, half).reshape(half, width, cols)
    mirror_ref[...] = ghosts(half - here, half).reshape(half, width, cols)
    weights = jnp.dot(pair, cot_ref[...], preferred_element_type=F32).astype(BF)
    step = min(share, depth)
    for j in range(blocks):
        for kind in range(2):
            block = weights[kind * depth : (kind + 1) * depth, j * cols : (j + 1) * cols]
            for part in range(depth // step):
                at = (j * 2 + kind) * depth + part * step
                low = at % share
                send_ref[at // share, low : low + step, :] = block[part * step : (part + 1) * step]


def seated(refs, seat):
    if len(refs) == 1:
        return [(j, refs[0].at[j]) for j in range(refs[0].shape[0])]
    return [(seat ^ k, ref) for k, ref in enumerate(refs)]


def store_kernel(held_ref, out_ref):
    out_ref[...] = held_ref[...]


def sum_kernel(stored_ref, mirror_ref, *refs):
    got_refs, sum_ref = refs[:-1], refs[-1]
    total = jnp.zeros(sum_ref.shape, F32)
    for got_ref in got_refs if len(got_refs) > 1 else [got_refs[0].at[j] for j in range(got_refs[0].shape[0])]:
        total = total + got_ref[...].astype(F32)
    sum_ref[...] = total.astype(BF)


def deal_kernel(ghost_ref, mirror_ref, *out_refs):
    width = ghost_ref.shape[1]
    for k in range(ghost_ref.shape[0]):
        out_ref = out_refs[k] if len(out_refs) > 1 else out_refs[0].at[k]
        out_ref[:width, :] = ghost_ref[k]
        out_ref[width:, :] = mirror_ref[k]


def total_kernel(own_ref, other_ref, part_ref):
    total = (own_ref[...].astype(F32) + other_ref[...].astype(F32)).astype(BF)
    part_ref[...] = jnp.broadcast_to(total, part_ref.shape)


def near_rows(slots, hub_here, start, mark_ref, got_ref):
    half, width, cols = got_ref.shape
    cut = pl.ds(pl.multiple_of(start * width, 128), half * width)
    added = jnp.dot(mark_ref[:, cut], got_ref[...].reshape(half * width, cols), preferred_element_type=F32)
    first = slots + hub_here
    bias = jnp.zeros((2, cols), F32)
    for j in range(half):
        bias = bias + got_ref[j, first : first + 2, :].astype(F32)
    return added, jnp.sum(bias, axis=0, keepdims=True)


def grad_kernel(scale, slots, hub_here, side_ref, seat_ref, back_ref, mark_ref, *refs):
    got_refs, (grad_ref, bias_ref, near_ref, far_ref) = refs[:-4], refs[-4:]
    half, width = near_ref.shape[:2]
    for j, got_ref in seated(got_refs, seat_ref[0]):
        near_ref[j] = got_ref[:width, :]
        far_ref[j] = got_ref[width:, :]
    here = side_ref[0] * half
    near, near_bias = near_rows(slots, hub_here, here, mark_ref, near_ref)
    far, far_bias = near_rows(slots, hub_here, half - here, mark_ref, far_ref)
    grad_ref[...] = (back_ref[...] + near + far).astype(BF)
    bias_ref[...] = (near_bias + far_bias) * scale


def spread_kernel(scale, seat_ref, *refs):
    got_refs, (self_ref, neigh_ref, wide_ref, sems) = refs[:-4], refs[-4:]
    depth, full = self_ref.shape
    cols = got_refs[0].shape[-1]
    blocks = full // cols
    if len(got_refs) > 1:
        parts = [(j, ref[...]) for j, ref in seated(got_refs, seat_ref[0])]
    else:
        whole = got_refs[0][...].reshape(2 * blocks * depth, cols)
        parts = [(j, whole[2 * j * depth : 2 * (j + 1) * depth]) for j in range(blocks)]
    copies = []
    for at, (j, part) in enumerate(parts):
        wide_ref[at] = part.astype(F32) * scale
        cut = pl.ds(pl.multiple_of(j * cols, cols), cols)
        for kind, out_ref in enumerate((self_ref, neigh_ref)):
            copy = pltpu.make_async_copy(
                wide_ref.at[at, kind * depth : (kind + 1) * depth, :], out_ref.at[:, cut], sems.at[2 * at + kind]
            )
            copy.start()
            copies.append(copy)
    for copy in copies:
        copy.wait()


VMEM = pl.BlockSpec(memory_space=pltpu.VMEM)
SMEM = pl.BlockSpec(memory_space=pltpu.SMEM)
ANY = pl.BlockSpec(memory_space=pl.ANY)
HBM = pl.BlockSpec(memory_space=pltpu.HBM)
PARAMS = pltpu.CompilerParams(vmem_limit_bytes=40 * 1024 * 1024)


def shape(dims, kind):
    return jax.ShapeDtypeStruct(dims, kind)


def kept(dims, kind):
    return pltpu.VMEM(dims, kind)


def partner(block, axis, k):
    return lax.ppermute(block, axis, [(i, i ^ k) for i in range(lax.axis_size(axis))])


def exchange(blocks, groups=None):
    return lax.all_to_all(blocks, "dom", split_axis=0, concat_axis=0, axis_index_groups=groups, tiled=True)


def swap(blocks):
    return [blocks[0]] + [partner(block, "dom", k) for k, block in enumerate(blocks) if k]


def on_device(
    features,
    w_self,
    w_neigh,
    bias,
    cotangent,
    tile_vals,
    tile_pos,
    tile_count,
    send_rows,
    recv_dest,
    ghost_weight,
    recv_count,
    hub_rows,
    hub_weight,
):
    rows, cols = features.shape
    depth, full = w_self.shape
    blocks = full // cols
    peers, slots = send_rows.shape[1:]
    hub_here = hub_rows.shape[-1]
    width = -(-(slots + hub_here + 2) // 16) * 16
    lanes = peers * width
    half = peers // 2
    share = 2 * blocks * depth // half
    direct = half == blocks
    count = half if direct else 1
    halves = [list(range(half)), list(range(half, peers))]
    scale = 1.0 / math.sqrt(peers * rows)
    feats = lax.axis_size("feat")
    me = lax.axis_index("feat").astype(jnp.int32).reshape(1)
    side = (lax.axis_index("dom") >= half).astype(jnp.int32).reshape(1)
    seat = lax.rem(lax.axis_index("dom"), half).astype(jnp.int32).reshape(1)
    pack_rows = 2 * blocks * depth + 2 * rows + 16

    def pinned(*arrays):
        return [pltpu.with_memory_space_constraint(a, pltpu.HBM) for a in arrays]

    first = pinned(features, cotangent, w_self, w_neigh, bias.reshape(1, cols), send_rows, hub_rows)
    edges = pinned(tile_pos, recv_count, tile_vals, recv_dest, ghost_weight, hub_weight.T)
    moved = (send_rows, hub_rows, *edges)
    outgoing, pack, *moved = pl.pallas_call(
        functools.partial(send_kernel, width),
        out_shape=(
            kept((peers, width, cols), BF),
            shape((pack_rows, cols), BF),
            *(shape(a.shape, a.dtype) for a in moved),
        ),
        in_specs=[HBM] * (len(first) + len(edges)),
        out_specs=(VMEM,) * (2 + len(moved)),
        scratch_shapes=[
            pltpu.VMEM((1, cols), BF),
            pltpu.VMEM((lanes, slots), BF),
            pltpu.SemaphoreType.DMA((11 + 2 * blocks,)),
        ],
        compiler_params=PARAMS,
    )(*first, *edges)

    far = partner(pack, "feat", 2)
    near = partner(pack, "feat", 1)
    incoming = exchange(outgoing)
    mix, turned, mark = pl.pallas_call(
        functools.partial(mix_kernel, width),
        out_shape=(
            shape((rows, rows + lanes), BF),
            shape((rows + lanes, rows), BF),
            shape((rows, lanes), BF),
        ),
        in_specs=[VMEM] * (1 + len(moved)),
        out_specs=(VMEM,) * 3,
        compiler_params=PARAMS,
        cost_estimate=pl.CostEstimate(flops=10**8, bytes_accessed=3 * 10**6, transcendentals=0),
    )(tile_count.reshape(1, 1), *moved)
    neigh, far = pl.pallas_call(
        neigh_kernel,
        out_shape=(shape((rows, cols), BF), shape((pack_rows, cols), BF)),
        in_specs=[VMEM, VMEM, ANY, VMEM],
        out_specs=(VMEM, ANY),
        input_output_aliases={2: 1},
        compiler_params=PARAMS,
    )(features, mix, far, incoming)
    last = partner(far, "feat", 1)
    far_neigh = partner(neigh, "feat", 2)
    every = [neigh, partner(neigh, "feat", 1), far_neigh, partner(far_neigh, "feat", 1)]

    output, back, ghosts, mirror, *returned = pl.pallas_call(
        functools.partial(dense_kernel, slots, hub_here, feats, width, count),
        out_shape=(
            kept((rows, cols), BF),
            shape((rows, cols), F32),
            shape((half, width, cols), BF),
            shape((half, width, cols), BF),
            *([shape((share, cols), BF)] * half if direct else [shape((half, share, cols), BF)]),
        ),
        in_specs=[SMEM] * 3 + [VMEM] * (4 + 2 * feats),
        out_specs=(VMEM,) * (4 + count),
        scratch_shapes=[
            pltpu.VMEM((rows, full), F32),
            pltpu.VMEM((rows, full), BF),
            pltpu.VMEM((16, full), BF),
        ],
        compiler_params=PARAMS,
    )(me, side, seat, features, w_self, w_neigh, turned, pack, near, far, last, *every)

    arrived = swap(returned)[::-1] if direct else [exchange(returned[0], halves)]
    mirror = partner(mirror, "dom", half)
    output = pl.pallas_call(
        store_kernel,
        out_shape=shape((rows, cols), BF),
        in_specs=[VMEM],
        out_specs=VMEM,
        compiler_params=PARAMS,
        cost_estimate=pl.CostEstimate(flops=10**8, bytes_accessed=10**6, transcendentals=0),
    )(output)
    half_sum = pl.pallas_call(
        sum_kernel,
        out_shape=shape((share, cols), BF),
        in_specs=[HBM, VMEM] + [VMEM] * count,
        out_specs=VMEM,
        compiler_params=PARAMS,
    )(*pinned(output), mirror, *arrived)
    other_sum = partner(half_sum, "dom", half)
    dealt = pl.pallas_call(
        deal_kernel,
        out_shape=[shape((2 * width, cols), BF)] * half if direct else [shape((half, 2 * width, cols), BF)],
        in_specs=[VMEM] * 2,
        out_specs=[VMEM] * count,
        compiler_params=PARAMS,
    )(ghosts, mirror)
    dealt = swap(dealt) if direct else [exchange(dealt[0], halves)]
    part = pl.pallas_call(
        total_kernel,
        out_shape=shape((share, cols) if direct else (half, share, cols), BF),
        in_specs=[VMEM, VMEM],
        out_specs=VMEM,
        compiler_params=PARAMS,
    )(half_sum, other_sum)
    parts = swap([part] * half) if direct else [exchange(part, halves)]
    grad_features, grad_bias = pl.pallas_call(
        functools.partial(grad_kernel, scale, slots, hub_here),
        out_shape=(shape((rows, cols), BF), shape((1, cols), F32)),
        in_specs=[SMEM] * 2 + [VMEM] * (2 + count),
        out_specs=(VMEM,) * 2,
        scratch_shapes=[pltpu.VMEM((half, width, cols), BF)] * 2,
        compiler_params=PARAMS,
        cost_estimate=pl.CostEstimate(flops=2 * 10**9, bytes_accessed=10**6, transcendentals=0),
    )(side, seat, back, mark, *dealt)
    grad_self, grad_neigh = pl.pallas_call(
        functools.partial(spread_kernel, scale),
        out_shape=(shape((depth, full), F32), shape((depth, full), F32)),
        in_specs=[SMEM] + [VMEM] * count,
        out_specs=(HBM,) * 2,
        scratch_shapes=[pltpu.VMEM((blocks, 2 * depth, cols), F32), pltpu.SemaphoreType.DMA((2 * blocks,))],
        compiler_params=PARAMS,
    )(seat, *parts)
    return output, grad_features, grad_self, grad_neigh, grad_bias.reshape(cols)


def solution(mesh):
    placed = (
        P("dom", "feat"),
        P("feat", None),
        P("feat", None),
        P("feat"),
        P("dom", "feat"),
        P("dom", None, None, None),
        P("dom", None),
        P("dom"),
        P("dom", None, None),
        P("dom", None, None),
        P("dom", None, None),
        P("dom", None),
        P("dom", None),
        P("dom", None),
    )
    return jax.shard_map(
        on_device,
        mesh=mesh,
        in_specs=placed,
        out_specs=(P("dom", "feat"), P("dom", "feat"), P("feat", None), P("feat", None), P("feat")),
        check_vma=False,
    )
```

```python
import functools
import math

import jax
import jax.numpy as jnp
from jax import lax
from jax.experimental import pallas as pl
from jax.experimental.pallas import tpu as pltpu
from jax.sharding import PartitionSpec as P

BF = jnp.bfloat16
F32 = jnp.float32


def spread_rows(table, width):
    peers, slots = table.shape
    lanes = peers * width
    lane = lax.broadcasted_iota(jnp.int32, (slots, lanes), 1)
    slot = lax.broadcasted_iota(jnp.int32, (slots, lanes), 0)
    place = jnp.where(lane % width == slot, 1.0, 0.0).astype(BF)
    wide = jnp.dot(table.astype(BF), place, preferred_element_type=F32)
    peer = lax.broadcasted_iota(jnp.int32, (peers, lanes), 0)
    at = lax.broadcasted_iota(jnp.int32, (peers, lanes), 1)
    return jnp.sum(jnp.where(at // width == peer, wide, 0.0), axis=0, keepdims=True)


def source_matrix(send, hubs, rows, width):
    peers, slots = send.shape
    hub_here = hubs.shape[1]
    lanes = peers * width
    lane = lax.broadcasted_iota(jnp.int32, (1, lanes), 1) % width
    index = spread_rows(send.astype(F32), width)
    for k in range(hub_here):
        index = jnp.where(lane == slots + k, hubs[0:1, k : k + 1].astype(F32), index)
    index = jnp.where(lane < slots + hub_here, index, -1.0)
    row = lax.broadcasted_iota(jnp.int32, (rows, lanes), 0).astype(F32)
    return jnp.where(row == index, 1.0, 0.0).astype(BF)


def source_places(peers, slots, width):
    lanes = peers * width
    slot = lax.broadcasted_iota(jnp.int32, (lanes, slots), 0) % width
    return jnp.where(slot == lax.broadcasted_iota(jnp.int32, (lanes, slots), 1), 1.0, 0.0).astype(BF)


def source_rows(place, send, hubs, rows, width):
    peers, slots = send.shape
    hub_here = hubs.shape[1]
    lanes = peers * width
    wide = lax.dot_general(
        place, send.astype(F32).astype(BF), (((1,), (1,)), ((), ())), preferred_element_type=F32
    )
    line = lax.broadcasted_iota(jnp.int32, (lanes, peers), 0)
    for k in range(hub_here):
        wide = jnp.where(line % width == slots + k, hubs[0:1, k : k + 1].astype(F32), wide)
    wide = jnp.where(line % width < slots + hub_here, wide, -1.0)
    wide = jnp.where(line // width == lax.broadcasted_iota(jnp.int32, (lanes, peers), 1), wide, 0.0)
    index = jnp.dot(wide.astype(BF), jnp.ones((peers, rows), BF), preferred_element_type=F32)
    row = lax.broadcasted_iota(jnp.int32, (lanes, rows), 1).astype(F32)
    return jnp.where(row == index, 1.0, 0.0).astype(BF)


def send_kernel(
    width, x_ref, cot_ref, ws_ref, wn_ref, bias_ref, send_ref, hub_ref, pos_ref, live_ref, tile_ref, dest_ref, gw_ref, hw_ref,
    out_ref, pack_ref, send_v, hub_v, pos_v, live_v, tile_v, dest_v, gw_v, hw_v, bias_v, place_ref, sems,
):
    rows, cols = x_ref.shape
    depth, full = ws_ref.shape
    blocks = full // cols
    base = 2 * blocks * depth
    moves = [
        (send_ref, send_v),
        (hub_ref, hub_v),
        (x_ref, pack_ref.at[base : base + rows, :]),
        (bias_ref, bias_v),
        (cot_ref, pack_ref.at[base + rows : base + 2 * rows, :]),
    ]
    for kind, w_ref in enumerate((ws_ref, wn_ref)):
        for j in range(blocks):
            at = (kind * blocks + j) * depth
            moves.append((w_ref.at[:, j * cols : (j + 1) * cols], pack_ref.at[at : at + depth, :]))
    moves += [
        (pos_ref, pos_v), (live_ref, live_v), (tile_ref, tile_v), (dest_ref, dest_v),
        (gw_ref, gw_v), (hw_ref, hw_v),
    ]
    copies = [pltpu.make_async_copy(src, dst, sems.at[i]) for i, (src, dst) in enumerate(moves)]
    for copy in copies:
        copy.start()
    peers, slots = send_v.shape[1:]
    place_ref[...] = source_places(peers, slots, width)
    for copy in copies[:2]:
        copy.wait()
    mark = source_rows(place_ref[...], send_v[0], hub_v[...], rows, width)
    copies[2].wait()
    taken = jnp.dot(mark, pack_ref[base : base + rows, :], preferred_element_type=F32).astype(BF)
    out_ref[...] = taken.reshape(out_ref.shape)
    for copy in copies[3:]:
        copy.wait()
    pack_ref[base + 2 * rows :, :] = jnp.broadcast_to(bias_v[...], (16, cols))


def mix_kernel(width, count_ref, send_v, hub_v, pos_v, live_v, tile_v, dest_v, gw_v, hw_v, mix_ref, turned_ref, mark_ref):
    rows = mix_ref.shape[0]
    tiles, tile = tile_v.shape[1:3]
    peers, slots = dest_v.shape[1:]
    side = rows // tile
    lanes = peers * width
    hubs = hw_v.shape[0]
    hub_here = hubs // peers
    for r in range(side):
        for c in range(side):
            total = jnp.zeros((tile, tile), BF)
            for t in range(tiles):
                used = jnp.logical_and(pos_v[0:1, t : t + 1] == r * side + c, t < count_ref[...])
                total = jnp.where(used, tile_v[0, t], total)
            mix_ref[r * tile : (r + 1) * tile, c * tile : (c + 1) * tile] = total
    dest = spread_rows(dest_v[0].astype(F32), width)
    coef = spread_rows(gw_v[0], width)
    peer = lax.broadcasted_iota(jnp.int32, (peers, lanes), 0)
    at = lax.broadcasted_iota(jnp.int32, (peers, lanes), 1)
    owner = jnp.where(at // width == peer, 1.0, 0.0).astype(BF)
    limit = jnp.dot(live_v[...].astype(F32).astype(BF), owner, preferred_element_type=F32)
    lane = lax.broadcasted_iota(jnp.int32, (1, lanes), 1) % width
    coef = jnp.where(jnp.logical_and(lane.astype(F32) < limit, lane < slots), coef, 0.0)
    row = lax.broadcasted_iota(jnp.int32, (rows, lanes), 0).astype(F32)
    ghost = jnp.where(row == dest, coef, 0.0)
    hub = lax.broadcasted_iota(jnp.int32, (hubs, lanes), 0)
    at = lax.broadcasted_iota(jnp.int32, (hubs, lanes), 1)
    place = jnp.where(
        jnp.logical_and(at // width == hub // hub_here, at % width == slots + hub % hub_here), 1.0, 0.0
    ).astype(BF)
    hub_mix = lax.dot_general(hw_v[...], place, (((0,), (0,)), ((), ())), preferred_element_type=F32)
    mix_ref[:, rows:] = (ghost + hub_mix).astype(BF)
    turned_ref[...] = mix_ref[...].T
    mark_ref[...] = source_matrix(send_v[0], hub_v[...], rows, width)


def neigh_kernel(x_ref, mix_ref, far_ref, got_ref, neigh_ref, passed_ref):
    rows, cols = x_ref.shape
    lanes = mix_ref.shape[1] - rows
    total = jnp.dot(mix_ref[:, :rows], x_ref[...], preferred_element_type=F32)
    total = total + jnp.dot(mix_ref[:, rows:], got_ref[...].reshape(lanes, cols), preferred_element_type=F32)
    neigh_ref[...] = total.astype(BF)


def dense_kernel(slots, hub_here, feats, width, count, me_ref, side_ref, seat_ref, x_ref, ws_ref, wn_ref, turned_ref, *refs):
    pack_refs, n_refs = refs[:feats], refs[feats : 2 * feats]
    out_ref, back_ref, ghost_ref, mirror_ref = refs[2 * feats : 2 * feats + 4]
    send_refs = refs[2 * feats + 4 : 2 * feats + 4 + count]
    pre_ref, cot_ref, bias_ref = refs[2 * feats + 4 + count :]
    rows, cols = x_ref.shape
    depth, full = ws_ref.shape
    blocks = full // cols
    half = mirror_ref.shape[0]
    share = send_refs[0].shape[-2]
    me = me_ref[0]
    base = 2 * blocks * depth
    left = []
    for d, pack in enumerate(pack_refs):
        owner = me ^ d
        cut = pl.ds(pl.multiple_of(owner * cols, cols), cols)
        cot_ref[:, cut] = pack[base + rows : base + 2 * rows, :]
        bias_ref[:, cut] = pack[base + 2 * rows : base + 2 * rows + 16, :]
        left += [pack[base : base + rows, :], n_refs[d][...]]
    left = jnp.concatenate(left, axis=1)
    both = jnp.concatenate([ws_ref[...], wn_ref[...]], axis=0)
    into = jnp.zeros((rows, 2 * depth), F32)
    span = 2
    for j in range(0, blocks, span):
        right = [
            jnp.concatenate([pack[(kind * blocks + i) * depth : (kind * blocks + i + 1) * depth, :] for i in range(j, j + span)], axis=1)
            for pack in pack_refs
            for kind in range(2)
        ]
        cut = slice(j * cols, (j + span) * cols)
        pre = jnp.dot(left, jnp.concatenate(right, axis=0), preferred_element_type=F32)
        pre = pre + bias_ref[0:1, cut].astype(F32)
        pre_ref[:, cut] = pre
        sig = jax.nn.sigmoid(pre)
        grad = (cot_ref[:, cut].astype(F32) * sig * (1.0 + pre * (1.0 - sig))).astype(BF)
        cot_ref[:, cut] = grad
        into = into + lax.dot_general(
            grad, both[:, cut], (((1,), (1,)), ((), ())), preferred_element_type=F32
        )
    mine = pl.ds(pl.multiple_of(me * cols, cols), cols)
    own = pre_ref[:, mine]
    out_ref[...] = (own * jax.nn.sigmoid(own)).astype(BF)
    neigh_grad = into[:, depth:].astype(BF)
    back_ref[...] = into[:, :depth] + jnp.dot(turned_ref[:rows, :], neigh_grad, preferred_element_type=F32)
    sums = jnp.sum(cot_ref[:, mine].astype(F32), axis=0, keepdims=True)
    high = sums.astype(BF).astype(F32)
    here = side_ref[0] * half

    def ghosts(start, peers):
        line = lax.broadcasted_iota(jnp.int32, (peers * width, cols), 0) % width
        cut = pl.ds(pl.multiple_of(rows + start * width, 16), peers * width)
        away = jnp.dot(turned_ref[cut, :], neigh_grad, preferred_element_type=F32)
        away = jnp.where(line == slots + hub_here, high, away)
        away = jnp.where(line == slots + hub_here + 1, sums - high, away)
        return away.astype(BF)

    pair = jnp.concatenate([x_ref[...], n_refs[0][...]], axis=1).T
    if count > 1:
        for k, ref in enumerate(send_refs):
            peer = seat_ref[0] ^ k
            ghost_ref[k] = ghosts(here + peer, 1)
            mirror_ref[k] = ghosts(half - here + peer, 1)
            block = cot_ref[:, pl.ds(pl.multiple_of(peer * cols, cols), cols)]
            ref[...] = jnp.dot(pair, block, preferred_element_type=F32).astype(BF)
        return
    send_ref = send_refs[0]
    ghost_ref[...] = ghosts(here, half).reshape(half, width, cols)
    mirror_ref[...] = ghosts(half - here, half).reshape(half, width, cols)
    weights = jnp.dot(pair, cot_ref[...], preferred_element_type=F32).astype(BF)
    step = min(share, depth)
    for j in range(blocks):
        for kind in range(2):
            block = weights[kind * depth : (kind + 1) * depth, j * cols : (j + 1) * cols]
            for part in range(depth // step):
                at = (j * 2 + kind) * depth + part * step
                low = at % share
                send_ref[at // share, low : low + step, :] = block[part * step : (part + 1) * step]


def seated(refs, seat):
    if len(refs) == 1:
        return [(j, refs[0].at[j]) for j in range(refs[0].shape[0])]
    return [(seat ^ k, ref) for k, ref in enumerate(refs)]


def store_kernel(held_ref, out_ref):
    out_ref[...] = held_ref[...]


def sum_kernel(stored_ref, *refs):
    got_refs, sum_ref = refs[:-1], refs[-1]
    total = jnp.zeros(sum_ref.shape, F32)
    for got_ref in got_refs if len(got_refs) > 1 else [got_refs[0].at[j] for j in range(got_refs[0].shape[0])]:
        total = total + got_ref[...].astype(F32)
    sum_ref[...] = total.astype(BF)


def deal_kernel(ghost_ref, mirror_ref, *out_refs):
    width = ghost_ref.shape[1]
    for k in range(ghost_ref.shape[0]):
        out_ref = out_refs[k] if len(out_refs) > 1 else out_refs[0].at[k]
        out_ref[:width, :] = ghost_ref[k]
        out_ref[width:, :] = mirror_ref[k]


def total_kernel(own_ref, other_ref, part_ref):
    total = (own_ref[...].astype(F32) + other_ref[...].astype(F32)).astype(BF)
    part_ref[...] = jnp.broadcast_to(total, part_ref.shape)


def near_rows(slots, hub_here, start, mark_ref, got_ref):
    half, width, cols = got_ref.shape
    cut = pl.ds(pl.multiple_of(start * width, 128), half * width)
    added = jnp.dot(mark_ref[:, cut], got_ref[...].reshape(half * width, cols), preferred_element_type=F32)
    first = slots + hub_here
    bias = jnp.zeros((2, cols), F32)
    for j in range(half):
        bias = bias + got_ref[j, first : first + 2, :].astype(F32)
    return added, jnp.sum(bias, axis=0, keepdims=True)


def grad_kernel(scale, slots, hub_here, side_ref, seat_ref, back_ref, mark_ref, *refs):
    got_refs, (grad_ref, bias_ref, near_ref, far_ref) = refs[:-4], refs[-4:]
    half, width = near_ref.shape[:2]
    for j, got_ref in seated(got_refs, seat_ref[0]):
        near_ref[j] = got_ref[:width, :]
        far_ref[j] = got_ref[width:, :]
    here = side_ref[0] * half
    near, near_bias = near_rows(slots, hub_here, here, mark_ref, near_ref)
    far, far_bias = near_rows(slots, hub_here, half - here, mark_ref, far_ref)
    grad_ref[...] = (back_ref[...] + near + far).astype(BF)
    bias_ref[...] = (near_bias + far_bias) * scale


def write_blocks(scale, parts, self_ref, neigh_ref, wide_ref, sems):
    depth, full = self_ref.shape
    cols = wide_ref.shape[-1]
    copies = []
    for at, (j, part) in enumerate(parts):
        wide_ref[at] = part.astype(F32) * scale
        cut = pl.ds(pl.multiple_of(j * cols, cols), cols)
        for kind, out_ref in enumerate((self_ref, neigh_ref)):
            copy = pltpu.make_async_copy(
                wide_ref.at[at, kind * depth : (kind + 1) * depth, :], out_ref.at[:, cut], sems.at[2 * at + kind]
            )
            copy.start()
            copies.append(copy)
    for copy in copies:
        copy.wait()


def spread_kernel(scale, seat_ref, *refs):
    got_refs, (self_ref, neigh_ref, wide_ref, sems) = refs[:-4], refs[-4:]
    depth, full = self_ref.shape
    cols = wide_ref.shape[-1]
    if len(got_refs) > 1:
        parts = [(j, ref[...]) for j, ref in seated(got_refs, seat_ref[0])]
    else:
        whole = got_refs[0][...].reshape(2 * full // cols * depth, cols)
        parts = [(j, whole[2 * j * depth : 2 * (j + 1) * depth]) for j in range(full // cols)]
    write_blocks(scale, parts, self_ref, neigh_ref, wide_ref, sems)


def finish_kernel(scale, k, seat_ref, got_ref, begun_self_ref, begun_neigh_ref, self_ref, neigh_ref, wide_ref, sems):
    write_blocks(scale, [(seat_ref[0] ^ k, got_ref[...])], self_ref, neigh_ref, wide_ref, sems)


VMEM = pl.BlockSpec(memory_space=pltpu.VMEM)
SMEM = pl.BlockSpec(memory_space=pltpu.SMEM)
ANY = pl.BlockSpec(memory_space=pl.ANY)
HBM = pl.BlockSpec(memory_space=pltpu.HBM)
PARAMS = pltpu.CompilerParams(vmem_limit_bytes=40 * 1024 * 1024)


def shape(dims, kind):
    return jax.ShapeDtypeStruct(dims, kind)


def kept(dims, kind):
    return pltpu.VMEM(dims, kind)


def partner(block, axis, k):
    return lax.ppermute(block, axis, [(i, i ^ k) for i in range(lax.axis_size(axis))])


def exchange(blocks, groups=None):
    return lax.all_to_all(blocks, "dom", split_axis=0, concat_axis=0, axis_index_groups=groups, tiled=True)


def swap(blocks):
    return [blocks[0]] + [partner(block, "dom", k) for k, block in enumerate(blocks) if k]


def on_device(
    features,
    w_self,
    w_neigh,
    bias,
    cotangent,
    tile_vals,
    tile_pos,
    tile_count,
    send_rows,
    recv_dest,
    ghost_weight,
    recv_count,
    hub_rows,
    hub_weight,
):
    rows, cols = features.shape
    depth, full = w_self.shape
    blocks = full // cols
    peers, slots = send_rows.shape[1:]
    hub_here = hub_rows.shape[-1]
    width = -(-(slots + hub_here + 2) // 16) * 16
    lanes = peers * width
    half = peers // 2
    share = 2 * blocks * depth // half
    direct = half == blocks
    count = half if direct else 1
    halves = [list(range(half)), list(range(half, peers))]
    scale = 1.0 / math.sqrt(peers * rows)
    feats = lax.axis_size("feat")
    me = lax.axis_index("feat").astype(jnp.int32).reshape(1)
    side = (lax.axis_index("dom") >= half).astype(jnp.int32).reshape(1)
    seat = lax.rem(lax.axis_index("dom"), half).astype(jnp.int32).reshape(1)
    pack_rows = 2 * blocks * depth + 2 * rows + 16

    def pinned(*arrays):
        return [pltpu.with_memory_space_constraint(a, pltpu.HBM) for a in arrays]

    first = pinned(features, cotangent, w_self, w_neigh, bias.reshape(1, cols), send_rows, hub_rows)
    edges = pinned(tile_pos, recv_count, tile_vals, recv_dest, ghost_weight, hub_weight.T)
    moved = (send_rows, hub_rows, *edges)
    outgoing, pack, *moved = pl.pallas_call(
        functools.partial(send_kernel, width),
        out_shape=(
            kept((peers, width, cols), BF),
            shape((pack_rows, cols), BF),
            *(shape(a.shape, a.dtype) for a in moved),
        ),
        in_specs=[HBM] * (len(first) + len(edges)),
        out_specs=(VMEM,) * (2 + len(moved)),
        scratch_shapes=[
            pltpu.VMEM((1, cols), BF),
            pltpu.VMEM((lanes, slots), BF),
            pltpu.SemaphoreType.DMA((11 + 2 * blocks,)),
        ],
        compiler_params=PARAMS,
    )(*first, *edges)

    far = partner(pack, "feat", 2)
    near = partner(pack, "feat", 1)
    incoming = exchange(outgoing)
    mix, turned, mark = pl.pallas_call(
        functools.partial(mix_kernel, width),
        out_shape=(
            shape((rows, rows + lanes), BF),
            shape((rows + lanes, rows), BF),
            shape((rows, lanes), BF),
        ),
        in_specs=[VMEM] * (1 + len(moved)),
        out_specs=(VMEM,) * 3,
        compiler_params=PARAMS,
        cost_estimate=pl.CostEstimate(flops=10**8, bytes_accessed=3 * 10**6, transcendentals=0),
    )(tile_count.reshape(1, 1), *moved)
    neigh, far = pl.pallas_call(
        neigh_kernel,
        out_shape=(shape((rows, cols), BF), shape((pack_rows, cols), BF)),
        in_specs=[VMEM, VMEM, ANY, VMEM],
        out_specs=(VMEM, ANY),
        input_output_aliases={2: 1},
        compiler_params=PARAMS,
    )(features, mix, far, incoming)
    last = partner(far, "feat", 1)
    far_neigh = partner(neigh, "feat", 2)
    every = [neigh, partner(neigh, "feat", 1), far_neigh, partner(far_neigh, "feat", 1)]

    output, back, ghosts, mirror, *returned = pl.pallas_call(
        functools.partial(dense_kernel, slots, hub_here, feats, width, count),
        out_shape=(
            kept((rows, cols), BF),
            shape((rows, cols), F32),
            shape((half, width, cols), BF),
            shape((half, width, cols), BF),
            *([shape((share, cols), BF)] * half if direct else [shape((half, share, cols), BF)]),
        ),
        in_specs=[SMEM] * 3 + [VMEM] * (4 + 2 * feats),
        out_specs=(VMEM,) * (4 + count),
        scratch_shapes=[
            pltpu.VMEM((rows, full), F32),
            pltpu.VMEM((rows, full), BF),
            pltpu.VMEM((16, full), BF),
        ],
        compiler_params=PARAMS,
    )(me, side, seat, features, w_self, w_neigh, turned, pack, near, far, last, *every)

    arrived = swap(returned)[::-1] if direct else [exchange(returned[0], halves)]
    mirror = partner(mirror, "dom", half)
    output = pl.pallas_call(
        store_kernel,
        out_shape=shape((rows, cols), BF),
        in_specs=[VMEM],
        out_specs=VMEM,
        compiler_params=PARAMS,
        cost_estimate=pl.CostEstimate(flops=10**8, bytes_accessed=10**6, transcendentals=0),
    )(output)
    half_sum = pl.pallas_call(
        sum_kernel,
        out_shape=shape((share, cols), BF),
        in_specs=[HBM] + [VMEM] * count,
        out_specs=VMEM,
        compiler_params=PARAMS,
    )(*pinned(output), *arrived)
    other_sum = partner(half_sum, "dom", half)
    dealt = pl.pallas_call(
        deal_kernel,
        out_shape=[shape((2 * width, cols), BF)] * half if direct else [shape((half, 2 * width, cols), BF)],
        in_specs=[VMEM] * 2,
        out_specs=[VMEM] * count,
        compiler_params=PARAMS,
    )(ghosts, mirror)
    dealt = swap(dealt) if direct else [exchange(dealt[0], halves)]
    part = pl.pallas_call(
        total_kernel,
        out_shape=shape((share, cols) if direct else (half, share, cols), BF),
        in_specs=[VMEM, VMEM],
        out_specs=VMEM,
        compiler_params=PARAMS,
    )(half_sum, other_sum)
    parts = swap([part] * half) if direct else [exchange(part, halves)]
    grad_features, grad_bias = pl.pallas_call(
        functools.partial(grad_kernel, scale, slots, hub_here),
        out_shape=(shape((rows, cols), BF), shape((1, cols), F32)),
        in_specs=[SMEM] * 2 + [VMEM] * (2 + count),
        out_specs=(VMEM,) * 2,
        scratch_shapes=[pltpu.VMEM((half, width, cols), BF)] * 2,
        compiler_params=PARAMS,
        cost_estimate=pl.CostEstimate(flops=2 * 10**9, bytes_accessed=10**6, transcendentals=0),
    )(side, seat, back, mark, *dealt)
    early = half - 1 if direct else 1
    grad_self, grad_neigh = pl.pallas_call(
        functools.partial(spread_kernel, scale),
        out_shape=(shape((depth, full), F32), shape((depth, full), F32)),
        in_specs=[SMEM] + [VMEM] * early,
        out_specs=(HBM,) * 2,
        scratch_shapes=[pltpu.VMEM((blocks, 2 * depth, cols), F32), pltpu.SemaphoreType.DMA((2 * blocks,))],
        compiler_params=PARAMS,
    )(seat, *parts[:early])
    if direct:
        grad_self, grad_neigh = pl.pallas_call(
            functools.partial(finish_kernel, scale, early),
            out_shape=(shape((depth, full), F32), shape((depth, full), F32)),
            in_specs=[SMEM, VMEM, HBM, HBM],
            out_specs=(HBM,) * 2,
            scratch_shapes=[pltpu.VMEM((1, 2 * depth, cols), F32), pltpu.SemaphoreType.DMA((2,))],
            input_output_aliases={2: 0, 3: 1},
            compiler_params=PARAMS,
        )(seat, parts[early], *pinned(grad_self, grad_neigh))
    return output, grad_features, grad_self, grad_neigh, grad_bias.reshape(cols)


def solution(mesh):
    placed = (
        P("dom", "feat"),
        P("feat", None),
        P("feat", None),
        P("feat"),
        P("dom", "feat"),
        P("dom", None, None, None),
        P("dom", None),
        P("dom"),
        P("dom", None, None),
        P("dom", None, None),
        P("dom", None, None),
        P("dom", None),
        P("dom", None),
        P("dom", None),
    )
    return jax.shard_map(
        on_device,
        mesh=mesh,
        in_specs=placed,
        out_specs=(P("dom", "feat"), P("dom", "feat"), P("feat", None), P("feat", None), P("feat")),
        check_vma=False,
    )
```

```python
import functools
import math

import jax
import jax.numpy as jnp
from jax import lax
from jax.experimental import pallas as pl
from jax.experimental.pallas import tpu as pltpu
from jax.sharding import PartitionSpec as P

BF = jnp.bfloat16
F32 = jnp.float32


def slot_places(peers, slots, width):
    lanes = peers * width
    lane = lax.broadcasted_iota(jnp.int32, (slots, lanes), 1)
    slot = lax.broadcasted_iota(jnp.int32, (slots, lanes), 0)
    return jnp.where(lane % width == slot, 1.0, 0.0).astype(BF)


def spread_rows(table, width, place=None):
    peers, slots = table.shape
    lanes = peers * width
    if place is None:
        place = slot_places(peers, slots, width)
    wide = jnp.dot(table.astype(BF), place, preferred_element_type=F32)
    peer = lax.broadcasted_iota(jnp.int32, (peers, lanes), 0)
    at = lax.broadcasted_iota(jnp.int32, (peers, lanes), 1)
    return jnp.sum(jnp.where(at // width == peer, wide, 0.0), axis=0, keepdims=True)


def source_matrix(send, hubs, rows, width, place=None):
    peers, slots = send.shape
    hub_here = hubs.shape[1]
    lanes = peers * width
    lane = lax.broadcasted_iota(jnp.int32, (1, lanes), 1) % width
    index = spread_rows(send.astype(F32), width, place)
    for k in range(hub_here):
        index = jnp.where(lane == slots + k, hubs[0:1, k : k + 1].astype(F32), index)
    index = jnp.where(lane < slots + hub_here, index, -1.0)
    row = lax.broadcasted_iota(jnp.int32, (rows, lanes), 0).astype(F32)
    return jnp.where(row == index, 1.0, 0.0).astype(BF)


def send_kernel(
    width, x_ref, cot_ref, ws_ref, wn_ref, bias_ref, send_ref, hub_ref, pos_ref, live_ref, tile_ref, dest_ref, gw_ref, hw_ref,
    out_ref, pack_ref, send_v, hub_v, pos_v, live_v, tile_v, dest_v, gw_v, hw_v, bias_v, place_ref, sems,
):
    rows, cols = x_ref.shape
    depth, full = ws_ref.shape
    blocks = full // cols
    base = 2 * blocks * depth
    moves = [
        (send_ref, send_v),
        (hub_ref, hub_v),
        (x_ref, pack_ref.at[base : base + rows, :]),
        (bias_ref, bias_v),
        (cot_ref, pack_ref.at[base + rows : base + 2 * rows, :]),
    ]
    for kind, w_ref in enumerate((ws_ref, wn_ref)):
        for j in range(blocks):
            at = (kind * blocks + j) * depth
            moves.append((w_ref.at[:, j * cols : (j + 1) * cols], pack_ref.at[at : at + depth, :]))
    moves += [
        (pos_ref, pos_v), (live_ref, live_v), (tile_ref, tile_v), (dest_ref, dest_v),
        (gw_ref, gw_v), (hw_ref, hw_v),
    ]
    copies = [pltpu.make_async_copy(src, dst, sems.at[i]) for i, (src, dst) in enumerate(moves)]
    for copy in copies:
        copy.start()
    peers, slots = send_v.shape[1:]
    place_ref[...] = slot_places(peers, slots, width)
    for copy in copies[:2]:
        copy.wait()
    mark = source_matrix(send_v[0], hub_v[...], rows, width, place_ref[...])
    copies[2].wait()
    taken = lax.dot_general(
        mark, pack_ref[base : base + rows, :], (((0,), (0,)), ((), ())), preferred_element_type=F32
    ).astype(BF)
    out_ref[...] = taken.reshape(out_ref.shape)
    for copy in copies[3:]:
        copy.wait()
    pack_ref[base + 2 * rows :, :] = jnp.broadcast_to(bias_v[...], (16, cols))


def mix_kernel(width, count_ref, send_v, hub_v, pos_v, live_v, tile_v, dest_v, gw_v, hw_v, mix_ref, turned_ref, mark_ref):
    rows = mix_ref.shape[0]
    tiles, tile = tile_v.shape[1:3]
    peers, slots = dest_v.shape[1:]
    side = rows // tile
    lanes = peers * width
    hubs = hw_v.shape[0]
    hub_here = hubs // peers
    for r in range(side):
        for c in range(side):
            total = jnp.zeros((tile, tile), BF)
            for t in range(tiles):
                used = jnp.logical_and(pos_v[0:1, t : t + 1] == r * side + c, t < count_ref[...])
                total = jnp.where(used, tile_v[0, t], total)
            mix_ref[r * tile : (r + 1) * tile, c * tile : (c + 1) * tile] = total
    dest = spread_rows(dest_v[0].astype(F32), width)
    coef = spread_rows(gw_v[0], width)
    peer = lax.broadcasted_iota(jnp.int32, (peers, lanes), 0)
    at = lax.broadcasted_iota(jnp.int32, (peers, lanes), 1)
    owner = jnp.where(at // width == peer, 1.0, 0.0).astype(BF)
    limit = jnp.dot(live_v[...].astype(F32).astype(BF), owner, preferred_element_type=F32)
    lane = lax.broadcasted_iota(jnp.int32, (1, lanes), 1) % width
    coef = jnp.where(jnp.logical_and(lane.astype(F32) < limit, lane < slots), coef, 0.0)
    row = lax.broadcasted_iota(jnp.int32, (rows, lanes), 0).astype(F32)
    ghost = jnp.where(row == dest, coef, 0.0)
    hub = lax.broadcasted_iota(jnp.int32, (hubs, lanes), 0)
    at = lax.broadcasted_iota(jnp.int32, (hubs, lanes), 1)
    place = jnp.where(
        jnp.logical_and(at // width == hub // hub_here, at % width == slots + hub % hub_here), 1.0, 0.0
    ).astype(BF)
    hub_mix = lax.dot_general(hw_v[...], place, (((0,), (0,)), ((), ())), preferred_element_type=F32)
    mix_ref[:, rows:] = (ghost + hub_mix).astype(BF)
    turned_ref[...] = mix_ref[...].T
    mark_ref[...] = source_matrix(send_v[0], hub_v[...], rows, width)


def neigh_kernel(x_ref, mix_ref, far_ref, got_ref, neigh_ref, passed_ref):
    rows, cols = x_ref.shape
    lanes = mix_ref.shape[1] - rows
    total = jnp.dot(mix_ref[:, :rows], x_ref[...], preferred_element_type=F32)
    total = total + jnp.dot(mix_ref[:, rows:], got_ref[...].reshape(lanes, cols), preferred_element_type=F32)
    neigh_ref[...] = total.astype(BF)


def ghost_rows(slots, hub_here, width, start, peers, turned_ref, neigh_grad, sums):
    rows, cols = neigh_grad.shape
    high = sums.astype(BF).astype(F32)
    line = lax.broadcasted_iota(jnp.int32, (peers * width, cols), 0) % width
    cut = pl.ds(pl.multiple_of(rows + start * width, 16), peers * width)
    away = jnp.dot(turned_ref[cut, :], neigh_grad, preferred_element_type=F32)
    away = jnp.where(line == slots + hub_here, high, away)
    away = jnp.where(line == slots + hub_here + 1, sums - high, away)
    return away.astype(BF)


def dense_kernel(slots, hub_here, feats, width, count, me_ref, side_ref, seat_ref, x_ref, ws_ref, wn_ref, turned_ref, *refs):
    pack_refs, n_refs = refs[:feats], refs[feats : 2 * feats]
    own_ref, cot_ref, slope_ref, sums_ref, mirror_ref = refs[2 * feats : 2 * feats + 5]
    send_refs = refs[2 * feats + 5 : 2 * feats + 5 + count]
    pre_ref, bias_ref = refs[2 * feats + 5 + count :]
    rows, cols = x_ref.shape
    depth, full = ws_ref.shape
    blocks = full // cols
    half = mirror_ref.shape[0]
    share = send_refs[0].shape[-2]
    me = me_ref[0]
    base = 2 * blocks * depth
    left = []
    for d, pack in enumerate(pack_refs):
        owner = me ^ d
        cut = pl.ds(pl.multiple_of(owner * cols, cols), cols)
        cot_ref[:, cut] = pack[base + rows : base + 2 * rows, :]
        bias_ref[:, cut] = pack[base + 2 * rows : base + 2 * rows + 16, :]
        left += [pack[base : base + rows, :], n_refs[d][...]]
    left = jnp.concatenate(left, axis=1)
    into = jnp.zeros((rows, depth), F32)
    span = 2
    for j in range(0, blocks, span):
        right = [
            jnp.concatenate([pack[(kind * blocks + i) * depth : (kind * blocks + i + 1) * depth, :] for i in range(j, j + span)], axis=1)
            for pack in pack_refs
            for kind in range(2)
        ]
        cut = slice(j * cols, (j + span) * cols)
        pre = jnp.dot(left, jnp.concatenate(right, axis=0), preferred_element_type=F32)
        pre = pre + bias_ref[0:1, cut].astype(F32)
        pre_ref[:, cut] = pre
        sig = jax.nn.sigmoid(pre)
        grad = (cot_ref[:, cut].astype(F32) * sig * (1.0 + pre * (1.0 - sig))).astype(BF)
        cot_ref[:, cut] = grad
        into = into + lax.dot_general(
            grad, wn_ref[:, cut], (((1,), (1,)), ((), ())), preferred_element_type=F32
        )
    mine = pl.ds(pl.multiple_of(me * cols, cols), cols)
    own_ref[...] = pre_ref[:, mine]
    neigh_grad = into.astype(BF)
    slope_ref[...] = neigh_grad
    sums = jnp.sum(cot_ref[:, mine].astype(F32), axis=0, keepdims=True)
    sums_ref[...] = sums
    there = half - side_ref[0] * half
    pair = jnp.concatenate([x_ref[...], n_refs[0][...]], axis=1).T
    if count > 1:
        for k, ref in enumerate(send_refs):
            peer = seat_ref[0] ^ k
            mirror_ref[k] = ghost_rows(slots, hub_here, width, there + peer, 1, turned_ref, neigh_grad, sums)
            block = cot_ref[:, pl.ds(pl.multiple_of(peer * cols, cols), cols)]
            ref[...] = jnp.dot(pair, block, preferred_element_type=F32).astype(BF)
        return
    send_ref = send_refs[0]
    mirror_ref[...] = ghost_rows(
        slots, hub_here, width, there, half, turned_ref, neigh_grad, sums
    ).reshape(half, width, cols)
    weights = jnp.dot(pair, cot_ref[...], preferred_element_type=F32).astype(BF)
    step = min(share, depth)
    for j in range(blocks):
        for kind in range(2):
            block = weights[kind * depth : (kind + 1) * depth, j * cols : (j + 1) * cols]
            for part in range(depth // step):
                at = (j * 2 + kind) * depth + part * step
                low = at % share
                send_ref[at // share, low : low + step, :] = block[part * step : (part + 1) * step]


def seated(refs, seat):
    if len(refs) == 1:
        return [(j, refs[0].at[j]) for j in range(refs[0].shape[0])]
    return [(seat ^ k, ref) for k, ref in enumerate(refs)]


def side_kernel(
    slots, hub_here, count, side_ref, seat_ref, own_ref, grad_ref, slope_ref, sums_ref, turned_ref, ws_ref,
    out_ref, back_ref, ghost_ref,
):
    own = own_ref[...]
    out_ref[...] = (own * jax.nn.sigmoid(own)).astype(BF)
    rows, cols = own.shape
    half, width = ghost_ref.shape[:2]
    slope, sums = slope_ref[...], sums_ref[...]
    back = lax.dot_general(grad_ref[...], ws_ref[...], (((1,), (1,)), ((), ())), preferred_element_type=F32)
    back_ref[...] = back + jnp.dot(turned_ref[:rows, :], slope, preferred_element_type=F32)
    here = side_ref[0] * half
    if count > 1:
        for k in range(half):
            peer = here + (seat_ref[0] ^ k)
            ghost_ref[k] = ghost_rows(slots, hub_here, width, peer, 1, turned_ref, slope, sums)
        return
    ghost_ref[...] = ghost_rows(slots, hub_here, width, here, half, turned_ref, slope, sums).reshape(half, width, cols)


def sum_kernel(stored_ref, *refs):
    got_refs, sum_ref = refs[:-1], refs[-1]
    total = jnp.zeros(sum_ref.shape, F32)
    for got_ref in got_refs if len(got_refs) > 1 else [got_refs[0].at[j] for j in range(got_refs[0].shape[0])]:
        total = total + got_ref[...].astype(F32)
    sum_ref[...] = total.astype(BF)


def deal_kernel(ghost_ref, mirror_ref, *out_refs):
    width = ghost_ref.shape[1]
    for k in range(ghost_ref.shape[0]):
        out_ref = out_refs[k] if len(out_refs) > 1 else out_refs[0].at[k]
        out_ref[:width, :] = ghost_ref[k]
        out_ref[width:, :] = mirror_ref[k]


def total_kernel(own_ref, other_ref, part_ref):
    total = (own_ref[...].astype(F32) + other_ref[...].astype(F32)).astype(BF)
    part_ref[...] = jnp.broadcast_to(total, part_ref.shape)


def near_rows(slots, hub_here, start, mark_ref, got_ref):
    half, width, cols = got_ref.shape
    cut = pl.ds(pl.multiple_of(start * width, 128), half * width)
    added = jnp.dot(mark_ref[:, cut], got_ref[...].reshape(half * width, cols), preferred_element_type=F32)
    first = slots + hub_here
    bias = jnp.zeros((2, cols), F32)
    for j in range(half):
        bias = bias + got_ref[j, first : first + 2, :].astype(F32)
    return added, jnp.sum(bias, axis=0, keepdims=True)


def grad_kernel(scale, slots, hub_here, side_ref, seat_ref, back_ref, mark_ref, *refs):
    got_refs, (grad_ref, bias_ref, near_ref, far_ref) = refs[:-4], refs[-4:]
    half, width = near_ref.shape[:2]
    for j, got_ref in seated(got_refs, seat_ref[0]):
        near_ref[j] = got_ref[:width, :]
        far_ref[j] = got_ref[width:, :]
    here = side_ref[0] * half
    near, near_bias = near_rows(slots, hub_here, here, mark_ref, near_ref)
    far, far_bias = near_rows(slots, hub_here, half - here, mark_ref, far_ref)
    grad_ref[...] = (back_ref[...] + near + far).astype(BF)
    bias_ref[...] = (near_bias + far_bias) * scale


def write_blocks(scale, parts, self_ref, neigh_ref, wide_ref, sems):
    depth, full = self_ref.shape
    cols = wide_ref.shape[-1]
    copies = []
    for at, (j, part) in enumerate(parts):
        wide_ref[at] = part.astype(F32) * scale
        cut = pl.ds(pl.multiple_of(j * cols, cols), cols)
        for kind, out_ref in enumerate((self_ref, neigh_ref)):
            copy = pltpu.make_async_copy(
                wide_ref.at[at, kind * depth : (kind + 1) * depth, :], out_ref.at[:, cut], sems.at[2 * at + kind]
            )
            copy.start()
            copies.append(copy)
    for copy in copies:
        copy.wait()


def spread_kernel(scale, seat_ref, *refs):
    got_refs, (self_ref, neigh_ref, wide_ref, sems) = refs[:-4], refs[-4:]
    depth, full = self_ref.shape
    cols = wide_ref.shape[-1]
    if len(got_refs) > 1:
        parts = [(j, ref[...]) for j, ref in seated(got_refs, seat_ref[0])]
    else:
        whole = got_refs[0][...].reshape(2 * full // cols * depth, cols)
        parts = [(j, whole[2 * j * depth : 2 * (j + 1) * depth]) for j in range(full // cols)]
    write_blocks(scale, parts, self_ref, neigh_ref, wide_ref, sems)


def finish_kernel(scale, k, seat_ref, got_ref, begun_self_ref, begun_neigh_ref, self_ref, neigh_ref, wide_ref, sems):
    write_blocks(scale, [(seat_ref[0] ^ k, got_ref[...])], self_ref, neigh_ref, wide_ref, sems)


VMEM = pl.BlockSpec(memory_space=pltpu.VMEM)
SMEM = pl.BlockSpec(memory_space=pltpu.SMEM)
ANY = pl.BlockSpec(memory_space=pl.ANY)
HBM = pl.BlockSpec(memory_space=pltpu.HBM)
PARAMS = pltpu.CompilerParams(vmem_limit_bytes=40 * 1024 * 1024)


def shape(dims, kind):
    return jax.ShapeDtypeStruct(dims, kind)


def partner(block, axis, k):
    return lax.ppermute(block, axis, [(i, i ^ k) for i in range(lax.axis_size(axis))])


def exchange(blocks, groups=None):
    return lax.all_to_all(blocks, "dom", split_axis=0, concat_axis=0, axis_index_groups=groups, tiled=True)


def swap(blocks):
    return [blocks[0]] + [partner(block, "dom", k) for k, block in enumerate(blocks) if k]


def on_device(
    features,
    w_self,
    w_neigh,
    bias,
    cotangent,
    tile_vals,
    tile_pos,
    tile_count,
    send_rows,
    recv_dest,
    ghost_weight,
    recv_count,
    hub_rows,
    hub_weight,
):
    rows, cols = features.shape
    depth, full = w_self.shape
    blocks = full // cols
    peers, slots = send_rows.shape[1:]
    hub_here = hub_rows.shape[-1]
    width = -(-(slots + hub_here + 2) // 16) * 16
    lanes = peers * width
    half = peers // 2
    share = 2 * blocks * depth // half
    direct = half == blocks
    count = half if direct else 1
    halves = [list(range(half)), list(range(half, peers))]
    scale = 1.0 / math.sqrt(peers * rows)
    feats = lax.axis_size("feat")
    me = lax.axis_index("feat").astype(jnp.int32).reshape(1)
    side = (lax.axis_index("dom") >= half).astype(jnp.int32).reshape(1)
    seat = lax.rem(lax.axis_index("dom"), half).astype(jnp.int32).reshape(1)
    pack_rows = 2 * blocks * depth + 2 * rows + 16

    def pinned(*arrays):
        return [pltpu.with_memory_space_constraint(a, pltpu.HBM) for a in arrays]

    first = pinned(features, cotangent, w_self, w_neigh, bias.reshape(1, cols), send_rows, hub_rows)
    edges = pinned(tile_pos, recv_count, tile_vals, recv_dest, ghost_weight, hub_weight.T)
    moved = (send_rows, hub_rows, *edges)
    outgoing, pack, *moved = pl.pallas_call(
        functools.partial(send_kernel, width),
        out_shape=(
            shape((peers, width, cols), BF),
            shape((pack_rows, cols), BF),
            *(shape(a.shape, a.dtype) for a in moved),
        ),
        in_specs=[HBM] * (len(first) + len(edges)),
        out_specs=(VMEM,) * (2 + len(moved)),
        scratch_shapes=[
            pltpu.VMEM((1, cols), BF),
            pltpu.VMEM((slots, lanes), BF),
            pltpu.SemaphoreType.DMA((11 + 2 * blocks,)),
        ],
        compiler_params=PARAMS,
    )(*first, *edges)

    far = partner(pack, "feat", 2)
    near = partner(pack, "feat", 1)
    incoming = exchange(outgoing)
    mix, turned, mark = pl.pallas_call(
        functools.partial(mix_kernel, width),
        out_shape=(
            shape((rows, rows + lanes), BF),
            shape((rows + lanes, rows), BF),
            shape((rows, lanes), BF),
        ),
        in_specs=[VMEM] * (1 + len(moved)),
        out_specs=(VMEM,) * 3,
        compiler_params=PARAMS,
        cost_estimate=pl.CostEstimate(flops=10**8, bytes_accessed=3 * 10**6, transcendentals=0),
    )(tile_count.reshape(1, 1), *moved)
    neigh, far = pl.pallas_call(
        neigh_kernel,
        out_shape=(shape((rows, cols), BF), shape((pack_rows, cols), BF)),
        in_specs=[VMEM, VMEM, ANY, VMEM],
        out_specs=(VMEM, ANY),
        input_output_aliases={2: 1},
        compiler_params=PARAMS,
    )(features, mix, far, incoming)
    last = partner(far, "feat", 1)
    far_neigh = partner(neigh, "feat", 2)
    every = [neigh, partner(neigh, "feat", 1), far_neigh, partner(far_neigh, "feat", 1)]

    own, grad, slope, sums, mirror, *returned = pl.pallas_call(
        functools.partial(dense_kernel, slots, hub_here, feats, width, count),
        out_shape=(
            shape((rows, cols), F32),
            shape((rows, full), BF),
            shape((rows, cols), BF),
            shape((1, cols), F32),
            shape((half, width, cols), BF),
            *([shape((share, cols), BF)] * half if direct else [shape((half, share, cols), BF)]),
        ),
        in_specs=[SMEM] * 3 + [VMEM] * (4 + 2 * feats),
        out_specs=(VMEM,) * (5 + count),
        scratch_shapes=[
            pltpu.VMEM((rows, full), F32),
            pltpu.VMEM((16, full), BF),
        ],
        compiler_params=PARAMS,
    )(me, side, seat, features, w_self, w_neigh, turned, pack, near, far, last, *every)

    arrived = swap(returned)[::-1] if direct else [exchange(returned[0], halves)]
    mirror = partner(mirror, "dom", half)
    output, back, ghosts = pl.pallas_call(
        functools.partial(side_kernel, slots, hub_here, count),
        out_shape=(shape((rows, cols), BF), shape((rows, cols), F32), shape((half, width, cols), BF)),
        in_specs=[SMEM] * 2 + [VMEM] * 6,
        out_specs=(VMEM,) * 3,
        compiler_params=PARAMS,
        cost_estimate=pl.CostEstimate(flops=10**8, bytes_accessed=10**6, transcendentals=0),
    )(side, seat, own, grad, slope, sums, turned, w_self)
    half_sum = pl.pallas_call(
        sum_kernel,
        out_shape=shape((share, cols), BF),
        in_specs=[HBM] + [VMEM] * count,
        out_specs=VMEM,
        compiler_params=PARAMS,
    )(*pinned(output), *arrived)
    other_sum = partner(half_sum, "dom", half)
    dealt = pl.pallas_call(
        deal_kernel,
        out_shape=[shape((2 * width, cols), BF)] * half if direct else [shape((half, 2 * width, cols), BF)],
        in_specs=[VMEM] * 2,
        out_specs=[VMEM] * count,
        compiler_params=PARAMS,
    )(ghosts, mirror)
    dealt = swap(dealt) if direct else [exchange(dealt[0], halves)]
    part = pl.pallas_call(
        total_kernel,
        out_shape=shape((share, cols) if direct else (half, share, cols), BF),
        in_specs=[VMEM, VMEM],
        out_specs=VMEM,
        compiler_params=PARAMS,
    )(half_sum, other_sum)
    parts = swap([part] * half) if direct else [exchange(part, halves)]
    grad_features, grad_bias = pl.pallas_call(
        functools.partial(grad_kernel, scale, slots, hub_here),
        out_shape=(shape((rows, cols), BF), shape((1, cols), F32)),
        in_specs=[SMEM] * 2 + [VMEM] * (2 + count),
        out_specs=(VMEM,) * 2,
        scratch_shapes=[pltpu.VMEM((half, width, cols), BF)] * 2,
        compiler_params=PARAMS,
        cost_estimate=pl.CostEstimate(flops=2 * 10**9, bytes_accessed=10**6, transcendentals=0),
    )(side, seat, back, mark, *dealt)
    early = half - 1 if direct else 1
    grad_self, grad_neigh = pl.pallas_call(
        functools.partial(spread_kernel, scale),
        out_shape=(shape((depth, full), F32), shape((depth, full), F32)),
        in_specs=[SMEM] + [VMEM] * early,
        out_specs=(HBM,) * 2,
        scratch_shapes=[pltpu.VMEM((blocks, 2 * depth, cols), F32), pltpu.SemaphoreType.DMA((2 * blocks,))],
        compiler_params=PARAMS,
    )(seat, *parts[:early])
    if direct:
        grad_self, grad_neigh = pl.pallas_call(
            functools.partial(finish_kernel, scale, early),
            out_shape=(shape((depth, full), F32), shape((depth, full), F32)),
            in_specs=[SMEM, VMEM, HBM, HBM],
            out_specs=(HBM,) * 2,
            scratch_shapes=[pltpu.VMEM((1, 2 * depth, cols), F32), pltpu.SemaphoreType.DMA((2,))],
            input_output_aliases={2: 0, 3: 1},
            compiler_params=PARAMS,
        )(seat, parts[early], *pinned(grad_self, grad_neigh))
    return output, grad_features, grad_self, grad_neigh, grad_bias.reshape(cols)


def solution(mesh):
    placed = (
        P("dom", "feat"),
        P("feat", None),
        P("feat", None),
        P("feat"),
        P("dom", "feat"),
        P("dom", None, None, None),
        P("dom", None),
        P("dom"),
        P("dom", None, None),
        P("dom", None, None),
        P("dom", None, None),
        P("dom", None),
        P("dom", None),
        P("dom", None),
    )
    return jax.shard_map(
        on_device,
        mesh=mesh,
        in_specs=placed,
        out_specs=(P("dom", "feat"), P("dom", "feat"), P("feat", None), P("feat", None), P("feat")),
        check_vma=False,
    )
```

```python
import functools
import math

import jax
import jax.numpy as jnp
from jax import lax
from jax.experimental import pallas as pl
from jax.experimental.pallas import tpu as pltpu
from jax.sharding import PartitionSpec as P

BF = jnp.bfloat16
F32 = jnp.float32


def slot_places(peers, slots, width):
    lanes = peers * width
    lane = lax.broadcasted_iota(jnp.int32, (slots, lanes), 1)
    slot = lax.broadcasted_iota(jnp.int32, (slots, lanes), 0)
    return jnp.where(lane % width == slot, 1.0, 0.0).astype(BF)


def spread_rows(table, width, place=None):
    peers, slots = table.shape
    lanes = peers * width
    if place is None:
        place = slot_places(peers, slots, width)
    wide = jnp.dot(table.astype(BF), place, preferred_element_type=F32)
    peer = lax.broadcasted_iota(jnp.int32, (peers, lanes), 0)
    at = lax.broadcasted_iota(jnp.int32, (peers, lanes), 1)
    return jnp.sum(jnp.where(at // width == peer, wide, 0.0), axis=0, keepdims=True)


def source_matrix(send, hubs, rows, width, place=None):
    peers, slots = send.shape
    hub_here = hubs.shape[1]
    lanes = peers * width
    lane = lax.broadcasted_iota(jnp.int32, (1, lanes), 1) % width
    index = spread_rows(send.astype(F32), width, place)
    for k in range(hub_here):
        index = jnp.where(lane == slots + k, hubs[0:1, k : k + 1].astype(F32), index)
    index = jnp.where(lane < slots + hub_here, index, -1.0)
    row = lax.broadcasted_iota(jnp.int32, (rows, lanes), 0).astype(F32)
    return jnp.where(row == index, 1.0, 0.0).astype(BF)


def send_kernel(
    width, x_ref, cot_ref, ws_ref, wn_ref, bias_ref, send_ref, hub_ref, pos_ref, live_ref, tile_ref, dest_ref, gw_ref, hw_ref,
    out_ref, pack_ref, send_v, hub_v, pos_v, live_v, tile_v, dest_v, gw_v, hw_v, bias_v, place_ref, sems,
):
    rows, cols = x_ref.shape
    depth, full = ws_ref.shape
    blocks = full // cols
    base = 2 * blocks * depth
    moves = [
        (send_ref, send_v),
        (hub_ref, hub_v),
        (x_ref, pack_ref.at[base : base + rows, :]),
        (bias_ref, bias_v),
        (cot_ref, pack_ref.at[base + rows : base + 2 * rows, :]),
    ]
    for kind, w_ref in enumerate((ws_ref, wn_ref)):
        for j in range(blocks):
            at = (kind * blocks + j) * depth
            moves.append((w_ref.at[:, j * cols : (j + 1) * cols], pack_ref.at[at : at + depth, :]))
    moves += [
        (pos_ref, pos_v), (live_ref, live_v), (tile_ref, tile_v), (dest_ref, dest_v),
        (gw_ref, gw_v), (hw_ref, hw_v),
    ]
    copies = [pltpu.make_async_copy(src, dst, sems.at[i]) for i, (src, dst) in enumerate(moves)]
    for copy in copies:
        copy.start()
    peers, slots = send_v.shape[1:]
    place_ref[...] = slot_places(peers, slots, width)
    for copy in copies[:2]:
        copy.wait()
    mark = source_matrix(send_v[0], hub_v[...], rows, width, place_ref[...])
    copies[2].wait()
    taken = lax.dot_general(
        mark, pack_ref[base : base + rows, :], (((0,), (0,)), ((), ())), preferred_element_type=F32
    ).astype(BF)
    kept = out_ref.shape[1]
    for q in range(peers):
        out_ref[q] = taken[q * width : q * width + kept]
    for copy in copies[3:]:
        copy.wait()
    pack_ref[base + 2 * rows :, :] = jnp.broadcast_to(bias_v[...], (16, cols))


def mix_kernel(width, count_ref, send_v, hub_v, pos_v, live_v, tile_v, dest_v, gw_v, hw_v, mix_ref, turned_ref, mark_ref):
    rows = mix_ref.shape[0]
    tiles, tile = tile_v.shape[1:3]
    peers, slots = dest_v.shape[1:]
    side = rows // tile
    lanes = peers * width
    hubs = hw_v.shape[0]
    hub_here = hubs // peers
    for r in range(side):
        for c in range(side):
            total = jnp.zeros((tile, tile), BF)
            for t in range(tiles):
                used = jnp.logical_and(pos_v[0:1, t : t + 1] == r * side + c, t < count_ref[...])
                total = jnp.where(used, tile_v[0, t], total)
            mix_ref[r * tile : (r + 1) * tile, c * tile : (c + 1) * tile] = total
    dest = spread_rows(dest_v[0].astype(F32), width)
    coef = spread_rows(gw_v[0], width)
    peer = lax.broadcasted_iota(jnp.int32, (peers, lanes), 0)
    at = lax.broadcasted_iota(jnp.int32, (peers, lanes), 1)
    owner = jnp.where(at // width == peer, 1.0, 0.0).astype(BF)
    limit = jnp.dot(live_v[...].astype(F32).astype(BF), owner, preferred_element_type=F32)
    lane = lax.broadcasted_iota(jnp.int32, (1, lanes), 1) % width
    coef = jnp.where(jnp.logical_and(lane.astype(F32) < limit, lane < slots), coef, 0.0)
    row = lax.broadcasted_iota(jnp.int32, (rows, lanes), 0).astype(F32)
    ghost = jnp.where(row == dest, coef, 0.0)
    hub = lax.broadcasted_iota(jnp.int32, (hubs, lanes), 0)
    at = lax.broadcasted_iota(jnp.int32, (hubs, lanes), 1)
    place = jnp.where(
        jnp.logical_and(at // width == hub // hub_here, at % width == slots + hub % hub_here), 1.0, 0.0
    ).astype(BF)
    hub_mix = lax.dot_general(hw_v[...], place, (((0,), (0,)), ((), ())), preferred_element_type=F32)
    mix_ref[:, rows:] = (ghost + hub_mix).astype(BF)
    turned_ref[...] = mix_ref[...].T
    mark_ref[...] = source_matrix(send_v[0], hub_v[...], rows, width)


def neigh_kernel(x_ref, mix_ref, far_ref, got_ref, neigh_ref, passed_ref, wide_ref):
    rows, cols = x_ref.shape
    lanes = mix_ref.shape[1] - rows
    wide_ref[...] = jnp.zeros_like(wide_ref)
    wide_ref[:, : got_ref.shape[1], :] = got_ref[...]
    total = jnp.dot(mix_ref[:, :rows], x_ref[...], preferred_element_type=F32)
    total = total + jnp.dot(mix_ref[:, rows:], wide_ref[...].reshape(lanes, cols), preferred_element_type=F32)
    neigh_ref[...] = total.astype(BF)


def ghost_rows(slots, hub_here, width, start, peers, turned_ref, neigh_grad, sums):
    rows, cols = neigh_grad.shape
    high = sums.astype(BF).astype(F32)
    line = lax.broadcasted_iota(jnp.int32, (peers * width, cols), 0) % width
    cut = pl.ds(pl.multiple_of(rows + start * width, 16), peers * width)
    away = jnp.dot(turned_ref[cut, :], neigh_grad, preferred_element_type=F32)
    away = jnp.where(line == slots + hub_here, high, away)
    away = jnp.where(line == slots + hub_here + 1, sums - high, away)
    return away.astype(BF)


def dense_kernel(slots, hub_here, feats, width, count, me_ref, side_ref, seat_ref, x_ref, ws_ref, wn_ref, turned_ref, *refs):
    pack_refs, n_refs = refs[:feats], refs[feats : 2 * feats]
    own_ref, cot_ref, slope_ref, sums_ref, mirror_ref = refs[2 * feats : 2 * feats + 5]
    send_refs = refs[2 * feats + 5 : 2 * feats + 5 + count]
    pre_ref, bias_ref = refs[2 * feats + 5 + count :]
    rows, cols = x_ref.shape
    depth, full = ws_ref.shape
    blocks = full // cols
    half = mirror_ref.shape[0]
    share = send_refs[0].shape[-2]
    me = me_ref[0]
    base = 2 * blocks * depth
    left = []
    for d, pack in enumerate(pack_refs):
        owner = me ^ d
        cut = pl.ds(pl.multiple_of(owner * cols, cols), cols)
        cot_ref[:, cut] = pack[base + rows : base + 2 * rows, :]
        bias_ref[:, cut] = pack[base + 2 * rows : base + 2 * rows + 16, :]
        left += [pack[base : base + rows, :], n_refs[d][...]]
    left = jnp.concatenate(left, axis=1)
    into = jnp.zeros((rows, depth), F32)
    span = 2
    for j in range(0, blocks, span):
        right = [
            jnp.concatenate([pack[(kind * blocks + i) * depth : (kind * blocks + i + 1) * depth, :] for i in range(j, j + span)], axis=1)
            for pack in pack_refs
            for kind in range(2)
        ]
        cut = slice(j * cols, (j + span) * cols)
        pre = jnp.dot(left, jnp.concatenate(right, axis=0), preferred_element_type=F32)
        pre = pre + bias_ref[0:1, cut].astype(F32)
        pre_ref[:, cut] = pre
        sig = jax.nn.sigmoid(pre)
        grad = (cot_ref[:, cut].astype(F32) * sig * (1.0 + pre * (1.0 - sig))).astype(BF)
        cot_ref[:, cut] = grad
        into = into + lax.dot_general(
            grad, wn_ref[:, cut], (((1,), (1,)), ((), ())), preferred_element_type=F32
        )
    mine = pl.ds(pl.multiple_of(me * cols, cols), cols)
    own_ref[...] = pre_ref[:, mine]
    neigh_grad = into.astype(BF)
    slope_ref[...] = neigh_grad
    sums = jnp.sum(cot_ref[:, mine].astype(F32), axis=0, keepdims=True)
    sums_ref[...] = sums
    there = half - side_ref[0] * half
    pair = jnp.concatenate([x_ref[...], n_refs[0][...]], axis=1).T
    if count > 1:
        for k, ref in enumerate(send_refs):
            peer = seat_ref[0] ^ k
            away = ghost_rows(slots, hub_here, width, there + peer, 1, turned_ref, neigh_grad, sums)
            mirror_ref[k] = away[: mirror_ref.shape[1]]
            block = cot_ref[:, pl.ds(pl.multiple_of(peer * cols, cols), cols)]
            ref[...] = jnp.dot(pair, block, preferred_element_type=F32).astype(BF)
        return
    send_ref = send_refs[0]
    away = ghost_rows(slots, hub_here, width, there, half, turned_ref, neigh_grad, sums).reshape(half, width, cols)
    mirror_ref[...] = away[:, : mirror_ref.shape[1]]
    weights = jnp.dot(pair, cot_ref[...], preferred_element_type=F32).astype(BF)
    step = min(share, depth)
    for j in range(blocks):
        for kind in range(2):
            block = weights[kind * depth : (kind + 1) * depth, j * cols : (j + 1) * cols]
            for part in range(depth // step):
                at = (j * 2 + kind) * depth + part * step
                low = at % share
                send_ref[at // share, low : low + step, :] = block[part * step : (part + 1) * step]


def seated(refs, seat):
    if len(refs) == 1:
        return [(j, refs[0].at[j]) for j in range(refs[0].shape[0])]
    return [(seat ^ k, ref) for k, ref in enumerate(refs)]


def side_kernel(
    slots, hub_here, count, side_ref, seat_ref, own_ref, grad_ref, slope_ref, sums_ref, turned_ref, ws_ref,
    out_ref, back_ref, ghost_ref,
):
    own = own_ref[...]
    out_ref[...] = (own * jax.nn.sigmoid(own)).astype(BF)
    rows, cols = own.shape
    half, width = ghost_ref.shape[:2]
    slope, sums = slope_ref[...], sums_ref[...]
    back = lax.dot_general(grad_ref[...], ws_ref[...], (((1,), (1,)), ((), ())), preferred_element_type=F32)
    back_ref[...] = back + jnp.dot(turned_ref[:rows, :], slope, preferred_element_type=F32)
    here = side_ref[0] * half
    if count > 1:
        for k in range(half):
            peer = here + (seat_ref[0] ^ k)
            ghost_ref[k] = ghost_rows(slots, hub_here, width, peer, 1, turned_ref, slope, sums)
        return
    ghost_ref[...] = ghost_rows(slots, hub_here, width, here, half, turned_ref, slope, sums).reshape(half, width, cols)


def sum_kernel(stored_ref, *refs):
    got_refs, sum_ref = refs[:-1], refs[-1]
    total = jnp.zeros(sum_ref.shape, F32)
    for got_ref in got_refs if len(got_refs) > 1 else [got_refs[0].at[j] for j in range(got_refs[0].shape[0])]:
        total = total + got_ref[...].astype(F32)
    sum_ref[...] = total.astype(BF)


def deal_kernel(ghost_ref, mirror_ref, *out_refs):
    width = ghost_ref.shape[1]
    for k in range(ghost_ref.shape[0]):
        out_ref = out_refs[k] if len(out_refs) > 1 else out_refs[0].at[k]
        out_ref[:width, :] = ghost_ref[k]
        out_ref[width:, :] = jnp.zeros(ghost_ref.shape[1:], BF)
        out_ref[width : width + mirror_ref.shape[1], :] = mirror_ref[k]


def total_kernel(own_ref, other_ref, part_ref):
    total = (own_ref[...].astype(F32) + other_ref[...].astype(F32)).astype(BF)
    part_ref[...] = jnp.broadcast_to(total, part_ref.shape)


def near_rows(slots, hub_here, start, mark_ref, got_ref):
    half, width, cols = got_ref.shape
    cut = pl.ds(pl.multiple_of(start * width, 128), half * width)
    added = jnp.dot(mark_ref[:, cut], got_ref[...].reshape(half * width, cols), preferred_element_type=F32)
    first = slots + hub_here
    bias = jnp.zeros((2, cols), F32)
    for j in range(half):
        bias = bias + got_ref[j, first : first + 2, :].astype(F32)
    return added, jnp.sum(bias, axis=0, keepdims=True)


def grad_kernel(scale, slots, hub_here, side_ref, seat_ref, back_ref, mark_ref, *refs):
    got_refs, (grad_ref, bias_ref, near_ref, far_ref) = refs[:-4], refs[-4:]
    half, width = near_ref.shape[:2]
    for j, got_ref in seated(got_refs, seat_ref[0]):
        near_ref[j] = got_ref[:width, :]
        far_ref[j] = got_ref[width:, :]
    here = side_ref[0] * half
    near, near_bias = near_rows(slots, hub_here, here, mark_ref, near_ref)
    far, far_bias = near_rows(slots, hub_here, half - here, mark_ref, far_ref)
    grad_ref[...] = (back_ref[...] + near + far).astype(BF)
    bias_ref[...] = (near_bias + far_bias) * scale


def write_blocks(scale, parts, self_ref, neigh_ref, wide_ref, sems):
    depth, full = self_ref.shape
    cols = wide_ref.shape[-1]
    copies = []
    for at, (j, part) in enumerate(parts):
        wide_ref[at] = part.astype(F32) * scale
        cut = pl.ds(pl.multiple_of(j * cols, cols), cols)
        for kind, out_ref in enumerate((self_ref, neigh_ref)):
            copy = pltpu.make_async_copy(
                wide_ref.at[at, kind * depth : (kind + 1) * depth, :], out_ref.at[:, cut], sems.at[2 * at + kind]
            )
            copy.start()
            copies.append(copy)
    for copy in copies:
        copy.wait()


def spread_kernel(scale, seat_ref, *refs):
    got_refs, (self_ref, neigh_ref, wide_ref, sems) = refs[:-4], refs[-4:]
    depth, full = self_ref.shape
    cols = wide_ref.shape[-1]
    if len(got_refs) > 1:
        parts = [(j, ref[...]) for j, ref in seated(got_refs, seat_ref[0])]
    else:
        whole = got_refs[0][...].reshape(2 * full // cols * depth, cols)
        parts = [(j, whole[2 * j * depth : 2 * (j + 1) * depth]) for j in range(full // cols)]
    write_blocks(scale, parts, self_ref, neigh_ref, wide_ref, sems)


def finish_kernel(scale, k, seat_ref, got_ref, begun_self_ref, begun_neigh_ref, self_ref, neigh_ref, wide_ref, sems):
    write_blocks(scale, [(seat_ref[0] ^ k, got_ref[...])], self_ref, neigh_ref, wide_ref, sems)


VMEM = pl.BlockSpec(memory_space=pltpu.VMEM)
SMEM = pl.BlockSpec(memory_space=pltpu.SMEM)
ANY = pl.BlockSpec(memory_space=pl.ANY)
HBM = pl.BlockSpec(memory_space=pltpu.HBM)
PARAMS = pltpu.CompilerParams(vmem_limit_bytes=40 * 1024 * 1024)


def shape(dims, kind):
    return jax.ShapeDtypeStruct(dims, kind)


def partner(block, axis, k):
    return lax.ppermute(block, axis, [(i, i ^ k) for i in range(lax.axis_size(axis))])


def exchange(blocks, groups=None):
    return lax.all_to_all(blocks, "dom", split_axis=0, concat_axis=0, axis_index_groups=groups, tiled=True)


def swap(blocks):
    return [blocks[0]] + [partner(block, "dom", k) for k, block in enumerate(blocks) if k]


def on_device(
    features,
    w_self,
    w_neigh,
    bias,
    cotangent,
    tile_vals,
    tile_pos,
    tile_count,
    send_rows,
    recv_dest,
    ghost_weight,
    recv_count,
    hub_rows,
    hub_weight,
):
    rows, cols = features.shape
    depth, full = w_self.shape
    blocks = full // cols
    peers, slots = send_rows.shape[1:]
    hub_here = hub_rows.shape[-1]
    width = -(-(slots + hub_here + 2) // 16) * 16
    sent = -(-(slots + hub_here + 2) // 8) * 8
    lanes = peers * width
    half = peers // 2
    share = 2 * blocks * depth // half
    direct = half == blocks
    count = half if direct else 1
    halves = [list(range(half)), list(range(half, peers))]
    scale = 1.0 / math.sqrt(peers * rows)
    feats = lax.axis_size("feat")
    me = lax.axis_index("feat").astype(jnp.int32).reshape(1)
    side = (lax.axis_index("dom") >= half).astype(jnp.int32).reshape(1)
    seat = lax.rem(lax.axis_index("dom"), half).astype(jnp.int32).reshape(1)
    pack_rows = 2 * blocks * depth + 2 * rows + 16

    def pinned(*arrays):
        return [pltpu.with_memory_space_constraint(a, pltpu.HBM) for a in arrays]

    first = pinned(features, cotangent, w_self, w_neigh, bias.reshape(1, cols), send_rows, hub_rows)
    edges = pinned(tile_pos, recv_count, tile_vals, recv_dest, ghost_weight, hub_weight.T)
    moved = (send_rows, hub_rows, *edges)
    outgoing, pack, *moved = pl.pallas_call(
        functools.partial(send_kernel, width),
        out_shape=(
            shape((peers, sent, cols), BF),
            shape((pack_rows, cols), BF),
            *(shape(a.shape, a.dtype) for a in moved),
        ),
        in_specs=[HBM] * (len(first) + len(edges)),
        out_specs=(VMEM,) * (2 + len(moved)),
        scratch_shapes=[
            pltpu.VMEM((1, cols), BF),
            pltpu.VMEM((slots, lanes), BF),
            pltpu.SemaphoreType.DMA((11 + 2 * blocks,)),
        ],
        compiler_params=PARAMS,
    )(*first, *edges)

    far = partner(pack, "feat", 2)
    near = partner(pack, "feat", 1)
    incoming = exchange(outgoing)
    mix, turned, mark = pl.pallas_call(
        functools.partial(mix_kernel, width),
        out_shape=(
            shape((rows, rows + lanes), BF),
            shape((rows + lanes, rows), BF),
            shape((rows, lanes), BF),
        ),
        in_specs=[VMEM] * (1 + len(moved)),
        out_specs=(VMEM,) * 3,
        compiler_params=PARAMS,
        cost_estimate=pl.CostEstimate(flops=10**8, bytes_accessed=3 * 10**6, transcendentals=0),
    )(tile_count.reshape(1, 1), *moved)
    neigh, far = pl.pallas_call(
        neigh_kernel,
        out_shape=(shape((rows, cols), BF), shape((pack_rows, cols), BF)),
        in_specs=[VMEM, VMEM, ANY, VMEM],
        out_specs=(VMEM, ANY),
        input_output_aliases={2: 1},
        scratch_shapes=[pltpu.VMEM((peers, width, cols), BF)],
        compiler_params=PARAMS,
    )(features, mix, far, incoming)
    last = partner(far, "feat", 1)
    far_neigh = partner(neigh, "feat", 2)
    every = [neigh, partner(neigh, "feat", 1), far_neigh, partner(far_neigh, "feat", 1)]

    own, grad, slope, sums, mirror, *returned = pl.pallas_call(
        functools.partial(dense_kernel, slots, hub_here, feats, width, count),
        out_shape=(
            shape((rows, cols), F32),
            shape((rows, full), BF),
            shape((rows, cols), BF),
            shape((1, cols), F32),
            shape((half, sent, cols), BF),
            *([shape((share, cols), BF)] * half if direct else [shape((half, share, cols), BF)]),
        ),
        in_specs=[SMEM] * 3 + [VMEM] * (4 + 2 * feats),
        out_specs=(VMEM,) * (5 + count),
        scratch_shapes=[
            pltpu.VMEM((rows, full), F32),
            pltpu.VMEM((16, full), BF),
        ],
        compiler_params=PARAMS,
    )(me, side, seat, features, w_self, w_neigh, turned, pack, near, far, last, *every)

    arrived = swap(returned)[::-1] if direct else [exchange(returned[0], halves)]
    mirror = partner(mirror, "dom", half)
    output, back, ghosts = pl.pallas_call(
        functools.partial(side_kernel, slots, hub_here, count),
        out_shape=(shape((rows, cols), BF), shape((rows, cols), F32), shape((half, width, cols), BF)),
        in_specs=[SMEM] * 2 + [VMEM] * 6,
        out_specs=(VMEM,) * 3,
        compiler_params=PARAMS,
        cost_estimate=pl.CostEstimate(flops=10**8, bytes_accessed=10**6, transcendentals=0),
    )(side, seat, own, grad, slope, sums, turned, w_self)
    half_sum = pl.pallas_call(
        sum_kernel,
        out_shape=shape((share, cols), BF),
        in_specs=[HBM] + [VMEM] * count,
        out_specs=VMEM,
        compiler_params=PARAMS,
    )(*pinned(output), *arrived)
    other_sum = partner(half_sum, "dom", half)
    dealt = pl.pallas_call(
        deal_kernel,
        out_shape=[shape((2 * width, cols), BF)] * half if direct else [shape((half, 2 * width, cols), BF)],
        in_specs=[VMEM] * 2,
        out_specs=[VMEM] * count,
        compiler_params=PARAMS,
    )(ghosts, mirror)
    dealt = swap(dealt) if direct else [exchange(dealt[0], halves)]
    part = pl.pallas_call(
        total_kernel,
        out_shape=shape((share, cols) if direct else (half, share, cols), BF),
        in_specs=[VMEM, VMEM],
        out_specs=VMEM,
        compiler_params=PARAMS,
    )(half_sum, other_sum)
    parts = swap([part] * half) if direct else [exchange(part, halves)]
    grad_features, grad_bias = pl.pallas_call(
        functools.partial(grad_kernel, scale, slots, hub_here),
        out_shape=(shape((rows, cols), BF), shape((1, cols), F32)),
        in_specs=[SMEM] * 2 + [VMEM] * (2 + count),
        out_specs=(VMEM,) * 2,
        scratch_shapes=[pltpu.VMEM((half, width, cols), BF)] * 2,
        compiler_params=PARAMS,
        cost_estimate=pl.CostEstimate(flops=2 * 10**9, bytes_accessed=10**6, transcendentals=0),
    )(side, seat, back, mark, *dealt)
    early = half - 1 if direct else 1
    grad_self, grad_neigh = pl.pallas_call(
        functools.partial(spread_kernel, scale),
        out_shape=(shape((depth, full), F32), shape((depth, full), F32)),
        in_specs=[SMEM] + [VMEM] * early,
        out_specs=(HBM,) * 2,
        scratch_shapes=[pltpu.VMEM((blocks, 2 * depth, cols), F32), pltpu.SemaphoreType.DMA((2 * blocks,))],
        compiler_params=PARAMS,
    )(seat, *parts[:early])
    if direct:
        grad_self, grad_neigh = pl.pallas_call(
            functools.partial(finish_kernel, scale, early),
            out_shape=(shape((depth, full), F32), shape((depth, full), F32)),
            in_specs=[SMEM, VMEM, HBM, HBM],
            out_specs=(HBM,) * 2,
            scratch_shapes=[pltpu.VMEM((1, 2 * depth, cols), F32), pltpu.SemaphoreType.DMA((2,))],
            input_output_aliases={2: 0, 3: 1},
            compiler_params=PARAMS,
        )(seat, parts[early], *pinned(grad_self, grad_neigh))
    return output, grad_features, grad_self, grad_neigh, grad_bias.reshape(cols)


def solution(mesh):
    placed = (
        P("dom", "feat"),
        P("feat", None),
        P("feat", None),
        P("feat"),
        P("dom", "feat"),
        P("dom", None, None, None),
        P("dom", None),
        P("dom"),
        P("dom", None, None),
        P("dom", None, None),
        P("dom", None, None),
        P("dom", None),
        P("dom", None),
        P("dom", None),
    )
    return jax.shard_map(
        on_device,
        mesh=mesh,
        in_specs=placed,
        out_specs=(P("dom", "feat"), P("dom", "feat"), P("feat", None), P("feat", None), P("feat")),
        check_vma=False,
    )
```

```python
import functools
import math

import jax
import jax.numpy as jnp
from jax import lax
from jax.experimental import pallas as pl
from jax.experimental.pallas import tpu as pltpu
from jax.sharding import PartitionSpec as P

BF = jnp.bfloat16
F32 = jnp.float32


def slot_places(peers, slots, width):
    lanes = peers * width
    lane = lax.broadcasted_iota(jnp.int32, (slots, lanes), 1)
    slot = lax.broadcasted_iota(jnp.int32, (slots, lanes), 0)
    return jnp.where(lane % width == slot, 1.0, 0.0).astype(BF)


def spread_rows(table, width, place=None):
    peers, slots = table.shape
    lanes = peers * width
    if place is None:
        place = slot_places(peers, slots, width)
    wide = jnp.dot(table.astype(BF), place, preferred_element_type=F32)
    peer = lax.broadcasted_iota(jnp.int32, (peers, lanes), 0)
    at = lax.broadcasted_iota(jnp.int32, (peers, lanes), 1)
    return jnp.sum(jnp.where(at // width == peer, wide, 0.0), axis=0, keepdims=True)


def source_matrix(send, hubs, rows, width, place=None):
    peers, slots = send.shape
    hub_here = hubs.shape[1]
    lanes = peers * width
    lane = lax.broadcasted_iota(jnp.int32, (1, lanes), 1) % width
    index = spread_rows(send.astype(F32), width, place)
    for k in range(hub_here):
        index = jnp.where(lane == slots + k, hubs[0:1, k : k + 1].astype(F32), index)
    index = jnp.where(lane < slots + hub_here, index, -1.0)
    row = lax.broadcasted_iota(jnp.int32, (rows, lanes), 0).astype(F32)
    return jnp.where(row == index, 1.0, 0.0).astype(BF)


def send_kernel(
    width, x_ref, cot_ref, ws_ref, wn_ref, bias_ref, send_ref, hub_ref, pos_ref, live_ref, tile_ref, dest_ref, gw_ref, hw_ref,
    out_ref, pack_ref, send_v, hub_v, pos_v, live_v, tile_v, dest_v, gw_v, hw_v, bias_v, place_ref, sems,
):
    rows, cols = x_ref.shape
    depth, full = ws_ref.shape
    blocks = full // cols
    base = 2 * blocks * depth
    moves = [
        (send_ref, send_v),
        (hub_ref, hub_v),
        (x_ref, pack_ref.at[base : base + rows, :]),
        (bias_ref, bias_v),
        (cot_ref, pack_ref.at[base + rows : base + 2 * rows, :]),
    ]
    for kind, w_ref in enumerate((ws_ref, wn_ref)):
        for j in range(blocks):
            at = (kind * blocks + j) * depth
            moves.append((w_ref.at[:, j * cols : (j + 1) * cols], pack_ref.at[at : at + depth, :]))
    moves += [
        (pos_ref, pos_v), (live_ref, live_v), (tile_ref, tile_v), (dest_ref, dest_v),
        (gw_ref, gw_v), (hw_ref, hw_v),
    ]
    copies = [pltpu.make_async_copy(src, dst, sems.at[i]) for i, (src, dst) in enumerate(moves)]
    for copy in copies:
        copy.start()
    peers, slots = send_v.shape[1:]
    place_ref[...] = slot_places(peers, slots, width)
    for copy in copies[:2]:
        copy.wait()
    mark = source_matrix(send_v[0], hub_v[...], rows, width, place_ref[...])
    copies[2].wait()
    taken = lax.dot_general(
        mark, pack_ref[base : base + rows, :], (((0,), (0,)), ((), ())), preferred_element_type=F32
    ).astype(BF)
    kept = out_ref.shape[1]
    for q in range(peers):
        out_ref[q] = taken[q * width : q * width + kept]
    for copy in copies[3:]:
        copy.wait()
    pack_ref[base + 2 * rows :, :] = jnp.broadcast_to(bias_v[...], (16, cols))


def mix_kernel(width, count_ref, send_v, hub_v, pos_v, live_v, tile_v, dest_v, gw_v, hw_v, mix_ref, turned_ref, mark_ref):
    rows = mix_ref.shape[0]
    tiles, tile = tile_v.shape[1:3]
    peers, slots = dest_v.shape[1:]
    side = rows // tile
    lanes = peers * width
    hubs = hw_v.shape[0]
    hub_here = hubs // peers
    for r in range(side):
        for c in range(side):
            total = jnp.zeros((tile, tile), BF)
            for t in range(tiles):
                used = jnp.logical_and(pos_v[0:1, t : t + 1] == r * side + c, t < count_ref[...])
                total = jnp.where(used, tile_v[0, t], total)
            mix_ref[r * tile : (r + 1) * tile, c * tile : (c + 1) * tile] = total
    dest = spread_rows(dest_v[0].astype(F32), width)
    coef = spread_rows(gw_v[0], width)
    peer = lax.broadcasted_iota(jnp.int32, (peers, lanes), 0)
    at = lax.broadcasted_iota(jnp.int32, (peers, lanes), 1)
    owner = jnp.where(at // width == peer, 1.0, 0.0).astype(BF)
    limit = jnp.dot(live_v[...].astype(F32).astype(BF), owner, preferred_element_type=F32)
    lane = lax.broadcasted_iota(jnp.int32, (1, lanes), 1) % width
    coef = jnp.where(jnp.logical_and(lane.astype(F32) < limit, lane < slots), coef, 0.0)
    row = lax.broadcasted_iota(jnp.int32, (rows, lanes), 0).astype(F32)
    ghost = jnp.where(row == dest, coef, 0.0)
    hub = lax.broadcasted_iota(jnp.int32, (hubs, lanes), 0)
    at = lax.broadcasted_iota(jnp.int32, (hubs, lanes), 1)
    place = jnp.where(
        jnp.logical_and(at // width == hub // hub_here, at % width == slots + hub % hub_here), 1.0, 0.0
    ).astype(BF)
    hub_mix = lax.dot_general(hw_v[...], place, (((0,), (0,)), ((), ())), preferred_element_type=F32)
    mix_ref[:, rows:] = (ghost + hub_mix).astype(BF)
    turned_ref[...] = mix_ref[...].T
    mark_ref[...] = source_matrix(send_v[0], hub_v[...], rows, width)


def neigh_kernel(x_ref, mix_ref, far_ref, got_ref, neigh_ref, passed_ref, wide_ref):
    rows, cols = x_ref.shape
    lanes = mix_ref.shape[1] - rows
    wide_ref[...] = jnp.zeros_like(wide_ref)
    wide_ref[:, : got_ref.shape[1], :] = got_ref[...]
    total = jnp.dot(mix_ref[:, :rows], x_ref[...], preferred_element_type=F32)
    total = total + jnp.dot(mix_ref[:, rows:], wide_ref[...].reshape(lanes, cols), preferred_element_type=F32)
    neigh_ref[...] = total.astype(BF)


def ghost_rows(slots, hub_here, width, start, peers, turned_ref, neigh_grad, sums):
    rows, cols = neigh_grad.shape
    high = sums.astype(BF).astype(F32)
    line = lax.broadcasted_iota(jnp.int32, (peers * width, cols), 0) % width
    cut = pl.ds(pl.multiple_of(rows + start * width, 16), peers * width)
    away = jnp.dot(turned_ref[cut, :], neigh_grad, preferred_element_type=F32)
    away = jnp.where(line == slots + hub_here, high, away)
    away = jnp.where(line == slots + hub_here + 1, sums - high, away)
    return away.astype(BF)


def dense_kernel(slots, hub_here, feats, width, count, me_ref, side_ref, seat_ref, x_ref, ws_ref, wn_ref, turned_ref, *refs):
    pack_refs, n_refs = refs[:feats], refs[feats : 2 * feats]
    own_ref, cot_ref, slope_ref, sums_ref, mirror_ref = refs[2 * feats : 2 * feats + 5]
    send_refs = refs[2 * feats + 5 : 2 * feats + 5 + count]
    pre_ref, bias_ref = refs[2 * feats + 5 + count :]
    rows, cols = x_ref.shape
    depth, full = ws_ref.shape
    blocks = full // cols
    half = mirror_ref.shape[0]
    share = send_refs[0].shape[-2]
    me = me_ref[0]
    base = 2 * blocks * depth
    left = []
    for d, pack in enumerate(pack_refs):
        owner = me ^ d
        cut = pl.ds(pl.multiple_of(owner * cols, cols), cols)
        cot_ref[:, cut] = pack[base + rows : base + 2 * rows, :]
        bias_ref[:, cut] = pack[base + 2 * rows : base + 2 * rows + 16, :]
        left += [pack[base : base + rows, :], n_refs[d][...]]
    left = jnp.concatenate(left, axis=1)
    into = jnp.zeros((rows, depth), F32)
    span = 2
    for j in range(0, blocks, span):
        right = [
            jnp.concatenate([pack[(kind * blocks + i) * depth : (kind * blocks + i + 1) * depth, :] for i in range(j, j + span)], axis=1)
            for pack in pack_refs
            for kind in range(2)
        ]
        cut = slice(j * cols, (j + span) * cols)
        pre = jnp.dot(left, jnp.concatenate(right, axis=0), preferred_element_type=F32)
        pre = pre + bias_ref[0:1, cut].astype(F32)
        pre_ref[:, cut] = pre
        sig = jax.nn.sigmoid(pre)
        grad = (cot_ref[:, cut].astype(F32) * sig * (1.0 + pre * (1.0 - sig))).astype(BF)
        cot_ref[:, cut] = grad
        into = into + lax.dot_general(
            grad, wn_ref[:, cut], (((1,), (1,)), ((), ())), preferred_element_type=F32
        )
    mine = pl.ds(pl.multiple_of(me * cols, cols), cols)
    own_ref[...] = pre_ref[:, mine]
    neigh_grad = into.astype(BF)
    slope_ref[...] = neigh_grad
    sums = jnp.sum(cot_ref[:, mine].astype(F32), axis=0, keepdims=True)
    sums_ref[...] = sums
    there = half - side_ref[0] * half
    pair = jnp.concatenate([x_ref[...], n_refs[0][...]], axis=1).T
    if count > 1:
        for k, ref in enumerate(send_refs):
            peer = seat_ref[0] ^ k
            away = ghost_rows(slots, hub_here, width, there + peer, 1, turned_ref, neigh_grad, sums)
            mirror_ref[k] = away[: mirror_ref.shape[1]]
            block = cot_ref[:, pl.ds(pl.multiple_of(peer * cols, cols), cols)]
            ref[...] = jnp.dot(pair, block, preferred_element_type=F32).astype(BF)
        return
    send_ref = send_refs[0]
    away = ghost_rows(slots, hub_here, width, there, half, turned_ref, neigh_grad, sums).reshape(half, width, cols)
    mirror_ref[...] = away[:, : mirror_ref.shape[1]]
    weights = jnp.dot(pair, cot_ref[...], preferred_element_type=F32).astype(BF)
    step = min(share, depth)
    for j in range(blocks):
        for kind in range(2):
            block = weights[kind * depth : (kind + 1) * depth, j * cols : (j + 1) * cols]
            for part in range(depth // step):
                at = (j * 2 + kind) * depth + part * step
                low = at % share
                send_ref[at // share, low : low + step, :] = block[part * step : (part + 1) * step]


def seated(refs, seat):
    if len(refs) == 1:
        return [(j, refs[0].at[j]) for j in range(refs[0].shape[0])]
    return [(seat ^ k, ref) for k, ref in enumerate(refs)]


def side_kernel(
    slots, hub_here, count, side_ref, seat_ref, own_ref, grad_ref, slope_ref, sums_ref, turned_ref, ws_ref,
    out_ref, back_ref, ghost_ref,
):
    own = own_ref[...]
    out_ref[...] = (own * jax.nn.sigmoid(own)).astype(BF)
    rows, cols = own.shape
    half, width = ghost_ref.shape[:2]
    slope, sums = slope_ref[...], sums_ref[...]
    back = lax.dot_general(grad_ref[...], ws_ref[...], (((1,), (1,)), ((), ())), preferred_element_type=F32)
    back_ref[...] = back + jnp.dot(turned_ref[:rows, :], slope, preferred_element_type=F32)
    here = side_ref[0] * half
    if count > 1:
        for k in range(half):
            peer = here + (seat_ref[0] ^ k)
            ghost_ref[k] = ghost_rows(slots, hub_here, width, peer, 1, turned_ref, slope, sums)
        return
    ghost_ref[...] = ghost_rows(slots, hub_here, width, here, half, turned_ref, slope, sums).reshape(half, width, cols)


def sum_kernel(stored_ref, *refs):
    got_refs, sum_ref = refs[:-1], refs[-1]
    total = jnp.zeros(sum_ref.shape, F32)
    for got_ref in got_refs if len(got_refs) > 1 else [got_refs[0].at[j] for j in range(got_refs[0].shape[0])]:
        total = total + got_ref[...].astype(F32)
    sum_ref[...] = total.astype(BF)


def deal_kernel(ghost_ref, mirror_ref, *out_refs):
    width = ghost_ref.shape[1]
    for k in range(ghost_ref.shape[0]):
        out_ref = out_refs[k] if len(out_refs) > 1 else out_refs[0].at[k]
        out_ref[:width, :] = ghost_ref[k]
        out_ref[width:, :] = jnp.zeros(ghost_ref.shape[1:], BF)
        out_ref[width : width + mirror_ref.shape[1], :] = mirror_ref[k]


def total_kernel(own_ref, other_ref, part_ref):
    total = (own_ref[...].astype(F32) + other_ref[...].astype(F32)).astype(BF)
    part_ref[...] = jnp.broadcast_to(total, part_ref.shape)


def near_rows(slots, hub_here, start, mark_ref, got_ref):
    half, width, cols = got_ref.shape
    cut = pl.ds(pl.multiple_of(start * width, 128), half * width)
    added = jnp.dot(mark_ref[:, cut], got_ref[...].reshape(half * width, cols), preferred_element_type=F32)
    first = slots + hub_here
    bias = jnp.zeros((2, cols), F32)
    for j in range(half):
        bias = bias + got_ref[j, first : first + 2, :].astype(F32)
    return added, jnp.sum(bias, axis=0, keepdims=True)


def grad_kernel(scale, slots, hub_here, side_ref, seat_ref, back_ref, mark_ref, *refs):
    got_refs, (grad_ref, bias_ref, near_ref, far_ref) = refs[:-4], refs[-4:]
    half, width = near_ref.shape[:2]
    for j, got_ref in seated(got_refs, seat_ref[0]):
        near_ref[j] = got_ref[:width, :]
        far_ref[j] = got_ref[width:, :]
    here = side_ref[0] * half
    near, near_bias = near_rows(slots, hub_here, here, mark_ref, near_ref)
    far, far_bias = near_rows(slots, hub_here, half - here, mark_ref, far_ref)
    grad_ref[...] = (back_ref[...] + near + far).astype(BF)
    bias_ref[...] = (near_bias + far_bias) * scale


def write_blocks(scale, parts, self_ref, neigh_ref, wide_ref, sems):
    depth, full = self_ref.shape
    cols = wide_ref.shape[-1]
    copies = []
    for at, (j, part) in enumerate(parts):
        wide_ref[at] = part.astype(F32) * scale
        cut = pl.ds(pl.multiple_of(j * cols, cols), cols)
        for kind, out_ref in enumerate((self_ref, neigh_ref)):
            copy = pltpu.make_async_copy(
                wide_ref.at[at, kind * depth : (kind + 1) * depth, :], out_ref.at[:, cut], sems.at[2 * at + kind]
            )
            copy.start()
            copies.append(copy)
    for copy in copies:
        copy.wait()


def spread_kernel(scale, seat_ref, *refs):
    got_refs, (self_ref, neigh_ref, wide_ref, sems) = refs[:-4], refs[-4:]
    depth, full = self_ref.shape
    cols = wide_ref.shape[-1]
    if len(got_refs) > 1:
        parts = [(j, ref[...]) for j, ref in seated(got_refs, seat_ref[0])]
    else:
        whole = got_refs[0][...].reshape(2 * full // cols * depth, cols)
        parts = [(j, whole[2 * j * depth : 2 * (j + 1) * depth]) for j in range(full // cols)]
    write_blocks(scale, parts, self_ref, neigh_ref, wide_ref, sems)


def finish_kernel(scale, k, seat_ref, got_ref, begun_self_ref, begun_neigh_ref, self_ref, neigh_ref, wide_ref, sems):
    write_blocks(scale, [(seat_ref[0] ^ k, got_ref[...])], self_ref, neigh_ref, wide_ref, sems)


VMEM = pl.BlockSpec(memory_space=pltpu.VMEM)
SMEM = pl.BlockSpec(memory_space=pltpu.SMEM)
ANY = pl.BlockSpec(memory_space=pl.ANY)
HBM = pl.BlockSpec(memory_space=pltpu.HBM)
PARAMS = pltpu.CompilerParams(vmem_limit_bytes=40 * 1024 * 1024)


def shape(dims, kind):
    return jax.ShapeDtypeStruct(dims, kind)


def partner(block, axis, k):
    return lax.ppermute(block, axis, [(i, i ^ k) for i in range(lax.axis_size(axis))])


def exchange(blocks, groups=None):
    return lax.all_to_all(blocks, "dom", split_axis=0, concat_axis=0, axis_index_groups=groups, tiled=True)


def swap(blocks):
    return [blocks[0]] + [partner(block, "dom", k) for k, block in enumerate(blocks) if k]


def on_device(
    features,
    w_self,
    w_neigh,
    bias,
    cotangent,
    tile_vals,
    tile_pos,
    tile_count,
    send_rows,
    recv_dest,
    ghost_weight,
    recv_count,
    hub_rows,
    hub_weight,
):
    rows, cols = features.shape
    depth, full = w_self.shape
    blocks = full // cols
    peers, slots = send_rows.shape[1:]
    hub_here = hub_rows.shape[-1]
    width = -(-(slots + hub_here + 2) // 16) * 16
    sent = -(-(slots + hub_here + 2) // 8) * 8
    lanes = peers * width
    half = peers // 2
    share = 2 * blocks * depth // half
    direct = half == blocks
    count = half if direct else 1
    halves = [list(range(half)), list(range(half, peers))]
    scale = 1.0 / math.sqrt(peers * rows)
    feats = lax.axis_size("feat")
    me = lax.axis_index("feat").astype(jnp.int32).reshape(1)
    side = (lax.axis_index("dom") >= half).astype(jnp.int32).reshape(1)
    seat = lax.rem(lax.axis_index("dom"), half).astype(jnp.int32).reshape(1)
    pack_rows = 2 * blocks * depth + 2 * rows + 16

    def pinned(*arrays):
        return [pltpu.with_memory_space_constraint(a, pltpu.HBM) for a in arrays]

    first = pinned(features, cotangent, w_self, w_neigh, bias.reshape(1, cols), send_rows, hub_rows)
    edges = pinned(tile_pos, recv_count, tile_vals, recv_dest, ghost_weight, hub_weight.T)
    moved = (send_rows, hub_rows, *edges)
    outgoing, pack, *moved = pl.pallas_call(
        functools.partial(send_kernel, width),
        out_shape=(
            shape((peers, sent, cols), BF),
            shape((pack_rows, cols), BF),
            *(shape(a.shape, a.dtype) for a in moved),
        ),
        in_specs=[HBM] * (len(first) + len(edges)),
        out_specs=(VMEM,) * (2 + len(moved)),
        scratch_shapes=[
            pltpu.VMEM((1, cols), BF),
            pltpu.VMEM((slots, lanes), BF),
            pltpu.SemaphoreType.DMA((11 + 2 * blocks,)),
        ],
        compiler_params=PARAMS,
    )(*first, *edges)

    far = partner(pack, "feat", 2)
    near = partner(pack, "feat", 1)
    incoming = exchange(outgoing)
    mix, turned, mark = pl.pallas_call(
        functools.partial(mix_kernel, width),
        out_shape=(
            shape((rows, rows + lanes), BF),
            shape((rows + lanes, rows), BF),
            shape((rows, lanes), BF),
        ),
        in_specs=[VMEM] * (1 + len(moved)),
        out_specs=(VMEM,) * 3,
        compiler_params=PARAMS,
        cost_estimate=pl.CostEstimate(flops=10**8, bytes_accessed=3 * 10**6, transcendentals=0),
    )(tile_count.reshape(1, 1), *moved)
    neigh, far = pl.pallas_call(
        neigh_kernel,
        out_shape=(shape((rows, cols), BF), shape((pack_rows, cols), BF)),
        in_specs=[VMEM, VMEM, ANY, VMEM],
        out_specs=(VMEM, ANY),
        input_output_aliases={2: 1},
        scratch_shapes=[pltpu.VMEM((peers, width, cols), BF)],
        compiler_params=PARAMS,
    )(features, mix, far, incoming)
    last = partner(far, "feat", 1)
    far_neigh = partner(neigh, "feat", 2)
    every = [neigh, partner(neigh, "feat", 1), far_neigh, partner(far_neigh, "feat", 1)]

    own, grad, slope, sums, mirror, *returned = pl.pallas_call(
        functools.partial(dense_kernel, slots, hub_here, feats, width, count),
        out_shape=(
            shape((rows, cols), F32),
            shape((rows, full), BF),
            shape((rows, cols), BF),
            shape((1, cols), F32),
            shape((half, sent, cols), BF),
            *([shape((share, cols), BF)] * half if direct else [shape((half, share, cols), BF)]),
        ),
        in_specs=[SMEM] * 3 + [VMEM] * (4 + 2 * feats),
        out_specs=(VMEM,) * (5 + count),
        scratch_shapes=[
            pltpu.VMEM((rows, full), F32),
            pltpu.VMEM((16, full), BF),
        ],
        compiler_params=PARAMS,
    )(me, side, seat, features, w_self, w_neigh, turned, pack, near, far, last, *every)

    arrived = swap(returned) if direct else [exchange(returned[0], halves)]
    if direct:
        arrived = arrived[-2:0:-1] + arrived[-1:] + arrived[:1]
    mirror = partner(mirror, "dom", half)
    output, back, ghosts = pl.pallas_call(
        functools.partial(side_kernel, slots, hub_here, count),
        out_shape=(shape((rows, cols), BF), shape((rows, cols), F32), shape((half, width, cols), BF)),
        in_specs=[SMEM] * 2 + [VMEM] * 6,
        out_specs=(VMEM,) * 3,
        compiler_params=PARAMS,
        cost_estimate=pl.CostEstimate(flops=10**8, bytes_accessed=10**6, transcendentals=0),
    )(side, seat, own, grad, slope, sums, turned, w_self)
    half_sum = pl.pallas_call(
        sum_kernel,
        out_shape=shape((share, cols), BF),
        in_specs=[HBM] + [VMEM] * count,
        out_specs=VMEM,
        compiler_params=PARAMS,
    )(*pinned(output), *arrived)
    other_sum = partner(half_sum, "dom", half)
    dealt = pl.pallas_call(
        deal_kernel,
        out_shape=[shape((2 * width, cols), BF)] * half if direct else [shape((half, 2 * width, cols), BF)],
        in_specs=[VMEM] * 2,
        out_specs=[VMEM] * count,
        compiler_params=PARAMS,
    )(ghosts, mirror)
    dealt = swap(dealt) if direct else [exchange(dealt[0], halves)]
    part = pl.pallas_call(
        total_kernel,
        out_shape=shape((share, cols) if direct else (half, share, cols), BF),
        in_specs=[VMEM, VMEM],
        out_specs=VMEM,
        compiler_params=PARAMS,
    )(half_sum, other_sum)
    parts = swap([part] * half) if direct else [exchange(part, halves)]
    grad_features, grad_bias = pl.pallas_call(
        functools.partial(grad_kernel, scale, slots, hub_here),
        out_shape=(shape((rows, cols), BF), shape((1, cols), F32)),
        in_specs=[SMEM] * 2 + [VMEM] * (2 + count),
        out_specs=(VMEM,) * 2,
        scratch_shapes=[pltpu.VMEM((half, width, cols), BF)] * 2,
        compiler_params=PARAMS,
        cost_estimate=pl.CostEstimate(flops=2 * 10**9, bytes_accessed=10**6, transcendentals=0),
    )(side, seat, back, mark, *dealt)
    early = half - 1 if direct else 1
    grad_self, grad_neigh = pl.pallas_call(
        functools.partial(spread_kernel, scale),
        out_shape=(shape((depth, full), F32), shape((depth, full), F32)),
        in_specs=[SMEM] + [VMEM] * early,
        out_specs=(HBM,) * 2,
        scratch_shapes=[pltpu.VMEM((blocks, 2 * depth, cols), F32), pltpu.SemaphoreType.DMA((2 * blocks,))],
        compiler_params=PARAMS,
    )(seat, *parts[:early])
    if direct:
        grad_self, grad_neigh = pl.pallas_call(
            functools.partial(finish_kernel, scale, early),
            out_shape=(shape((depth, full), F32), shape((depth, full), F32)),
            in_specs=[SMEM, VMEM, HBM, HBM],
            out_specs=(HBM,) * 2,
            scratch_shapes=[pltpu.VMEM((1, 2 * depth, cols), F32), pltpu.SemaphoreType.DMA((2,))],
            input_output_aliases={2: 0, 3: 1},
            compiler_params=PARAMS,
        )(seat, parts[early], *pinned(grad_self, grad_neigh))
    return output, grad_features, grad_self, grad_neigh, grad_bias.reshape(cols)


def solution(mesh):
    placed = (
        P("dom", "feat"),
        P("feat", None),
        P("feat", None),
        P("feat"),
        P("dom", "feat"),
        P("dom", None, None, None),
        P("dom", None),
        P("dom"),
        P("dom", None, None),
        P("dom", None, None),
        P("dom", None, None),
        P("dom", None),
        P("dom", None),
        P("dom", None),
    )
    return jax.shard_map(
        on_device,
        mesh=mesh,
        in_specs=placed,
        out_specs=(P("dom", "feat"), P("dom", "feat"), P("feat", None), P("feat", None), P("feat")),
        check_vma=False,
    )
```

```python
import functools
import math

import jax
import jax.numpy as jnp
from jax import lax
from jax.experimental import pallas as pl
from jax.experimental.pallas import tpu as pltpu
from jax.sharding import PartitionSpec as P

BF = jnp.bfloat16
F32 = jnp.float32


def slot_places(peers, slots, width):
    lanes = peers * width
    lane = lax.broadcasted_iota(jnp.int32, (slots, lanes), 1)
    slot = lax.broadcasted_iota(jnp.int32, (slots, lanes), 0)
    return jnp.where(lane % width == slot, 1.0, 0.0).astype(BF)


def spread_rows(table, width, place=None):
    peers, slots = table.shape
    lanes = peers * width
    if place is None:
        place = slot_places(peers, slots, width)
    wide = jnp.dot(table.astype(BF), place, preferred_element_type=F32)
    peer = lax.broadcasted_iota(jnp.int32, (peers, lanes), 0)
    at = lax.broadcasted_iota(jnp.int32, (peers, lanes), 1)
    return jnp.sum(jnp.where(at // width == peer, wide, 0.0), axis=0, keepdims=True)


def source_matrix(send, hubs, rows, width, place=None):
    peers, slots = send.shape
    hub_here = hubs.shape[1]
    lanes = peers * width
    lane = lax.broadcasted_iota(jnp.int32, (1, lanes), 1) % width
    index = spread_rows(send.astype(F32), width, place)
    for k in range(hub_here):
        index = jnp.where(lane == slots + k, hubs[0:1, k : k + 1].astype(F32), index)
    index = jnp.where(lane < slots + hub_here, index, -1.0)
    row = lax.broadcasted_iota(jnp.int32, (rows, lanes), 0).astype(F32)
    return jnp.where(row == index, 1.0, 0.0).astype(BF)


def send_kernel(
    width, x_ref, cot_ref, ws_ref, wn_ref, bias_ref, send_ref, hub_ref, pos_ref, live_ref, tile_ref, dest_ref, gw_ref, hw_ref,
    out_ref, pack_ref, send_v, hub_v, pos_v, live_v, tile_v, dest_v, gw_v, hw_v, bias_v, place_ref, taken_ref, sems,
):
    rows, cols = x_ref.shape
    depth, full = ws_ref.shape
    blocks = full // cols
    base = 2 * blocks * depth
    moves = [
        (send_ref, send_v),
        (hub_ref, hub_v),
        (x_ref, pack_ref.at[base : base + rows, :]),
        (bias_ref, bias_v),
        (cot_ref, pack_ref.at[base + rows : base + 2 * rows, :]),
    ]
    for kind, w_ref in enumerate((ws_ref, wn_ref)):
        for j in range(blocks):
            at = (kind * blocks + j) * depth
            moves.append((w_ref.at[:, j * cols : (j + 1) * cols], pack_ref.at[at : at + depth, :]))
    moves += [
        (pos_ref, pos_v), (live_ref, live_v), (tile_ref, tile_v), (dest_ref, dest_v),
        (gw_ref, gw_v), (hw_ref, hw_v),
    ]
    copies = [pltpu.make_async_copy(src, dst, sems.at[i]) for i, (src, dst) in enumerate(moves)]
    for copy in copies:
        copy.start()
    peers, slots = send_v.shape[1:]
    place_ref[...] = slot_places(peers, slots, width)
    for copy in copies[:2]:
        copy.wait()
    mark = source_matrix(send_v[0], hub_v[...], rows, width, place_ref[...])
    copies[2].wait()
    kept = out_ref.shape[1]
    half = peers // 2
    for part in range(2):
        taken = lax.dot_general(
            mark[:, part * half * width : (part + 1) * half * width],
            pack_ref[base : base + rows, :],
            (((0,), (0,)), ((), ())),
            preferred_element_type=F32,
        ).astype(BF)
        for q in range(half):
            taken_ref[part * half + q] = taken[q * width : q * width + kept]
        mine = pl.ds(part * half, half)
        copies.append(pltpu.make_async_copy(taken_ref.at[mine], out_ref.at[mine], sems.at[len(copies)]))
        copies[-1].start()
    copies[3].wait()
    pack_ref[base + 2 * rows :, :] = jnp.broadcast_to(bias_v[...], (16, cols))
    for copy in copies[4:]:
        copy.wait()


def mix_kernel(width, count_ref, send_v, hub_v, pos_v, live_v, tile_v, dest_v, gw_v, hw_v, mix_ref, turned_ref, mark_ref):
    rows = mix_ref.shape[0]
    tiles, tile = tile_v.shape[1:3]
    peers, slots = dest_v.shape[1:]
    side = rows // tile
    lanes = peers * width
    hubs = hw_v.shape[0]
    hub_here = hubs // peers
    for r in range(side):
        for c in range(side):
            total = jnp.zeros((tile, tile), BF)
            for t in range(tiles):
                used = jnp.logical_and(pos_v[0:1, t : t + 1] == r * side + c, t < count_ref[...])
                total = jnp.where(used, tile_v[0, t], total)
            mix_ref[r * tile : (r + 1) * tile, c * tile : (c + 1) * tile] = total
    dest = spread_rows(dest_v[0].astype(F32), width)
    coef = spread_rows(gw_v[0], width)
    peer = lax.broadcasted_iota(jnp.int32, (peers, lanes), 0)
    at = lax.broadcasted_iota(jnp.int32, (peers, lanes), 1)
    owner = jnp.where(at // width == peer, 1.0, 0.0).astype(BF)
    limit = jnp.dot(live_v[...].astype(F32).astype(BF), owner, preferred_element_type=F32)
    lane = lax.broadcasted_iota(jnp.int32, (1, lanes), 1) % width
    coef = jnp.where(jnp.logical_and(lane.astype(F32) < limit, lane < slots), coef, 0.0)
    row = lax.broadcasted_iota(jnp.int32, (rows, lanes), 0).astype(F32)
    ghost = jnp.where(row == dest, coef, 0.0)
    hub = lax.broadcasted_iota(jnp.int32, (hubs, lanes), 0)
    at = lax.broadcasted_iota(jnp.int32, (hubs, lanes), 1)
    place = jnp.where(
        jnp.logical_and(at // width == hub // hub_here, at % width == slots + hub % hub_here), 1.0, 0.0
    ).astype(BF)
    hub_mix = lax.dot_general(hw_v[...], place, (((0,), (0,)), ((), ())), preferred_element_type=F32)
    mix_ref[:, rows:] = (ghost + hub_mix).astype(BF)
    turned_ref[...] = mix_ref[...].T
    mark_ref[...] = source_matrix(send_v[0], hub_v[...], rows, width)


def neigh_kernel(x_ref, mix_ref, far_ref, got_ref, neigh_ref, passed_ref, wide_ref):
    rows, cols = x_ref.shape
    lanes = mix_ref.shape[1] - rows
    wide_ref[...] = jnp.zeros_like(wide_ref)
    wide_ref[:, : got_ref.shape[1], :] = got_ref[...]
    total = jnp.dot(mix_ref[:, :rows], x_ref[...], preferred_element_type=F32)
    total = total + jnp.dot(mix_ref[:, rows:], wide_ref[...].reshape(lanes, cols), preferred_element_type=F32)
    neigh_ref[...] = total.astype(BF)


def ghost_rows(slots, hub_here, width, start, peers, turned_ref, neigh_grad, sums):
    rows, cols = neigh_grad.shape
    high = sums.astype(BF).astype(F32)
    line = lax.broadcasted_iota(jnp.int32, (peers * width, cols), 0) % width
    cut = pl.ds(pl.multiple_of(rows + start * width, 16), peers * width)
    away = jnp.dot(turned_ref[cut, :], neigh_grad, preferred_element_type=F32)
    away = jnp.where(line == slots + hub_here, high, away)
    away = jnp.where(line == slots + hub_here + 1, sums - high, away)
    return away.astype(BF)


def dense_kernel(slots, hub_here, feats, width, count, me_ref, side_ref, seat_ref, x_ref, ws_ref, wn_ref, turned_ref, *refs):
    pack_refs, n_refs = refs[:feats], refs[feats : 2 * feats]
    own_ref, cot_ref, slope_ref, sums_ref, mirror_ref = refs[2 * feats : 2 * feats + 5]
    send_refs = refs[2 * feats + 5 : 2 * feats + 5 + count]
    pre_ref, bias_ref = refs[2 * feats + 5 + count :]
    rows, cols = x_ref.shape
    depth, full = ws_ref.shape
    blocks = full // cols
    half = mirror_ref.shape[0]
    share = send_refs[0].shape[-2]
    me = me_ref[0]
    base = 2 * blocks * depth
    left = []
    for d, pack in enumerate(pack_refs):
        owner = me ^ d
        cut = pl.ds(pl.multiple_of(owner * cols, cols), cols)
        cot_ref[:, cut] = pack[base + rows : base + 2 * rows, :]
        bias_ref[:, cut] = pack[base + 2 * rows : base + 2 * rows + 16, :]
        left += [pack[base : base + rows, :], n_refs[d][...]]
    left = jnp.concatenate(left, axis=1)
    into = jnp.zeros((rows, depth), F32)
    span = 2
    for j in range(0, blocks, span):
        right = [
            jnp.concatenate([pack[(kind * blocks + i) * depth : (kind * blocks + i + 1) * depth, :] for i in range(j, j + span)], axis=1)
            for pack in pack_refs
            for kind in range(2)
        ]
        cut = slice(j * cols, (j + span) * cols)
        pre = jnp.dot(left, jnp.concatenate(right, axis=0), preferred_element_type=F32)
        pre = pre + bias_ref[0:1, cut].astype(F32)
        pre_ref[:, cut] = pre
        sig = jax.nn.sigmoid(pre)
        grad = (cot_ref[:, cut].astype(F32) * sig * (1.0 + pre * (1.0 - sig))).astype(BF)
        cot_ref[:, cut] = grad
        into = into + lax.dot_general(
            grad, wn_ref[:, cut], (((1,), (1,)), ((), ())), preferred_element_type=F32
        )
    mine = pl.ds(pl.multiple_of(me * cols, cols), cols)
    own_ref[...] = pre_ref[:, mine]
    neigh_grad = into.astype(BF)
    slope_ref[...] = neigh_grad
    sums = jnp.sum(cot_ref[:, mine].astype(F32), axis=0, keepdims=True)
    sums_ref[...] = sums
    there = half - side_ref[0] * half
    pair = jnp.concatenate([x_ref[...], n_refs[0][...]], axis=1).T
    if count > 1:
        for k, ref in enumerate(send_refs):
            peer = seat_ref[0] ^ k
            away = ghost_rows(slots, hub_here, width, there + peer, 1, turned_ref, neigh_grad, sums)
            mirror_ref[k] = away[: mirror_ref.shape[1]]
            block = cot_ref[:, pl.ds(pl.multiple_of(peer * cols, cols), cols)]
            ref[...] = jnp.dot(pair, block, preferred_element_type=F32).astype(BF)
        return
    send_ref = send_refs[0]
    away = ghost_rows(slots, hub_here, width, there, half, turned_ref, neigh_grad, sums).reshape(half, width, cols)
    mirror_ref[...] = away[:, : mirror_ref.shape[1]]
    weights = jnp.dot(pair, cot_ref[...], preferred_element_type=F32).astype(BF)
    step = min(share, depth)
    for j in range(blocks):
        for kind in range(2):
            block = weights[kind * depth : (kind + 1) * depth, j * cols : (j + 1) * cols]
            for part in range(depth // step):
                at = (j * 2 + kind) * depth + part * step
                low = at % share
                send_ref[at // share, low : low + step, :] = block[part * step : (part + 1) * step]


def seated(refs, seat):
    if len(refs) == 1:
        return [(j, refs[0].at[j]) for j in range(refs[0].shape[0])]
    return [(seat ^ k, ref) for k, ref in enumerate(refs)]


def side_kernel(
    slots, hub_here, count, side_ref, seat_ref, own_ref, grad_ref, slope_ref, sums_ref, turned_ref, ws_ref,
    out_ref, back_ref, ghost_ref,
):
    own = own_ref[...]
    out_ref[...] = (own * jax.nn.sigmoid(own)).astype(BF)
    rows, cols = own.shape
    half, width = ghost_ref.shape[:2]
    slope, sums = slope_ref[...], sums_ref[...]
    back = lax.dot_general(grad_ref[...], ws_ref[...], (((1,), (1,)), ((), ())), preferred_element_type=F32)
    back_ref[...] = back + jnp.dot(turned_ref[:rows, :], slope, preferred_element_type=F32)
    here = side_ref[0] * half
    if count > 1:
        for k in range(half):
            peer = here + (seat_ref[0] ^ k)
            ghost_ref[k] = ghost_rows(slots, hub_here, width, peer, 1, turned_ref, slope, sums)
        return
    ghost_ref[...] = ghost_rows(slots, hub_here, width, here, half, turned_ref, slope, sums).reshape(half, width, cols)


def sum_kernel(stored_ref, *refs):
    got_refs, sum_ref = refs[:-1], refs[-1]
    total = jnp.zeros(sum_ref.shape, F32)
    for got_ref in got_refs if len(got_refs) > 1 else [got_refs[0].at[j] for j in range(got_refs[0].shape[0])]:
        total = total + got_ref[...].astype(F32)
    sum_ref[...] = total.astype(BF)


def deal_kernel(ghost_ref, mirror_ref, *out_refs):
    width = ghost_ref.shape[1]
    for k in range(ghost_ref.shape[0]):
        out_ref = out_refs[k] if len(out_refs) > 1 else out_refs[0].at[k]
        out_ref[:width, :] = ghost_ref[k]
        out_ref[width:, :] = jnp.zeros(ghost_ref.shape[1:], BF)
        out_ref[width : width + mirror_ref.shape[1], :] = mirror_ref[k]


def total_kernel(own_ref, other_ref, part_ref):
    total = (own_ref[...].astype(F32) + other_ref[...].astype(F32)).astype(BF)
    part_ref[...] = jnp.broadcast_to(total, part_ref.shape)


def near_rows(slots, hub_here, start, mark_ref, got_ref):
    half, width, cols = got_ref.shape
    cut = pl.ds(pl.multiple_of(start * width, 128), half * width)
    added = jnp.dot(mark_ref[:, cut], got_ref[...].reshape(half * width, cols), preferred_element_type=F32)
    first = slots + hub_here
    bias = jnp.zeros((2, cols), F32)
    for j in range(half):
        bias = bias + got_ref[j, first : first + 2, :].astype(F32)
    return added, jnp.sum(bias, axis=0, keepdims=True)


def grad_kernel(scale, slots, hub_here, side_ref, seat_ref, back_ref, mark_ref, *refs):
    got_refs, (grad_ref, bias_ref, near_ref, far_ref) = refs[:-4], refs[-4:]
    half, width = near_ref.shape[:2]
    for j, got_ref in seated(got_refs, seat_ref[0]):
        near_ref[j] = got_ref[:width, :]
        far_ref[j] = got_ref[width:, :]
    here = side_ref[0] * half
    near, near_bias = near_rows(slots, hub_here, here, mark_ref, near_ref)
    far, far_bias = near_rows(slots, hub_here, half - here, mark_ref, far_ref)
    grad_ref[...] = (back_ref[...] + near + far).astype(BF)
    bias_ref[...] = (near_bias + far_bias) * scale


def write_blocks(scale, parts, self_ref, neigh_ref, wide_ref, sems):
    depth, full = self_ref.shape
    cols = wide_ref.shape[-1]
    copies = []
    for at, (j, part) in enumerate(parts):
        wide_ref[at] = part.astype(F32) * scale
        cut = pl.ds(pl.multiple_of(j * cols, cols), cols)
        for kind, out_ref in enumerate((self_ref, neigh_ref)):
            copy = pltpu.make_async_copy(
                wide_ref.at[at, kind * depth : (kind + 1) * depth, :], out_ref.at[:, cut], sems.at[2 * at + kind]
            )
            copy.start()
            copies.append(copy)
    for copy in copies:
        copy.wait()


def spread_kernel(scale, seat_ref, *refs):
    got_refs, (self_ref, neigh_ref, wide_ref, sems) = refs[:-4], refs[-4:]
    depth, full = self_ref.shape
    cols = wide_ref.shape[-1]
    if len(got_refs) > 1:
        parts = [(j, ref[...]) for j, ref in seated(got_refs, seat_ref[0])]
    else:
        whole = got_refs[0][...].reshape(2 * full // cols * depth, cols)
        parts = [(j, whole[2 * j * depth : 2 * (j + 1) * depth]) for j in range(full // cols)]
    write_blocks(scale, parts, self_ref, neigh_ref, wide_ref, sems)


def finish_kernel(scale, k, seat_ref, got_ref, begun_self_ref, begun_neigh_ref, self_ref, neigh_ref, wide_ref, sems):
    write_blocks(scale, [(seat_ref[0] ^ k, got_ref[...])], self_ref, neigh_ref, wide_ref, sems)


VMEM = pl.BlockSpec(memory_space=pltpu.VMEM)
SMEM = pl.BlockSpec(memory_space=pltpu.SMEM)
ANY = pl.BlockSpec(memory_space=pl.ANY)
HBM = pl.BlockSpec(memory_space=pltpu.HBM)
PARAMS = pltpu.CompilerParams(vmem_limit_bytes=40 * 1024 * 1024)


def shape(dims, kind):
    return jax.ShapeDtypeStruct(dims, kind)


def partner(block, axis, k):
    return lax.ppermute(block, axis, [(i, i ^ k) for i in range(lax.axis_size(axis))])


def exchange(blocks, groups=None):
    return lax.all_to_all(blocks, "dom", split_axis=0, concat_axis=0, axis_index_groups=groups, tiled=True)


def swap(blocks):
    return [blocks[0]] + [partner(block, "dom", k) for k, block in enumerate(blocks) if k]


def on_device(
    features,
    w_self,
    w_neigh,
    bias,
    cotangent,
    tile_vals,
    tile_pos,
    tile_count,
    send_rows,
    recv_dest,
    ghost_weight,
    recv_count,
    hub_rows,
    hub_weight,
):
    rows, cols = features.shape
    depth, full = w_self.shape
    blocks = full // cols
    peers, slots = send_rows.shape[1:]
    hub_here = hub_rows.shape[-1]
    width = -(-(slots + hub_here + 2) // 16) * 16
    sent = -(-(slots + hub_here + 2) // 8) * 8
    lanes = peers * width
    half = peers // 2
    share = 2 * blocks * depth // half
    direct = half == blocks
    count = half if direct else 1
    halves = [list(range(half)), list(range(half, peers))]
    scale = 1.0 / math.sqrt(peers * rows)
    feats = lax.axis_size("feat")
    me = lax.axis_index("feat").astype(jnp.int32).reshape(1)
    side = (lax.axis_index("dom") >= half).astype(jnp.int32).reshape(1)
    seat = lax.rem(lax.axis_index("dom"), half).astype(jnp.int32).reshape(1)
    pack_rows = 2 * blocks * depth + 2 * rows + 16

    def pinned(*arrays):
        return [pltpu.with_memory_space_constraint(a, pltpu.HBM) for a in arrays]

    first = pinned(features, cotangent, w_self, w_neigh, bias.reshape(1, cols), send_rows, hub_rows)
    edges = pinned(tile_pos, recv_count, tile_vals, recv_dest, ghost_weight, hub_weight.T)
    moved = (send_rows, hub_rows, *edges)
    outgoing, pack, *moved = pl.pallas_call(
        functools.partial(send_kernel, width),
        out_shape=(
            shape((peers, sent, cols), BF),
            shape((pack_rows, cols), BF),
            *(shape(a.shape, a.dtype) for a in moved),
        ),
        in_specs=[HBM] * (len(first) + len(edges)),
        out_specs=(HBM,) + (VMEM,) * (1 + len(moved)),
        scratch_shapes=[
            pltpu.VMEM((1, cols), BF),
            pltpu.VMEM((slots, lanes), BF),
            pltpu.VMEM((peers, sent, cols), BF),
            pltpu.SemaphoreType.DMA((13 + 2 * blocks,)),
        ],
        compiler_params=PARAMS,
    )(*first, *edges)

    far = partner(pack, "feat", 2)
    near = partner(pack, "feat", 1)
    incoming = exchange(outgoing)
    mix, turned, mark = pl.pallas_call(
        functools.partial(mix_kernel, width),
        out_shape=(
            shape((rows, rows + lanes), BF),
            shape((rows + lanes, rows), BF),
            shape((rows, lanes), BF),
        ),
        in_specs=[VMEM] * (1 + len(moved)),
        out_specs=(VMEM,) * 3,
        compiler_params=PARAMS,
        cost_estimate=pl.CostEstimate(flops=10**8, bytes_accessed=3 * 10**6, transcendentals=0),
    )(tile_count.reshape(1, 1), *moved)
    neigh, far = pl.pallas_call(
        neigh_kernel,
        out_shape=(shape((rows, cols), BF), shape((pack_rows, cols), BF)),
        in_specs=[VMEM, VMEM, ANY, VMEM],
        out_specs=(VMEM, ANY),
        input_output_aliases={2: 1},
        scratch_shapes=[pltpu.VMEM((peers, width, cols), BF)],
        compiler_params=PARAMS,
    )(features, mix, far, incoming)
    last = partner(far, "feat", 1)
    far_neigh = partner(neigh, "feat", 2)
    every = [neigh, partner(neigh, "feat", 1), far_neigh, partner(far_neigh, "feat", 1)]

    own, grad, slope, sums, mirror, *returned = pl.pallas_call(
        functools.partial(dense_kernel, slots, hub_here, feats, width, count),
        out_shape=(
            shape((rows, cols), F32),
            shape((rows, full), BF),
            shape((rows, cols), BF),
            shape((1, cols), F32),
            shape((half, sent, cols), BF),
            *([shape((share, cols), BF)] * half if direct else [shape((half, share, cols), BF)]),
        ),
        in_specs=[SMEM] * 3 + [VMEM] * (4 + 2 * feats),
        out_specs=(VMEM,) * (5 + count),
        scratch_shapes=[
            pltpu.VMEM((rows, full), F32),
            pltpu.VMEM((16, full), BF),
        ],
        compiler_params=PARAMS,
    )(me, side, seat, features, w_self, w_neigh, turned, pack, near, far, last, *every)

    arrived = swap(returned)[::-1] if direct else [exchange(returned[0], halves)]
    mirror = partner(mirror, "dom", half)
    output, back, ghosts = pl.pallas_call(
        functools.partial(side_kernel, slots, hub_here, count),
        out_shape=(shape((rows, cols), BF), shape((rows, cols), F32), shape((half, width, cols), BF)),
        in_specs=[SMEM] * 2 + [VMEM] * 6,
        out_specs=(VMEM,) * 3,
        compiler_params=PARAMS,
        cost_estimate=pl.CostEstimate(flops=10**8, bytes_accessed=10**6, transcendentals=0),
    )(side, seat, own, grad, slope, sums, turned, w_self)
    half_sum = pl.pallas_call(
        sum_kernel,
        out_shape=shape((share, cols), BF),
        in_specs=[HBM] + [VMEM] * count,
        out_specs=VMEM,
        compiler_params=PARAMS,
    )(*pinned(output), *arrived)
    other_sum = partner(half_sum, "dom", half)
    dealt = pl.pallas_call(
        deal_kernel,
        out_shape=[shape((2 * width, cols), BF)] * half if direct else [shape((half, 2 * width, cols), BF)],
        in_specs=[VMEM] * 2,
        out_specs=[VMEM] * count,
        compiler_params=PARAMS,
    )(ghosts, mirror)
    dealt = swap(dealt) if direct else [exchange(dealt[0], halves)]
    part = pl.pallas_call(
        total_kernel,
        out_shape=shape((share, cols) if direct else (half, share, cols), BF),
        in_specs=[VMEM, VMEM],
        out_specs=VMEM,
        compiler_params=PARAMS,
    )(half_sum, other_sum)
    parts = swap([part] * half) if direct else [exchange(part, halves)]
    grad_features, grad_bias = pl.pallas_call(
        functools.partial(grad_kernel, scale, slots, hub_here),
        out_shape=(shape((rows, cols), BF), shape((1, cols), F32)),
        in_specs=[SMEM] * 2 + [VMEM] * (2 + count),
        out_specs=(VMEM,) * 2,
        scratch_shapes=[pltpu.VMEM((half, width, cols), BF)] * 2,
        compiler_params=PARAMS,
        cost_estimate=pl.CostEstimate(flops=2 * 10**9, bytes_accessed=10**6, transcendentals=0),
    )(side, seat, back, mark, *dealt)
    early = half - 1 if direct else 1
    grad_self, grad_neigh = pl.pallas_call(
        functools.partial(spread_kernel, scale),
        out_shape=(shape((depth, full), F32), shape((depth, full), F32)),
        in_specs=[SMEM] + [VMEM] * early,
        out_specs=(HBM,) * 2,
        scratch_shapes=[pltpu.VMEM((blocks, 2 * depth, cols), F32), pltpu.SemaphoreType.DMA((2 * blocks,))],
        compiler_params=PARAMS,
    )(seat, *parts[:early])
    if direct:
        grad_self, grad_neigh = pl.pallas_call(
            functools.partial(finish_kernel, scale, early),
            out_shape=(shape((depth, full), F32), shape((depth, full), F32)),
            in_specs=[SMEM, VMEM, HBM, HBM],
            out_specs=(HBM,) * 2,
            scratch_shapes=[pltpu.VMEM((1, 2 * depth, cols), F32), pltpu.SemaphoreType.DMA((2,))],
            input_output_aliases={2: 0, 3: 1},
            compiler_params=PARAMS,
        )(seat, parts[early], *pinned(grad_self, grad_neigh))
    return output, grad_features, grad_self, grad_neigh, grad_bias.reshape(cols)


def solution(mesh):
    placed = (
        P("dom", "feat"),
        P("feat", None),
        P("feat", None),
        P("feat"),
        P("dom", "feat"),
        P("dom", None, None, None),
        P("dom", None),
        P("dom"),
        P("dom", None, None),
        P("dom", None, None),
        P("dom", None, None),
        P("dom", None),
        P("dom", None),
        P("dom", None),
    )
    return jax.shard_map(
        on_device,
        mesh=mesh,
        in_specs=placed,
        out_specs=(P("dom", "feat"), P("dom", "feat"), P("feat", None), P("feat", None), P("feat")),
        check_vma=False,
    )
```

```python
import functools
import math

import jax
import jax.numpy as jnp
from jax import lax
from jax.experimental import pallas as pl
from jax.experimental.pallas import tpu as pltpu
from jax.sharding import PartitionSpec as P

BF = jnp.bfloat16
F32 = jnp.float32


def slot_places(peers, slots, width):
    lanes = peers * width
    lane = lax.broadcasted_iota(jnp.int32, (slots, lanes), 1)
    slot = lax.broadcasted_iota(jnp.int32, (slots, lanes), 0)
    return jnp.where(lane % width == slot, 1.0, 0.0).astype(BF)


def spread_rows(table, width, place=None):
    peers, slots = table.shape
    lanes = peers * width
    if place is None:
        place = slot_places(peers, slots, width)
    wide = jnp.dot(table.astype(BF), place, preferred_element_type=F32)
    peer = lax.broadcasted_iota(jnp.int32, (peers, lanes), 0)
    at = lax.broadcasted_iota(jnp.int32, (peers, lanes), 1)
    return jnp.sum(jnp.where(at // width == peer, wide, 0.0), axis=0, keepdims=True)


def source_matrix(send, hubs, rows, width, place=None):
    peers, slots = send.shape
    hub_here = hubs.shape[1]
    lanes = peers * width
    lane = lax.broadcasted_iota(jnp.int32, (1, lanes), 1) % width
    index = spread_rows(send.astype(F32), width, place)
    for k in range(hub_here):
        index = jnp.where(lane == slots + k, hubs[0:1, k : k + 1].astype(F32), index)
    index = jnp.where(lane < slots + hub_here, index, -1.0)
    row = lax.broadcasted_iota(jnp.int32, (rows, lanes), 0).astype(F32)
    return jnp.where(row == index, 1.0, 0.0).astype(BF)


def send_kernel(
    width, x_ref, cot_ref, ws_ref, wn_ref, bias_ref, send_ref, hub_ref, pos_ref, live_ref, tile_ref, dest_ref, gw_ref, hw_ref,
    out_ref, pack_ref, send_v, hub_v, pos_v, live_v, tile_v, dest_v, gw_v, hw_v, bias_v, place_ref, taken_ref, sems,
):
    rows, cols = x_ref.shape
    depth, full = ws_ref.shape
    blocks = full // cols
    base = 2 * blocks * depth
    moves = [
        (send_ref, send_v),
        (hub_ref, hub_v),
        (x_ref, pack_ref.at[base : base + rows, :]),
        (bias_ref, bias_v),
        (cot_ref, pack_ref.at[base + rows : base + 2 * rows, :]),
    ]
    for kind, w_ref in enumerate((ws_ref, wn_ref)):
        for j in range(blocks):
            at = (kind * blocks + j) * depth
            moves.append((w_ref.at[:, j * cols : (j + 1) * cols], pack_ref.at[at : at + depth, :]))
    moves += [
        (pos_ref, pos_v), (live_ref, live_v), (tile_ref, tile_v), (dest_ref, dest_v),
        (gw_ref, gw_v), (hw_ref, hw_v),
    ]
    copies = [pltpu.make_async_copy(src, dst, sems.at[i]) for i, (src, dst) in enumerate(moves)]
    for copy in copies:
        copy.start()
    peers, slots = send_v.shape[1:]
    place_ref[...] = slot_places(peers, slots, width)
    for copy in copies[:2]:
        copy.wait()
    mark = source_matrix(send_v[0], hub_v[...], rows, width, place_ref[...])
    copies[2].wait()
    kept = out_ref.shape[1]
    half = peers // 2
    for part in range(2):
        taken = lax.dot_general(
            mark[:, part * half * width : (part + 1) * half * width],
            pack_ref[base : base + rows, :],
            (((0,), (0,)), ((), ())),
            preferred_element_type=F32,
        ).astype(BF)
        for q in range(half):
            taken_ref[part * half + q] = taken[q * width : q * width + kept]
        mine = pl.ds(part * half, half)
        copies.append(pltpu.make_async_copy(taken_ref.at[mine], out_ref.at[mine], sems.at[len(copies)]))
        copies[-1].start()
    copies[3].wait()
    pack_ref[base + 2 * rows :, :] = jnp.broadcast_to(bias_v[...], (16, cols))
    for copy in copies[4:]:
        copy.wait()


def mix_kernel(width, count_ref, send_v, hub_v, pos_v, live_v, tile_v, dest_v, gw_v, hw_v, mix_ref, turned_ref, mark_ref):
    rows = mix_ref.shape[0]
    tiles, tile = tile_v.shape[1:3]
    peers, slots = dest_v.shape[1:]
    side = rows // tile
    lanes = peers * width
    hubs = hw_v.shape[0]
    hub_here = hubs // peers
    for r in range(side):
        for c in range(side):
            total = jnp.zeros((tile, tile), BF)
            for t in range(tiles):
                used = jnp.logical_and(pos_v[0:1, t : t + 1] == r * side + c, t < count_ref[...])
                total = jnp.where(used, tile_v[0, t], total)
            mix_ref[r * tile : (r + 1) * tile, c * tile : (c + 1) * tile] = total
    dest = spread_rows(dest_v[0].astype(F32), width)
    coef = spread_rows(gw_v[0], width)
    peer = lax.broadcasted_iota(jnp.int32, (peers, lanes), 0)
    at = lax.broadcasted_iota(jnp.int32, (peers, lanes), 1)
    owner = jnp.where(at // width == peer, 1.0, 0.0).astype(BF)
    limit = jnp.dot(live_v[...].astype(F32).astype(BF), owner, preferred_element_type=F32)
    lane = lax.broadcasted_iota(jnp.int32, (1, lanes), 1) % width
    coef = jnp.where(jnp.logical_and(lane.astype(F32) < limit, lane < slots), coef, 0.0)
    row = lax.broadcasted_iota(jnp.int32, (rows, lanes), 0).astype(F32)
    ghost = jnp.where(row == dest, coef, 0.0)
    hub = lax.broadcasted_iota(jnp.int32, (hubs, lanes), 0)
    at = lax.broadcasted_iota(jnp.int32, (hubs, lanes), 1)
    place = jnp.where(
        jnp.logical_and(at // width == hub // hub_here, at % width == slots + hub % hub_here), 1.0, 0.0
    ).astype(BF)
    hub_mix = lax.dot_general(hw_v[...], place, (((0,), (0,)), ((), ())), preferred_element_type=F32)
    mix_ref[:, rows:] = (ghost + hub_mix).astype(BF)
    turned_ref[...] = mix_ref[...].T
    mark_ref[...] = source_matrix(send_v[0], hub_v[...], rows, width)


def neigh_kernel(x_ref, mix_ref, far_ref, got_ref, neigh_ref, passed_ref, wide_ref):
    rows, cols = x_ref.shape
    lanes = mix_ref.shape[1] - rows
    wide_ref[...] = jnp.zeros_like(wide_ref)
    wide_ref[:, : got_ref.shape[1], :] = got_ref[...]
    total = jnp.dot(mix_ref[:, :rows], x_ref[...], preferred_element_type=F32)
    total = total + jnp.dot(mix_ref[:, rows:], wide_ref[...].reshape(lanes, cols), preferred_element_type=F32)
    neigh_ref[...] = total.astype(BF)


def ghost_rows(slots, hub_here, width, start, peers, turned_ref, neigh_grad, sums):
    rows, cols = neigh_grad.shape
    high = sums.astype(BF).astype(F32)
    line = lax.broadcasted_iota(jnp.int32, (peers * width, cols), 0) % width
    cut = pl.ds(pl.multiple_of(rows + start * width, 16), peers * width)
    away = jnp.dot(turned_ref[cut, :], neigh_grad, preferred_element_type=F32)
    away = jnp.where(line == slots + hub_here, high, away)
    away = jnp.where(line == slots + hub_here + 1, sums - high, away)
    return away.astype(BF)


def dense_kernel(feats, count, me_ref, seat_ref, x_ref, ws_ref, wn_ref, *refs):
    pack_refs, n_refs = refs[:feats], refs[feats : 2 * feats]
    own_ref, cot_ref, slope_ref, sums_ref = refs[2 * feats : 2 * feats + 4]
    send_refs = refs[2 * feats + 4 : 2 * feats + 4 + count]
    pre_ref, bias_ref = refs[2 * feats + 4 + count :]
    rows, cols = x_ref.shape
    depth, full = ws_ref.shape
    blocks = full // cols
    share = send_refs[0].shape[-2]
    me = me_ref[0]
    base = 2 * blocks * depth
    left = []
    for d, pack in enumerate(pack_refs):
        owner = me ^ d
        cut = pl.ds(pl.multiple_of(owner * cols, cols), cols)
        cot_ref[:, cut] = pack[base + rows : base + 2 * rows, :]
        bias_ref[:, cut] = pack[base + 2 * rows : base + 2 * rows + 16, :]
        left += [pack[base : base + rows, :], n_refs[d][...]]
    left = jnp.concatenate(left, axis=1)
    into = jnp.zeros((rows, depth), F32)
    span = 2
    for j in range(0, blocks, span):
        right = [
            jnp.concatenate([pack[(kind * blocks + i) * depth : (kind * blocks + i + 1) * depth, :] for i in range(j, j + span)], axis=1)
            for pack in pack_refs
            for kind in range(2)
        ]
        cut = slice(j * cols, (j + span) * cols)
        pre = jnp.dot(left, jnp.concatenate(right, axis=0), preferred_element_type=F32)
        pre = pre + bias_ref[0:1, cut].astype(F32)
        pre_ref[:, cut] = pre
        sig = jax.nn.sigmoid(pre)
        grad = (cot_ref[:, cut].astype(F32) * sig * (1.0 + pre * (1.0 - sig))).astype(BF)
        cot_ref[:, cut] = grad
        into = into + lax.dot_general(
            grad, wn_ref[:, cut], (((1,), (1,)), ((), ())), preferred_element_type=F32
        )
    mine = pl.ds(pl.multiple_of(me * cols, cols), cols)
    own_ref[...] = pre_ref[:, mine]
    slope_ref[...] = into.astype(BF)
    sums_ref[...] = jnp.sum(cot_ref[:, mine].astype(F32), axis=0, keepdims=True)
    pair = jnp.concatenate([x_ref[...], n_refs[0][...]], axis=1).T
    if count > 1:
        for k, ref in enumerate(send_refs):
            peer = seat_ref[0] ^ k
            block = cot_ref[:, pl.ds(pl.multiple_of(peer * cols, cols), cols)]
            ref[...] = jnp.dot(pair, block, preferred_element_type=F32).astype(BF)
        return
    send_ref = send_refs[0]
    weights = jnp.dot(pair, cot_ref[...], preferred_element_type=F32).astype(BF)
    step = min(share, depth)
    for j in range(blocks):
        for kind in range(2):
            block = weights[kind * depth : (kind + 1) * depth, j * cols : (j + 1) * cols]
            for part in range(depth // step):
                at = (j * 2 + kind) * depth + part * step
                low = at % share
                send_ref[at // share, low : low + step, :] = block[part * step : (part + 1) * step]


def seated(refs, seat):
    if len(refs) == 1:
        return [(j, refs[0].at[j]) for j in range(refs[0].shape[0])]
    return [(seat ^ k, ref) for k, ref in enumerate(refs)]


def mirror_kernel(slots, hub_here, width, count, side_ref, seat_ref, slope_ref, sums_ref, turned_ref, mirror_ref):
    half, sent, cols = mirror_ref.shape
    slope, sums = slope_ref[...], sums_ref[...]
    there = half - side_ref[0] * half
    if count > 1:
        for k in range(half):
            peer = there + (seat_ref[0] ^ k)
            mirror_ref[k] = ghost_rows(slots, hub_here, width, peer, 1, turned_ref, slope, sums)[:sent]
        return
    away = ghost_rows(slots, hub_here, width, there, half, turned_ref, slope, sums).reshape(half, width, cols)
    mirror_ref[...] = away[:, :sent]


def side_kernel(
    slots, hub_here, count, side_ref, seat_ref, own_ref, grad_ref, slope_ref, sums_ref, turned_ref, ws_ref,
    out_ref, back_ref, ghost_ref,
):
    own = own_ref[...]
    out_ref[...] = (own * jax.nn.sigmoid(own)).astype(BF)
    rows, cols = own.shape
    half, width = ghost_ref.shape[:2]
    slope, sums = slope_ref[...], sums_ref[...]
    back = lax.dot_general(grad_ref[...], ws_ref[...], (((1,), (1,)), ((), ())), preferred_element_type=F32)
    back_ref[...] = back + jnp.dot(turned_ref[:rows, :], slope, preferred_element_type=F32)
    here = side_ref[0] * half
    if count > 1:
        for k in range(half):
            peer = here + (seat_ref[0] ^ k)
            ghost_ref[k] = ghost_rows(slots, hub_here, width, peer, 1, turned_ref, slope, sums)
        return
    ghost_ref[...] = ghost_rows(slots, hub_here, width, here, half, turned_ref, slope, sums).reshape(half, width, cols)


def sum_kernel(stored_ref, *refs):
    got_refs, sum_ref = refs[:-1], refs[-1]
    total = jnp.zeros(sum_ref.shape, F32)
    for got_ref in got_refs if len(got_refs) > 1 else [got_refs[0].at[j] for j in range(got_refs[0].shape[0])]:
        total = total + got_ref[...].astype(F32)
    sum_ref[...] = total.astype(BF)


def deal_kernel(ghost_ref, mirror_ref, *out_refs):
    width = ghost_ref.shape[1]
    for k in range(ghost_ref.shape[0]):
        out_ref = out_refs[k] if len(out_refs) > 1 else out_refs[0].at[k]
        out_ref[:width, :] = ghost_ref[k]
        out_ref[width:, :] = jnp.zeros(ghost_ref.shape[1:], BF)
        out_ref[width : width + mirror_ref.shape[1], :] = mirror_ref[k]


def total_kernel(own_ref, other_ref, part_ref):
    total = (own_ref[...].astype(F32) + other_ref[...].astype(F32)).astype(BF)
    part_ref[...] = jnp.broadcast_to(total, part_ref.shape)


def near_rows(slots, hub_here, start, mark_ref, got_ref):
    half, width, cols = got_ref.shape
    cut = pl.ds(pl.multiple_of(start * width, 128), half * width)
    added = jnp.dot(mark_ref[:, cut], got_ref[...].reshape(half * width, cols), preferred_element_type=F32)
    first = slots + hub_here
    bias = jnp.zeros((2, cols), F32)
    for j in range(half):
        bias = bias + got_ref[j, first : first + 2, :].astype(F32)
    return added, jnp.sum(bias, axis=0, keepdims=True)


def grad_kernel(scale, slots, hub_here, side_ref, seat_ref, back_ref, mark_ref, *refs):
    got_refs, (grad_ref, bias_ref, near_ref, far_ref) = refs[:-4], refs[-4:]
    half, width = near_ref.shape[:2]
    for j, got_ref in seated(got_refs, seat_ref[0]):
        near_ref[j] = got_ref[:width, :]
        far_ref[j] = got_ref[width:, :]
    here = side_ref[0] * half
    near, near_bias = near_rows(slots, hub_here, here, mark_ref, near_ref)
    far, far_bias = near_rows(slots, hub_here, half - here, mark_ref, far_ref)
    grad_ref[...] = (back_ref[...] + near + far).astype(BF)
    bias_ref[...] = (near_bias + far_bias) * scale


def write_blocks(scale, parts, self_ref, neigh_ref, wide_ref, sems):
    depth, full = self_ref.shape
    cols = wide_ref.shape[-1]
    copies = []
    for at, (j, part) in enumerate(parts):
        wide_ref[at] = part.astype(F32) * scale
        cut = pl.ds(pl.multiple_of(j * cols, cols), cols)
        for kind, out_ref in enumerate((self_ref, neigh_ref)):
            copy = pltpu.make_async_copy(
                wide_ref.at[at, kind * depth : (kind + 1) * depth, :], out_ref.at[:, cut], sems.at[2 * at + kind]
            )
            copy.start()
            copies.append(copy)
    for copy in copies:
        copy.wait()


def spread_kernel(scale, seat_ref, *refs):
    got_refs, (self_ref, neigh_ref, wide_ref, sems) = refs[:-4], refs[-4:]
    depth, full = self_ref.shape
    cols = wide_ref.shape[-1]
    if len(got_refs) > 1:
        parts = [(j, ref[...]) for j, ref in seated(got_refs, seat_ref[0])]
    else:
        whole = got_refs[0][...].reshape(2 * full // cols * depth, cols)
        parts = [(j, whole[2 * j * depth : 2 * (j + 1) * depth]) for j in range(full // cols)]
    write_blocks(scale, parts, self_ref, neigh_ref, wide_ref, sems)


def finish_kernel(scale, k, seat_ref, got_ref, begun_self_ref, begun_neigh_ref, self_ref, neigh_ref, wide_ref, sems):
    write_blocks(scale, [(seat_ref[0] ^ k, got_ref[...])], self_ref, neigh_ref, wide_ref, sems)


VMEM = pl.BlockSpec(memory_space=pltpu.VMEM)
SMEM = pl.BlockSpec(memory_space=pltpu.SMEM)
ANY = pl.BlockSpec(memory_space=pl.ANY)
HBM = pl.BlockSpec(memory_space=pltpu.HBM)
PARAMS = pltpu.CompilerParams(vmem_limit_bytes=40 * 1024 * 1024)


def shape(dims, kind):
    return jax.ShapeDtypeStruct(dims, kind)


def partner(block, axis, k):
    return lax.ppermute(block, axis, [(i, i ^ k) for i in range(lax.axis_size(axis))])


def exchange(blocks, groups=None):
    return lax.all_to_all(blocks, "dom", split_axis=0, concat_axis=0, axis_index_groups=groups, tiled=True)


def swap(blocks):
    return [blocks[0]] + [partner(block, "dom", k) for k, block in enumerate(blocks) if k]


def on_device(
    features,
    w_self,
    w_neigh,
    bias,
    cotangent,
    tile_vals,
    tile_pos,
    tile_count,
    send_rows,
    recv_dest,
    ghost_weight,
    recv_count,
    hub_rows,
    hub_weight,
):
    rows, cols = features.shape
    depth, full = w_self.shape
    blocks = full // cols
    peers, slots = send_rows.shape[1:]
    hub_here = hub_rows.shape[-1]
    width = -(-(slots + hub_here + 2) // 16) * 16
    sent = -(-(slots + hub_here + 2) // 8) * 8
    lanes = peers * width
    half = peers // 2
    share = 2 * blocks * depth // half
    direct = half == blocks
    count = half if direct else 1
    halves = [list(range(half)), list(range(half, peers))]
    scale = 1.0 / math.sqrt(peers * rows)
    feats = lax.axis_size("feat")
    me = lax.axis_index("feat").astype(jnp.int32).reshape(1)
    side = (lax.axis_index("dom") >= half).astype(jnp.int32).reshape(1)
    seat = lax.rem(lax.axis_index("dom"), half).astype(jnp.int32).reshape(1)
    pack_rows = 2 * blocks * depth + 2 * rows + 16

    def pinned(*arrays):
        return [pltpu.with_memory_space_constraint(a, pltpu.HBM) for a in arrays]

    first = pinned(features, cotangent, w_self, w_neigh, bias.reshape(1, cols), send_rows, hub_rows)
    edges = pinned(tile_pos, recv_count, tile_vals, recv_dest, ghost_weight, hub_weight.T)
    moved = (send_rows, hub_rows, *edges)
    outgoing, pack, *moved = pl.pallas_call(
        functools.partial(send_kernel, width),
        out_shape=(
            shape((peers, sent, cols), BF),
            shape((pack_rows, cols), BF),
            *(shape(a.shape, a.dtype) for a in moved),
        ),
        in_specs=[HBM] * (len(first) + len(edges)),
        out_specs=(HBM,) + (VMEM,) * (1 + len(moved)),
        scratch_shapes=[
            pltpu.VMEM((1, cols), BF),
            pltpu.VMEM((slots, lanes), BF),
            pltpu.VMEM((peers, sent, cols), BF),
            pltpu.SemaphoreType.DMA((13 + 2 * blocks,)),
        ],
        compiler_params=PARAMS,
    )(*first, *edges)

    far = partner(pack, "feat", 2)
    near = partner(pack, "feat", 1)
    incoming = exchange(outgoing)
    mix, turned, mark = pl.pallas_call(
        functools.partial(mix_kernel, width),
        out_shape=(
            shape((rows, rows + lanes), BF),
            shape((rows + lanes, rows), BF),
            shape((rows, lanes), BF),
        ),
        in_specs=[VMEM] * (1 + len(moved)),
        out_specs=(VMEM,) * 3,
        compiler_params=PARAMS,
        cost_estimate=pl.CostEstimate(flops=10**8, bytes_accessed=3 * 10**6, transcendentals=0),
    )(tile_count.reshape(1, 1), *moved)
    neigh, far = pl.pallas_call(
        neigh_kernel,
        out_shape=(shape((rows, cols), BF), shape((pack_rows, cols), BF)),
        in_specs=[VMEM, VMEM, ANY, VMEM],
        out_specs=(VMEM, ANY),
        input_output_aliases={2: 1},
        scratch_shapes=[pltpu.VMEM((peers, width, cols), BF)],
        compiler_params=PARAMS,
    )(features, mix, far, incoming)
    last = partner(far, "feat", 1)
    far_neigh = partner(neigh, "feat", 2)
    every = [neigh, partner(neigh, "feat", 1), far_neigh, partner(far_neigh, "feat", 1)]

    own, grad, slope, sums, *returned = pl.pallas_call(
        functools.partial(dense_kernel, feats, count),
        out_shape=(
            shape((rows, cols), F32),
            shape((rows, full), BF),
            shape((rows, cols), BF),
            shape((1, cols), F32),
            *([shape((share, cols), BF)] * half if direct else [shape((half, share, cols), BF)]),
        ),
        in_specs=[SMEM] * 2 + [VMEM] * (3 + 2 * feats),
        out_specs=(VMEM,) * (4 + count),
        scratch_shapes=[
            pltpu.VMEM((rows, full), F32),
            pltpu.VMEM((16, full), BF),
        ],
        compiler_params=PARAMS,
    )(me, seat, features, w_self, w_neigh, pack, near, far, last, *every)

    arrived = swap(returned)[::-1] if direct else [exchange(returned[0], halves)]
    mirror = pl.pallas_call(
        functools.partial(mirror_kernel, slots, hub_here, width, count),
        out_shape=shape((half, sent, cols), BF),
        in_specs=[SMEM] * 2 + [VMEM] * 3,
        out_specs=VMEM,
        compiler_params=PARAMS,
    )(side, seat, slope, sums, turned)
    mirror = partner(mirror, "dom", half)
    output, back, ghosts = pl.pallas_call(
        functools.partial(side_kernel, slots, hub_here, count),
        out_shape=(shape((rows, cols), BF), shape((rows, cols), F32), shape((half, width, cols), BF)),
        in_specs=[SMEM] * 2 + [VMEM] * 6,
        out_specs=(VMEM,) * 3,
        compiler_params=PARAMS,
        cost_estimate=pl.CostEstimate(flops=10**8, bytes_accessed=10**6, transcendentals=0),
    )(side, seat, own, grad, slope, sums, turned, w_self)
    half_sum = pl.pallas_call(
        sum_kernel,
        out_shape=shape((share, cols), BF),
        in_specs=[HBM] + [VMEM] * count,
        out_specs=VMEM,
        compiler_params=PARAMS,
    )(*pinned(output), *arrived)
    other_sum = partner(half_sum, "dom", half)
    dealt = pl.pallas_call(
        deal_kernel,
        out_shape=[shape((2 * width, cols), BF)] * half if direct else [shape((half, 2 * width, cols), BF)],
        in_specs=[VMEM] * 2,
        out_specs=[VMEM] * count,
        compiler_params=PARAMS,
    )(ghosts, mirror)
    dealt = swap(dealt) if direct else [exchange(dealt[0], halves)]
    part = pl.pallas_call(
        total_kernel,
        out_shape=shape((share, cols) if direct else (half, share, cols), BF),
        in_specs=[VMEM, VMEM],
        out_specs=VMEM,
        compiler_params=PARAMS,
    )(half_sum, other_sum)
    parts = swap([part] * half) if direct else [exchange(part, halves)]
    grad_features, grad_bias = pl.pallas_call(
        functools.partial(grad_kernel, scale, slots, hub_here),
        out_shape=(shape((rows, cols), BF), shape((1, cols), F32)),
        in_specs=[SMEM] * 2 + [VMEM] * (2 + count),
        out_specs=(VMEM,) * 2,
        scratch_shapes=[pltpu.VMEM((half, width, cols), BF)] * 2,
        compiler_params=PARAMS,
        cost_estimate=pl.CostEstimate(flops=2 * 10**9, bytes_accessed=10**6, transcendentals=0),
    )(side, seat, back, mark, *dealt)
    early = half - 1 if direct else 1
    grad_self, grad_neigh = pl.pallas_call(
        functools.partial(spread_kernel, scale),
        out_shape=(shape((depth, full), F32), shape((depth, full), F32)),
        in_specs=[SMEM] + [VMEM] * early,
        out_specs=(HBM,) * 2,
        scratch_shapes=[pltpu.VMEM((blocks, 2 * depth, cols), F32), pltpu.SemaphoreType.DMA((2 * blocks,))],
        compiler_params=PARAMS,
    )(seat, *parts[:early])
    if direct:
        grad_self, grad_neigh = pl.pallas_call(
            functools.partial(finish_kernel, scale, early),
            out_shape=(shape((depth, full), F32), shape((depth, full), F32)),
            in_specs=[SMEM, VMEM, HBM, HBM],
            out_specs=(HBM,) * 2,
            scratch_shapes=[pltpu.VMEM((1, 2 * depth, cols), F32), pltpu.SemaphoreType.DMA((2,))],
            input_output_aliases={2: 0, 3: 1},
            compiler_params=PARAMS,
        )(seat, parts[early], *pinned(grad_self, grad_neigh))
    return output, grad_features, grad_self, grad_neigh, grad_bias.reshape(cols)


def solution(mesh):
    placed = (
        P("dom", "feat"),
        P("feat", None),
        P("feat", None),
        P("feat"),
        P("dom", "feat"),
        P("dom", None, None, None),
        P("dom", None),
        P("dom"),
        P("dom", None, None),
        P("dom", None, None),
        P("dom", None, None),
        P("dom", None),
        P("dom", None),
        P("dom", None),
    )
    return jax.shard_map(
        on_device,
        mesh=mesh,
        in_specs=placed,
        out_specs=(P("dom", "feat"), P("dom", "feat"), P("feat", None), P("feat", None), P("feat")),
        check_vma=False,
    )
```

```python
import functools
import math

import jax
import jax.numpy as jnp
from jax import lax
from jax.experimental import pallas as pl
from jax.experimental.pallas import tpu as pltpu
from jax.sharding import PartitionSpec as P

BF = jnp.bfloat16
F32 = jnp.float32


def slot_places(peers, slots, width):
    lanes = peers * width
    lane = lax.broadcasted_iota(jnp.int32, (slots, lanes), 1)
    slot = lax.broadcasted_iota(jnp.int32, (slots, lanes), 0)
    return jnp.where(lane % width == slot, 1.0, 0.0).astype(BF)


def spread_rows(table, width, place=None):
    peers, slots = table.shape
    lanes = peers * width
    if place is None:
        place = slot_places(peers, slots, width)
    wide = jnp.dot(table.astype(BF), place, preferred_element_type=F32)
    peer = lax.broadcasted_iota(jnp.int32, (peers, lanes), 0)
    at = lax.broadcasted_iota(jnp.int32, (peers, lanes), 1)
    return jnp.sum(jnp.where(at // width == peer, wide, 0.0), axis=0, keepdims=True)


def source_matrix(send, hubs, rows, width, place=None):
    peers, slots = send.shape
    hub_here = hubs.shape[1]
    lanes = peers * width
    lane = lax.broadcasted_iota(jnp.int32, (1, lanes), 1) % width
    index = spread_rows(send.astype(F32), width, place)
    for k in range(hub_here):
        index = jnp.where(lane == slots + k, hubs[0:1, k : k + 1].astype(F32), index)
    index = jnp.where(lane < slots + hub_here, index, -1.0)
    row = lax.broadcasted_iota(jnp.int32, (rows, lanes), 0).astype(F32)
    return jnp.where(row == index, 1.0, 0.0).astype(BF)


def send_kernel(
    width, x_ref, cot_ref, ws_ref, wn_ref, bias_ref, send_ref, hub_ref, pos_ref, live_ref, tile_ref, dest_ref, gw_ref, hw_ref,
    out_ref, pack_ref, send_v, hub_v, pos_v, live_v, tile_v, dest_v, gw_v, hw_v, bias_v, place_ref, taken_ref, sems,
):
    rows, cols = x_ref.shape
    depth, full = ws_ref.shape
    blocks = full // cols
    base = 2 * blocks * depth
    moves = [
        (send_ref, send_v),
        (hub_ref, hub_v),
        (x_ref, pack_ref.at[base : base + rows, :]),
        (bias_ref, bias_v),
        (cot_ref, pack_ref.at[base + rows : base + 2 * rows, :]),
    ]
    for kind, w_ref in enumerate((ws_ref, wn_ref)):
        for j in range(blocks):
            at = (kind * blocks + j) * depth
            moves.append((w_ref.at[:, j * cols : (j + 1) * cols], pack_ref.at[at : at + depth, :]))
    moves += [
        (pos_ref, pos_v), (live_ref, live_v), (tile_ref, tile_v), (dest_ref, dest_v),
        (gw_ref, gw_v), (hw_ref, hw_v),
    ]
    copies = [pltpu.make_async_copy(src, dst, sems.at[i]) for i, (src, dst) in enumerate(moves)]
    for copy in copies:
        copy.start()
    peers, slots = send_v.shape[1:]
    place_ref[...] = slot_places(peers, slots, width)
    for copy in copies[:2]:
        copy.wait()
    mark = source_matrix(send_v[0], hub_v[...], rows, width, place_ref[...])
    copies[2].wait()
    kept = out_ref.shape[1]
    half = peers // 2
    for part in range(2):
        taken = lax.dot_general(
            mark[:, part * half * width : (part + 1) * half * width],
            pack_ref[base : base + rows, :],
            (((0,), (0,)), ((), ())),
            preferred_element_type=F32,
        ).astype(BF)
        for q in range(half):
            taken_ref[part * half + q] = taken[q * width : q * width + kept]
        mine = pl.ds(part * half, half)
        copies.append(pltpu.make_async_copy(taken_ref.at[mine], out_ref.at[mine], sems.at[len(copies)]))
        copies[-1].start()
    copies[3].wait()
    pack_ref[base + 2 * rows :, :] = jnp.broadcast_to(bias_v[...], (16, cols))
    for copy in copies[4:]:
        copy.wait()


def mix_kernel(width, count_ref, send_v, hub_v, pos_v, live_v, tile_v, dest_v, gw_v, hw_v, mix_ref, turned_ref, mark_ref):
    rows = mix_ref.shape[0]
    tiles, tile = tile_v.shape[1:3]
    peers, slots = dest_v.shape[1:]
    side = rows // tile
    lanes = peers * width
    hubs = hw_v.shape[0]
    hub_here = hubs // peers
    for r in range(side):
        for c in range(side):
            total = jnp.zeros((tile, tile), BF)
            for t in range(tiles):
                used = jnp.logical_and(pos_v[0:1, t : t + 1] == r * side + c, t < count_ref[...])
                total = jnp.where(used, tile_v[0, t], total)
            mix_ref[r * tile : (r + 1) * tile, c * tile : (c + 1) * tile] = total
    dest = spread_rows(dest_v[0].astype(F32), width)
    coef = spread_rows(gw_v[0], width)
    peer = lax.broadcasted_iota(jnp.int32, (peers, lanes), 0)
    at = lax.broadcasted_iota(jnp.int32, (peers, lanes), 1)
    owner = jnp.where(at // width == peer, 1.0, 0.0).astype(BF)
    limit = jnp.dot(live_v[...].astype(F32).astype(BF), owner, preferred_element_type=F32)
    lane = lax.broadcasted_iota(jnp.int32, (1, lanes), 1) % width
    coef = jnp.where(jnp.logical_and(lane.astype(F32) < limit, lane < slots), coef, 0.0)
    row = lax.broadcasted_iota(jnp.int32, (rows, lanes), 0).astype(F32)
    ghost = jnp.where(row == dest, coef, 0.0)
    hub = lax.broadcasted_iota(jnp.int32, (hubs, lanes), 0)
    at = lax.broadcasted_iota(jnp.int32, (hubs, lanes), 1)
    place = jnp.where(
        jnp.logical_and(at // width == hub // hub_here, at % width == slots + hub % hub_here), 1.0, 0.0
    ).astype(BF)
    hub_mix = lax.dot_general(hw_v[...], place, (((0,), (0,)), ((), ())), preferred_element_type=F32)
    mix_ref[:, rows:] = (ghost + hub_mix).astype(BF)
    turned_ref[...] = mix_ref[...].T
    mark_ref[...] = source_matrix(send_v[0], hub_v[...], rows, width)


def pass_kernel(held_ref, passed_ref):
    pass


def neigh_kernel(x_ref, mix_ref, far_ref, got_ref, neigh_ref, passed_ref, wide_ref):
    rows, cols = x_ref.shape
    lanes = mix_ref.shape[1] - rows
    wide_ref[...] = jnp.zeros_like(wide_ref)
    wide_ref[:, : got_ref.shape[1], :] = got_ref[...]
    total = jnp.dot(mix_ref[:, :rows], x_ref[...], preferred_element_type=F32)
    total = total + jnp.dot(mix_ref[:, rows:], wide_ref[...].reshape(lanes, cols), preferred_element_type=F32)
    neigh_ref[...] = total.astype(BF)


def ghost_rows(slots, hub_here, width, start, peers, turned_ref, neigh_grad, sums):
    rows, cols = neigh_grad.shape
    high = sums.astype(BF).astype(F32)
    line = lax.broadcasted_iota(jnp.int32, (peers * width, cols), 0) % width
    cut = pl.ds(pl.multiple_of(rows + start * width, 16), peers * width)
    away = jnp.dot(turned_ref[cut, :], neigh_grad, preferred_element_type=F32)
    away = jnp.where(line == slots + hub_here, high, away)
    away = jnp.where(line == slots + hub_here + 1, sums - high, away)
    return away.astype(BF)


def dense_kernel(slots, hub_here, feats, width, count, me_ref, side_ref, seat_ref, x_ref, ws_ref, wn_ref, turned_ref, *refs):
    pack_refs, n_refs = refs[:feats], refs[feats : 2 * feats]
    own_ref, cot_ref, slope_ref, sums_ref, mirror_ref = refs[2 * feats : 2 * feats + 5]
    send_refs = refs[2 * feats + 5 : 2 * feats + 5 + count]
    pre_ref, bias_ref = refs[2 * feats + 5 + count :]
    rows, cols = x_ref.shape
    depth, full = ws_ref.shape
    blocks = full // cols
    half = mirror_ref.shape[0]
    share = send_refs[0].shape[-2]
    me = me_ref[0]
    base = 2 * blocks * depth
    left = []
    for d, pack in enumerate(pack_refs):
        owner = me ^ d
        cut = pl.ds(pl.multiple_of(owner * cols, cols), cols)
        cot_ref[:, cut] = pack[base + rows : base + 2 * rows, :]
        bias_ref[:, cut] = pack[base + 2 * rows : base + 2 * rows + 16, :]
        left += [pack[base : base + rows, :], n_refs[d][...]]
    left = jnp.concatenate(left, axis=1)
    into = jnp.zeros((rows, depth), F32)
    span = 2
    for j in range(0, blocks, span):
        right = [
            jnp.concatenate([pack[(kind * blocks + i) * depth : (kind * blocks + i + 1) * depth, :] for i in range(j, j + span)], axis=1)
            for pack in pack_refs
            for kind in range(2)
        ]
        cut = slice(j * cols, (j + span) * cols)
        pre = jnp.dot(left, jnp.concatenate(right, axis=0), preferred_element_type=F32)
        pre = pre + bias_ref[0:1, cut].astype(F32)
        pre_ref[:, cut] = pre
        sig = jax.nn.sigmoid(pre)
        grad = (cot_ref[:, cut].astype(F32) * sig * (1.0 + pre * (1.0 - sig))).astype(BF)
        cot_ref[:, cut] = grad
        into = into + lax.dot_general(
            grad, wn_ref[:, cut], (((1,), (1,)), ((), ())), preferred_element_type=F32
        )
    mine = pl.ds(pl.multiple_of(me * cols, cols), cols)
    own_ref[...] = pre_ref[:, mine]
    neigh_grad = into.astype(BF)
    slope_ref[...] = neigh_grad
    sums = jnp.sum(cot_ref[:, mine].astype(F32), axis=0, keepdims=True)
    sums_ref[...] = sums
    there = half - side_ref[0] * half
    pair = jnp.concatenate([x_ref[...], n_refs[0][...]], axis=1).T
    if count > 1:
        for k, ref in enumerate(send_refs):
            peer = seat_ref[0] ^ k
            away = ghost_rows(slots, hub_here, width, there + peer, 1, turned_ref, neigh_grad, sums)
            mirror_ref[k] = away[: mirror_ref.shape[1]]
            block = cot_ref[:, pl.ds(pl.multiple_of(peer * cols, cols), cols)]
            ref[...] = jnp.dot(pair, block, preferred_element_type=F32).astype(BF)
        return
    send_ref = send_refs[0]
    away = ghost_rows(slots, hub_here, width, there, half, turned_ref, neigh_grad, sums).reshape(half, width, cols)
    mirror_ref[...] = away[:, : mirror_ref.shape[1]]
    weights = jnp.dot(pair, cot_ref[...], preferred_element_type=F32).astype(BF)
    step = min(share, depth)
    for j in range(blocks):
        for kind in range(2):
            block = weights[kind * depth : (kind + 1) * depth, j * cols : (j + 1) * cols]
            for part in range(depth // step):
                at = (j * 2 + kind) * depth + part * step
                low = at % share
                send_ref[at // share, low : low + step, :] = block[part * step : (part + 1) * step]


def seated(refs, seat):
    if len(refs) == 1:
        return [(j, refs[0].at[j]) for j in range(refs[0].shape[0])]
    return [(seat ^ k, ref) for k, ref in enumerate(refs)]


def side_kernel(
    slots, hub_here, count, side_ref, seat_ref, own_ref, grad_ref, slope_ref, sums_ref, turned_ref, ws_ref,
    out_ref, back_ref, ghost_ref,
):
    own = own_ref[...]
    out_ref[...] = (own * jax.nn.sigmoid(own)).astype(BF)
    rows, cols = own.shape
    half, width = ghost_ref.shape[:2]
    slope, sums = slope_ref[...], sums_ref[...]
    back = lax.dot_general(grad_ref[...], ws_ref[...], (((1,), (1,)), ((), ())), preferred_element_type=F32)
    back_ref[...] = back + jnp.dot(turned_ref[:rows, :], slope, preferred_element_type=F32)
    here = side_ref[0] * half
    if count > 1:
        for k in range(half):
            peer = here + (seat_ref[0] ^ k)
            ghost_ref[k] = ghost_rows(slots, hub_here, width, peer, 1, turned_ref, slope, sums)
        return
    ghost_ref[...] = ghost_rows(slots, hub_here, width, here, half, turned_ref, slope, sums).reshape(half, width, cols)


def sum_kernel(stored_ref, *refs):
    got_refs, sum_ref = refs[:-1], refs[-1]
    total = jnp.zeros(sum_ref.shape, F32)
    for got_ref in got_refs if len(got_refs) > 1 else [got_refs[0].at[j] for j in range(got_refs[0].shape[0])]:
        total = total + got_ref[...].astype(F32)
    sum_ref[...] = total.astype(BF)


def deal_kernel(ghost_ref, mirror_ref, *out_refs):
    width = ghost_ref.shape[1]
    for k in range(ghost_ref.shape[0]):
        out_ref = out_refs[k] if len(out_refs) > 1 else out_refs[0].at[k]
        out_ref[:width, :] = ghost_ref[k]
        out_ref[width:, :] = jnp.zeros(ghost_ref.shape[1:], BF)
        out_ref[width : width + mirror_ref.shape[1], :] = mirror_ref[k]


def total_kernel(own_ref, other_ref, part_ref):
    total = (own_ref[...].astype(F32) + other_ref[...].astype(F32)).astype(BF)
    part_ref[...] = jnp.broadcast_to(total, part_ref.shape)


def near_rows(slots, hub_here, start, mark_ref, got_ref):
    half, width, cols = got_ref.shape
    cut = pl.ds(pl.multiple_of(start * width, 128), half * width)
    added = jnp.dot(mark_ref[:, cut], got_ref[...].reshape(half * width, cols), preferred_element_type=F32)
    first = slots + hub_here
    bias = jnp.zeros((2, cols), F32)
    for j in range(half):
        bias = bias + got_ref[j, first : first + 2, :].astype(F32)
    return added, jnp.sum(bias, axis=0, keepdims=True)


def grad_kernel(scale, slots, hub_here, side_ref, seat_ref, back_ref, mark_ref, *refs):
    got_refs, (grad_ref, bias_ref, near_ref, far_ref) = refs[:-4], refs[-4:]
    half, width = near_ref.shape[:2]
    for j, got_ref in seated(got_refs, seat_ref[0]):
        near_ref[j] = got_ref[:width, :]
        far_ref[j] = got_ref[width:, :]
    here = side_ref[0] * half
    near, near_bias = near_rows(slots, hub_here, here, mark_ref, near_ref)
    far, far_bias = near_rows(slots, hub_here, half - here, mark_ref, far_ref)
    grad_ref[...] = (back_ref[...] + near + far).astype(BF)
    bias_ref[...] = (near_bias + far_bias) * scale


def write_blocks(scale, parts, self_ref, neigh_ref, wide_ref, sems):
    depth, full = self_ref.shape
    cols = wide_ref.shape[-1]
    copies = []
    for at, (j, part) in enumerate(parts):
        wide_ref[at] = part.astype(F32) * scale
        cut = pl.ds(pl.multiple_of(j * cols, cols), cols)
        for kind, out_ref in enumerate((self_ref, neigh_ref)):
            copy = pltpu.make_async_copy(
                wide_ref.at[at, kind * depth : (kind + 1) * depth, :], out_ref.at[:, cut], sems.at[2 * at + kind]
            )
            copy.start()
            copies.append(copy)
    for copy in copies:
        copy.wait()


def spread_kernel(scale, seat_ref, *refs):
    got_refs, (self_ref, neigh_ref, wide_ref, sems) = refs[:-4], refs[-4:]
    depth, full = self_ref.shape
    cols = wide_ref.shape[-1]
    if len(got_refs) > 1:
        parts = [(j, ref[...]) for j, ref in seated(got_refs, seat_ref[0])]
    else:
        whole = got_refs[0][...].reshape(2 * full // cols * depth, cols)
        parts = [(j, whole[2 * j * depth : 2 * (j + 1) * depth]) for j in range(full // cols)]
    write_blocks(scale, parts, self_ref, neigh_ref, wide_ref, sems)


def finish_kernel(scale, k, seat_ref, got_ref, begun_self_ref, begun_neigh_ref, self_ref, neigh_ref, wide_ref, sems):
    write_blocks(scale, [(seat_ref[0] ^ k, got_ref[...])], self_ref, neigh_ref, wide_ref, sems)


VMEM = pl.BlockSpec(memory_space=pltpu.VMEM)
SMEM = pl.BlockSpec(memory_space=pltpu.SMEM)
ANY = pl.BlockSpec(memory_space=pl.ANY)
HBM = pl.BlockSpec(memory_space=pltpu.HBM)
PARAMS = pltpu.CompilerParams(vmem_limit_bytes=40 * 1024 * 1024)


def shape(dims, kind):
    return jax.ShapeDtypeStruct(dims, kind)


def partner(block, axis, k):
    return lax.ppermute(block, axis, [(i, i ^ k) for i in range(lax.axis_size(axis))])


def exchange(blocks, groups=None):
    return lax.all_to_all(blocks, "dom", split_axis=0, concat_axis=0, axis_index_groups=groups, tiled=True)


def swap(blocks):
    return [blocks[0]] + [partner(block, "dom", k) for k, block in enumerate(blocks) if k]


def on_device(
    features,
    w_self,
    w_neigh,
    bias,
    cotangent,
    tile_vals,
    tile_pos,
    tile_count,
    send_rows,
    recv_dest,
    ghost_weight,
    recv_count,
    hub_rows,
    hub_weight,
):
    rows, cols = features.shape
    depth, full = w_self.shape
    blocks = full // cols
    peers, slots = send_rows.shape[1:]
    hub_here = hub_rows.shape[-1]
    width = -(-(slots + hub_here + 2) // 16) * 16
    sent = -(-(slots + hub_here + 2) // 8) * 8
    lanes = peers * width
    half = peers // 2
    share = 2 * blocks * depth // half
    direct = half == blocks
    count = half if direct else 1
    halves = [list(range(half)), list(range(half, peers))]
    scale = 1.0 / math.sqrt(peers * rows)
    feats = lax.axis_size("feat")
    me = lax.axis_index("feat").astype(jnp.int32).reshape(1)
    side = (lax.axis_index("dom") >= half).astype(jnp.int32).reshape(1)
    seat = lax.rem(lax.axis_index("dom"), half).astype(jnp.int32).reshape(1)
    pack_rows = 2 * blocks * depth + 2 * rows + 16

    def pinned(*arrays):
        return [pltpu.with_memory_space_constraint(a, pltpu.HBM) for a in arrays]

    first = pinned(features, cotangent, w_self, w_neigh, bias.reshape(1, cols), send_rows, hub_rows)
    edges = pinned(tile_pos, recv_count, tile_vals, recv_dest, ghost_weight, hub_weight.T)
    moved = (send_rows, hub_rows, *edges)
    outgoing, pack, *moved = pl.pallas_call(
        functools.partial(send_kernel, width),
        out_shape=(
            shape((peers, sent, cols), BF),
            shape((pack_rows, cols), BF),
            *(shape(a.shape, a.dtype) for a in moved),
        ),
        in_specs=[HBM] * (len(first) + len(edges)),
        out_specs=(HBM,) + (VMEM,) * (1 + len(moved)),
        scratch_shapes=[
            pltpu.VMEM((1, cols), BF),
            pltpu.VMEM((slots, lanes), BF),
            pltpu.VMEM((peers, sent, cols), BF),
            pltpu.SemaphoreType.DMA((13 + 2 * blocks,)),
        ],
        compiler_params=PARAMS,
    )(*first, *edges)

    far = partner(pack, "feat", 2)
    near = partner(pack, "feat", 1)
    incoming = exchange(outgoing)
    mix, turned, mark = pl.pallas_call(
        functools.partial(mix_kernel, width),
        out_shape=(
            shape((rows, rows + lanes), BF),
            shape((rows + lanes, rows), BF),
            shape((rows, lanes), BF),
        ),
        in_specs=[VMEM] * (1 + len(moved)),
        out_specs=(VMEM,) * 3,
        compiler_params=PARAMS,
        cost_estimate=pl.CostEstimate(flops=10**8, bytes_accessed=3 * 10**6, transcendentals=0),
    )(tile_count.reshape(1, 1), *moved)
    neigh, far = pl.pallas_call(
        neigh_kernel,
        out_shape=(shape((rows, cols), BF), shape((pack_rows, cols), BF)),
        in_specs=[VMEM, VMEM, ANY, VMEM],
        out_specs=(VMEM, ANY),
        input_output_aliases={2: 1},
        scratch_shapes=[pltpu.VMEM((peers, width, cols), BF)],
        compiler_params=PARAMS,
    )(features, mix, far, incoming)
    last = partner(far, "feat", 1)
    far_neigh = pl.pallas_call(
        pass_kernel,
        out_shape=shape((rows, cols), BF),
        in_specs=[ANY],
        out_specs=ANY,
        input_output_aliases={0: 0},
        compiler_params=PARAMS,
        cost_estimate=pl.CostEstimate(flops=10**10, bytes_accessed=10**7, transcendentals=0),
    )(partner(neigh, "feat", 2))
    every = [neigh, partner(neigh, "feat", 1), far_neigh, partner(far_neigh, "feat", 1)]

    own, grad, slope, sums, mirror, *returned = pl.pallas_call(
        functools.partial(dense_kernel, slots, hub_here, feats, width, count),
        out_shape=(
            shape((rows, cols), F32),
            shape((rows, full), BF),
            shape((rows, cols), BF),
            shape((1, cols), F32),
            shape((half, sent, cols), BF),
            *([shape((share, cols), BF)] * half if direct else [shape((half, share, cols), BF)]),
        ),
        in_specs=[SMEM] * 3 + [VMEM] * (4 + 2 * feats),
        out_specs=(VMEM,) * (5 + count),
        scratch_shapes=[
            pltpu.VMEM((rows, full), F32),
            pltpu.VMEM((16, full), BF),
        ],
        compiler_params=PARAMS,
    )(me, side, seat, features, w_self, w_neigh, turned, pack, near, far, last, *every)

    arrived = swap(returned)[::-1] if direct else [exchange(returned[0], halves)]
    mirror = partner(mirror, "dom", half)
    output, back, ghosts = pl.pallas_call(
        functools.partial(side_kernel, slots, hub_here, count),
        out_shape=(shape((rows, cols), BF), shape((rows, cols), F32), shape((half, width, cols), BF)),
        in_specs=[SMEM] * 2 + [VMEM] * 6,
        out_specs=(VMEM,) * 3,
        compiler_params=PARAMS,
        cost_estimate=pl.CostEstimate(flops=10**8, bytes_accessed=10**6, transcendentals=0),
    )(side, seat, own, grad, slope, sums, turned, w_self)
    half_sum = pl.pallas_call(
        sum_kernel,
        out_shape=shape((share, cols), BF),
        in_specs=[HBM] + [VMEM] * count,
        out_specs=VMEM,
        compiler_params=PARAMS,
    )(*pinned(output), *arrived)
    other_sum = partner(half_sum, "dom", half)
    dealt = pl.pallas_call(
        deal_kernel,
        out_shape=[shape((2 * width, cols), BF)] * half if direct else [shape((half, 2 * width, cols), BF)],
        in_specs=[VMEM] * 2,
        out_specs=[VMEM] * count,
        compiler_params=PARAMS,
    )(ghosts, mirror)
    dealt = swap(dealt) if direct else [exchange(dealt[0], halves)]
    part = pl.pallas_call(
        total_kernel,
        out_shape=shape((share, cols) if direct else (half, share, cols), BF),
        in_specs=[VMEM, VMEM],
        out_specs=VMEM,
        compiler_params=PARAMS,
    )(half_sum, other_sum)
    parts = swap([part] * half) if direct else [exchange(part, halves)]
    grad_features, grad_bias = pl.pallas_call(
        functools.partial(grad_kernel, scale, slots, hub_here),
        out_shape=(shape((rows, cols), BF), shape((1, cols), F32)),
        in_specs=[SMEM] * 2 + [VMEM] * (2 + count),
        out_specs=(VMEM,) * 2,
        scratch_shapes=[pltpu.VMEM((half, width, cols), BF)] * 2,
        compiler_params=PARAMS,
        cost_estimate=pl.CostEstimate(flops=2 * 10**9, bytes_accessed=10**6, transcendentals=0),
    )(side, seat, back, mark, *dealt)
    early = half - 1 if direct else 1
    grad_self, grad_neigh = pl.pallas_call(
        functools.partial(spread_kernel, scale),
        out_shape=(shape((depth, full), F32), shape((depth, full), F32)),
        in_specs=[SMEM] + [VMEM] * early,
        out_specs=(HBM,) * 2,
        scratch_shapes=[pltpu.VMEM((blocks, 2 * depth, cols), F32), pltpu.SemaphoreType.DMA((2 * blocks,))],
        compiler_params=PARAMS,
    )(seat, *parts[:early])
    if direct:
        grad_self, grad_neigh = pl.pallas_call(
            functools.partial(finish_kernel, scale, early),
            out_shape=(shape((depth, full), F32), shape((depth, full), F32)),
            in_specs=[SMEM, VMEM, HBM, HBM],
            out_specs=(HBM,) * 2,
            scratch_shapes=[pltpu.VMEM((1, 2 * depth, cols), F32), pltpu.SemaphoreType.DMA((2,))],
            input_output_aliases={2: 0, 3: 1},
            compiler_params=PARAMS,
        )(seat, parts[early], *pinned(grad_self, grad_neigh))
    return output, grad_features, grad_self, grad_neigh, grad_bias.reshape(cols)


def solution(mesh):
    placed = (
        P("dom", "feat"),
        P("feat", None),
        P("feat", None),
        P("feat"),
        P("dom", "feat"),
        P("dom", None, None, None),
        P("dom", None),
        P("dom"),
        P("dom", None, None),
        P("dom", None, None),
        P("dom", None, None),
        P("dom", None),
        P("dom", None),
        P("dom", None),
    )
    return jax.shard_map(
        on_device,
        mesh=mesh,
        in_specs=placed,
        out_specs=(P("dom", "feat"), P("dom", "feat"), P("feat", None), P("feat", None), P("feat")),
        check_vma=False,
    )
```

```python
import functools
import math

import jax
import jax.numpy as jnp
from jax import lax
from jax.experimental import pallas as pl
from jax.experimental.pallas import tpu as pltpu
from jax.sharding import PartitionSpec as P

BF = jnp.bfloat16
F32 = jnp.float32


def slot_places(peers, slots, width):
    lanes = peers * width
    lane = lax.broadcasted_iota(jnp.int32, (slots, lanes), 1)
    slot = lax.broadcasted_iota(jnp.int32, (slots, lanes), 0)
    return jnp.where(lane % width == slot, 1.0, 0.0).astype(BF)


def spread_rows(table, width, place=None):
    peers, slots = table.shape
    lanes = peers * width
    if place is None:
        place = slot_places(peers, slots, width)
    wide = jnp.dot(table.astype(BF), place, preferred_element_type=F32)
    peer = lax.broadcasted_iota(jnp.int32, (peers, lanes), 0)
    at = lax.broadcasted_iota(jnp.int32, (peers, lanes), 1)
    return jnp.sum(jnp.where(at // width == peer, wide, 0.0), axis=0, keepdims=True)


def source_matrix(send, hubs, rows, width, place=None):
    peers, slots = send.shape
    hub_here = hubs.shape[1]
    lanes = peers * width
    lane = lax.broadcasted_iota(jnp.int32, (1, lanes), 1) % width
    index = spread_rows(send.astype(F32), width, place)
    for k in range(hub_here):
        index = jnp.where(lane == slots + k, hubs[0:1, k : k + 1].astype(F32), index)
    index = jnp.where(lane < slots + hub_here, index, -1.0)
    row = lax.broadcasted_iota(jnp.int32, (rows, lanes), 0).astype(F32)
    return jnp.where(row == index, 1.0, 0.0).astype(BF)


def send_kernel(
    width, x_ref, cot_ref, ws_ref, wn_ref, bias_ref, send_ref, hub_ref, pos_ref, live_ref, tile_ref, dest_ref, gw_ref, hw_ref,
    out_ref, pack_ref, send_v, hub_v, pos_v, live_v, tile_v, dest_v, gw_v, hw_v, bias_v, place_ref, taken_ref, sems,
):
    rows, cols = x_ref.shape
    depth, full = ws_ref.shape
    blocks = full // cols
    base = 2 * blocks * depth
    moves = [
        (send_ref, send_v),
        (hub_ref, hub_v),
        (x_ref, pack_ref.at[base : base + rows, :]),
        (bias_ref, bias_v),
        (cot_ref, pack_ref.at[base + rows : base + 2 * rows, :]),
    ]
    for kind, w_ref in enumerate((ws_ref, wn_ref)):
        for j in range(blocks):
            at = (kind * blocks + j) * depth
            moves.append((w_ref.at[:, j * cols : (j + 1) * cols], pack_ref.at[at : at + depth, :]))
    moves += [
        (pos_ref, pos_v), (live_ref, live_v), (tile_ref, tile_v), (dest_ref, dest_v),
        (gw_ref, gw_v), (hw_ref, hw_v),
    ]
    copies = [pltpu.make_async_copy(src, dst, sems.at[i]) for i, (src, dst) in enumerate(moves)]
    for copy in copies:
        copy.start()
    peers, slots = send_v.shape[1:]
    place_ref[...] = slot_places(peers, slots, width)
    for copy in copies[:2]:
        copy.wait()
    mark = source_matrix(send_v[0], hub_v[...], rows, width, place_ref[...])
    copies[2].wait()
    kept = out_ref.shape[1]
    half = peers // 2
    for part in range(2):
        taken = lax.dot_general(
            mark[:, part * half * width : (part + 1) * half * width],
            pack_ref[base : base + rows, :],
            (((0,), (0,)), ((), ())),
            preferred_element_type=F32,
        ).astype(BF)
        for q in range(half):
            taken_ref[part * half + q] = taken[q * width : q * width + kept]
        mine = pl.ds(part * half, half)
        copies.append(pltpu.make_async_copy(taken_ref.at[mine], out_ref.at[mine], sems.at[len(copies)]))
        copies[-1].start()
    copies[3].wait()
    pack_ref[base + 2 * rows :, :] = jnp.broadcast_to(bias_v[...], (16, cols))
    for copy in copies[4:]:
        copy.wait()


def mix_kernel(width, count_ref, send_v, hub_v, pos_v, live_v, tile_v, dest_v, gw_v, hw_v, mix_ref, turned_ref, mark_ref):
    rows = mix_ref.shape[0]
    tiles, tile = tile_v.shape[1:3]
    peers, slots = dest_v.shape[1:]
    side = rows // tile
    lanes = peers * width
    hubs = hw_v.shape[0]
    hub_here = hubs // peers
    for r in range(side):
        for c in range(side):
            total = jnp.zeros((tile, tile), BF)
            for t in range(tiles):
                used = jnp.logical_and(pos_v[0:1, t : t + 1] == r * side + c, t < count_ref[...])
                total = jnp.where(used, tile_v[0, t], total)
            mix_ref[r * tile : (r + 1) * tile, c * tile : (c + 1) * tile] = total
    dest = spread_rows(dest_v[0].astype(F32), width)
    coef = spread_rows(gw_v[0], width)
    peer = lax.broadcasted_iota(jnp.int32, (peers, lanes), 0)
    at = lax.broadcasted_iota(jnp.int32, (peers, lanes), 1)
    owner = jnp.where(at // width == peer, 1.0, 0.0).astype(BF)
    limit = jnp.dot(live_v[...].astype(F32).astype(BF), owner, preferred_element_type=F32)
    lane = lax.broadcasted_iota(jnp.int32, (1, lanes), 1) % width
    coef = jnp.where(jnp.logical_and(lane.astype(F32) < limit, lane < slots), coef, 0.0)
    row = lax.broadcasted_iota(jnp.int32, (rows, lanes), 0).astype(F32)
    ghost = jnp.where(row == dest, coef, 0.0)
    hub = lax.broadcasted_iota(jnp.int32, (hubs, lanes), 0)
    at = lax.broadcasted_iota(jnp.int32, (hubs, lanes), 1)
    place = jnp.where(
        jnp.logical_and(at // width == hub // hub_here, at % width == slots + hub % hub_here), 1.0, 0.0
    ).astype(BF)
    hub_mix = lax.dot_general(hw_v[...], place, (((0,), (0,)), ((), ())), preferred_element_type=F32)
    mix_ref[:, rows:] = (ghost + hub_mix).astype(BF)
    turned_ref[...] = mix_ref[...].T
    mark_ref[...] = source_matrix(send_v[0], hub_v[...], rows, width)


def pass_kernel(held_ref, passed_ref):
    pass


def neigh_kernel(x_ref, mix_ref, far_ref, got_ref, neigh_ref, passed_ref, wide_ref):
    rows, cols = x_ref.shape
    lanes = mix_ref.shape[1] - rows
    wide_ref[...] = jnp.zeros_like(wide_ref)
    wide_ref[:, : got_ref.shape[1], :] = got_ref[...]
    total = jnp.dot(mix_ref[:, :rows], x_ref[...], preferred_element_type=F32)
    total = total + jnp.dot(mix_ref[:, rows:], wide_ref[...].reshape(lanes, cols), preferred_element_type=F32)
    neigh_ref[...] = total.astype(BF)


def ghost_rows(slots, hub_here, width, start, peers, turned_ref, neigh_grad, sums):
    rows, cols = neigh_grad.shape
    high = sums.astype(BF).astype(F32)
    line = lax.broadcasted_iota(jnp.int32, (peers * width, cols), 0) % width
    cut = pl.ds(pl.multiple_of(rows + start * width, 16), peers * width)
    away = jnp.dot(turned_ref[cut, :], neigh_grad, preferred_element_type=F32)
    away = jnp.where(line == slots + hub_here, high, away)
    away = jnp.where(line == slots + hub_here + 1, sums - high, away)
    return away.astype(BF)


def dense_kernel(slots, hub_here, feats, width, count, me_ref, side_ref, seat_ref, x_ref, ws_ref, wn_ref, turned_ref, *refs):
    pack_refs, n_refs = refs[:feats], refs[feats : 2 * feats]
    own_ref, cot_ref, slope_ref, sums_ref, mirror_ref = refs[2 * feats : 2 * feats + 5]
    send_refs = refs[2 * feats + 5 : 2 * feats + 5 + count]
    pre_ref, bias_ref = refs[2 * feats + 5 + count :]
    rows, cols = x_ref.shape
    depth, full = ws_ref.shape
    blocks = full // cols
    half = mirror_ref.shape[0]
    share = send_refs[0].shape[-2]
    me = me_ref[0]
    base = 2 * blocks * depth
    left = []
    for d, pack in enumerate(pack_refs):
        owner = me ^ d
        cut = pl.ds(pl.multiple_of(owner * cols, cols), cols)
        cot_ref[:, cut] = pack[base + rows : base + 2 * rows, :]
        bias_ref[:, cut] = pack[base + 2 * rows : base + 2 * rows + 16, :]
        left += [pack[base : base + rows, :], n_refs[d][...]]
    left = jnp.concatenate(left, axis=1)
    into = jnp.zeros((rows, depth), F32)
    span = 2
    for j in range(0, blocks, span):
        right = [
            jnp.concatenate([pack[(kind * blocks + i) * depth : (kind * blocks + i + 1) * depth, :] for i in range(j, j + span)], axis=1)
            for pack in pack_refs
            for kind in range(2)
        ]
        cut = slice(j * cols, (j + span) * cols)
        pre = jnp.dot(left, jnp.concatenate(right, axis=0), preferred_element_type=F32)
        pre = pre + bias_ref[0:1, cut].astype(F32)
        pre_ref[:, cut] = pre
        sig = jax.nn.sigmoid(pre)
        grad = (cot_ref[:, cut].astype(F32) * sig * (1.0 + pre * (1.0 - sig))).astype(BF)
        cot_ref[:, cut] = grad
        into = into + lax.dot_general(
            grad, wn_ref[:, cut], (((1,), (1,)), ((), ())), preferred_element_type=F32
        )
    mine = pl.ds(pl.multiple_of(me * cols, cols), cols)
    own_ref[...] = pre_ref[:, mine]
    neigh_grad = into.astype(BF)
    slope_ref[...] = neigh_grad
    sums = jnp.sum(cot_ref[:, mine].astype(F32), axis=0, keepdims=True)
    sums_ref[...] = sums
    there = half - side_ref[0] * half
    pair = jnp.concatenate([x_ref[...], n_refs[0][...]], axis=1).T
    if count > 1:
        for k, ref in enumerate(send_refs):
            peer = seat_ref[0] ^ k
            away = ghost_rows(slots, hub_here, width, there + peer, 1, turned_ref, neigh_grad, sums)
            mirror_ref[k] = away[: mirror_ref.shape[1]]
            block = cot_ref[:, pl.ds(pl.multiple_of(peer * cols, cols), cols)]
            ref[...] = jnp.dot(pair, block, preferred_element_type=F32).astype(BF)
        return
    send_ref = send_refs[0]
    away = ghost_rows(slots, hub_here, width, there, half, turned_ref, neigh_grad, sums).reshape(half, width, cols)
    mirror_ref[...] = away[:, : mirror_ref.shape[1]]
    weights = jnp.dot(pair, cot_ref[...], preferred_element_type=F32).astype(BF)
    step = min(share, depth)
    for j in range(blocks):
        for kind in range(2):
            block = weights[kind * depth : (kind + 1) * depth, j * cols : (j + 1) * cols]
            for part in range(depth // step):
                at = (j * 2 + kind) * depth + part * step
                low = at % share
                send_ref[at // share, low : low + step, :] = block[part * step : (part + 1) * step]


def seated(refs, seat):
    if len(refs) == 1:
        return [(j, refs[0].at[j]) for j in range(refs[0].shape[0])]
    return [(seat ^ k, ref) for k, ref in enumerate(refs)]


def side_kernel(
    slots, hub_here, count, side_ref, seat_ref, own_ref, grad_ref, slope_ref, sums_ref, turned_ref, ws_ref,
    out_ref, back_ref, ghost_ref,
):
    own = own_ref[...]
    out_ref[...] = (own * jax.nn.sigmoid(own)).astype(BF)
    rows, cols = own.shape
    half, width = ghost_ref.shape[:2]
    slope, sums = slope_ref[...], sums_ref[...]
    back = lax.dot_general(grad_ref[...], ws_ref[...], (((1,), (1,)), ((), ())), preferred_element_type=F32)
    back_ref[...] = back + jnp.dot(turned_ref[:rows, :], slope, preferred_element_type=F32)
    here = side_ref[0] * half
    if count > 1:
        for k in range(half):
            peer = here + (seat_ref[0] ^ k)
            ghost_ref[k] = ghost_rows(slots, hub_here, width, peer, 1, turned_ref, slope, sums)
        return
    ghost_ref[...] = ghost_rows(slots, hub_here, width, here, half, turned_ref, slope, sums).reshape(half, width, cols)


def sum_kernel(stored_ref, *refs):
    got_refs, sum_ref = refs[:-1], refs[-1]
    total = jnp.zeros(sum_ref.shape, F32)
    for got_ref in got_refs if len(got_refs) > 1 else [got_refs[0].at[j] for j in range(got_refs[0].shape[0])]:
        total = total + got_ref[...].astype(F32)
    sum_ref[...] = total.astype(BF)


def deal_kernel(ghost_ref, mirror_ref, *out_refs):
    width = ghost_ref.shape[1]
    for k in range(ghost_ref.shape[0]):
        out_ref = out_refs[k] if len(out_refs) > 1 else out_refs[0].at[k]
        out_ref[:width, :] = ghost_ref[k]
        out_ref[width:, :] = jnp.zeros(ghost_ref.shape[1:], BF)
        out_ref[width : width + mirror_ref.shape[1], :] = mirror_ref[k]


def total_kernel(own_ref, other_ref, part_ref):
    total = (own_ref[...].astype(F32) + other_ref[...].astype(F32)).astype(BF)
    part_ref[...] = jnp.broadcast_to(total, part_ref.shape)


def near_rows(slots, hub_here, start, mark_ref, got_ref):
    half, width, cols = got_ref.shape
    cut = pl.ds(pl.multiple_of(start * width, 128), half * width)
    added = jnp.dot(mark_ref[:, cut], got_ref[...].reshape(half * width, cols), preferred_element_type=F32)
    first = slots + hub_here
    bias = jnp.zeros((2, cols), F32)
    for j in range(half):
        bias = bias + got_ref[j, first : first + 2, :].astype(F32)
    return added, jnp.sum(bias, axis=0, keepdims=True)


def grad_kernel(scale, slots, hub_here, side_ref, seat_ref, back_ref, mark_ref, *refs):
    got_refs, (grad_ref, bias_ref, near_ref, far_ref) = refs[:-4], refs[-4:]
    half, width = near_ref.shape[:2]
    for j, got_ref in seated(got_refs[::-1], seat_ref[0]):
        near_ref[j] = got_ref[:width, :]
        far_ref[j] = got_ref[width:, :]
    here = side_ref[0] * half
    near, near_bias = near_rows(slots, hub_here, here, mark_ref, near_ref)
    far, far_bias = near_rows(slots, hub_here, half - here, mark_ref, far_ref)
    grad_ref[...] = (back_ref[...] + near + far).astype(BF)
    bias_ref[...] = (near_bias + far_bias) * scale


def write_blocks(scale, parts, self_ref, neigh_ref, wide_ref, sems):
    depth, full = self_ref.shape
    cols = wide_ref.shape[-1]
    copies = []
    for at, (j, part) in enumerate(parts):
        wide_ref[at] = part.astype(F32) * scale
        cut = pl.ds(pl.multiple_of(j * cols, cols), cols)
        for kind, out_ref in enumerate((self_ref, neigh_ref)):
            copy = pltpu.make_async_copy(
                wide_ref.at[at, kind * depth : (kind + 1) * depth, :], out_ref.at[:, cut], sems.at[2 * at + kind]
            )
            copy.start()
            copies.append(copy)
    for copy in copies:
        copy.wait()


def spread_kernel(scale, seat_ref, *refs):
    got_refs, (self_ref, neigh_ref, wide_ref, sems) = refs[:-4], refs[-4:]
    depth, full = self_ref.shape
    cols = wide_ref.shape[-1]
    if len(got_refs) > 1:
        parts = [(j, ref[...]) for j, ref in seated(got_refs, seat_ref[0])]
    else:
        whole = got_refs[0][...].reshape(2 * full // cols * depth, cols)
        parts = [(j, whole[2 * j * depth : 2 * (j + 1) * depth]) for j in range(full // cols)]
    write_blocks(scale, parts, self_ref, neigh_ref, wide_ref, sems)


def finish_kernel(scale, k, seat_ref, got_ref, begun_self_ref, begun_neigh_ref, self_ref, neigh_ref, wide_ref, sems):
    write_blocks(scale, [(seat_ref[0] ^ k, got_ref[...])], self_ref, neigh_ref, wide_ref, sems)


VMEM = pl.BlockSpec(memory_space=pltpu.VMEM)
SMEM = pl.BlockSpec(memory_space=pltpu.SMEM)
ANY = pl.BlockSpec(memory_space=pl.ANY)
HBM = pl.BlockSpec(memory_space=pltpu.HBM)
PARAMS = pltpu.CompilerParams(vmem_limit_bytes=40 * 1024 * 1024)


def shape(dims, kind):
    return jax.ShapeDtypeStruct(dims, kind)


def partner(block, axis, k):
    return lax.ppermute(block, axis, [(i, i ^ k) for i in range(lax.axis_size(axis))])


def exchange(blocks, groups=None):
    return lax.all_to_all(blocks, "dom", split_axis=0, concat_axis=0, axis_index_groups=groups, tiled=True)


def swap(blocks):
    return [blocks[0]] + [partner(block, "dom", k) for k, block in enumerate(blocks) if k]


def on_device(
    features,
    w_self,
    w_neigh,
    bias,
    cotangent,
    tile_vals,
    tile_pos,
    tile_count,
    send_rows,
    recv_dest,
    ghost_weight,
    recv_count,
    hub_rows,
    hub_weight,
):
    rows, cols = features.shape
    depth, full = w_self.shape
    blocks = full // cols
    peers, slots = send_rows.shape[1:]
    hub_here = hub_rows.shape[-1]
    width = -(-(slots + hub_here + 2) // 16) * 16
    sent = -(-(slots + hub_here + 2) // 8) * 8
    lanes = peers * width
    half = peers // 2
    share = 2 * blocks * depth // half
    direct = half == blocks
    count = half if direct else 1
    halves = [list(range(half)), list(range(half, peers))]
    scale = 1.0 / math.sqrt(peers * rows)
    feats = lax.axis_size("feat")
    me = lax.axis_index("feat").astype(jnp.int32).reshape(1)
    side = (lax.axis_index("dom") >= half).astype(jnp.int32).reshape(1)
    seat = lax.rem(lax.axis_index("dom"), half).astype(jnp.int32).reshape(1)
    pack_rows = 2 * blocks * depth + 2 * rows + 16

    def pinned(*arrays):
        return [pltpu.with_memory_space_constraint(a, pltpu.HBM) for a in arrays]

    first = pinned(features, cotangent, w_self, w_neigh, bias.reshape(1, cols), send_rows, hub_rows)
    edges = pinned(tile_pos, recv_count, tile_vals, recv_dest, ghost_weight, hub_weight.T)
    moved = (send_rows, hub_rows, *edges)
    outgoing, pack, *moved = pl.pallas_call(
        functools.partial(send_kernel, width),
        out_shape=(
            shape((peers, sent, cols), BF),
            shape((pack_rows, cols), BF),
            *(shape(a.shape, a.dtype) for a in moved),
        ),
        in_specs=[HBM] * (len(first) + len(edges)),
        out_specs=(HBM,) + (VMEM,) * (1 + len(moved)),
        scratch_shapes=[
            pltpu.VMEM((1, cols), BF),
            pltpu.VMEM((slots, lanes), BF),
            pltpu.VMEM((peers, sent, cols), BF),
            pltpu.SemaphoreType.DMA((13 + 2 * blocks,)),
        ],
        compiler_params=PARAMS,
    )(*first, *edges)

    far = partner(pack, "feat", 2)
    near = partner(pack, "feat", 1)
    incoming = exchange(outgoing)
    mix, turned, mark = pl.pallas_call(
        functools.partial(mix_kernel, width),
        out_shape=(
            shape((rows, rows + lanes), BF),
            shape((rows + lanes, rows), BF),
            shape((rows, lanes), BF),
        ),
        in_specs=[VMEM] * (1 + len(moved)),
        out_specs=(VMEM,) * 3,
        compiler_params=PARAMS,
        cost_estimate=pl.CostEstimate(flops=10**8, bytes_accessed=3 * 10**6, transcendentals=0),
    )(tile_count.reshape(1, 1), *moved)
    neigh, far = pl.pallas_call(
        neigh_kernel,
        out_shape=(shape((rows, cols), BF), shape((pack_rows, cols), BF)),
        in_specs=[VMEM, VMEM, ANY, VMEM],
        out_specs=(VMEM, ANY),
        input_output_aliases={2: 1},
        scratch_shapes=[pltpu.VMEM((peers, width, cols), BF)],
        compiler_params=PARAMS,
    )(features, mix, far, incoming)
    last = partner(far, "feat", 1)
    far_neigh = pl.pallas_call(
        pass_kernel,
        out_shape=shape((rows, cols), BF),
        in_specs=[ANY],
        out_specs=ANY,
        input_output_aliases={0: 0},
        compiler_params=PARAMS,
        cost_estimate=pl.CostEstimate(flops=10**10, bytes_accessed=10**7, transcendentals=0),
    )(partner(neigh, "feat", 2))
    every = [neigh, partner(neigh, "feat", 1), far_neigh, partner(far_neigh, "feat", 1)]

    own, grad, slope, sums, mirror, *returned = pl.pallas_call(
        functools.partial(dense_kernel, slots, hub_here, feats, width, count),
        out_shape=(
            shape((rows, cols), F32),
            shape((rows, full), BF),
            shape((rows, cols), BF),
            shape((1, cols), F32),
            shape((half, sent, cols), BF),
            *([shape((share, cols), BF)] * half if direct else [shape((half, share, cols), BF)]),
        ),
        in_specs=[SMEM] * 3 + [VMEM] * (4 + 2 * feats),
        out_specs=(VMEM,) * (5 + count),
        scratch_shapes=[
            pltpu.VMEM((rows, full), F32),
            pltpu.VMEM((16, full), BF),
        ],
        compiler_params=PARAMS,
    )(me, side, seat, features, w_self, w_neigh, turned, pack, near, far, last, *every)

    arrived = swap(returned)[::-1] if direct else [exchange(returned[0], halves)]
    mirror = partner(mirror, "dom", half)
    output, back, ghosts = pl.pallas_call(
        functools.partial(side_kernel, slots, hub_here, count),
        out_shape=(shape((rows, cols), BF), shape((rows, cols), F32), shape((half, width, cols), BF)),
        in_specs=[SMEM] * 2 + [VMEM] * 6,
        out_specs=(VMEM,) * 3,
        compiler_params=PARAMS,
        cost_estimate=pl.CostEstimate(flops=10**8, bytes_accessed=10**6, transcendentals=0),
    )(side, seat, own, grad, slope, sums, turned, w_self)
    half_sum = pl.pallas_call(
        sum_kernel,
        out_shape=shape((share, cols), BF),
        in_specs=[HBM] + [VMEM] * count,
        out_specs=VMEM,
        compiler_params=PARAMS,
    )(*pinned(output), *arrived)
    other_sum = partner(half_sum, "dom", half)
    dealt = pl.pallas_call(
        deal_kernel,
        out_shape=[shape((2 * width, cols), BF)] * half if direct else [shape((half, 2 * width, cols), BF)],
        in_specs=[VMEM] * 2,
        out_specs=[VMEM] * count,
        compiler_params=PARAMS,
    )(ghosts, mirror)
    dealt = swap(dealt) if direct else [exchange(dealt[0], halves)]
    part = pl.pallas_call(
        total_kernel,
        out_shape=shape((share, cols) if direct else (half, share, cols), BF),
        in_specs=[VMEM, VMEM],
        out_specs=VMEM,
        compiler_params=PARAMS,
    )(half_sum, other_sum)
    parts = swap([part] * half) if direct else [exchange(part, halves)]
    grad_features, grad_bias = pl.pallas_call(
        functools.partial(grad_kernel, scale, slots, hub_here),
        out_shape=(shape((rows, cols), BF), shape((1, cols), F32)),
        in_specs=[SMEM] * 2 + [VMEM] * (2 + count),
        out_specs=(VMEM,) * 2,
        scratch_shapes=[pltpu.VMEM((half, width, cols), BF)] * 2,
        compiler_params=PARAMS,
        cost_estimate=pl.CostEstimate(flops=2 * 10**9, bytes_accessed=10**6, transcendentals=0),
    )(side, seat, back, mark, *dealt[::-1])
    early = half - 1 if direct else 1
    grad_self, grad_neigh = pl.pallas_call(
        functools.partial(spread_kernel, scale),
        out_shape=(shape((depth, full), F32), shape((depth, full), F32)),
        in_specs=[SMEM] + [VMEM] * early,
        out_specs=(HBM,) * 2,
        scratch_shapes=[pltpu.VMEM((blocks, 2 * depth, cols), F32), pltpu.SemaphoreType.DMA((2 * blocks,))],
        compiler_params=PARAMS,
    )(seat, *parts[:early])
    if direct:
        grad_self, grad_neigh = pl.pallas_call(
            functools.partial(finish_kernel, scale, early),
            out_shape=(shape((depth, full), F32), shape((depth, full), F32)),
            in_specs=[SMEM, VMEM, HBM, HBM],
            out_specs=(HBM,) * 2,
            scratch_shapes=[pltpu.VMEM((1, 2 * depth, cols), F32), pltpu.SemaphoreType.DMA((2,))],
            input_output_aliases={2: 0, 3: 1},
            compiler_params=PARAMS,
        )(seat, parts[early], *pinned(grad_self, grad_neigh))
    return output, grad_features, grad_self, grad_neigh, grad_bias.reshape(cols)


def solution(mesh):
    placed = (
        P("dom", "feat"),
        P("feat", None),
        P("feat", None),
        P("feat"),
        P("dom", "feat"),
        P("dom", None, None, None),
        P("dom", None),
        P("dom"),
        P("dom", None, None),
        P("dom", None, None),
        P("dom", None, None),
        P("dom", None),
        P("dom", None),
        P("dom", None),
    )
    return jax.shard_map(
        on_device,
        mesh=mesh,
        in_specs=placed,
        out_specs=(P("dom", "feat"), P("dom", "feat"), P("feat", None), P("feat", None), P("feat")),
        check_vma=False,
    )
```

```python
import functools
import math

import jax
import jax.numpy as jnp
from jax import lax
from jax.experimental import pallas as pl
from jax.experimental.pallas import tpu as pltpu
from jax.sharding import PartitionSpec as P

BF = jnp.bfloat16
F32 = jnp.float32


def slot_places(peers, slots, width):
    lanes = peers * width
    lane = lax.broadcasted_iota(jnp.int32, (slots, lanes), 1)
    slot = lax.broadcasted_iota(jnp.int32, (slots, lanes), 0)
    return jnp.where(lane % width == slot, 1.0, 0.0).astype(BF)


def spread_rows(table, width, place=None):
    peers, slots = table.shape
    lanes = peers * width
    if place is None:
        place = slot_places(peers, slots, width)
    wide = jnp.dot(table.astype(BF), place, preferred_element_type=F32)
    peer = lax.broadcasted_iota(jnp.int32, (peers, lanes), 0)
    at = lax.broadcasted_iota(jnp.int32, (peers, lanes), 1)
    return jnp.sum(jnp.where(at // width == peer, wide, 0.0), axis=0, keepdims=True)


def source_matrix(send, hubs, rows, width, place=None):
    peers, slots = send.shape
    hub_here = hubs.shape[1]
    lanes = peers * width
    lane = lax.broadcasted_iota(jnp.int32, (1, lanes), 1) % width
    index = spread_rows(send.astype(F32), width, place)
    for k in range(hub_here):
        index = jnp.where(lane == slots + k, hubs[0:1, k : k + 1].astype(F32), index)
    index = jnp.where(lane < slots + hub_here, index, -1.0)
    row = lax.broadcasted_iota(jnp.int32, (rows, lanes), 0).astype(F32)
    return jnp.where(row == index, 1.0, 0.0).astype(BF)


def send_kernel(
    width, x_ref, cot_ref, ws_ref, wn_ref, bias_ref, send_ref, hub_ref, pos_ref, live_ref, tile_ref, dest_ref, gw_ref, hw_ref,
    out_ref, pack_ref, send_v, hub_v, pos_v, live_v, tile_v, dest_v, gw_v, hw_v, bias_v, place_ref, taken_ref, sems,
):
    rows, cols = x_ref.shape
    depth, full = ws_ref.shape
    blocks = full // cols
    base = 2 * blocks * depth
    moves = [
        (send_ref, send_v),
        (hub_ref, hub_v),
        (x_ref, pack_ref.at[base : base + rows, :]),
        (bias_ref, bias_v),
        (cot_ref, pack_ref.at[base + rows : base + 2 * rows, :]),
    ]
    for kind, w_ref in enumerate((ws_ref, wn_ref)):
        for j in range(blocks):
            at = (kind * blocks + j) * depth
            moves.append((w_ref.at[:, j * cols : (j + 1) * cols], pack_ref.at[at : at + depth, :]))
    moves += [
        (pos_ref, pos_v), (live_ref, live_v), (tile_ref, tile_v), (dest_ref, dest_v),
        (gw_ref, gw_v), (hw_ref, hw_v),
    ]
    copies = [pltpu.make_async_copy(src, dst, sems.at[i]) for i, (src, dst) in enumerate(moves)]
    for copy in copies:
        copy.start()
    peers, slots = send_v.shape[1:]
    place_ref[...] = slot_places(peers, slots, width)
    for copy in copies[:2]:
        copy.wait()
    mark = source_matrix(send_v[0], hub_v[...], rows, width, place_ref[...])
    copies[2].wait()
    kept = out_ref.shape[1]
    half = peers // 2
    for part in range(2):
        taken = lax.dot_general(
            mark[:, part * half * width : (part + 1) * half * width],
            pack_ref[base : base + rows, :],
            (((0,), (0,)), ((), ())),
            preferred_element_type=F32,
        ).astype(BF)
        for q in range(half):
            taken_ref[part * half + q] = taken[q * width : q * width + kept]
        mine = pl.ds(part * half, half)
        copies.append(pltpu.make_async_copy(taken_ref.at[mine], out_ref.at[mine], sems.at[len(copies)]))
        copies[-1].start()
    copies[3].wait()
    pack_ref[base + 2 * rows :, :] = jnp.broadcast_to(bias_v[...], (16, cols))
    for copy in copies[4:]:
        copy.wait()


def mix_kernel(width, count_ref, send_v, hub_v, pos_v, live_v, tile_v, dest_v, gw_v, hw_v, mix_ref, turned_ref, mark_ref):
    rows = mix_ref.shape[0]
    tiles, tile = tile_v.shape[1:3]
    peers, slots = dest_v.shape[1:]
    side = rows // tile
    lanes = peers * width
    hubs = hw_v.shape[0]
    hub_here = hubs // peers
    for r in range(side):
        for c in range(side):
            total = jnp.zeros((tile, tile), BF)
            for t in range(tiles):
                used = jnp.logical_and(pos_v[0:1, t : t + 1] == r * side + c, t < count_ref[...])
                total = jnp.where(used, tile_v[0, t], total)
            mix_ref[r * tile : (r + 1) * tile, c * tile : (c + 1) * tile] = total
    dest = spread_rows(dest_v[0].astype(F32), width)
    coef = spread_rows(gw_v[0], width)
    peer = lax.broadcasted_iota(jnp.int32, (peers, lanes), 0)
    at = lax.broadcasted_iota(jnp.int32, (peers, lanes), 1)
    owner = jnp.where(at // width == peer, 1.0, 0.0).astype(BF)
    limit = jnp.dot(live_v[...].astype(F32).astype(BF), owner, preferred_element_type=F32)
    lane = lax.broadcasted_iota(jnp.int32, (1, lanes), 1) % width
    coef = jnp.where(jnp.logical_and(lane.astype(F32) < limit, lane < slots), coef, 0.0)
    row = lax.broadcasted_iota(jnp.int32, (rows, lanes), 0).astype(F32)
    ghost = jnp.where(row == dest, coef, 0.0)
    hub = lax.broadcasted_iota(jnp.int32, (hubs, lanes), 0)
    at = lax.broadcasted_iota(jnp.int32, (hubs, lanes), 1)
    place = jnp.where(
        jnp.logical_and(at // width == hub // hub_here, at % width == slots + hub % hub_here), 1.0, 0.0
    ).astype(BF)
    hub_mix = lax.dot_general(hw_v[...], place, (((0,), (0,)), ((), ())), preferred_element_type=F32)
    mix_ref[:, rows:] = (ghost + hub_mix).astype(BF)
    turned_ref[...] = mix_ref[...].T
    mark_ref[...] = source_matrix(send_v[0], hub_v[...], rows, width)


def pass_kernel(held_ref, passed_ref):
    pass


def neigh_kernel(x_ref, mix_ref, far_ref, got_ref, neigh_ref, passed_ref, wide_ref):
    rows, cols = x_ref.shape
    lanes = mix_ref.shape[1] - rows
    wide_ref[...] = jnp.zeros_like(wide_ref)
    wide_ref[:, : got_ref.shape[1], :] = got_ref[...]
    total = jnp.dot(mix_ref[:, :rows], x_ref[...], preferred_element_type=F32)
    total = total + jnp.dot(mix_ref[:, rows:], wide_ref[...].reshape(lanes, cols), preferred_element_type=F32)
    neigh_ref[...] = total.astype(BF)


def ghost_rows(slots, hub_here, width, start, peers, turned_ref, neigh_grad, sums):
    rows, cols = neigh_grad.shape
    high = sums.astype(BF).astype(F32)
    line = lax.broadcasted_iota(jnp.int32, (peers * width, cols), 0) % width
    cut = pl.ds(pl.multiple_of(rows + start * width, 16), peers * width)
    away = jnp.dot(turned_ref[cut, :], neigh_grad, preferred_element_type=F32)
    away = jnp.where(line == slots + hub_here, high, away)
    away = jnp.where(line == slots + hub_here + 1, sums - high, away)
    return away.astype(BF)


def dense_kernel(slots, hub_here, feats, width, count, me_ref, side_ref, seat_ref, x_ref, ws_ref, wn_ref, turned_ref, *refs):
    pack_refs, n_refs = refs[:feats], refs[feats : 2 * feats]
    own_ref, cot_ref, slope_ref, sums_ref, mirror_ref = refs[2 * feats : 2 * feats + 5]
    send_refs = refs[2 * feats + 5 : 2 * feats + 5 + count]
    pre_ref, bias_ref = refs[2 * feats + 5 + count :]
    rows, cols = x_ref.shape
    depth, full = ws_ref.shape
    blocks = full // cols
    half = mirror_ref.shape[0]
    share = send_refs[0].shape[-2]
    me = me_ref[0]
    base = 2 * blocks * depth
    left = []
    for d, pack in enumerate(pack_refs):
        owner = me ^ d
        cut = pl.ds(pl.multiple_of(owner * cols, cols), cols)
        cot_ref[:, cut] = pack[base + rows : base + 2 * rows, :]
        bias_ref[:, cut] = pack[base + 2 * rows : base + 2 * rows + 16, :]
        left += [pack[base : base + rows, :], n_refs[d][...]]
    left = jnp.concatenate(left, axis=1)
    into = jnp.zeros((rows, depth), F32)
    span = 2
    for j in range(0, blocks, span):
        right = [
            jnp.concatenate([pack[(kind * blocks + i) * depth : (kind * blocks + i + 1) * depth, :] for i in range(j, j + span)], axis=1)
            for pack in pack_refs
            for kind in range(2)
        ]
        cut = slice(j * cols, (j + span) * cols)
        pre = jnp.dot(left, jnp.concatenate(right, axis=0), preferred_element_type=F32)
        pre = pre + bias_ref[0:1, cut].astype(F32)
        pre_ref[:, cut] = pre
        sig = jax.nn.sigmoid(pre)
        grad = (cot_ref[:, cut].astype(F32) * sig * (1.0 + pre * (1.0 - sig))).astype(BF)
        cot_ref[:, cut] = grad
        into = into + lax.dot_general(
            grad, wn_ref[:, cut], (((1,), (1,)), ((), ())), preferred_element_type=F32
        )
    mine = pl.ds(pl.multiple_of(me * cols, cols), cols)
    own_ref[...] = pre_ref[:, mine]
    neigh_grad = into.astype(BF)
    slope_ref[...] = neigh_grad
    sums = jnp.sum(cot_ref[:, mine].astype(F32), axis=0, keepdims=True)
    sums_ref[...] = sums
    there = half - side_ref[0] * half
    pair = jnp.concatenate([x_ref[...], n_refs[0][...]], axis=1).T
    if count > 1:
        for k, ref in enumerate(send_refs):
            peer = seat_ref[0] ^ k
            away = ghost_rows(slots, hub_here, width, there + peer, 1, turned_ref, neigh_grad, sums)
            mirror_ref[k] = away[: mirror_ref.shape[1]]
            block = cot_ref[:, pl.ds(pl.multiple_of(peer * cols, cols), cols)]
            ref[...] = jnp.dot(pair, block, preferred_element_type=F32).astype(BF)
        return
    send_ref = send_refs[0]
    away = ghost_rows(slots, hub_here, width, there, half, turned_ref, neigh_grad, sums).reshape(half, width, cols)
    mirror_ref[...] = away[:, : mirror_ref.shape[1]]
    weights = jnp.dot(pair, cot_ref[...], preferred_element_type=F32).astype(BF)
    step = min(share, depth)
    for j in range(blocks):
        for kind in range(2):
            block = weights[kind * depth : (kind + 1) * depth, j * cols : (j + 1) * cols]
            for part in range(depth // step):
                at = (j * 2 + kind) * depth + part * step
                low = at % share
                send_ref[at // share, low : low + step, :] = block[part * step : (part + 1) * step]


def seated(refs, seat):
    if len(refs) == 1:
        return [(j, refs[0].at[j]) for j in range(refs[0].shape[0])]
    return [(seat ^ k, ref) for k, ref in enumerate(refs)]


def side_kernel(
    slots, hub_here, count, side_ref, seat_ref, own_ref, grad_ref, slope_ref, sums_ref, turned_ref, ws_ref,
    out_ref, back_ref, ghost_ref,
):
    own = own_ref[...]
    out_ref[...] = (own * jax.nn.sigmoid(own)).astype(BF)
    rows, cols = own.shape
    half, width = ghost_ref.shape[:2]
    slope, sums = slope_ref[...], sums_ref[...]
    back = lax.dot_general(grad_ref[...], ws_ref[...], (((1,), (1,)), ((), ())), preferred_element_type=F32)
    back_ref[...] = back + jnp.dot(turned_ref[:rows, :], slope, preferred_element_type=F32)
    here = side_ref[0] * half
    if count > 1:
        for k in range(half):
            peer = here + (seat_ref[0] ^ k)
            ghost_ref[k] = ghost_rows(slots, hub_here, width, peer, 1, turned_ref, slope, sums)
        return
    ghost_ref[...] = ghost_rows(slots, hub_here, width, here, half, turned_ref, slope, sums).reshape(half, width, cols)


def sum_kernel(stored_ref, *refs):
    got_refs, sum_ref = refs[:-1], refs[-1]
    total = jnp.zeros(sum_ref.shape, F32)
    for got_ref in got_refs if len(got_refs) > 1 else [got_refs[0].at[j] for j in range(got_refs[0].shape[0])]:
        total = total + got_ref[...].astype(F32)
    sum_ref[...] = total.astype(BF)


def deal_kernel(ghost_ref, mirror_ref, *out_refs):
    width = ghost_ref.shape[1]
    for k in range(ghost_ref.shape[0]):
        out_ref = out_refs[k] if len(out_refs) > 1 else out_refs[0].at[k]
        out_ref[:width, :] = ghost_ref[k]
        out_ref[width:, :] = jnp.zeros(ghost_ref.shape[1:], BF)
        out_ref[width : width + mirror_ref.shape[1], :] = mirror_ref[k]


def total_kernel(own_ref, other_ref, part_ref):
    total = (own_ref[...].astype(F32) + other_ref[...].astype(F32)).astype(BF)
    part_ref[...] = jnp.broadcast_to(total, part_ref.shape)


def near_rows(slots, hub_here, start, mark_ref, got_ref):
    half, width, cols = got_ref.shape
    cut = pl.ds(pl.multiple_of(start * width, 128), half * width)
    added = jnp.dot(mark_ref[:, cut], got_ref[...].reshape(half * width, cols), preferred_element_type=F32)
    first = slots + hub_here
    bias = jnp.zeros((2, cols), F32)
    for j in range(half):
        bias = bias + got_ref[j, first : first + 2, :].astype(F32)
    return added, jnp.sum(bias, axis=0, keepdims=True)


def grad_kernel(scale, slots, hub_here, side_ref, seat_ref, back_ref, mark_ref, *refs):
    got_refs, (grad_ref, bias_ref, near_ref, far_ref) = refs[:-4], refs[-4:]
    half, width = near_ref.shape[:2]
    for j, got_ref in seated(got_refs, seat_ref[0]):
        near_ref[j] = got_ref[:width, :]
        far_ref[j] = got_ref[width:, :]
    here = side_ref[0] * half
    near, near_bias = near_rows(slots, hub_here, here, mark_ref, near_ref)
    far, far_bias = near_rows(slots, hub_here, half - here, mark_ref, far_ref)
    grad_ref[...] = (back_ref[...] + near + far).astype(BF)
    bias_ref[...] = (near_bias + far_bias) * scale


def write_blocks(scale, parts, self_ref, neigh_ref, wide_ref, sems):
    depth, full = self_ref.shape
    cols = wide_ref.shape[-1]
    copies = []
    for at, (j, part) in enumerate(parts):
        wide_ref[at] = part.astype(F32) * scale
        cut = pl.ds(pl.multiple_of(j * cols, cols), cols)
        for kind, out_ref in enumerate((self_ref, neigh_ref)):
            copy = pltpu.make_async_copy(
                wide_ref.at[at, kind * depth : (kind + 1) * depth, :], out_ref.at[:, cut], sems.at[2 * at + kind]
            )
            copy.start()
            copies.append(copy)
    for copy in copies:
        copy.wait()


def spread_kernel(scale, seat_ref, *refs):
    got_refs, (self_ref, neigh_ref, wide_ref, sems) = refs[:-4], refs[-4:]
    depth, full = self_ref.shape
    cols = wide_ref.shape[-1]
    if len(got_refs) > 1:
        parts = [(j, ref[...]) for j, ref in seated(got_refs[::-1], seat_ref[0])]
    else:
        whole = got_refs[0][...].reshape(2 * full // cols * depth, cols)
        parts = [(j, whole[2 * j * depth : 2 * (j + 1) * depth]) for j in range(full // cols)]
    write_blocks(scale, parts, self_ref, neigh_ref, wide_ref, sems)


def finish_kernel(scale, k, seat_ref, got_ref, begun_self_ref, begun_neigh_ref, self_ref, neigh_ref, wide_ref, sems):
    write_blocks(scale, [(seat_ref[0] ^ k, got_ref[...])], self_ref, neigh_ref, wide_ref, sems)


VMEM = pl.BlockSpec(memory_space=pltpu.VMEM)
SMEM = pl.BlockSpec(memory_space=pltpu.SMEM)
ANY = pl.BlockSpec(memory_space=pl.ANY)
HBM = pl.BlockSpec(memory_space=pltpu.HBM)
PARAMS = pltpu.CompilerParams(vmem_limit_bytes=40 * 1024 * 1024)


def shape(dims, kind):
    return jax.ShapeDtypeStruct(dims, kind)


def partner(block, axis, k):
    return lax.ppermute(block, axis, [(i, i ^ k) for i in range(lax.axis_size(axis))])


def exchange(blocks, groups=None):
    return lax.all_to_all(blocks, "dom", split_axis=0, concat_axis=0, axis_index_groups=groups, tiled=True)


def swap(blocks):
    return [blocks[0]] + [partner(block, "dom", k) for k, block in enumerate(blocks) if k]


def on_device(
    features,
    w_self,
    w_neigh,
    bias,
    cotangent,
    tile_vals,
    tile_pos,
    tile_count,
    send_rows,
    recv_dest,
    ghost_weight,
    recv_count,
    hub_rows,
    hub_weight,
):
    rows, cols = features.shape
    depth, full = w_self.shape
    blocks = full // cols
    peers, slots = send_rows.shape[1:]
    hub_here = hub_rows.shape[-1]
    width = -(-(slots + hub_here + 2) // 16) * 16
    sent = -(-(slots + hub_here + 2) // 8) * 8
    lanes = peers * width
    half = peers // 2
    share = 2 * blocks * depth // half
    direct = half == blocks
    count = half if direct else 1
    halves = [list(range(half)), list(range(half, peers))]
    scale = 1.0 / math.sqrt(peers * rows)
    feats = lax.axis_size("feat")
    me = lax.axis_index("feat").astype(jnp.int32).reshape(1)
    side = (lax.axis_index("dom") >= half).astype(jnp.int32).reshape(1)
    seat = lax.rem(lax.axis_index("dom"), half).astype(jnp.int32).reshape(1)
    pack_rows = 2 * blocks * depth + 2 * rows + 16

    def pinned(*arrays):
        return [pltpu.with_memory_space_constraint(a, pltpu.HBM) for a in arrays]

    first = pinned(features, cotangent, w_self, w_neigh, bias.reshape(1, cols), send_rows, hub_rows)
    edges = pinned(tile_pos, recv_count, tile_vals, recv_dest, ghost_weight, hub_weight.T)
    moved = (send_rows, hub_rows, *edges)
    outgoing, pack, *moved = pl.pallas_call(
        functools.partial(send_kernel, width),
        out_shape=(
            shape((peers, sent, cols), BF),
            shape((pack_rows, cols), BF),
            *(shape(a.shape, a.dtype) for a in moved),
        ),
        in_specs=[HBM] * (len(first) + len(edges)),
        out_specs=(HBM,) + (VMEM,) * (1 + len(moved)),
        scratch_shapes=[
            pltpu.VMEM((1, cols), BF),
            pltpu.VMEM((slots, lanes), BF),
            pltpu.VMEM((peers, sent, cols), BF),
            pltpu.SemaphoreType.DMA((13 + 2 * blocks,)),
        ],
        compiler_params=PARAMS,
    )(*first, *edges)

    far = partner(pack, "feat", 2)
    near = partner(pack, "feat", 1)
    incoming = exchange(outgoing)
    mix, turned, mark = pl.pallas_call(
        functools.partial(mix_kernel, width),
        out_shape=(
            shape((rows, rows + lanes), BF),
            shape((rows + lanes, rows), BF),
            shape((rows, lanes), BF),
        ),
        in_specs=[VMEM] * (1 + len(moved)),
        out_specs=(VMEM,) * 3,
        compiler_params=PARAMS,
        cost_estimate=pl.CostEstimate(flops=10**8, bytes_accessed=3 * 10**6, transcendentals=0),
    )(tile_count.reshape(1, 1), *moved)
    neigh, far = pl.pallas_call(
        neigh_kernel,
        out_shape=(shape((rows, cols), BF), shape((pack_rows, cols), BF)),
        in_specs=[VMEM, VMEM, ANY, VMEM],
        out_specs=(VMEM, ANY),
        input_output_aliases={2: 1},
        scratch_shapes=[pltpu.VMEM((peers, width, cols), BF)],
        compiler_params=PARAMS,
    )(features, mix, far, incoming)
    last = partner(far, "feat", 1)
    far_neigh = pl.pallas_call(
        pass_kernel,
        out_shape=shape((rows, cols), BF),
        in_specs=[ANY],
        out_specs=ANY,
        input_output_aliases={0: 0},
        compiler_params=PARAMS,
        cost_estimate=pl.CostEstimate(flops=10**10, bytes_accessed=10**7, transcendentals=0),
    )(partner(neigh, "feat", 2))
    every = [neigh, partner(neigh, "feat", 1), far_neigh, partner(far_neigh, "feat", 1)]

    own, grad, slope, sums, mirror, *returned = pl.pallas_call(
        functools.partial(dense_kernel, slots, hub_here, feats, width, count),
        out_shape=(
            shape((rows, cols), F32),
            shape((rows, full), BF),
            shape((rows, cols), BF),
            shape((1, cols), F32),
            shape((half, sent, cols), BF),
            *([shape((share, cols), BF)] * half if direct else [shape((half, share, cols), BF)]),
        ),
        in_specs=[SMEM] * 3 + [VMEM] * (4 + 2 * feats),
        out_specs=(VMEM,) * (5 + count),
        scratch_shapes=[
            pltpu.VMEM((rows, full), F32),
            pltpu.VMEM((16, full), BF),
        ],
        compiler_params=PARAMS,
    )(me, side, seat, features, w_self, w_neigh, turned, pack, near, far, last, *every)

    arrived = swap(returned)[::-1] if direct else [exchange(returned[0], halves)]
    mirror = partner(mirror, "dom", half)
    output, back, ghosts = pl.pallas_call(
        functools.partial(side_kernel, slots, hub_here, count),
        out_shape=(shape((rows, cols), BF), shape((rows, cols), F32), shape((half, width, cols), BF)),
        in_specs=[SMEM] * 2 + [VMEM] * 6,
        out_specs=(VMEM,) * 3,
        compiler_params=PARAMS,
        cost_estimate=pl.CostEstimate(flops=10**8, bytes_accessed=10**6, transcendentals=0),
    )(side, seat, own, grad, slope, sums, turned, w_self)
    half_sum = pl.pallas_call(
        sum_kernel,
        out_shape=shape((share, cols), BF),
        in_specs=[HBM] + [VMEM] * count,
        out_specs=VMEM,
        compiler_params=PARAMS,
    )(*pinned(output), *arrived)
    other_sum = partner(half_sum, "dom", half)
    dealt = pl.pallas_call(
        deal_kernel,
        out_shape=[shape((2 * width, cols), BF)] * half if direct else [shape((half, 2 * width, cols), BF)],
        in_specs=[VMEM] * 2,
        out_specs=[VMEM] * count,
        compiler_params=PARAMS,
    )(ghosts, mirror)
    dealt = swap(dealt) if direct else [exchange(dealt[0], halves)]
    part = pl.pallas_call(
        total_kernel,
        out_shape=shape((share, cols) if direct else (half, share, cols), BF),
        in_specs=[VMEM, VMEM],
        out_specs=VMEM,
        compiler_params=PARAMS,
    )(half_sum, other_sum)
    parts = swap([part] * half) if direct else [exchange(part, halves)]
    grad_features, grad_bias = pl.pallas_call(
        functools.partial(grad_kernel, scale, slots, hub_here),
        out_shape=(shape((rows, cols), BF), shape((1, cols), F32)),
        in_specs=[SMEM] * 2 + [VMEM] * (2 + count),
        out_specs=(VMEM,) * 2,
        scratch_shapes=[pltpu.VMEM((half, width, cols), BF)] * 2,
        compiler_params=PARAMS,
        cost_estimate=pl.CostEstimate(flops=2 * 10**9, bytes_accessed=10**6, transcendentals=0),
    )(side, seat, back, mark, *dealt)
    early = half - 1 if direct else 1
    grad_self, grad_neigh = pl.pallas_call(
        functools.partial(spread_kernel, scale),
        out_shape=(shape((depth, full), F32), shape((depth, full), F32)),
        in_specs=[SMEM] + [VMEM] * early,
        out_specs=(HBM,) * 2,
        scratch_shapes=[pltpu.VMEM((blocks, 2 * depth, cols), F32), pltpu.SemaphoreType.DMA((2 * blocks,))],
        compiler_params=PARAMS,
    )(seat, *parts[:early][::-1])
    if direct:
        grad_self, grad_neigh = pl.pallas_call(
            functools.partial(finish_kernel, scale, early),
            out_shape=(shape((depth, full), F32), shape((depth, full), F32)),
            in_specs=[SMEM, VMEM, HBM, HBM],
            out_specs=(HBM,) * 2,
            scratch_shapes=[pltpu.VMEM((1, 2 * depth, cols), F32), pltpu.SemaphoreType.DMA((2,))],
            input_output_aliases={2: 0, 3: 1},
            compiler_params=PARAMS,
        )(seat, parts[early], *pinned(grad_self, grad_neigh))
    return output, grad_features, grad_self, grad_neigh, grad_bias.reshape(cols)


def solution(mesh):
    placed = (
        P("dom", "feat"),
        P("feat", None),
        P("feat", None),
        P("feat"),
        P("dom", "feat"),
        P("dom", None, None, None),
        P("dom", None),
        P("dom"),
        P("dom", None, None),
        P("dom", None, None),
        P("dom", None, None),
        P("dom", None),
        P("dom", None),
        P("dom", None),
    )
    return jax.shard_map(
        on_device,
        mesh=mesh,
        in_specs=placed,
        out_specs=(P("dom", "feat"), P("dom", "feat"), P("feat", None), P("feat", None), P("feat")),
        check_vma=False,
    )
```
